32 devices in a mesh: pipe: 2 (over core), dp: 16 (over z, y, x).
Axes of the slice: x: 2, y: 2, z: 4, core: 2. Of those that a mesh axis runs over, the one named last changes fastest.
Arguments:
- images: bfloat16 [128, 16, 24, 1024], P('dp'), may hold values from -6 to 6
- cotangent: bfloat16 [128, 8, 12, 2048], P('dp'), may hold values from -6 to 6
- heights: int32 [128], P('dp'), may hold values from 4 to 8, as said below
- widths: int32 [128], P('dp'), may hold values from 6 to 12, as said below
- assign: int32 [16, 8], P('dp'), may hold values from 0 to 7, each once within a row
- w_narrow: float32 [12288, 512], P(('pipe', 'dp')), may hold values from -0.09375 to 0.09375
- w_wide: float32 [2048, 2048], P(('pipe', 'dp')), may hold values from -0.1875 to 0.1875
- bn_mid: float32 [8, 512], P(None, ('pipe', 'dp')), may hold values from -1 to 1.6, as said below
- bn_wide: float32 [6, 2048], P(None, ('pipe', 'dp')), may hold values from -1 to 1.6, as said below
- mom_narrow: float32 [12288, 512], P(('pipe', 'dp')), may hold values from -0.015625 to 0.015625
- mom_wide: float32 [2048, 2048], P(('pipe', 'dp')), may hold values from -0.03125 to 0.03125
- mom_bn_mid: float32 [8, 512], P(None, ('pipe', 'dp')), may hold values from -2 to 2
- mom_bn_wide: float32 [6, 2048], P(None, ('pipe', 'dp')), may hold values from -2 to 2
Outputs:
- block_out: bfloat16 [128, 8, 12, 2048], P('dp', None, None, 'pipe')
- grad_input: bfloat16 [128, 16, 24, 1024], P('dp', None, None, 'pipe')
- grad_narrow: float32 [12288, 512], P(('pipe', 'dp'))
- grad_wide: float32 [2048, 2048], P(('pipe', 'dp'))
- grad_bn_mid: float32 [8, 512], P(None, ('pipe', 'dp'))
- grad_bn_wide: float32 [6, 2048], P(None, ('pipe', 'dp'))
- new_mom_narrow: float32 [12288, 512], P(('pipe', 'dp'))
- new_mom_wide: float32 [2048, 2048], P(('pipe', 'dp'))
- new_mom_bn_mid: float32 [8, 512], P(None, ('pipe', 'dp'))
- new_mom_bn_wide: float32 [6, 2048], P(None, ('pipe', 'dp'))
- new_narrow: float32 [12288, 512], P(('pipe', 'dp'))
- new_wide: float32 [2048, 2048], P(('pipe', 'dp'))
- new_bn_mid: float32 [8, 512], P(None, ('pipe', 'dp'))
- new_bn_wide: float32 [6, 2048], P(None, ('pipe', 'dp'))
The draws below stay inside these ranges and needn't reach their ends.
Inputs may be any that keep to these rules, and one draw needn't show every extreme that they name: `heights`: some image has height 8. `widths`: some image has width 12. `assign`: each row is a permutation of 0 to 7. `bn_mid`: even rows are gains, odd rows biases. `bn_wide`: even rows are gains, odd rows biases.
All inputs are finite; a program needn't handle non-finite values.
Results may differ from the reference program's by a relative error of at most 0.018.
Values may be sent and summed in bfloat16 or wider, within the bound.
No kernel may reach another device: no remote copies, remote signals or barrier semaphores. Data moves between devices by JAX's collectives and lax.ppermute only.
A program may use at most 384 MiB of HBM per device.

```python
import jax
import jax.numpy as jnp
from jax import lax

C_IN = 1024
C_MID = 512
C_OUT = 2048
HB = 8
WB = 12
MB = 4
IMG_MB = 2
IMG_DEV = 8
IMAGES = 128
R_N = 12288
R_W = 2048
N_DP = 16


def bucket_sides(key, largest):
    first_key, second_key = jax.random.split(key)
    sides = jax.random.randint(first_key, (IMAGES,), max(largest // 2, 1), largest + 1)
    chosen = jax.random.randint(second_key, (), 0, IMAGES)
    return jnp.where(jnp.arange(IMAGES) == chosen, largest, sides).astype(jnp.int32)


def draw_heights(key, part):
    key = jax.random.fold_in(key, 11)
    return bucket_sides(key, HB)


def draw_widths(key, part):
    key = jax.random.fold_in(key, 23)
    return bucket_sides(key, WB)


def gain_table(key, rows, cols, gain_floor, gain_top, bias_size):
    first_key, second_key = jax.random.split(key)
    gains = jax.random.uniform(first_key, (rows // 2, cols), jnp.float32, gain_floor, gain_top)
    biases = jax.random.uniform(second_key, (rows // 2, cols), jnp.float32, -bias_size, bias_size)
    return jnp.stack([gains, biases], axis=1).reshape(rows, cols)


def draw_bn_mid(key, part):
    key = jax.random.fold_in(key, 37)
    return gain_table(key, 8, C_MID, 0.5, 1.5, 0.5)


def draw_bn_wide(key, part):
    key = jax.random.fold_in(key, 41)
    return gain_table(key, 6, C_OUT, 0.5, 1.5, 0.5)


def shard_levels(stream_key, dims, pieces, least, high):
    gain = 1.0
    for axis_at, parts in pieces:
        steps = jax.random.uniform(jax.random.fold_in(jax.random.fold_in(stream_key, 6), axis_at), (parts,), jnp.float32, least / len(pieces), high / len(pieces))
        gain = gain * jnp.repeat(jnp.exp(steps), dims[axis_at] // parts).reshape((-1,) + (1,) * (len(dims) - 1 - axis_at))
    return gain


def gaussian(key, extent, scale, bound, shards=(), kind=jnp.bfloat16):
    factor_of = shard_levels(key, extent, shards, -0.22, 0.18) if shards else 1.0
    array = jax.random.normal(key, extent, jnp.float32) * scale * factor_of
    return jnp.minimum(jnp.maximum(array, -bound), bound).astype(kind)


def setup_inputs(seed: int = 0) -> dict:
    key_of = jax.random.split(jax.random.key(seed), 14)
    return {
        "images": gaussian(key_of[0], (IMAGES, 2 * HB, 2 * WB, C_IN), 1.0, 6.0, ((0, 16),)),
        "cotangent": gaussian(key_of[1], (IMAGES, HB, WB, C_OUT), 1.0, 6.0, ((0, 16),)),
        "heights": draw_heights(jax.random.fold_in(key_of[13], 71), 0),
        "widths": draw_widths(jax.random.fold_in(key_of[13], 71), 0),
        "assign": jax.vmap(lambda own: jax.random.permutation(own, IMG_DEV))(jax.random.split(key_of[4], N_DP)).reshape((N_DP, IMG_DEV)).astype(jnp.int32),
        "w_narrow": gaussian(key_of[5], (R_N, C_MID), (9 * C_MID) ** -0.5, 0.09375, ((0, 32),), jnp.float32),
        "w_wide": gaussian(key_of[6], (R_W, C_OUT), C_IN ** -0.5, 0.1875, ((0, 32),), jnp.float32),
        "bn_mid": draw_bn_mid(jax.random.fold_in(key_of[13], 71), 0),
        "bn_wide": draw_bn_wide(jax.random.fold_in(key_of[13], 71), 0),
        "mom_narrow": gaussian(key_of[9], (R_N, C_MID), (29 * 9 * C_MID) ** -0.5, 0.015625, ((0, 32),), jnp.float32),
        "mom_wide": gaussian(key_of[10], (R_W, C_OUT), (29 * C_IN) ** -0.5, 0.03125, ((0, 32),), jnp.float32),
        "mom_bn_mid": gaussian(key_of[11], (8, C_MID), 0.14, 2.0, ((1, 32),), jnp.float32),
        "mom_bn_wide": gaussian(key_of[12], (6, C_OUT), 0.14, 2.0, ((1, 32),), jnp.float32),
    }


EPS = 1e-05
MOMENTUM = 0.9
DECAY = 5e-05
TRUST = 0.001
RATE = 29.0
PRECISE = lax.Precision.HIGHEST

@jax.custom_vjp
def low(v):
    return lax.optimization_barrier(v.astype(jnp.bfloat16)).astype(jnp.float32)

@jax.custom_vjp
def low_back(v):
    return v

def low_keep(v):
    return (low(v), None)

def low_pass(kept, grad):
    return (grad,)

def back_keep(v):
    return (v, None)

def back_low(kept, grad):
    return (low(grad),)
low.defvjp(low_keep, low_pass)
low_back.defvjp(back_keep, back_low)

def smooth_gate(values):
    return values * jax.nn.sigmoid(values)

def patches(feature, stride):
    padded = jnp.pad(feature, ((0, 0), (1, 1), (1, 1), (0, 0)))
    rows_out = feature.shape[1] // stride
    cols_out = feature.shape[2] // stride
    tap_list = []
    for tap_row in range(3):
        for tap_col in range(3):
            tap_list.append(padded[:, tap_row:tap_row + stride * rows_out:stride, tap_col:tap_col + stride * cols_out:stride, :])
    return jnp.concatenate(tap_list, axis=3)

def project(feature, weight):
    return jnp.einsum('bhwc,cd->bhwd', feature, weight, precision=PRECISE)

def pixel_masks(heights, widths, rows, cols):
    row_ids = jnp.arange(rows, dtype=jnp.int32)
    col_ids = jnp.arange(cols, dtype=jnp.int32)
    inside = (row_ids[:, None] < heights[..., None, None]) & (col_ids[None, :] < widths[..., None, None])
    return inside.astype(jnp.float32)[..., None]

def batch_norm(values, pixel_mask, gain_row, bias_row):
    pixel_total = jnp.sum(pixel_mask)
    mean_row = lax.optimization_barrier(jnp.sum(values * pixel_mask, axis=(0, 1, 2))) / pixel_total
    spread = lax.optimization_barrier(jnp.sum(values * values * pixel_mask, axis=(0, 1, 2))) / pixel_total - mean_row * mean_row
    return (values - mean_row) * lax.rsqrt(spread + EPS) * gain_row + bias_row

def split_params(narrow, wide):
    first_edge = C_IN
    second_edge = C_IN + 9 * C_MID
    third_edge = second_edge + C_OUT
    return (narrow[:first_edge], narrow[first_edge:second_edge], wide[:C_MID], wide[C_MID:C_MID + C_IN], narrow[second_edge:third_edge], narrow[third_edge:], wide[C_MID + C_IN:])

def forward(inputs, narrow, wide, table_mid, table_wide, masks_in, masks_out):
    weight_one, weight_two, weight_three, weight_short, weight_four, weight_five, weight_six = split_params(low(narrow), low(wide))
    table_mid = low(table_mid)
    table_wide = low(table_wide)
    outputs = []
    for batch_index in range(MB):
        mask_in = masks_in[batch_index]
        mask_out = masks_out[batch_index]
        masked = inputs[batch_index] * mask_in
        conv_one = low_back(project(masked, weight_one))
        act_one = low(smooth_gate(batch_norm(conv_one, mask_in, table_mid[0], table_mid[1])) * mask_in)
        conv_two = low_back(project(patches(act_one, 2), weight_two))
        act_two = low(smooth_gate(batch_norm(conv_two, mask_out, table_mid[2], table_mid[3])) * mask_out)
        conv_three = low_back(project(act_two, weight_three))
        conv_short = low_back(project(masked[:, ::2, ::2], weight_short))
        joined = batch_norm(conv_three, mask_out, table_wide[0], table_wide[1]) + batch_norm(conv_short, mask_out, table_wide[2], table_wide[3])
        middle = low_back(low(smooth_gate(joined) * mask_out))
        conv_four = low_back(project(middle, weight_four))
        act_four = low(smooth_gate(batch_norm(conv_four, mask_out, table_mid[4], table_mid[5])) * mask_out)
        conv_five = low_back(project(patches(act_four, 1), weight_five))
        act_five = low(smooth_gate(batch_norm(conv_five, mask_out, table_mid[6], table_mid[7])) * mask_out)
        conv_six = low_back(project(act_five, weight_six))
        outputs.append(smooth_gate(batch_norm(conv_six, mask_out, table_wide[4], table_wide[5]) + middle) * mask_out)
    return jnp.stack(outputs)

def lars_update(weights, gradients, moments, bounds):
    new_moments = []
    for start_row, stop_row in bounds:
        weight_part = weights[start_row:stop_row]
        grad_part = gradients[start_row:stop_row]
        weight_norm = jnp.sqrt(jnp.sum(weight_part * weight_part))
        grad_norm = jnp.sqrt(jnp.sum(grad_part * grad_part))
        ratio = TRUST * weight_norm / (grad_norm + DECAY * weight_norm)
        new_moments.append(MOMENTUM * moments[start_row:stop_row] + RATE * ratio * (grad_part + DECAY * weight_part))
    moment_all = jnp.concatenate(new_moments, axis=0)
    return (weights - moment_all, moment_all)

def reference(images, cotangent, heights, widths, assign, w_narrow, w_wide, bn_mid, bn_wide, mom_narrow, mom_wide, mom_bn_mid, mom_bn_wide):
    image_order = assign + (jnp.arange(N_DP, dtype=jnp.int32) * IMG_DEV)[:, None]
    chosen_rows = image_order.reshape(N_DP, MB, IMG_MB).transpose(1, 0, 2).reshape(MB, N_DP * IMG_MB)
    inputs = images[chosen_rows].astype(jnp.float32)
    masks_in = pixel_masks(2 * heights[chosen_rows], 2 * widths[chosen_rows], 2 * HB, 2 * WB)
    masks_out = pixel_masks(heights[chosen_rows], widths[chosen_rows], HB, WB)

    def forward_all(inputs, narrow, wide, table_mid, table_wide):
        return forward(inputs, narrow, wide, table_mid, table_wide, masks_in, masks_out)
    outputs, pullback = jax.vjp(forward_all, inputs, w_narrow, w_wide, bn_mid, bn_wide)
    gradients = pullback(cotangent[chosen_rows].astype(jnp.float32))
    flat_rows = chosen_rows.reshape(-1)
    block_out = jnp.zeros(cotangent.shape, jnp.float32).at[flat_rows].set(outputs.reshape((-1,) + cotangent.shape[1:])).astype(jnp.bfloat16)
    grad_input = jnp.zeros(images.shape, jnp.float32).at[flat_rows].set(gradients[0].reshape((-1,) + images.shape[1:])).astype(jnp.bfloat16)
    first_edge = C_IN
    second_edge = C_IN + 9 * C_MID
    third_edge = second_edge + C_OUT
    narrow_bounds = [(0, first_edge), (first_edge, second_edge), (second_edge, third_edge), (third_edge, R_N)]
    wide_bounds = [(0, C_MID), (C_MID, C_MID + C_IN), (C_MID + C_IN, R_W)]
    new_narrow, new_mom_narrow = lars_update(w_narrow, gradients[1], mom_narrow, narrow_bounds)
    new_wide, new_mom_wide = lars_update(w_wide, gradients[2], mom_wide, wide_bounds)
    new_bn_mid, new_mom_bn_mid = lars_update(bn_mid, gradients[3], mom_bn_mid, [(row, row + 1) for row in range(8)])
    new_bn_wide, new_mom_bn_wide = lars_update(bn_wide, gradients[4], mom_bn_wide, [(row, row + 1) for row in range(6)])
    return (block_out, grad_input, gradients[1], gradients[2], gradients[3], gradients[4], new_mom_narrow, new_mom_wide, new_mom_bn_mid, new_mom_bn_wide, new_narrow, new_wide, new_bn_mid, new_bn_wide)
```

```python
import jax
import jax.numpy as jnp
import numpy as np
from jax import lax
from jax.experimental import pallas as pl
from jax.experimental.pallas import tpu as pltpu
from jax.sharding import PartitionSpec as P

C_IN = 1024
C_MID = 512
C_OUT = 2048
HB = 8
WB = 12
IMG_DEV = 8
SLOTS = 4
PIX = HB * WB
ROWS = SLOTS * PIX
HALF = ROWS // 2
PAD = 16
TILE = 512

EPS = 1e-05
MOMENTUM = 0.9
DECAY = 5e-05
TRUST = 0.001
RATE = 29.0
PRECISE = lax.Precision.HIGHEST
BFLOAT = jnp.bfloat16
SINGLE = jnp.float32
VMEM_LIMIT = 56 * 1024 * 1024


def dp_sum(value):
    size = lax.axis_size("dp")
    step = 1
    while step < size:
        value = value + lax.ppermute(value, "dp", [(i, i ^ step) for i in range(size)])
        step *= 2
    return value


def swap_pipe(value):
    return lax.ppermute(value, "pipe", [(0, 1), (1, 0)])


def dot(left, right):
    return jnp.dot(left, right, preferred_element_type=SINGLE)


def dot_back(left, right):
    return lax.dot_general(left, right, (((1,), (1,)), ((), ())), preferred_element_type=SINGLE)


def silu(value):
    return value * jax.nn.sigmoid(value)


def slope(value):
    gate = jax.nn.sigmoid(value)
    return gate * (1.0 + value * (1.0 - gate))


def put_sums(ref, values, first):
    for k, value in enumerate(values):
        for m in range(2):
            total = jnp.sum(value[m * HALF : (m + 1) * HALF], axis=0, keepdims=True)
            row = 2 * k + m
            ref[row : row + 1, :] = total if first else ref[row : row + 1, :] + total


def both(function):
    return jnp.concatenate([function(0), function(1)], axis=0)


def part(m):
    return slice(m * HALF, (m + 1) * HALF)


def moments(total_ref, inv_ref, m, scale=1.0):
    inv = inv_ref[m] * scale
    mean = total_ref[m : m + 1, :] * inv
    var = total_ref[2 + m : 3 + m, :] * inv - mean * mean
    return mean, lax.rsqrt(var + EPS)


def normed(a, total_ref, inv_ref, m, scale=1.0):
    mean, rstd = moments(total_ref, inv_ref, m, scale)
    return (a - mean) * rstd, rstd


def conv_grad(gz, xhat, rstd, gain, mask, sum_ref, inv_ref, m, scale=1.0, second=2):
    inv = inv_ref[m] * scale
    first_row = sum_ref[m : m + 1, :] * inv
    second_row = sum_ref[second + m : second + m + 1, :] * inv
    return (mask * ((rstd * gain) * (gz - first_row - xhat * second_row))).astype(BFLOAT)


def k_prep(slot_ref, img_ref, perm_ref, mask_ref, out_ref):
    planes = dot(perm_ref[...], img_ref[0])
    mask = mask_ref[...]
    for k in range(4):
        out_ref[k] = (planes[k * PIX : (k + 1) * PIX] * mask).astype(BFLOAT)


def k_first(x_ref, w_ref, a_ref, sum_ref):
    a = dot(x_ref[0], w_ref[...])
    a_ref[0] = a

    @pl.when(pl.program_id(0) == 0)
    def _():
        sum_ref[...] = jnp.zeros_like(sum_ref)

    put_sums(sum_ref, [a, a * a], False)


def shift_mask(edge_ref, di, dj):
    mask = None
    if di:
        mask = edge_ref[0 if di < 0 else 1]
    if dj:
        column = edge_ref[2 if dj < 0 else 3]
        mask = column if mask is None else mask * column
    return mask


def shifted(pad, edge_ref, di, dj):
    start = PAD + HB * dj + di
    rows = pad[start : start + ROWS, :]
    mask = shift_mask(edge_ref, di, dj)
    return (rows if mask is None else rows * mask).astype(BFLOAT)


def clear_pad(pad):
    pad[0:PAD, :] = jnp.zeros((PAD, pad.shape[1]), SINGLE)
    pad[PAD + ROWS : PAD + ROWS + PAD, :] = jnp.zeros((PAD, pad.shape[1]), SINGLE)


def parity(k):
    return (1, -1) if k == 0 else ((0, 0) if k == 1 else (1, 0))


def k_conv_two(inv_ref, total_ref, tab_ref, mask_ref, edge_ref, a_ref, w0, w1, w2, out_ref, col_ref, sum_ref, pad):
    step = pl.program_id(0)
    weights = (w0, w1, w2)
    gain, bias = tab_ref[0:1, :], tab_ref[1:2, :]
    for s in range(3):

        @pl.when(step == s)
        def _(s=s):
            if s < 2:
                for k in range(2):
                    plane = 2 * s + k
                    clear_pad(pad.at[plane])
                    for m in range(2):
                        xhat, _unused = normed(a_ref[k, part(m), :], total_ref, inv_ref, m, 0.25)
                        h = silu(xhat * gain + bias) * mask_ref[part(m), :]
                        pad[plane, PAD + m * HALF : PAD + (m + 1) * HALF, :] = h.astype(BFLOAT).astype(SINGLE)
            row_plane, di = parity((s + 1) % 3)
            for kx in range(3):
                col_plane, dj = parity(kx)
                tap = shifted(pad.at[2 * row_plane + col_plane], edge_ref, di, dj)
                col_ref[kx] = tap
                term = dot(tap, weights[kx][...])
                if s == 0 and kx == 0:
                    out_ref[...] = term
                else:
                    out_ref[...] += term
            if s == 2:
                a = out_ref[...]
                masked = a * mask_ref[...]
                put_sums(sum_ref, [masked, masked * a], True)


def k_conv_one(inv_ref, total_ref, tab_ref, mask_ref, edge_ref, a_ref, w0, w1, w2, out_ref, col_ref, sum_ref, pad):
    step = pl.program_id(0)
    weights = (w0, w1, w2)
    gain, bias = tab_ref[0:1, :], tab_ref[1:2, :]
    for s in range(3):

        @pl.when(step == s)
        def _(s=s):
            if s == 0:
                clear_pad(pad)
                for m in range(2):
                    xhat, _unused = normed(a_ref[part(m), :], total_ref, inv_ref, m)
                    h = silu(xhat * gain + bias) * mask_ref[part(m), :]
                    pad[PAD + m * HALF : PAD + (m + 1) * HALF, :] = h.astype(BFLOAT).astype(SINGLE)
            for kx in range(3):
                tap = shifted(pad, edge_ref, s - 1, kx - 1)
                col_ref[kx] = tap
                term = dot(tap, weights[kx][...])
                if s == 0 and kx == 0:
                    out_ref[...] = term
                else:
                    out_ref[...] += term
            if s == 2:
                a = out_ref[...]
                masked = a * mask_ref[...]
                put_sums(sum_ref, [masked, masked * a], True)


def k_expand(inv_ref, total_ref, tab_ref, mask_ref, a_ref, w_ref, h_ref, out_ref, sum_ref):
    @pl.when(pl.program_id(0) == 0)
    def _():
        gain, bias = tab_ref[0:1, :], tab_ref[1:2, :]
        for m in range(2):
            xhat, _unused = normed(a_ref[part(m), :], total_ref, inv_ref, m)
            h_ref[part(m), :] = (silu(xhat * gain + bias) * mask_ref[part(m), :]).astype(BFLOAT)

    a = dot(h_ref[...], w_ref[...])
    out_ref[...] = a
    put_sums(sum_ref, [a, a * a], True)


def k_short(x_ref, w0, w1, out_ref, sum_ref):
    a = dot(x_ref[0, :, :TILE], w0[...]) + dot(x_ref[0, :, TILE:], w1[...])
    out_ref[...] = a
    put_sums(sum_ref, [a, a * a], True)


def k_join(inv_ref, t3_ref, ts_ref, tab3_ref, tabs_ref, mask_ref, a3_ref, as_ref, w_ref, y_ref, out_ref, sum_ref):
    step = pl.program_id(0)
    for m in range(2):
        x3, _unused = normed(a3_ref[part(m), :], t3_ref, inv_ref, m)
        xs, _unused = normed(as_ref[part(m), :], ts_ref, inv_ref, m)
        joined = (x3 * tab3_ref[0:1, :] + tab3_ref[1:2, :]) + (xs * tabs_ref[0:1, :] + tabs_ref[1:2, :])
        y_ref[part(m), :] = (silu(joined) * mask_ref[part(m), :]).astype(BFLOAT)
    term = dot(y_ref[...], w_ref[...])

    @pl.when(step == 0)
    def _():
        out_ref[...] = term

    @pl.when(step > 0)
    def _():
        out_ref[...] += term

    @pl.when(step == pl.num_programs(0) - 1)
    def _():
        a = out_ref[...]
        put_sums(sum_ref, [a, a * a], True)


def k_head(slot_ref, inv_ref, total_ref, tab_ref, mask_ref, a_ref, y_ref, c0, c1, c2, c3, blk_ref, gz_ref, sum_ref):
    cots = (c0, c1, c2, c3)
    gain, bias = tab_ref[0:1, :], tab_ref[1:2, :]
    for m in range(2):
        mask = mask_ref[part(m), :]
        xhat, _unused = normed(a_ref[part(m), :], total_ref, inv_ref, m)
        z = (xhat * gain + bias) + y_ref[part(m), :].astype(SINGLE)
        gate = jax.nn.sigmoid(z)
        blk_ref[0, part(m), :] = (z * gate * mask).astype(BFLOAT)
        cot = jnp.concatenate([cots[2 * m][0], cots[2 * m + 1][0]], axis=0).astype(SINGLE)
        gz = cot * mask * (gate * (1.0 + z * (1.0 - gate)))
        gz_ref[part(m), :] = gz
        sum_ref[m : m + 1, :] = jnp.sum(gz, axis=0, keepdims=True)
        sum_ref[2 + m : 3 + m, :] = jnp.sum(gz * xhat, axis=0, keepdims=True)


def finish_back(gz_ref, sum_ref, grad, a_ref, total_ref, tab_ref, inv_ref, mask_ref):
    gain, bias = tab_ref[0:1, :], tab_ref[1:2, :]
    for m in range(2):
        xhat, _unused = normed(a_ref[part(m), :], total_ref, inv_ref, m)
        gz = grad[part(m)] * mask_ref[part(m), :] * slope(xhat * gain + bias)
        gz_ref[part(m), :] = gz
        sum_ref[m : m + 1, :] = jnp.sum(gz, axis=0, keepdims=True)
        sum_ref[2 + m : 3 + m, :] = jnp.sum(gz * xhat, axis=0, keepdims=True)


def k_back_six(inv_ref, gz_ref, a_ref, total_ref, s_ref, tab_ref, mask_ref, w_ref, low_ref, low_total, low_tab, ga_ref, out_ref, sum_ref, acc):
    step = pl.program_id(0)
    for m in range(2):
        xhat, rstd = normed(a_ref[part(m), :], total_ref, inv_ref, m)
        ga_ref[part(m), :] = conv_grad(
            gz_ref[part(m), :], xhat, rstd, tab_ref[0:1, :], mask_ref[part(m), :], s_ref, inv_ref, m
        )
    term = dot_back(ga_ref[...], w_ref[...])

    @pl.when(step == 0)
    def _():
        acc[...] = term

    @pl.when(step > 0)
    def _():
        acc[...] += term

    @pl.when(step == pl.num_programs(0) - 1)
    def _():
        finish_back(out_ref, sum_ref, acc[...], low_ref, low_total, low_tab, inv_ref, mask_ref)


def k_back_conv_one(inv_ref, gz_ref, a_ref, total_ref, s_ref, tab_ref, mask_ref, edge_ref, w0, w1, w2, low_ref, low_total, low_tab, ga_ref, out_ref, sum_ref, pad, acc):
    step = pl.program_id(0)
    weights = (w0, w1, w2)
    for s in range(3):

        @pl.when(step == s)
        def _(s=s):
            if s == 0:
                clear_pad(pad)
                for m in range(2):
                    xhat, rstd = normed(a_ref[part(m), :], total_ref, inv_ref, m)
                    ga = conv_grad(
                        gz_ref[part(m), :], xhat, rstd, tab_ref[0:1, :], mask_ref[part(m), :], s_ref, inv_ref, m
                    )
                    ga_ref[part(m), :] = ga
                    pad[PAD + m * HALF : PAD + (m + 1) * HALF, :] = ga.astype(SINGLE)
            for kx in range(3):
                term = dot_back(shifted(pad, edge_ref, 1 - s, 1 - kx), weights[kx][...])
                if s == 0 and kx == 0:
                    acc[...] = term
                else:
                    acc[...] += term
            if s == 2:
                finish_back(out_ref, sum_ref, acc[...], low_ref, low_total, low_tab, inv_ref, mask_ref)


def k_back_four(inv_ref, gz_ref, a_ref, total_ref, s_ref, tab_ref, mask_ref, w_ref, up_ref, a3_ref, as_ref, t3_ref, ts_ref, tab3_ref, tabs_ref, ga_ref, gj_ref, sum_ref):
    @pl.when(pl.program_id(0) == 0)
    def _():
        for m in range(2):
            xhat, rstd = normed(a_ref[part(m), :], total_ref, inv_ref, m)
            ga_ref[part(m), :] = conv_grad(
                gz_ref[part(m), :], xhat, rstd, tab_ref[0:1, :], mask_ref[part(m), :], s_ref, inv_ref, m
            )

    grad = dot_back(ga_ref[...], w_ref[...]) + up_ref[...]
    for m in range(2):
        x3, _unused = normed(a3_ref[part(m), :], t3_ref, inv_ref, m)
        xs, _unused = normed(as_ref[part(m), :], ts_ref, inv_ref, m)
        joined = (x3 * tab3_ref[0:1, :] + tab3_ref[1:2, :]) + (xs * tabs_ref[0:1, :] + tabs_ref[1:2, :])
        gj = grad[part(m)].astype(BFLOAT).astype(SINGLE) * mask_ref[part(m), :] * slope(joined)
        gj_ref[part(m), :] = gj
        for k, value in enumerate((gj, gj * x3, gj * xs)):
            row = 2 * k + m
            sum_ref[row : row + 1, :] = jnp.sum(value, axis=0, keepdims=True)


def k_back_three(inv_ref, gj_ref, a3_ref, as_ref, t3_ref, ts_ref, s_ref, tab3_ref, tabs_ref, mask_ref, w_ref, low_ref, low_total, low_tab, g3_ref, gs_ref, out_ref, sum_ref, acc):
    step = pl.program_id(0)
    for m in range(2):
        mask = mask_ref[part(m), :]
        gj = gj_ref[part(m), :]
        x3, r3 = normed(a3_ref[part(m), :], t3_ref, inv_ref, m)
        g3_ref[part(m), :] = conv_grad(gj, x3, r3, tab3_ref[0:1, :], mask, s_ref, inv_ref, m)
        xs, rs = normed(as_ref[part(m), :], ts_ref, inv_ref, m)
        gs_ref[part(m), :] = conv_grad(gj, xs, rs, tabs_ref[0:1, :], mask, s_ref, inv_ref, m, second=4)
    term = dot_back(g3_ref[...], w_ref[...])

    @pl.when(step == 0)
    def _():
        acc[...] = term

    @pl.when(step > 0)
    def _():
        acc[...] += term

    @pl.when(step == pl.num_programs(0) - 1)
    def _():
        finish_back(out_ref, sum_ref, acc[...], low_ref, low_total, low_tab, inv_ref, mask_ref)


def k_back_conv_two(inv_ref, gz_ref, a_ref, total_ref, s_ref, tab_ref, mask_ref, edge_ref, w0, w1, w2, low_ref, low_total, low_tab, ga_ref, out_ref, sum_ref, pad, acc):
    step = pl.program_id(0)
    weights = (w0, w1, w2)
    gain, bias = low_tab[0:1, :], low_tab[1:2, :]
    for s in range(3):

        @pl.when(step == s)
        def _(s=s):
            if s == 0:
                clear_pad(pad)
                for m in range(2):
                    xhat, rstd = normed(a_ref[part(m), :], total_ref, inv_ref, m)
                    ga = conv_grad(
                        gz_ref[part(m), :], xhat, rstd, tab_ref[0:1, :], mask_ref[part(m), :], s_ref, inv_ref, m
                    )
                    ga_ref[part(m), :] = ga
                    pad[PAD + m * HALF : PAD + (m + 1) * HALF, :] = ga.astype(SINGLE)
                sum_ref[...] = jnp.zeros_like(sum_ref)
            row_plane, di = parity((s + 1) % 3)
            for kx in (1, 0, 2):
                col_plane, dj = parity(kx)
                term = dot_back(shifted(pad, edge_ref, -di, -dj), weights[kx][...])
                if s == 2 or kx == 2:
                    acc[col_plane] += term
                else:
                    acc[col_plane] = term
            if s != 1:
                for k in range(2):
                    for m in range(2):
                        xhat, _unused = normed(low_ref[k, part(m), :], low_total, inv_ref, m, 0.25)
                        gz = acc[k, part(m), :] * mask_ref[part(m), :] * slope(xhat * gain + bias)
                        out_ref[k, part(m), :] = gz
                        for q, value in enumerate((gz, gz * xhat)):
                            row = 2 * q + m
                            sum_ref[row : row + 1, :] += jnp.sum(value, axis=0, keepdims=True)


def k_wide_back(g_ref, w_ref, out_ref):
    out_ref[...] = dot_back(g_ref[...], w_ref[...])


def k_last(slot_ref, inv_ref, gz_ref, a_ref, total_ref, s_ref, tab_ref, mask_ref, w_ref, short_ref, perm_ref, ga_ref, out_ref):
    m = pl.program_id(0) // 2
    inv = inv_ref[m] * 0.25
    mean = total_ref[pl.ds(m, 1), :] * inv
    var = total_ref[pl.ds(2 + m, 1), :] * inv - mean * mean
    rstd = lax.rsqrt(var + EPS)
    first_row = s_ref[pl.ds(m, 1), :] * inv
    second_row = s_ref[pl.ds(2 + m, 1), :] * inv
    mask = mask_ref[...]
    parts = []
    for k in range(4):
        xhat = (a_ref[k] - mean) * rstd
        ga = (mask * ((rstd * tab_ref[0:1, :]) * (gz_ref[k] - first_row - xhat * second_row))).astype(BFLOAT)
        ga_ref[k] = ga
        grad = dot_back(ga, w_ref[...])
        if k == 0:
            grad = grad + short_ref[...]
        parts.append((grad * mask).astype(BFLOAT))
    planes = jnp.concatenate(parts, axis=0)
    image = lax.dot_general(perm_ref[...], planes, (((0,), (0,)), ((), ())), preferred_element_type=SINGLE).astype(BFLOAT)
    core = slot_ref[SLOTS]
    out_ref[core, 0] = image[:, : C_IN // 2]
    out_ref[1 - core, 0] = image[:, C_IN // 2 :]


def k_place(slot_ref, own_ref, got_ref, out_ref):
    step = pl.program_id(0)

    @pl.when(step < SLOTS)
    def _():
        out_ref[0] = own_ref[0, 0]

    @pl.when(step >= SLOTS)
    def _():
        out_ref[0] = got_ref[0]


def k_grad(slot_ref, feature_ref, grad_ref, *refs):
    keep_ref, send_ref = refs[-2:]
    feature, grad = feature_ref[...], grad_ref[...]
    feature = feature.reshape(-1, feature.shape[-1])
    grad = grad.reshape(-1, grad.shape[-1])
    tile = lax.dot_general(feature, grad, (((0,), (0,)), ((), ())), preferred_element_type=SINGLE).astype(BFLOAT)
    half = tile.shape[1] // 2

    @pl.when(slot_ref[SLOTS] == 0)
    def _():
        keep_ref[...] = tile[:, :half]
        send_ref[...] = tile[:, half:]

    @pl.when(slot_ref[SLOTS] == 1)
    def _():
        keep_ref[...] = tile[:, half:]
        send_ref[...] = tile[:, :half]


def k_split(me_ref, *refs):
    own, got, outs = refs[:4], refs[4:8], refs[8:]
    for own_ref, got_ref, out_ref in zip(own, got, outs):
        out_ref[0] = (own_ref[...].astype(SINGLE) + got_ref[...].astype(SINGLE)).astype(BFLOAT)


def full(shape):
    zeros = (0,) * len(shape)
    return pl.BlockSpec(tuple(shape), lambda *_: zeros)


SCALARS = pl.BlockSpec(memory_space=pltpu.SMEM)


def spec(shape, index):
    return pl.BlockSpec(tuple(shape), index)


def call(kernel, name, grid, in_specs, out_specs, out_shape, scratch, args, prefetch=0):
    return pl.pallas_call(
        kernel,
        out_shape=out_shape,
        grid_spec=pltpu.PrefetchScalarGridSpec(
            num_scalar_prefetch=prefetch,
            grid=grid,
            in_specs=in_specs,
            out_specs=out_specs,
            scratch_shapes=scratch,
        ),
        compiler_params=pltpu.CompilerParams(vmem_limit_bytes=VMEM_LIMIT),
        name=name,
    )(*args)


def shape_of(shape, dtype=SINGLE):
    return jax.ShapeDtypeStruct(tuple(shape), dtype)


def permutation():
    table = np.zeros((4 * PIX, 4 * PIX), np.float32)
    for pi in range(2):
        for pj in range(2):
            for i in range(HB):
                for j in range(WB):
                    table[((2 * pi + pj) * WB + j) * HB + i, (2 * i + pi) * 2 * WB + 2 * j + pj] = 1.0
    return jnp.asarray(table, BFLOAT)


def edges():
    rows = np.arange(ROWS)
    i, j = rows % HB, (rows // HB) % WB
    return jnp.asarray(np.stack([i > 0, i < HB - 1, j > 0, j < WB - 1]).astype(np.float32)[..., None])


def group_table(start_index, rows_local, bounds):
    global_rows = start_index * rows_local + jnp.arange(rows_local, dtype=jnp.int32)
    group_ids = jnp.zeros((rows_local,), jnp.int32)
    for boundary in bounds:
        group_ids = group_ids + (global_rows >= boundary).astype(jnp.int32)
    return (group_ids[:, None] == jnp.arange(len(bounds) + 1, dtype=jnp.int32)[None, :]).astype(SINGLE)


def rounded(value):
    return lax.reduce_precision(value, 8, 7)


def split_group(name, keep, got, rows, index):
    cols = keep.shape[1]

    def block(which, sent):
        def at(q, me):
            other, low, high = (q >> 2) & 1, (q >> 1) & 1, q & 1
            pair = other * 2 + sent if which == 0 else sent * 2 + other
            return (index(which, me[0] ^ (high * 8 + low * 4 + pair)), 0)

        return spec((rows, cols), at)

    blocks = [block(which, sent) for which in range(2) for sent in range(2)]
    return call(
        k_split, name, (8,), blocks + blocks,
        [spec((1, rows, cols), lambda q, me: (q, 0, 0))] * 4,
        [shape_of((8, rows, cols), BFLOAT)] * 4, [],
        (lax.axis_index("dp")[None].astype(jnp.int32),) + (keep,) * 4 + (got,) * 4, prefetch=1,
    )


def halve(keep, send, bits):
    size = lax.axis_size("dp")
    for bit in bits:
        got = lax.ppermute(send, "dp", [(i, i ^ bit) for i in range(size)])
        total = keep.astype(SINGLE) + got.astype(SINGLE)
        half = total.shape[0] // 2
        if half:
            keep, send = total[:half].astype(BFLOAT), total[half:].astype(BFLOAT)
    return total[0]


def scatter_group(name, keep, send, block, by_rows):
    got = swap_pipe(send)
    size = lax.axis_size("dp")
    if size == 16:
        rows = block // 2 if by_rows else block
        index = (lambda which, m: 2 * m + which) if by_rows else (lambda which, m: 16 * which + m)
        keep0, send0, keep1, send1 = split_group("split_" + name, keep, got, rows, index)
        return halve(keep0, send0, (1, 2, 4, 8)), halve(keep1, send1, (2, 1, 4, 8))
    total = (keep.astype(SINGLE) + got.astype(SINGLE)).astype(BFLOAT)
    if by_rows:
        own = lax.psum_scatter(total, "dp", scatter_dimension=0, tiled=True).astype(SINGLE)
        return own[: block // 2], own[block // 2 :]
    middle = total.shape[0] // 2
    return tuple(lax.psum_scatter(p, "dp", scatter_dimension=0, tiled=True).astype(SINGLE) for p in (total[:middle], total[middle:]))


def on_device(images, cotangent, heights, widths, assign, w_narrow, w_wide, bn_mid, bn_wide, mom_narrow, mom_wide, mom_bn_mid, mom_bn_wide):
    core = lax.axis_index("pipe")
    shard = lax.axis_index(("pipe", "dp"))
    hot_narrow = group_table(shard, w_narrow.shape[0], (C_IN, C_IN + 9 * C_MID, C_IN + 9 * C_MID + C_OUT))
    hot_wide = group_table(shard, w_wide.shape[0], (C_MID, C_MID + C_IN))

    narrow = lax.all_gather(w_narrow.astype(BFLOAT), ("pipe", "dp"), axis=0, tiled=True)
    wide = lax.all_gather(w_wide.astype(BFLOAT), ("pipe", "dp"), axis=0, tiled=True)

    order = assign[0].reshape(2, SLOTS)
    own_slots = lax.dynamic_index_in_dim(order, core, 0, keepdims=False)
    other_slots = lax.dynamic_index_in_dim(order, 1 - core, 0, keepdims=False)
    slots = jnp.concatenate([own_slots, core[None].astype(jnp.int32), other_slots])

    counts = jnp.sum((heights * widths)[assign[0]].reshape(4, 2), axis=1).astype(SINGLE)
    mid_cols, wide_cols = bn_mid.shape[1], bn_wide.shape[1]
    tables = jnp.concatenate(
        [
            lax.dynamic_update_slice(jnp.zeros((8, C_MID), SINGLE), rounded(bn_mid), (0, shard * mid_cols)),
            lax.dynamic_update_slice(jnp.zeros((6, C_OUT), SINGLE), rounded(bn_wide), (0, shard * wide_cols)).reshape(24, C_MID),
        ]
    )
    tables = tables + swap_pipe(tables)
    count_rows = jnp.zeros((8, C_MID), SINGLE).at[0, :4].set(counts)
    gathered = dp_sum(jnp.concatenate([tables, count_rows]))
    mid, table = gathered[:8], gathered[8:32].reshape(6, C_OUT)
    inv = lax.dynamic_slice(1.0 / gathered[32, :4], (2 * core,), (2,))

    heights_own, widths_own = heights[own_slots], widths[own_slots]
    inside = (jnp.arange(HB)[None, None, :] < heights_own[:, None, None]) & (jnp.arange(WB)[None, :, None] < widths_own[:, None, None])
    mask = inside.astype(SINGLE).reshape(ROWS, 1)
    edge = edges()
    perm = permutation()

    mid1, mid2, mid4, mid5 = (mid[2 * k : 2 * k + 2] for k in range(4))
    tab3, tabs, tab6 = (table[2 * k : 2 * k + 2] for k in range(3))

    def weight_grad(name, feature, feature_spec, grad, tiles, shape, rows, base, bufs):
        out_spec = spec((rows, shape[1]), lambda t, slot: (base + t, 0))
        return pl.pallas_call(
            k_grad,
            out_shape=[shape_of(shape, BFLOAT)] * 2,
            grid_spec=pltpu.PrefetchScalarGridSpec(
                num_scalar_prefetch=1,
                grid=(tiles,),
                in_specs=[feature_spec, full(grad.shape)] + [pl.BlockSpec(memory_space=pl.ANY)] * (2 if bufs else 0),
                out_specs=[out_spec] * 2,
            ),
            input_output_aliases={3: 0, 4: 1} if bufs else {},
            compiler_params=pltpu.CompilerParams(vmem_limit_bytes=VMEM_LIMIT),
            name=name,
        )(slots, feature, grad, *(bufs or ()))

    wide_tile = spec((ROWS, 256), lambda t, slot: (0, t))
    tap_tile = spec((1, ROWS, C_MID), lambda t, slot: (t, 0, 0))
    full_row = full((4, C_MID))
    full_tab = full((2, C_MID))
    full_mask = full((ROWS, 1))
    full_edge = full((4, ROWS, 1))
    full_mid = full((ROWS, C_MID))

    def narrow_block(index):
        return spec((TILE, TILE), index)

    chunk = spec((ROWS, TILE), lambda k, *_: (0, k))
    chunk_sum = spec((4, TILE), lambda k, *_: (0, k))
    chunk_tab = spec((2, TILE), lambda k, *_: (0, k))

    x = call(
        k_prep, "prep", (SLOTS,),
        [spec((1, 4 * PIX, C_IN), lambda s, slot: (slot[s], 0, 0)), full((4 * PIX, 4 * PIX)), spec((PIX, 1), lambda s, slot: (s, 0))],
        spec((4, PIX, C_IN), lambda s, slot: (0, s, 0)),
        shape_of((4, ROWS, C_IN), BFLOAT), [],
        (slots, images.reshape(IMG_DEV, 4 * PIX, C_IN), perm, mask), prefetch=1,
    )

    a1, part1 = call(
        k_first, "a1", (4,),
        [spec((1, ROWS, C_IN), lambda k: (k, 0, 0)), full((C_IN, C_MID))],
        [spec((1, ROWS, C_MID), lambda k: (k, 0, 0)), full_row],
        [shape_of((4, ROWS, C_MID)), shape_of((4, C_MID))], [],
        (x, narrow),
    )
    a_s, part_s = call(
        k_short, "as", (4,),
        [spec((1, ROWS, C_IN), lambda k: (0, 0, 0)), spec((TILE, TILE), lambda k: (1, k)), spec((TILE, TILE), lambda k: (2, k))],
        [chunk, chunk_sum],
        [shape_of((ROWS, C_OUT)), shape_of((4, C_OUT))], [],
        (x, wide, wide),
    )
    total1 = dp_sum(part1)

    def conv_weights(first, order_of):
        return [narrow_block(lambda s, kx=kx: (first + 3 * order_of(s) + kx, 0)) for kx in range(3)]

    turned = lambda s: lax.rem(s + 1, 3)
    straight = lambda s: s

    a2, col1, part2 = call(
        k_conv_two, "a2", (3,),
        [SCALARS, full_row, full_tab, full_mask, full_edge, spec((2, ROWS, C_MID), lambda s: (jnp.minimum(s, 1), 0, 0))] + conv_weights(2, turned),
        [full_mid, spec((3, ROWS, C_MID), lambda s: (turned(s), 0, 0)), full_row],
        [shape_of((ROWS, C_MID)), shape_of((9, ROWS, C_MID), BFLOAT), shape_of((4, C_MID))],
        [pltpu.VMEM((4, PAD + ROWS + PAD, C_MID), SINGLE)],
        (inv, total1, mid1, mask, edge, a1, narrow, narrow, narrow),
    )
    total2 = dp_sum(part2)

    def expand(name, a, total, tab, row):
        return call(
            k_expand, name, (4,),
            [SCALARS, full_row, full_tab, full_mask, full_mid, spec((TILE, TILE), lambda k: (row, k))],
            [full_mid, chunk, chunk_sum],
            [shape_of((ROWS, C_MID), BFLOAT), shape_of((ROWS, C_OUT)), shape_of((4, C_OUT))], [],
            (inv, total, tab, mask, a, wide),
        )

    h2, a3, part3 = expand("a3", a2, total2, mid2, 0)
    total3s = dp_sum(jnp.concatenate([part3, part_s]))
    total3, total_s = total3s[:4], total3s[4:]

    y, a4, part4 = call(
        k_join, "a4", (4,),
        [SCALARS, chunk_sum, chunk_sum, chunk_tab, chunk_tab, full_mask, chunk, chunk, narrow_block(lambda k: (11 + k, 0))],
        [chunk, full_mid, full_row],
        [shape_of((ROWS, C_OUT), BFLOAT), shape_of((ROWS, C_MID)), shape_of((4, C_MID))], [],
        (inv, total3, total_s, tab3, tabs, mask, a3, a_s, narrow),
    )
    total4 = dp_sum(part4)

    a5, col4, part5 = call(
        k_conv_one, "a5", (3,),
        [SCALARS, full_row, full_tab, full_mask, full_edge, full_mid] + conv_weights(15, straight),
        [full_mid, spec((3, ROWS, C_MID), lambda s: (s, 0, 0)), full_row],
        [shape_of((ROWS, C_MID)), shape_of((9, ROWS, C_MID), BFLOAT), shape_of((4, C_MID))],
        [pltpu.VMEM((PAD + ROWS + PAD, C_MID), SINGLE)],
        (inv, total4, mid4, mask, edge, a4, narrow, narrow, narrow),
    )
    total5 = dp_sum(part5)
    h5, a6, part6 = expand("a6", a5, total5, mid5, 3)
    total6 = dp_sum(part6)

    cot = cotangent.transpose(0, 2, 1, 3).reshape(IMG_DEV, PIX, C_OUT)
    blk, gz6, s6 = call(
        k_head, "head", (4,),
        [SCALARS, chunk_sum, chunk_tab, full_mask, chunk, chunk]
        + [spec((1, PIX, TILE), lambda k, slot, s=s: (slot[s], 0, k)) for s in range(SLOTS)],
        [
            spec((1, ROWS, TILE), lambda k, slot: ((k // 2) ^ slot[SLOTS], 0, lax.rem(k, 2))),
            chunk,
            chunk_sum,
        ],
        [shape_of((2, ROWS, C_OUT // 2), BFLOAT), shape_of((ROWS, C_OUT)), shape_of((4, C_OUT))], [],
        (slots, inv, total6, tab6, mask, a6, y, cot, cot, cot, cot), prefetch=1,
    )
    sum6 = dp_sum(s6)

    ga6, gz5, s5 = call(
        k_back_six, "g5", (4,),
        [SCALARS, chunk, chunk, chunk_sum, chunk_sum, chunk_tab, full_mask, spec((TILE, TILE), lambda k: (3, k)), full_mid, full_row, full_tab],
        [chunk, full_mid, full_row],
        [shape_of((ROWS, C_OUT), BFLOAT), shape_of((ROWS, C_MID)), shape_of((4, C_MID))],
        [pltpu.VMEM((ROWS, C_MID), SINGLE)],
        (inv, gz6, a6, total6, sum6, tab6, mask, wide, a5, total5, mid5),
    )
    sum5 = dp_sum(s5)
    bufs_w = weight_grad("dw6", h5, wide_tile, ga6, 2, (2048, 1024), 256, 6, None)

    ga5, gz4, s4 = call(
        k_back_conv_one, "g4", (3,),
        [SCALARS, full_mid, full_mid, full_row, full_row, full_tab, full_mask, full_edge] + conv_weights(15, straight) + [full_mid, full_row, full_tab],
        [full_mid, full_mid, full_row],
        [shape_of((ROWS, C_MID), BFLOAT), shape_of((ROWS, C_MID)), shape_of((4, C_MID))],
        [pltpu.VMEM((PAD + ROWS + PAD, C_MID), SINGLE), pltpu.VMEM((ROWS, C_MID), SINGLE)],
        (inv, gz5, a5, total5, sum5, mid5, mask, edge, narrow, narrow, narrow, a4, total4, mid4),
    )
    sum4 = dp_sum(s4)
    bufs_b = weight_grad("dw5", col4, tap_tile, ga5, 9, (6144, 256), TILE, 3, None)

    ga4, gj, s3 = call(
        k_back_four, "gy", (4,),
        [SCALARS, full_mid, full_mid, full_row, full_row, full_tab, full_mask, narrow_block(lambda k: (11 + k, 0)),
         chunk, chunk, chunk, chunk_sum, chunk_sum, chunk_tab, chunk_tab],
        [full_mid, chunk, spec((6, TILE), lambda k: (0, k))],
        [shape_of((ROWS, C_MID), BFLOAT), shape_of((ROWS, C_OUT)), shape_of((6, C_OUT))], [],
        (inv, gz4, a4, total4, sum4, mid4, mask, narrow, gz6, a3, a_s, total3, total_s, tab3, tabs),
    )
    sum3 = dp_sum(s3)
    bufs_b = weight_grad("dw4b", y, spec((ROWS, TILE), lambda t, slot: (0, 1 + t)), ga4, 3, (6144, 256), TILE, 0, bufs_b)
    bufs_a = weight_grad("dw4a", y, spec((ROWS, TILE), lambda t, slot: (0, t)), ga4, 1, (6144, 256), TILE, 11, None)

    ga3, gas, gz2, s2 = call(
        k_back_three, "g2", (4,),
        [SCALARS, chunk, chunk, chunk, chunk_sum, chunk_sum, spec((6, TILE), lambda k: (0, k)), chunk_tab, chunk_tab, full_mask,
         spec((TILE, TILE), lambda k: (0, k)), full_mid, full_row, full_tab],
        [chunk, chunk, full_mid, full_row],
        [shape_of((ROWS, C_OUT), BFLOAT), shape_of((ROWS, C_OUT), BFLOAT), shape_of((ROWS, C_MID)), shape_of((4, C_MID))],
        [pltpu.VMEM((ROWS, C_MID), SINGLE)],
        (inv, gj, a3, a_s, total3, total_s, sum3, tab3, tabs, mask, wide, a2, total2, mid2),
    )
    sum2 = dp_sum(s2)
    bufs_w = weight_grad("dw3", h2, wide_tile, ga3, 2, (2048, 1024), 256, 0, bufs_w)
    bufs_w = weight_grad("dws", x, spec((1, ROWS, 256), lambda t, slot: (0, 0, t)), gas, 4, (2048, 1024), 256, 2, bufs_w)
    dxs = call(
        k_wide_back, "dxs", (2,),
        [full((ROWS, C_OUT)), spec((TILE, C_OUT), lambda k: (1 + k, 0))],
        spec((ROWS, TILE), lambda k: (0, k)),
        shape_of((ROWS, C_IN)), [],
        (gas, wide),
    )

    ga2, gz1, s1 = call(
        k_back_conv_two, "g1", (3,),
        [SCALARS, full_mid, full_mid, full_row, full_row, full_tab, full_mask, full_edge] + conv_weights(2, turned)
        + [spec((2, ROWS, C_MID), lambda s: (jnp.minimum(s, 1), 0, 0)), full_row, full_tab],
        [full_mid, spec((2, ROWS, C_MID), lambda s: (jnp.minimum(s, 1), 0, 0)), full_row],
        [shape_of((ROWS, C_MID), BFLOAT), shape_of((4, ROWS, C_MID)), shape_of((4, C_MID))],
        [pltpu.VMEM((PAD + ROWS + PAD, C_MID), SINGLE), pltpu.VMEM((2, ROWS, C_MID), SINGLE)],
        (inv, gz2, a2, total2, sum2, mid2, mask, edge, narrow, narrow, narrow, a1, total1, mid1),
    )
    sum1 = dp_sum(s1)
    bufs_a = weight_grad("dw2", col1, tap_tile, ga2, 9, (6144, 256), TILE, 2, bufs_a)

    image_part = spec((4, PIX, C_MID), lambda s, slot: (0, s, 0))
    ga1, image_grad = call(
        k_last, "gx", (SLOTS,),
        [SCALARS, image_part, image_part, full_row, full_row, full_tab, spec((PIX, 1), lambda s, slot: (s, 0)),
         full((C_IN, C_MID)), spec((PIX, C_IN), lambda s, slot: (s, 0)), full((4 * PIX, 4 * PIX))],
        [image_part, spec((2, 1, 4 * PIX, C_IN // 2), lambda s, slot: (0, s, 0, 0))],
        [shape_of((4, ROWS, C_MID), BFLOAT), shape_of((2, SLOTS, 4 * PIX, C_IN // 2), BFLOAT)], [],
        (slots, inv, gz1, a1, total1, sum1, mid1, mask, narrow, dxs, perm), prefetch=1,
    )
    bufs_a = weight_grad("dw1", x, spec((4, ROWS, TILE), lambda t, slot: (0, 0, t)), ga1, 2, (6144, 256), TILE, 0, bufs_a)

    def place(name, pair):
        got = swap_pipe(pair[1])
        block = (1,) + pair.shape[2:]
        return call(
            k_place, name, (IMG_DEV,),
            [
                spec((1,) + block, lambda t, slot: (0, jnp.minimum(t, SLOTS - 1), 0, 0)),
                spec(block, lambda t, slot: (jnp.maximum(t - SLOTS, 0), 0, 0)),
            ],
            spec(block, lambda t, slot: (slot[t + (t >= SLOTS)], 0, 0)),
            shape_of((IMG_DEV,) + pair.shape[2:], BFLOAT), [],
            (slots, pair, got), prefetch=1,
        )

    block_local = place("place_out", blk.reshape(2, SLOTS, PIX, C_OUT // 2)).reshape(IMG_DEV, WB, HB, C_OUT // 2).transpose(0, 2, 1, 3)
    grad_local = place("place_grad", image_grad).reshape(IMG_DEV, 2 * HB, 2 * WB, C_IN // 2)

    half_a0, half_a1 = scatter_group("a", *bufs_a, w_narrow.shape[0], True)
    half_w0, half_w1 = scatter_group("w", *bufs_w, w_wide.shape[0], False)
    sum_b = (bufs_b[0].astype(SINGLE) + swap_pipe(bufs_b[1]).astype(SINGLE)).astype(BFLOAT)
    half_b = lax.psum_scatter(sum_b, "dp", scatter_dimension=0, tiled=True).astype(SINGLE)
    half_a = jnp.concatenate([half_a0, half_a1], axis=0)

    def join_halves(first, second):
        mine = jnp.where(core == 0, first, second)
        got = swap_pipe(jnp.where(core == 0, second, first))
        return jnp.where(core == 0, jnp.concatenate([mine, got], axis=1), jnp.concatenate([got, mine], axis=1))

    grad_narrow = join_halves(half_a, half_b)
    grad_wide = join_halves(half_w0, half_w1)

    def pair_sum(rows):
        return rows[0] + rows[1]

    mid_rows = jnp.stack([pair_sum(v) for t in (sum1, sum2, sum4, sum5) for v in (t[2:4], t[0:2])])
    wide_rows = jnp.stack([pair_sum(v) for v in (sum3[2:4], sum3[0:2], sum3[4:6], sum3[0:2], sum6[2:4], sum6[0:2])])
    mid_rows = mid_rows + swap_pipe(mid_rows)
    wide_rows = wide_rows + swap_pipe(wide_rows)
    grad_mid = lax.dynamic_slice(mid_rows, (0, shard * mid_cols), (8, mid_cols))
    grad_table = lax.dynamic_slice(wide_rows, (0, shard * wide_cols), (6, wide_cols))

    def square_vector(narrow_rows, wide_rows, mid_part, table_part):
        return jnp.concatenate(
            [
                jnp.dot(jnp.sum(narrow_rows * narrow_rows, axis=1), hot_narrow, precision=PRECISE),
                jnp.dot(jnp.sum(wide_rows * wide_rows, axis=1), hot_wide, precision=PRECISE),
                jnp.sum(mid_part * mid_part, axis=1),
                jnp.sum(table_part * table_part, axis=1),
            ]
        )

    squares = jnp.stack([square_vector(w_narrow, w_wide, bn_mid, bn_wide), square_vector(grad_narrow, grad_wide, grad_mid, grad_table)])
    squares = dp_sum(squares + swap_pipe(squares))
    norms = jnp.sqrt(squares)
    weight_norms, grad_norms = norms[0], norms[1]
    ratios = TRUST * weight_norms / (grad_norms + DECAY * weight_norms)
    ratio_narrow = jnp.dot(hot_narrow, ratios[:4], precision=PRECISE)
    ratio_wide = jnp.dot(hot_wide, ratios[4:7], precision=PRECISE)

    def lars_step(weight, gradient, moment, ratio_rows):
        new_moment = MOMENTUM * moment + RATE * ratio_rows[:, None] * (gradient + DECAY * weight)
        return (weight - new_moment, new_moment)

    new_narrow, new_mom_narrow = lars_step(w_narrow, grad_narrow, mom_narrow, ratio_narrow)
    new_wide, new_mom_wide = lars_step(w_wide, grad_wide, mom_wide, ratio_wide)
    new_mid, new_mom_mid = lars_step(bn_mid, grad_mid, mom_bn_mid, ratios[7:15])
    new_table, new_mom_table = lars_step(bn_wide, grad_table, mom_bn_wide, ratios[15:21])
    return (
        block_local, grad_local, grad_narrow, grad_wide, grad_mid, grad_table,
        new_mom_narrow, new_mom_wide, new_mom_mid, new_mom_table,
        new_narrow, new_wide, new_mid, new_table,
    )


def solution(mesh):
    rows = P(("pipe", "dp"), None)
    columns = P(None, ("pipe", "dp"))
    feature = P("dp", None, None, None)
    return jax.shard_map(
        on_device,
        mesh=mesh,
        in_specs=(feature, feature, P("dp"), P("dp"), P("dp", None), rows, rows, columns, columns, rows, rows, columns, columns),
        out_specs=(P("dp", None, None, "pipe"), P("dp", None, None, "pipe"), rows, rows, columns, columns, rows, rows, columns, columns, rows, rows, columns, columns),
        check_vma=False,
    )
```

```python
import jax
import jax.numpy as jnp
import numpy as np
from jax import lax
from jax.experimental import pallas as pl
from jax.experimental.pallas import tpu as pltpu
from jax.sharding import PartitionSpec as P

C_IN = 1024
C_MID = 512
C_OUT = 2048
R_N = 12288
R_W = 2048
HB = 8
WB = 12
IMG_DEV = 8
SLOTS = 4
PIX = HB * WB
ROWS = SLOTS * PIX
HALF = ROWS // 2
PAD = 16
TILE = 512

EPS = 1e-05
MOMENTUM = 0.9
DECAY = 5e-05
TRUST = 0.001
RATE = 29.0
PRECISE = lax.Precision.HIGHEST
BFLOAT = jnp.bfloat16
SINGLE = jnp.float32
MIB = 1024 * 1024
BYTES_PER_US = 1200000
MICROSECONDS = {
    "prep": 5, "a1": 3, "a2": 5, "as": 4.5, "a3": 4, "a4": 4.7, "a5": 4, "a6": 3.7, "head": 5.3, "g5": 5.2, "g4": 5.4, "gy": 7,
    "g2": 7.3, "g1": 8, "g0": 3, "gx": 6.4, "dxs": 5, "dw1": 3.4, "dw2": 2.1, "dw3": 2.9, "dws": 2.9, "dw4a": 1.7, "dw4b": 1.9,
    "dw5": 1.5, "dw6": 2.8, "place_out": 3.4, "place_grad": 5, "wa": 3, "wb": 3, "turn": 1.7, "keep": 1.7,
}


def pairs(bit):
    return [(i, i ^ bit) for i in range(lax.axis_size("dp"))]


def exchange(value, bit):
    return lax.ppermute(value, "dp", pairs(bit))


def pin(value, after):
    return lax.optimization_barrier((value, after))[0]


def dp_sum(value, fillers=()):
    size = lax.axis_size("dp")
    results = []
    step = 1
    while step < size:
        got = exchange(value, step)
        if len(results) < len(fillers):
            result = fillers[len(results)](value)
            got, result = lax.optimization_barrier((got, result))
            results.append(result)
        value = value + got
        step *= 2
    for filler in fillers[len(results) :]:
        results.append(filler(value))
    return value, results


def swap_pipe(value):
    return lax.ppermute(value, "pipe", [(0, 1), (1, 0)])


def dot(left, right):
    return jnp.dot(left, right, preferred_element_type=SINGLE)


def dot_back(left, right):
    return lax.dot_general(left, right, (((1,), (1,)), ((), ())), preferred_element_type=SINGLE)


def silu(value):
    return value * jax.nn.sigmoid(value)


def slope(value):
    gate = jax.nn.sigmoid(value)
    return gate * (1.0 + value * (1.0 - gate))


def put_sums(ref, values, first):
    for k, value in enumerate(values):
        for m in range(2):
            total = jnp.sum(value[m * HALF : (m + 1) * HALF], axis=0, keepdims=True)
            row = 2 * k + m
            ref[row : row + 1, :] = total if first else ref[row : row + 1, :] + total


def both(function):
    return jnp.concatenate([function(0), function(1)], axis=0)


def part(m):
    return slice(m * HALF, (m + 1) * HALF)


def moments(total_ref, inv_ref, m, scale=1.0):
    inv = inv_ref[m] * scale
    mean = total_ref[m : m + 1, :] * inv
    var = total_ref[2 + m : 3 + m, :] * inv - mean * mean
    return mean, lax.rsqrt(var + EPS)


def normed(a, total_ref, inv_ref, m, scale=1.0):
    mean, rstd = moments(total_ref, inv_ref, m, scale)
    return (a - mean) * rstd, rstd


def conv_grad(gz, xhat, rstd, gain, mask, sum_ref, inv_ref, m, scale=1.0, second=2):
    inv = inv_ref[m] * scale
    first_row = sum_ref[m : m + 1, :] * inv
    second_row = sum_ref[second + m : second + m + 1, :] * inv
    return (mask * ((rstd * gain) * (gz - first_row - xhat * second_row))).astype(BFLOAT)


def k_prep(slot_ref, img_ref, perm_ref, mask_ref, out_ref):
    planes = dot(perm_ref[...], img_ref[0])
    mask = mask_ref[...]
    for k in range(4):
        out_ref[k] = (planes[k * PIX : (k + 1) * PIX] * mask).astype(BFLOAT)


def k_first(x_ref, w_ref, a_ref, sum_ref):
    a = dot(x_ref[0], w_ref[...])
    a_ref[0] = a

    @pl.when(pl.program_id(0) == 0)
    def _():
        sum_ref[...] = jnp.zeros_like(sum_ref)

    put_sums(sum_ref, [a, a * a], False)


def shift_mask(di, dj):
    if not di and not dj:
        return None
    pixel = lax.broadcasted_iota(jnp.int32, (SLOTS, PIX, 1), 1)
    inside = None
    if di:
        row = pixel & (HB - 1)
        inside = row >= -di if di < 0 else row < HB - di
    if dj:
        column = pixel >= -dj * HB if dj < 0 else pixel < PIX - dj * HB
        inside = column if inside is None else inside & column
    return jnp.where(inside, 1.0, 0.0).astype(SINGLE).reshape(ROWS, 1)


def rows_at(pad, di, dj):
    start = PAD + HB * dj + di
    rows = pad[start : start + ROWS, :]
    mask = shift_mask(di, dj)
    return rows if mask is None else rows * mask


def clear_pad(pad):
    pad[0:PAD, :] = jnp.zeros((PAD, pad.shape[1]), SINGLE)
    pad[PAD + ROWS : PAD + ROWS + PAD, :] = jnp.zeros((PAD, pad.shape[1]), SINGLE)


def body(pad, m):
    return pad.at[PAD + m * HALF : PAD + (m + 1) * HALF, :]


def carried(ref, fresh):
    return jnp.where(fresh, 0.0, ref[...])


def k_conv_two(inv_ref, total_ref, tab_ref, mask_ref, a_ref, w0, w1, w2, out_ref, h_ref, sum_ref, pad, moved):
    step = pl.program_id(0)
    gain, bias = tab_ref[0:1, :], tab_ref[1:2, :]

    @pl.when(step < 2)
    def _():
        for k in range(2):
            clear_pad(pad.at[k])
            clear_pad(moved.at[k])
            for m in range(2):
                xhat, _unused = normed(a_ref[k, part(m), :], total_ref, inv_ref, m, 0.25)
                h = (silu(xhat * gain + bias) * mask_ref[part(m), :]).astype(BFLOAT)
                h_ref[k, part(m), :] = h
                body(pad.at[k], m)[...] = h.astype(SINGLE)
                body(moved.at[k], m)[...] = h.astype(SINGLE)

    @pl.when(step == 2)
    def _():
        for k in range(2):
            moved[k, PAD : PAD + ROWS, :] = rows_at(pad.at[k], -1, 0)

    term = dot(rows_at(moved.at[0], 0, 0).astype(BFLOAT), w1[...])
    term += dot(rows_at(moved.at[1], 0, -1).astype(BFLOAT), w0[...])
    term += dot(rows_at(moved.at[1], 0, 0).astype(BFLOAT), w2[...])
    out_ref[...] = carried(out_ref, step == 0) + term

    @pl.when(step == 2)
    def _():
        a = out_ref[...]
        masked = a * mask_ref[...]
        put_sums(sum_ref, [masked, masked * a], True)


def k_conv_one(inv_ref, total_ref, tab_ref, mask_ref, a_ref, w0, w1, w2, out_ref, h_ref, sum_ref, pad, moved):
    step = pl.program_id(0)
    gain, bias = tab_ref[0:1, :], tab_ref[1:2, :]

    @pl.when(step == 0)
    def _():
        clear_pad(pad)
        clear_pad(moved)
        for m in range(2):
            xhat, _unused = normed(a_ref[part(m), :], total_ref, inv_ref, m)
            h = (silu(xhat * gain + bias) * mask_ref[part(m), :]).astype(BFLOAT)
            h_ref[part(m), :] = h
            body(pad, m)[...] = h.astype(SINGLE)

    for s in range(3):

        @pl.when(step == s)
        def _(s=s):
            moved[PAD : PAD + ROWS, :] = rows_at(pad, s - 1, 0)

    term = dot(rows_at(moved, 0, -1).astype(BFLOAT), w0[...])
    term += dot(rows_at(moved, 0, 0).astype(BFLOAT), w1[...])
    term += dot(rows_at(moved, 0, 1).astype(BFLOAT), w2[...])
    out_ref[...] = carried(out_ref, step == 0) + term

    @pl.when(step == 2)
    def _():
        a = out_ref[...]
        masked = a * mask_ref[...]
        put_sums(sum_ref, [masked, masked * a], True)


def k_expand(inv_ref, total_ref, tab_ref, mask_ref, a_ref, w_ref, h_ref, out_ref, sum_ref):
    @pl.when(pl.program_id(0) == 0)
    def _():
        gain, bias = tab_ref[0:1, :], tab_ref[1:2, :]
        for m in range(2):
            xhat, _unused = normed(a_ref[part(m), :], total_ref, inv_ref, m)
            h_ref[part(m), :] = (silu(xhat * gain + bias) * mask_ref[part(m), :]).astype(BFLOAT)

    a = dot(h_ref[...], w_ref[...])
    out_ref[...] = a
    put_sums(sum_ref, [a, a * a], True)


def k_short(x_ref, w0, w1, out_ref, sum_ref):
    a = dot(x_ref[0, :, :TILE], w0[...]) + dot(x_ref[0, :, TILE:], w1[...])
    out_ref[...] = a
    put_sums(sum_ref, [a, a * a], True)


def k_meet(inv_ref, t3_ref, ts_ref, tab3_ref, tabs_ref, mask_ref, a3_ref, as_ref, wa_ref, wb_ref, y_ref, out_ref, sum_ref):
    step = pl.program_id(0)
    for m in range(2):
        x3, _unused = normed(a3_ref[part(m), :], t3_ref, inv_ref, m)
        xs, _unused = normed(as_ref[part(m), :], ts_ref, inv_ref, m)
        joined = (x3 * tab3_ref[0:1, :] + tab3_ref[1:2, :]) + (xs * tabs_ref[0:1, :] + tabs_ref[1:2, :])
        y_ref[part(m), :] = (silu(joined) * mask_ref[part(m), :]).astype(BFLOAT)

    @pl.when(step == 0)
    def _():
        out_ref[...] = dot(y_ref[...], wa_ref[...])

    @pl.when(step > 0)
    def _():
        out_ref[...] += dot(y_ref[...], wb_ref[...])

    @pl.when(step == pl.num_programs(0) - 1)
    def _():
        a = out_ref[...]
        put_sums(sum_ref, [a, a * a], True)


def k_head(slot_ref, inv_ref, total_ref, tab_ref, mask_ref, a_ref, y_ref, c0, c1, c2, c3, blk_ref, gz_ref, sum_ref):
    cots = (c0, c1, c2, c3)
    gain, bias = tab_ref[0:1, :], tab_ref[1:2, :]
    for m in range(2):
        mask = mask_ref[part(m), :]
        xhat, _unused = normed(a_ref[part(m), :], total_ref, inv_ref, m)
        z = (xhat * gain + bias) + y_ref[part(m), :].astype(SINGLE)
        gate = jax.nn.sigmoid(z)
        blk_ref[0, part(m), :] = (z * gate * mask).astype(BFLOAT)
        cot = jnp.concatenate([cots[2 * m][0], cots[2 * m + 1][0]], axis=0).astype(SINGLE)
        gz = cot * mask * (gate * (1.0 + z * (1.0 - gate)))
        gz_ref[part(m), :] = gz
        sum_ref[m : m + 1, :] = jnp.sum(gz, axis=0, keepdims=True)
        sum_ref[2 + m : 3 + m, :] = jnp.sum(gz * xhat, axis=0, keepdims=True)


def finish_back(gz_ref, sum_ref, grad, a_ref, total_ref, tab_ref, inv_ref, mask_ref):
    gain, bias = tab_ref[0:1, :], tab_ref[1:2, :]
    for m in range(2):
        xhat, _unused = normed(a_ref[part(m), :], total_ref, inv_ref, m)
        gz = grad[part(m)] * mask_ref[part(m), :] * slope(xhat * gain + bias)
        gz_ref[part(m), :] = gz
        sum_ref[m : m + 1, :] = jnp.sum(gz, axis=0, keepdims=True)
        sum_ref[2 + m : 3 + m, :] = jnp.sum(gz * xhat, axis=0, keepdims=True)


def k_back_six(inv_ref, gz_ref, a_ref, total_ref, s_ref, tab_ref, mask_ref, w_ref, low_ref, low_total, low_tab, ga_ref, out_ref, sum_ref, acc):
    step = pl.program_id(0)
    for m in range(2):
        xhat, rstd = normed(a_ref[part(m), :], total_ref, inv_ref, m)
        ga_ref[part(m), :] = conv_grad(
            gz_ref[part(m), :], xhat, rstd, tab_ref[0:1, :], mask_ref[part(m), :], s_ref, inv_ref, m
        )
    term = dot_back(ga_ref[...], w_ref[...])

    @pl.when(step == 0)
    def _():
        acc[...] = term

    @pl.when(step > 0)
    def _():
        acc[...] += term

    @pl.when(step == pl.num_programs(0) - 1)
    def _():
        finish_back(out_ref, sum_ref, acc[...], low_ref, low_total, low_tab, inv_ref, mask_ref)


def k_back_conv_one(inv_ref, gz_ref, a_ref, total_ref, s_ref, tab_ref, mask_ref, w0, w1, w2, low_ref, low_total, low_tab, col_ref, out_ref, sum_ref, pad, moved, acc):
    step = pl.program_id(0)

    @pl.when(step == 0)
    def _():
        clear_pad(pad)
        clear_pad(moved)
        for m in range(2):
            xhat, rstd = normed(a_ref[part(m), :], total_ref, inv_ref, m)
            ga = conv_grad(gz_ref[part(m), :], xhat, rstd, tab_ref[0:1, :], mask_ref[part(m), :], s_ref, inv_ref, m)
            body(pad, m)[...] = ga.astype(SINGLE)

    for s in range(3):

        @pl.when(step == s)
        def _(s=s):
            moved[PAD : PAD + ROWS, :] = rows_at(pad, 1 - s, 0)

    term = None
    for kx, weight in enumerate((w0, w1, w2)):
        tap = rows_at(moved, 0, 1 - kx).astype(BFLOAT)
        col_ref[kx] = tap
        product = dot_back(tap, weight[...])
        term = product if term is None else term + product
    acc[...] = carried(acc, step == 0) + term

    @pl.when(step == 2)
    def _():
        finish_back(out_ref, sum_ref, acc[...], low_ref, low_total, low_tab, inv_ref, mask_ref)


def k_back_four(inv_ref, gz_ref, a_ref, total_ref, s_ref, tab_ref, mask_ref, wa_ref, wb_ref, up_ref, a3_ref, as_ref, t3_ref, ts_ref, tab3_ref, tabs_ref, ga_ref, gj_ref, sum_ref):
    @pl.when(pl.program_id(0) == 0)
    def _():
        for m in range(2):
            xhat, rstd = normed(a_ref[part(m), :], total_ref, inv_ref, m)
            ga_ref[part(m), :] = conv_grad(
                gz_ref[part(m), :], xhat, rstd, tab_ref[0:1, :], mask_ref[part(m), :], s_ref, inv_ref, m
            )

    weight = jnp.where(pl.program_id(0) == 0, wa_ref[...], wb_ref[...])
    grad = dot_back(ga_ref[...], weight) + up_ref[...]
    for m in range(2):
        x3, _unused = normed(a3_ref[part(m), :], t3_ref, inv_ref, m)
        xs, _unused = normed(as_ref[part(m), :], ts_ref, inv_ref, m)
        joined = (x3 * tab3_ref[0:1, :] + tab3_ref[1:2, :]) + (xs * tabs_ref[0:1, :] + tabs_ref[1:2, :])
        gj = grad[part(m)].astype(BFLOAT).astype(SINGLE) * mask_ref[part(m), :] * slope(joined)
        gj_ref[part(m), :] = gj
        for k, value in enumerate((gj, gj * x3, gj * xs)):
            row = 2 * k + m
            sum_ref[row : row + 1, :] = jnp.sum(value, axis=0, keepdims=True)


def k_back_three(inv_ref, gj_ref, a3_ref, as_ref, t3_ref, ts_ref, s_ref, tab3_ref, tabs_ref, mask_ref, w_ref, low_ref, low_total, low_tab, g3_ref, gs_ref, out_ref, sum_ref, acc):
    step = pl.program_id(0)
    for m in range(2):
        mask = mask_ref[part(m), :]
        gj = gj_ref[part(m), :]
        x3, r3 = normed(a3_ref[part(m), :], t3_ref, inv_ref, m)
        g3_ref[part(m), :] = conv_grad(gj, x3, r3, tab3_ref[0:1, :], mask, s_ref, inv_ref, m)
        xs, rs = normed(as_ref[part(m), :], ts_ref, inv_ref, m)
        gs_ref[part(m), :] = conv_grad(gj, xs, rs, tabs_ref[0:1, :], mask, s_ref, inv_ref, m, second=4)
    term = dot_back(g3_ref[...], w_ref[...])

    @pl.when(step == 0)
    def _():
        acc[...] = term

    @pl.when(step > 0)
    def _():
        acc[...] += term

    @pl.when(step == pl.num_programs(0) - 1)
    def _():
        finish_back(out_ref, sum_ref, acc[...], low_ref, low_total, low_tab, inv_ref, mask_ref)


def k_back_conv_two(inv_ref, gz_ref, a_ref, total_ref, s_ref, tab_ref, mask_ref, w0, w1, w2, low_ref, low_total, low_tab, col_ref, out_ref, sum_ref, pad, moved, acc):
    step = pl.program_id(0)
    gain, bias = low_tab[0:1, :], low_tab[1:2, :]

    @pl.when(step == 0)
    def _():
        clear_pad(pad)
        clear_pad(moved)
        for m in range(2):
            xhat, rstd = normed(a_ref[part(m), :], total_ref, inv_ref, m)
            ga = conv_grad(gz_ref[part(m), :], xhat, rstd, tab_ref[0:1, :], mask_ref[part(m), :], s_ref, inv_ref, m)
            body(pad, m)[...] = ga.astype(SINGLE)
            body(moved, m)[...] = ga.astype(SINGLE)
        sum_ref[...] = jnp.zeros_like(sum_ref)

    @pl.when(step == 2)
    def _():
        moved[PAD : PAD + ROWS, :] = rows_at(pad, 1, 0)

    plain = rows_at(moved, 0, 0).astype(BFLOAT)
    aside = rows_at(moved, 0, 1).astype(BFLOAT)
    col_ref[0], col_ref[1], col_ref[2] = aside, plain, plain
    acc[0] = carried(acc.at[0], step < 2) + dot_back(plain, w1[...])
    acc[1] = carried(acc.at[1], step < 2) + (dot_back(aside, w0[...]) + dot_back(plain, w2[...]))

    @pl.when(step != 1)
    def _():
        for k in range(2):
            for m in range(2):
                xhat, _unused = normed(low_ref[k, part(m), :], low_total, inv_ref, m, 0.25)
                gz = acc[k, part(m), :] * mask_ref[part(m), :] * slope(xhat * gain + bias)
                out_ref[k, part(m), :] = gz
                for q, value in enumerate((gz, gz * xhat)):
                    row = 2 * q + m
                    sum_ref[row : row + 1, :] += jnp.sum(value, axis=0, keepdims=True)


def k_wide_back(g_ref, w_ref, *refs):
    refs[-1][...] = dot_back(g_ref[...], w_ref[...])


def k_first_grad(inv_ref, gz_ref, a_ref, total_ref, s_ref, tab_ref, mask_ref, ga_ref):
    for m in range(2):
        xhat, rstd = normed(a_ref[0, part(m), :], total_ref, inv_ref, m, 0.25)
        ga_ref[0, part(m), :] = conv_grad(
            gz_ref[0, part(m), :], xhat, rstd, tab_ref[0:1, :], mask_ref[part(m), :], s_ref, inv_ref, m, 0.25
        )


def k_image_grad(slot_ref, ga_ref, mask_ref, w_ref, short_ref, perm_ref, *refs):
    out_ref = refs[-1]
    grads = dot_back(ga_ref[...].reshape(4 * PIX, C_MID), w_ref[...])
    mask = mask_ref[...]
    parts = []
    for k in range(4):
        grad = grads[k * PIX : (k + 1) * PIX]
        if k == 0:
            grad = grad + short_ref[...]
        parts.append((grad * mask).astype(BFLOAT))
    planes = jnp.concatenate(parts, axis=0)
    image = lax.dot_general(perm_ref[...], planes, (((0,), (0,)), ((), ())), preferred_element_type=SINGLE).astype(BFLOAT)
    core = slot_ref[SLOTS]
    out_ref[core, 0] = image[:, : C_IN // 2]
    out_ref[1 - core, 0] = image[:, C_IN // 2 :]


def k_place(slot_ref, own_ref, got_ref, *refs):
    out_ref = refs[-1]
    step = pl.program_id(0)

    @pl.when(step < SLOTS)
    def _():
        out_ref[0] = own_ref[0, 0]

    @pl.when(step >= SLOTS)
    def _():
        out_ref[0] = got_ref[0]


def k_turn(in_ref, *refs):
    refs[-1][...] = in_ref[...].reshape(in_ref.shape[-2:]).T


def k_grad(slot_ref, feature_ref, grad_ref, *refs):
    keep_ref, send_ref = refs[-2:]
    core = slot_ref[SLOTS]
    rows, half = feature_ref.shape[-2], grad_ref.shape[-1] // 2
    for k in range(grad_ref.shape[0]):
        feature = feature_ref[k % feature_ref.shape[0]]
        for ref, side in ((keep_ref, core), (send_ref, 1 - core)):
            columns = pl.ds(pl.multiple_of(side * half, half), half)
            ref[k * rows : (k + 1) * rows] = dot(feature, grad_ref[k, :, columns]).astype(BFLOAT)


def k_keep(in_ref, *refs):
    out_ref, sem = refs[-2:]
    copy = pltpu.make_async_copy(in_ref, out_ref, sem)
    copy.start()
    copy.wait()


def k_join(*refs):
    ins, outs, sems = refs[:4], refs[-3:-1], refs[-1]
    copies = []
    for which in range(2):
        for side in range(2):
            source = ins[2 * which + side]
            size = source.shape[0]
            copies.append(pltpu.make_async_copy(source, outs[which].at[pl.ds(side * size, size)], sems.at[len(copies)]))
    for copy in copies:
        copy.start()
    for copy in copies:
        copy.wait()


def k_gather(me_ref, *refs):
    ins, out_ref, sems = refs[:8], refs[8], refs[9]
    rows, cols = ins[0].shape[1:]
    copies = []
    for other in range(2):
        column = pl.multiple_of((1 - me_ref[1] if other else me_ref[1]) * cols, cols)
        for which in range(2):
            for came in range(2):
                source = ins[4 * other + 2 * which + came]
                for q in range(8):
                    third, low, high = q >> 2, (q >> 1) & 1, q & 1
                    pair = 2 * third + came if which == 0 else 2 * came + third
                    block = me_ref[0] ^ (8 * high + 4 * low + pair)
                    row = pl.multiple_of((2 * block + which) * rows, rows)
                    target = out_ref.at[pl.ds(row, rows), pl.ds(column, cols)]
                    copies.append(pltpu.make_async_copy(source.at[q], target, sems.at[len(copies)]))
    for copy in copies:
        copy.start()
    for copy in copies:
        copy.wait()


def k_split(me_ref, *refs):
    own, got, outs = refs[:4], refs[4:8], refs[8:]
    for own_ref, got_ref, out_ref in zip(own, got, outs):
        out_ref[0] = (own_ref[...].astype(SINGLE) + got_ref[...].astype(SINGLE)).astype(BFLOAT)


def full(shape):
    zeros = (0,) * len(shape)
    return pl.BlockSpec(tuple(shape), lambda *_: zeros)


SCALARS = pl.BlockSpec(memory_space=pltpu.SMEM)
ANYWHERE = pl.BlockSpec(memory_space=pl.ANY)


def spec(shape, index):
    return pl.BlockSpec(tuple(shape), index)


def call(kernel, name, grid, in_specs, out_specs, out_shape, scratch, args, prefetch=0, vmem=8, aliases=None):
    return pl.pallas_call(
        kernel,
        out_shape=out_shape,
        grid_spec=pltpu.PrefetchScalarGridSpec(
            num_scalar_prefetch=prefetch,
            grid=grid,
            in_specs=in_specs,
            out_specs=out_specs,
            scratch_shapes=scratch,
        ),
        input_output_aliases=aliases or {},
        compiler_params=pltpu.CompilerParams(vmem_limit_bytes=vmem * MIB),
        cost_estimate=pl.CostEstimate(flops=0, bytes_accessed=int(MICROSECONDS.get(name, 1) * BYTES_PER_US), transcendentals=0),
        name=name,
    )(*args)


def shape_of(shape, dtype=SINGLE):
    return jax.ShapeDtypeStruct(tuple(shape), dtype)


def vmem_of(shape, dtype=SINGLE):
    return pltpu.VMEM(tuple(shape), dtype)


def hbm_of(shape, dtype=SINGLE):
    return pltpu.HBM(tuple(shape), dtype)


def in_vmem(value):
    return pltpu.with_memory_space_constraint(value, pltpu.VMEM)


def in_hbm(value):
    return pltpu.with_memory_space_constraint(value, pltpu.HBM)


def permutation():
    table = np.zeros((4 * PIX, 4 * PIX), np.float32)
    for pi in range(2):
        for pj in range(2):
            for i in range(HB):
                for j in range(WB):
                    table[((2 * pi + pj) * WB + j) * HB + i, (2 * i + pi) * 2 * WB + 2 * j + pj] = 1.0
    return jnp.asarray(table, BFLOAT)


def group_table(start_index, rows_local, bounds):
    global_rows = start_index * rows_local + jnp.arange(rows_local, dtype=jnp.int32)
    group_ids = jnp.zeros((rows_local,), jnp.int32)
    for boundary in bounds:
        group_ids = group_ids + (global_rows >= boundary).astype(jnp.int32)
    return (group_ids[:, None] == jnp.arange(len(bounds) + 1, dtype=jnp.int32)[None, :]).astype(SINGLE)


def rounded(value):
    return lax.reduce_precision(value, 8, 7)


def split_group(name, keep, got, rows, index):
    cols = keep.shape[1]

    def block(which, sent):
        def at(q, me):
            other, low, high = (q >> 2) & 1, (q >> 1) & 1, q & 1
            pair = other * 2 + sent if which == 0 else sent * 2 + other
            return (index(which, me[0] ^ (high * 8 + low * 4 + pair)), 0)

        return spec((rows, cols), at)

    blocks = [block(which, sent) for which in range(2) for sent in range(2)]
    return call(
        k_split, name, (8,), blocks + blocks,
        [spec((1, rows, cols), lambda q, me: (q, 0, 0))] * 4,
        [shape_of((8, rows, cols), BFLOAT)] * 4, [],
        (lax.axis_index("dp")[None].astype(jnp.int32),) + (keep,) * 4 + (got,) * 4, prefetch=1,
    )


def halved(keep, got):
    total = keep.astype(SINGLE) + got.astype(SINGLE)
    half = total.shape[0] // 2
    return total[:half].astype(BFLOAT), total[half:].astype(BFLOAT)


def added(keep, got):
    return keep[0].astype(SINGLE) + got[0].astype(SINGLE)


def halve(keep, send, bits, came=None):
    for bit in bits:
        got, came = exchange(send, bit) if came is None else came, None
        if keep.shape[0] > 1:
            keep, send = halved(keep, got)
    return added(keep, got)


def scatter_plain(keep, got, block, by_rows):
    total = (keep.astype(SINGLE) + got.astype(SINGLE)).astype(BFLOAT)
    if by_rows:
        own = lax.psum_scatter(total, "dp", scatter_dimension=0, tiled=True).astype(SINGLE)
        return own[: block // 2], own[block // 2 :]
    middle = total.shape[0] // 2
    return tuple(lax.psum_scatter(p, "dp", scatter_dimension=0, tiled=True).astype(SINGLE) for p in (total[:middle], total[middle:]))


def joined(value, got):
    return jnp.concatenate([value, got], axis=0)


def gather_blocks(name, core, parts, others, out_shape):
    scalars = jnp.stack([lax.axis_index("dp"), core]).astype(jnp.int32)
    pieces = [a for pair in list(parts) + list(others) for a in pair]
    return call(
        k_gather, name, (), [ANYWHERE] * 8, ANYWHERE, vmem_of(out_shape, BFLOAT),
        [pltpu.SemaphoreType.DMA((64,))], (scalars, *pieces), prefetch=1, vmem=2,
    )


def swap_all(parts):
    return [tuple(swap_pipe(a) for a in pair) for pair in parts]


def join_two(stayed, came, token):
    pieces = (stayed[0], came[0], stayed[1], came[1])
    shape = (2 * stayed[0].shape[0],) + stayed[0].shape[1:]
    return call(
        k_join, "join", (), [ANYWHERE] * 5, [ANYWHERE] * 2, [vmem_of(shape, BFLOAT)] * 2,
        [pltpu.SemaphoreType.DMA((4,))], pieces + (token,), vmem=2,
    )


def keep_in_hbm(value):
    def filler(token):
        return call(
            k_keep, "keep", (), [ANYWHERE] * 2, ANYWHERE, hbm_of(value.shape, value.dtype),
            [pltpu.SemaphoreType.DMA], (in_vmem(value), token), vmem=2,
        )

    return filler


def nothing(token):
    return token


def both_of(*fillers):
    return lambda token: tuple(filler(token) for filler in fillers)


def on_device(images, cotangent, heights, widths, assign, w_narrow, w_wide, bn_mid, bn_wide, mom_narrow, mom_wide, mom_bn_mid, mom_bn_wide):
    core = lax.axis_index("pipe")
    shard = lax.axis_index(("pipe", "dp"))
    fast = lax.axis_size("dp") == 16

    own_narrow = w_narrow.astype(BFLOAT)
    own_wide = w_wide.astype(BFLOAT)
    rows_n, half_n = w_narrow.shape[0], C_MID // 2
    part_n = rows_n // 2
    whole_n = (R_N // 2, C_MID)
    if fast:
        sent = swap_pipe(jnp.where(core == 0, own_narrow[:, half_n:], own_narrow[:, :half_n]))
        kept = jnp.where(core == 0, own_narrow[:, :half_n], own_narrow[:, half_n:])
        mine_a, mine_b = jnp.where(core == 0, kept, sent), jnp.where(core == 0, sent, kept)
        a0, a1 = mine_a[None, :part_n], mine_a[None, part_n:]
        b0, b1 = mine_b[None, :part_n], mine_b[None, part_n:]
        got = lax.optimization_barrier((exchange(a0, 8), exchange(a1, 8)))
        a0, a1 = join_two((a0, a1), got, got[1])
        got = lax.optimization_barrier((exchange(a0, 4), exchange(a1, 4)))
        a0, a1 = join_two((a0, a1), got, got[1])
        got = lax.optimization_barrier((exchange(a0, 2), exchange(a1, 1)))
        a0, a1 = join_two((a0, a1), got, got[1])
        third_done = a1
        last0, last1 = exchange(a0, 1), exchange(a1, 2)
        stay_a = swap_all([(a0,), (a1,)])
        b0, b1 = pin((b0, b1), third_done)
        got = exchange(b0, 8), exchange(b1, 8)
        own_wide = pin(own_wide, third_done)
    else:
        narrow = lax.all_gather(own_narrow, ("pipe", "dp"), axis=0, tiled=True)
        narrow_a, narrow_b = narrow[: R_N // 2], narrow[R_N // 2 :]
        third_done = narrow
    wide = lax.all_gather(own_wide, ("pipe", "dp"), axis=0, tiled=True)

    own_heights, own_widths, own_assign = pin((heights, widths, assign), third_done)
    order = own_assign[0].reshape(2, SLOTS)
    own_slots = lax.dynamic_index_in_dim(order, core, 0, keepdims=False)
    other_slots = lax.dynamic_index_in_dim(order, 1 - core, 0, keepdims=False)
    slots = jnp.concatenate([own_slots, core[None].astype(jnp.int32), other_slots])
    heights_own, widths_own = own_heights[own_slots], own_widths[own_slots]
    inside = (jnp.arange(HB)[None, None, :] < heights_own[:, None, None]) & (jnp.arange(WB)[None, :, None] < widths_own[:, None, None])
    mask = in_vmem(inside.astype(SINGLE).reshape(ROWS, 1))
    perm = permutation()
    x = call(
        k_prep, "prep", (SLOTS,),
        [spec((1, 4 * PIX, C_IN), lambda s, slot: (slot[s], 0, 0)), full((4 * PIX, 4 * PIX)), spec((PIX, 1), lambda s, slot: (s, 0))],
        spec((4, PIX, C_IN), lambda s, slot: (0, s, 0)),
        vmem_of((4, ROWS, C_IN), BFLOAT), [],
        (slots, in_hbm(images.reshape(IMG_DEV, 4 * PIX, C_IN)), in_hbm(perm), mask), prefetch=1, vmem=10,
    )
    counts = jnp.sum((own_heights * own_widths)[own_assign[0]].reshape(4, 2), axis=1).astype(SINGLE)
    mid_cols, wide_cols = bn_mid.shape[1], bn_wide.shape[1]
    tables = jnp.concatenate(
        [
            lax.dynamic_update_slice(jnp.zeros((8, C_MID), SINGLE), rounded(bn_mid), (0, shard * mid_cols)),
            lax.dynamic_update_slice(jnp.zeros((6, C_OUT), SINGLE), rounded(bn_wide), (0, shard * wide_cols)).reshape(24, C_MID),
        ]
    )
    tables = pin(tables, third_done)
    tables = tables + swap_pipe(tables)
    tables = jnp.concatenate([tables, jnp.zeros((4, C_MID), SINGLE).at[0, :4].set(counts)])

    held = {}
    if fast:
        last0, last1, got, x, tables = lax.optimization_barrier((last0, last1, got, x, tables))
        came_a = swap_all([(last0,), (last1,)])
        own_b = join_two((b0, b1), got, got[1])
        held["got"] = exchange(own_b[0], 4), exchange(own_b[1], 4)
        narrow_a = gather_blocks("wa", core, [(a0, last0), (a1, last1)], [u + v for u, v in zip(stay_a, came_a)], whole_n)

    def turn(feature, feature_spec, grid, shape, index):
        def filler(token):
            return call(
                k_turn, "turn", grid, [feature_spec, ANYWHERE],
                spec((C_MID, ROWS), index), hbm_of(shape, BFLOAT), [], (feature, token),
            )

        return filler

    def weight_grad(name, feature, feature_spec, grad, grad_spec, tiles, shape, rows, base, bufs, token, space):
        out_spec = spec((rows, shape[1]), lambda t, slot: (base + t, 0))
        hold = in_vmem if space is vmem_of else in_hbm
        extra = tuple(hold(b) for b in bufs or ()) + (() if token is None else (token,))
        return call(
            k_grad, name, (tiles,), [feature_spec, grad_spec] + [ANYWHERE] * len(extra),
            [out_spec] * 2, [space(shape, BFLOAT)] * 2, [], (slots, feature, grad) + extra,
            prefetch=1, vmem=9, aliases={3: 0, 4: 1} if bufs else {},
        )

    full_row = full((4, C_MID))
    full_tab = full((2, C_MID))
    full_mask = full((ROWS, 1))
    full_mid = full((ROWS, C_MID))
    plane_pair = spec((2, ROWS, C_MID), lambda s: (jnp.minimum(s, 1), 0, 0))

    def narrow_block(index):
        return spec((TILE, TILE), index)

    chunk = spec((ROWS, TILE), lambda k, *_: (0, k))
    chunk_sum = spec((4, TILE), lambda k, *_: (0, k))
    chunk_tab = spec((2, TILE), lambda k, *_: (0, k))
    four_a = narrow_block(lambda k: (11, 0))
    four_b = narrow_block(lambda k: (jnp.maximum(k - 1, 0), 0))

    a1, part1 = call(
        k_first, "a1", (4,),
        [spec((1, ROWS, C_IN), lambda k: (k, 0, 0)), full((C_IN, C_MID))],
        [spec((1, ROWS, C_MID), lambda k: (k, 0, 0)), full_row],
        [hbm_of((4, ROWS, C_MID)), shape_of((4, C_MID))], [],
        (in_vmem(x), in_vmem(narrow_a)), vmem=8,
    )

    def third_b(token):
        if not fast:
            return token
        big = join_two(own_b, pin(held["got"], token), token)
        held["got"] = exchange(big[0], 2), exchange(big[1], 1)
        return big

    a1 = in_hbm(a1)
    first_sum, (a_kept, x_kept, big_b) = dp_sum(jnp.concatenate([part1, tables]), [keep_in_hbm(narrow_a), keep_in_hbm(x), third_b])
    x_kept, a_kept = in_hbm(x_kept), in_hbm(a_kept)
    total1, tables = first_sum[:4], first_sum[4:]
    mid, table = tables[:8], tables[8:32].reshape(6, C_OUT)
    inv = lax.dynamic_slice(1.0 / tables[32, :4], (2 * core,), (2,))
    mid1, mid2, mid4, mid5 = (mid[2 * k : 2 * k + 2] for k in range(4))
    tab3, tabs, tab6 = (table[2 * k : 2 * k + 2] for k in range(3))

    a_s, part_s = call(
        k_short, "as", (4,),
        [spec((1, ROWS, C_IN), lambda k: (0, 0, 0)), spec((TILE, TILE), lambda k: (1, k)), spec((TILE, TILE), lambda k: (2, k))],
        [chunk, chunk_sum],
        [vmem_of((ROWS, C_OUT)), shape_of((4, C_OUT))], [],
        (in_vmem(x), in_hbm(wide), in_hbm(wide)), vmem=8,
    )

    def conv_weights(first, order_of):
        return [narrow_block(lambda s, kx=kx: (first + 3 * order_of(s) + kx, 0)) for kx in range(3)]

    turned = lambda s: lax.rem(s + 1, 3)
    straight = lambda s: s

    a2, h1, part2 = call(
        k_conv_two, "a2", (3,),
        [SCALARS, full_row, full_tab, full_mask, plane_pair] + conv_weights(2, turned),
        [full_mid, plane_pair, full_row],
        [vmem_of((ROWS, C_MID)), vmem_of((4, ROWS, C_MID), BFLOAT), shape_of((4, C_MID))],
        [pltpu.VMEM((2, PAD + ROWS + PAD, C_MID), SINGLE)] * 2,
        (inv, total1, mid1, mask, a1) + (a_kept,) * 3, vmem=15,
    )
    a2 = in_vmem(a2)

    def fourth_b(token):
        if not fast:
            return token
        big = join_two(big_b, pin(held["got"], token), token)
        held["got"] = exchange(big[0], 1), exchange(big[1], 2)
        return big

    turn_h1 = turn(h1, spec((1, ROWS, C_MID), lambda k: (k, 0, 0)), (4,), (4 * C_MID, ROWS), lambda k: (k, 0))
    total2, (h1_t, _unused, whole_b) = dp_sum(part2, [turn_h1, nothing, fourth_b])

    def expand(name, a, total, tab, row):
        return call(
            k_expand, name, (4,),
            [SCALARS, full_row, full_tab, full_mask, full_mid, spec((TILE, TILE), lambda k: (row, k))],
            [full_mid, chunk, chunk_sum],
            [vmem_of((ROWS, C_MID), BFLOAT), vmem_of((ROWS, C_OUT)), shape_of((4, C_OUT))], [],
            (inv, total, tab, mask, a, in_hbm(wide)), vmem=8,
        )

    h2, a3, part3 = expand("a3", a2, total2, mid2, 0)
    whole = spec((ROWS, C_MID), lambda k: (0, 0))

    def swap_b(token):
        if not fast:
            return token
        ready = pin(whole_b + held["got"], token)
        return [(ready[0], ready[2]), (ready[1], ready[3])]

    def gather_b(token):
        if not fast:
            return narrow_b
        others = pin(held["others"], token)
        return gather_blocks("wb", core, held["parts"], others, whole_n)

    def start_swap_b(token):
        if fast:
            held["parts"] = swap_b(token)
            held["others"] = swap_all(held["parts"])
        return token

    total3s, ((h2_t, as_kept), (_unused, a3_kept), _unused, narrow_b) = dp_sum(
        jnp.concatenate([part3, part_s]),
        [
            both_of(turn(h2, whole, (1,), (C_MID, ROWS), lambda k: (0, 0)), keep_in_hbm(a_s)),
            both_of(start_swap_b, keep_in_hbm(a3)),
            nothing,
            gather_b,
        ],
    )
    as_kept, a3_kept = in_hbm(as_kept), in_hbm(a3_kept)
    total3, total_s = total3s[:4], total3s[4:]

    y, a4, part4 = call(
        k_meet, "a4", (4,),
        [SCALARS, chunk_sum, chunk_sum, chunk_tab, chunk_tab, full_mask, chunk, chunk, four_a, four_b],
        [chunk, full_mid, full_row],
        [vmem_of((ROWS, C_OUT), BFLOAT), vmem_of((ROWS, C_MID)), shape_of((4, C_MID))], [],
        (inv, total3, total_s, tab3, tabs, mask, in_vmem(a3), in_vmem(a_s), a_kept, in_vmem(narrow_b)), vmem=10,
    )
    a4 = in_vmem(a4)
    def turn_x(q, start, into):
        def filler(token):
            extra = () if into is None else (in_hbm(into[-1]),)
            held["x_t"] = call(
                k_turn, "turn", (2,), [spec((1, ROWS, C_MID), lambda k: (start + k, 0, q))] + [ANYWHERE] * (1 + len(extra)),
                spec((C_MID, ROWS), lambda k: (q, start + k)), hbm_of((C_IN, 4 * ROWS), BFLOAT), [], (x_kept, *extra, token),
                aliases={1: 0} if extra else {},
            )
            return held["x_t"]

        return filler

    total4, (y_t, y_kept, x_t0, x_t1) = dp_sum(
        part4,
        [
            turn(in_vmem(y), spec((ROWS, C_MID), lambda k: (0, k)), (4,), (4 * C_MID, ROWS), lambda k: (k, 0)),
            keep_in_hbm(y),
            turn_x(0, 0, None),
            lambda token: turn_x(0, 2, [held["x_t"]])(token),
        ],
    )
    del x_t0

    a5, h4, part5 = call(
        k_conv_one, "a5", (3,),
        [SCALARS, full_row, full_tab, full_mask, full_mid] + conv_weights(3, straight),
        [full_mid, full_mid, full_row],
        [vmem_of((ROWS, C_MID)), vmem_of((ROWS, C_MID), BFLOAT), shape_of((4, C_MID))],
        [pltpu.VMEM((PAD + ROWS + PAD, C_MID), SINGLE)] * 2,
        (inv, total4, mid4, mask, a4) + (in_vmem(narrow_b),) * 3, vmem=9,
    )
    a5 = in_vmem(a5)
    total5, (h4_t, b_kept, _unused, x_t) = dp_sum(
        part5,
        [
            turn(h4, whole, (1,), (C_MID, ROWS), lambda k: (0, 0)),
            keep_in_hbm(narrow_b),
            turn_x(1, 0, [x_t1]),
            lambda token: turn_x(1, 2, [held["x_t"]])(token),
        ],
    )
    b_kept = in_hbm(b_kept)
    h5, a6, part6 = expand("a6", a5, total5, mid5, 3)
    total6, (h5_t, a6_kept) = dp_sum(part6, [turn(h5, whole, (1,), (C_MID, ROWS), lambda k: (0, 0)), keep_in_hbm(a6)])
    a6_kept = in_hbm(a6_kept)

    cot = in_hbm(cotangent.transpose(0, 2, 1, 3).reshape(IMG_DEV, PIX, C_OUT))
    blk, gz6, s6 = call(
        k_head, "head", (4,),
        [SCALARS, chunk_sum, chunk_tab, full_mask, chunk, chunk]
        + [spec((1, PIX, TILE), lambda k, slot, s=s: (slot[s], 0, k)) for s in range(SLOTS)],
        [
            spec((1, ROWS, TILE), lambda k, slot: ((k // 2) ^ slot[SLOTS], 0, lax.rem(k, 2))),
            chunk,
            chunk_sum,
        ],
        [shape_of((2, ROWS, C_OUT // 2), BFLOAT), vmem_of((ROWS, C_OUT)), shape_of((4, C_OUT))], [],
        (slots, inv, total6, tab6, mask, in_vmem(a6), in_hbm(y_kept), cot, cot, cot, cot), prefetch=1, vmem=10,
    )
    gz6 = in_vmem(gz6)

    def place(name, pair, got, token):
        block = (1,) + pair.shape[2:]
        return call(
            k_place, name, (IMG_DEV,),
            [
                spec((1,) + block, lambda t, slot: (0, jnp.minimum(t, SLOTS - 1), 0, 0)),
                spec(block, lambda t, slot: (jnp.maximum(t - SLOTS, 0), 0, 0)),
                ANYWHERE,
            ],
            spec(block, lambda t, slot: (slot[t + (t >= SLOTS)], 0, 0)),
            shape_of((IMG_DEV,) + pair.shape[2:], BFLOAT), [],
            (slots, pair, got, token), prefetch=1, vmem=4,
        )

    blk = blk.reshape(2, SLOTS, PIX, C_OUT // 2)
    sum6, (got_blk, _unused, _unused, block_local) = dp_sum(
        s6,
        [
            lambda token: swap_pipe(pin(blk[1], token)),
            lambda token: token,
            lambda token: token,
            lambda token: token,
        ],
    )

    ga6, gz5, s5 = call(
        k_back_six, "g5", (4,),
        [SCALARS, chunk, chunk, chunk_sum, chunk_sum, chunk_tab, full_mask, spec((TILE, TILE), lambda k: (3, k)), full_mid, full_row, full_tab],
        [chunk, full_mid, full_row],
        [vmem_of((ROWS, C_OUT), BFLOAT), vmem_of((ROWS, C_MID)), shape_of((4, C_MID))],
        [pltpu.VMEM((ROWS, C_MID), SINGLE)],
        (inv, gz6, a6_kept, total6, sum6, tab6, mask, in_hbm(wide), a5, total5, mid5), vmem=11,
    )
    gz5 = in_vmem(gz5)

    def wide_rows(k):
        return spec((1, 256, ROWS), lambda t, slot: (0, t + k, 0))

    def whole_wide(grad):
        return grad.reshape((1,) + grad.shape), full((1,) + grad.shape)

    wide_shape, narrow_shape = (R_W, C_OUT // 2), (R_N // 2, C_MID // 2)
    sum5, (bufs_w, block_local) = dp_sum(
        s5,
        [
            lambda token: weight_grad("dw6", h5_t[None], wide_rows(0), *whole_wide(ga6), 2, wide_shape, 256, 6, None, token, hbm_of),
            lambda token: place("place_out", blk, got_blk, token),
        ],
    )
    block_local = block_local.reshape(IMG_DEV, WB, HB, C_OUT // 2).transpose(0, 2, 1, 3)

    col5, gz4, s4 = call(
        k_back_conv_one, "g4", (3,),
        [SCALARS, full_mid, full_mid, full_row, full_row, full_tab, full_mask] + conv_weights(3, straight) + [full_mid, full_row, full_tab],
        [spec((3, ROWS, C_MID), lambda s: (s, 0, 0)), full_mid, full_row],
        [vmem_of((9, ROWS, C_MID), BFLOAT), vmem_of((ROWS, C_MID)), shape_of((4, C_MID))],
        [pltpu.VMEM((PAD + ROWS + PAD, C_MID), SINGLE)] * 2 + [pltpu.VMEM((ROWS, C_MID), SINGLE)],
        (inv, gz5, a5, total5, sum5, mid5, mask, b_kept, b_kept, b_kept, a4, total4, mid4), vmem=13,
    )
    gz4 = in_vmem(gz4)
    one_turned = spec((1, C_MID, ROWS), lambda t, slot: (0, 0, 0))
    held_b = []

    def grad_five(k):
        def filler(token):
            grad_spec = spec((3, ROWS, C_MID), lambda t, slot: (k, 0, 0))
            held_b[:] = weight_grad("dw5", h4_t[None], one_turned, in_vmem(col5), grad_spec, 1, narrow_shape, 3 * TILE, 1 + k, list(held_b), token, vmem_of)
            return tuple(held_b)

        return filler

    sum4, results4 = dp_sum(s4, [grad_five(k) for k in range(3)])
    bufs_b = results4[2]

    ga4, gj, s3 = call(
        k_back_four, "gy", (4,),
        [SCALARS, full_mid, full_mid, full_row, full_row, full_tab, full_mask, four_a, four_b,
         chunk, chunk, chunk, chunk_sum, chunk_sum, chunk_tab, chunk_tab],
        [full_mid, chunk, spec((6, TILE), lambda k: (0, k))],
        [vmem_of((ROWS, C_MID), BFLOAT), vmem_of((ROWS, C_OUT)), shape_of((6, C_OUT))], [],
        (inv, gz4, a4, total4, sum4, mid4, mask, a_kept, b_kept, gz6, a3_kept, as_kept, total3, total_s, tab3, tabs), vmem=15,
    )
    gj = in_vmem(gj)

    by_rows = lambda which, m: 2 * m + which

    def grad_four(token):
        y_tiles = y_t.reshape(4, C_MID, ROWS)
        one = full((1, ROWS, C_MID))
        grad = in_vmem(ga4.reshape(1, ROWS, C_MID))
        held["grad_b"] = weight_grad("dw4b", y_tiles, spec((1, C_MID, ROWS), lambda t, slot: (1 + t, 0, 0)), grad, one, 3, narrow_shape, TILE, 0, bufs_b, token, vmem_of)
        return held["grad_b"]

    def grad_four_first(token):
        return weight_grad(
            "dw4a", y_t.reshape(4, C_MID, ROWS), spec((1, C_MID, ROWS), lambda t, slot: (0, 0, 0)), in_vmem(ga4.reshape(1, ROWS, C_MID)),
            full((1, ROWS, C_MID)), 1, narrow_shape, TILE, 11, None, token, vmem_of,
        )

    def swap_grad_b(token):
        held["got_b"] = swap_pipe(pin(held["grad_b"][1], token))
        return token

    def split_b(token):
        if not fast:
            return token
        keep, got = pin((held["grad_b"][0], held["got_b"]), token)
        state = split_group("split_b", in_vmem(keep), got, part_n, by_rows)
        held["came_b"] = exchange(state[1], 1), exchange(state[3], 2)
        return state

    sum3, results3 = dp_sum(s3, [grad_four, both_of(swap_grad_b, grad_four_first), split_b])
    bufs_b, bufs_a = results3[0], results3[1][1]
    held["b"] = results3[2]

    ga3, gas, gz2, s2 = call(
        k_back_three, "g2", (4,),
        [SCALARS, chunk, chunk, chunk, chunk_sum, chunk_sum, spec((6, TILE), lambda k: (0, k)), chunk_tab, chunk_tab, full_mask,
         spec((TILE, TILE), lambda k: (0, k)), full_mid, full_row, full_tab],
        [chunk, chunk, full_mid, full_row],
        [hbm_of((ROWS, C_OUT), BFLOAT), hbm_of((ROWS, C_OUT), BFLOAT), vmem_of((ROWS, C_MID)), shape_of((4, C_MID))],
        [pltpu.VMEM((ROWS, C_MID), SINGLE)],
        (inv, gj, a3_kept, as_kept, total3, total_s, sum3, tab3, tabs, mask, in_hbm(wide), a2, total2, mid2), vmem=14,
    )
    gz2 = in_vmem(gz2)

    def step_b(bits):
        def filler(token):
            if not fast:
                return token
            keep0, _sent, keep1, _sent = held["b"]
            came0, came1 = pin(held["came_b"], token)
            stay0, sent0 = halved(keep0, came0)
            stay1, sent1 = halved(keep1, came1)
            held["came_b"] = exchange(sent0, bits[0]), exchange(sent1, bits[1])
            return stay0, sent0, stay1, sent1

        return filler

    def grad_three(token):
        held["w"] = weight_grad("dw3", h2_t[None], wide_rows(0), *whole_wide(ga3), 2, wide_shape, 256, 0, bufs_w, token, hbm_of)
        return held["w"]

    def grad_short(q):
        def filler(token):
            held["w"] = weight_grad("dws", x_t[None], wide_rows(2 * q), *whole_wide(gas), 2, wide_shape, 256, 2 + 2 * q, held["w"], token, hbm_of)
            return held["w"]

        return filler

    sum2, results2 = dp_sum(s2, [grad_three, grad_short(0), step_b((2, 1)), grad_short(1)])
    held["b"], bufs_w = results2[2:]
    got_w = swap_pipe(bufs_w[1])

    col2, gz1, s1 = call(
        k_back_conv_two, "g1", (3,),
        [SCALARS, full_mid, full_mid, full_row, full_row, full_tab, full_mask] + conv_weights(2, turned)
        + [plane_pair, full_row, full_tab],
        [spec((3, ROWS, C_MID), lambda s: (turned(s), 0, 0)), plane_pair, full_row],
        [vmem_of((9, ROWS, C_MID), BFLOAT), vmem_of((4, ROWS, C_MID)), shape_of((4, C_MID))],
        [pltpu.VMEM((PAD + ROWS + PAD, C_MID), SINGLE)] * 2 + [pltpu.VMEM((2, ROWS, C_MID), SINGLE)],
        (inv, gz2, a2, total2, sum2, mid2, mask, a_kept, a_kept, a_kept, a1, total1, mid1), vmem=16,
    )
    gz1 = in_vmem(gz1)
    h1_planes = h1_t.reshape(4, C_MID, ROWS)

    def grad_two(row):
        def filler(token):
            first = 2 * (1 - (row & 1))
            held["a"] = weight_grad(
                "dw2", h1_planes, spec((1, C_MID, ROWS), lambda t, slot: (first + (1 - (t & 1)), 0, 0)), in_vmem(col2),
                spec((1, ROWS, C_MID), lambda t, slot: (3 * row + t, 0, 0)), 3, narrow_shape, TILE, 2 + 3 * row, held["a"], token, vmem_of,
            )
            return held["a"]

        return filler

    def wide_back(token):
        return call(
            k_wide_back, "dxs", (2,),
            [full((ROWS, C_OUT)), spec((TILE, C_OUT), lambda k: (1 + k, 0)), ANYWHERE],
            spec((ROWS, TILE), lambda k: (0, k)),
            hbm_of((ROWS, C_IN)), [],
            (in_hbm(gas), in_hbm(wide), token), vmem=11,
        )

    def split_w(token):
        if fast:
            keep, got = pin((bufs_w[0], got_w), token)
            held["split"] = split_group("split_w", keep, got, w_wide.shape[0], lambda which, m: 16 * which + m)
            return held["split"]
        return token

    def send_w(token):
        if fast:
            sent0, sent1 = pin((held["split"][1], held["split"][3]), token)
            held["came"] = exchange(sent0, 1), exchange(sent1, 2)
        return token

    held["a"] = bufs_a
    sum1, results1 = dp_sum(s1, [both_of(step_b((4, 4)), split_w), grad_two(0), both_of(send_w, grad_two(1)), grad_two(2)])
    held["b"], held["split"] = results1[0]
    bufs_a = results1[3]
    sum1, held["b"] = lax.optimization_barrier((sum1, step_b((8, 8))(sum1)))

    plane = spec((1, ROWS, C_MID), lambda k: (k, 0, 0))
    ga1 = call(
        k_first_grad, "g0", (4,), [SCALARS, plane, plane, full_row, full_row, full_tab, full_mask], plane,
        vmem_of((4, ROWS, C_MID), BFLOAT), [], (inv, gz1, a1, total1, sum1, mid1, mask),
    )
    if fast:
        came_w = held["came"]
        state_w = halved(held["split"][0], came_w[0]) + halved(held["split"][2], came_w[1])
        ga1, state_w = lax.optimization_barrier((ga1, state_w))
    flat_ga1 = in_vmem(ga1.reshape(1, 4 * ROWS, C_MID))
    bufs_a = weight_grad(
        "dw1", x_t.reshape(2, C_MID, 4 * ROWS), spec((1, C_MID, 4 * ROWS), lambda t, slot: (t, 0, 0)), flat_ga1, full((1, 4 * ROWS, C_MID)),
        2, narrow_shape, TILE, 0, bufs_a, None, vmem_of,
    )
    got_a = swap_pipe(bufs_a[1])
    dxs = wide_back(ga1)

    def image_grads(token):
        pair = call(
            k_image_grad, "gx", (SLOTS,),
            [spec((4, PIX, C_MID), lambda s, slot: (0, s, 0)), spec((PIX, 1), lambda s, slot: (s, 0)), full((C_IN, C_MID)),
             spec((PIX, C_IN), lambda s, slot: (s, 0)), full((4 * PIX, 4 * PIX)), ANYWHERE],
            spec((2, 1, 4 * PIX, C_IN // 2), lambda s, slot: (0, s, 0, 0)),
            shape_of((2, SLOTS, 4 * PIX, C_IN // 2), BFLOAT), [],
            (slots, in_vmem(ga1), mask, a_kept, in_hbm(dxs), in_hbm(perm), token), prefetch=1, vmem=10,
        )
        return pair, swap_pipe(pair[1])

    pair, got_pair = image_grads(ga1)
    grad_local = place("place_grad", pair, got_pair, ga1)
    if fast:
        state_a = split_group("split_a", in_vmem(bufs_a[0]), got_a, part_n, by_rows)
        half_b = jnp.concatenate([added(held["b"][k], held["came_b"][k // 2]) for k in (0, 2)], axis=0)
        half_w0 = halve(state_w[0], state_w[1], (2, 4, 8))
        half_w1 = halve(state_w[2], state_w[3], (1, 4, 8))
        half_a = jnp.concatenate([halve(state_a[0], state_a[1], (1, 2, 4, 8)), halve(state_a[2], state_a[3], (2, 1, 4, 8))], axis=0)
    else:
        half_a = jnp.concatenate(scatter_plain(bufs_a[0], got_a, rows_n, True), axis=0)
        half_w0, half_w1 = scatter_plain(bufs_w[0], got_w, w_wide.shape[0], False)
        half_b = jnp.concatenate(scatter_plain(bufs_b[0], held["got_b"], rows_n, True), axis=0)
    grad_local = grad_local.reshape(IMG_DEV, 2 * HB, 2 * WB, C_IN // 2)

    def join_halves(first, second):
        mine = jnp.where(core == 0, first, second)
        got = swap_pipe(jnp.where(core == 0, second, first))
        return jnp.where(core == 0, jnp.concatenate([mine, got], axis=1), jnp.concatenate([got, mine], axis=1))

    grad_narrow = join_halves(half_a, half_b)
    grad_wide = join_halves(half_w0, half_w1)

    hot_narrow = group_table(shard, w_narrow.shape[0], (C_IN, C_IN + 9 * C_MID, C_IN + 9 * C_MID + C_OUT))
    hot_wide = group_table(shard, w_wide.shape[0], (C_MID, C_MID + C_IN))

    def pair_sum(rows):
        return rows[0] + rows[1]

    mid_rows = jnp.stack([pair_sum(v) for t in (sum1, sum2, sum4, sum5) for v in (t[2:4], t[0:2])])
    wide_rows = jnp.stack([pair_sum(v) for v in (sum3[2:4], sum3[0:2], sum3[4:6], sum3[0:2], sum6[2:4], sum6[0:2])])
    mid_rows = mid_rows + swap_pipe(mid_rows)
    wide_rows = wide_rows + swap_pipe(wide_rows)
    grad_mid = lax.dynamic_slice(mid_rows, (0, shard * mid_cols), (8, mid_cols))
    grad_table = lax.dynamic_slice(wide_rows, (0, shard * wide_cols), (6, wide_cols))

    def square_vector(narrow_rows, wide_rows, mid_part, table_part):
        return jnp.concatenate(
            [
                jnp.dot(jnp.sum(narrow_rows * narrow_rows, axis=1), hot_narrow, precision=PRECISE),
                jnp.dot(jnp.sum(wide_rows * wide_rows, axis=1), hot_wide, precision=PRECISE),
                jnp.sum(mid_part * mid_part, axis=1),
                jnp.sum(table_part * table_part, axis=1),
            ]
        )

    squares = jnp.stack([square_vector(w_narrow, w_wide, bn_mid, bn_wide), square_vector(grad_narrow, grad_wide, grad_mid, grad_table)])
    squares, _unused = dp_sum(squares + swap_pipe(squares))
    norms = jnp.sqrt(squares)
    weight_norms, grad_norms = norms[0], norms[1]
    ratios = TRUST * weight_norms / (grad_norms + DECAY * weight_norms)
    ratio_narrow = jnp.dot(hot_narrow, ratios[:4], precision=PRECISE)
    ratio_wide = jnp.dot(hot_wide, ratios[4:7], precision=PRECISE)

    def lars_step(weight, gradient, moment, ratio_rows):
        new_moment = MOMENTUM * moment + RATE * ratio_rows[:, None] * (gradient + DECAY * weight)
        return (weight - new_moment, new_moment)

    new_narrow, new_mom_narrow = lars_step(w_narrow, grad_narrow, mom_narrow, ratio_narrow)
    new_wide, new_mom_wide = lars_step(w_wide, grad_wide, mom_wide, ratio_wide)
    new_mid, new_mom_mid = lars_step(bn_mid, grad_mid, mom_bn_mid, ratios[7:15])
    new_table, new_mom_table = lars_step(bn_wide, grad_table, mom_bn_wide, ratios[15:21])
    return (
        block_local, grad_local, grad_narrow, grad_wide, grad_mid, grad_table,
        new_mom_narrow, new_mom_wide, new_mom_mid, new_mom_table,
        new_narrow, new_wide, new_mid, new_table,
    )


def solution(mesh):
    rows = P(("pipe", "dp"), None)
    columns = P(None, ("pipe", "dp"))
    feature = P("dp", None, None, None)
    return jax.shard_map(
        on_device,
        mesh=mesh,
        in_specs=(feature, feature, P("dp"), P("dp"), P("dp", None), rows, rows, columns, columns, rows, rows, columns, columns),
        out_specs=(P("dp", None, None, "pipe"), P("dp", None, None, "pipe"), rows, rows, columns, columns, rows, rows, columns, columns, rows, rows, columns, columns),
        check_vma=False,
    )
```

```python
import functools

import jax
import jax.numpy as jnp
import numpy as np
from jax import lax
from jax.experimental import pallas as pl
from jax.experimental.pallas import tpu as pltpu
from jax.sharding import PartitionSpec as P

C_IN = 1024
C_MID = 512
C_OUT = 2048
R_N = 12288
R_W = 2048
HB = 8
WB = 12
IMG_DEV = 8
SLOTS = 4
PIX = HB * WB
ROWS = SLOTS * PIX
HALF = ROWS // 2
PAD = 16
TILE = 512

EPS = 1e-05
MOMENTUM = 0.9
DECAY = 5e-05
TRUST = 0.001
RATE = 29.0
NARROW_BOUNDS = (C_IN, C_IN + 9 * C_MID, C_IN + 9 * C_MID + C_OUT)
WIDE_BOUNDS = (C_MID, C_MID + C_IN)
BFLOAT = jnp.bfloat16
SINGLE = jnp.float32
MIB = 1024 * 1024
BYTES_PER_US = 1200000
MICROSECONDS = {
    "prep": 5, "a1": 3, "a2": 5, "as": 4.5, "a3": 4, "a4": 4.7, "a5": 4, "a6": 3.7, "head": 5.3, "g5": 5.2, "g4": 5.4, "gy": 7,
    "g2": 7.3, "g1": 8, "g0": 3, "gx": 6.4, "dxs": 5, "dw1": 3.4, "dw2": 2.1, "dw3": 2.9, "dws": 2.9, "dw4a": 1.7, "dw4b": 1.9,
    "dw5": 1.5, "dw6": 2.8, "place_out": 3.4, "place_grad": 5, "wa": 3, "wb": 3, "turn": 1.7, "keep": 1.7, "halve": 1, "squares": 2, "update": 3,
}


def pairs(bit):
    return [(i, i ^ bit) for i in range(lax.axis_size("dp"))]


def exchange(value, bit):
    return lax.ppermute(value, "dp", pairs(bit))


def pin(value, after):
    return lax.optimization_barrier((value, after))[0]


def dp_sum(value, fillers=(), first=None):
    size = lax.axis_size("dp")
    bits = [1 << k for k in range(size.bit_length() - 1)]
    if first in bits:
        at = bits.index(first)
        bits = bits[at:] + bits[:at]
    results = []
    for bit in bits:
        got = exchange(value, bit)
        if len(results) < len(fillers):
            result = fillers[len(results)](value)
            got, result = lax.optimization_barrier((got, result))
            results.append(result)
        value = value + got
    for filler in fillers[len(results) :]:
        results.append(filler(value))
    return value, results


def swap_pipe(value):
    return lax.ppermute(value, "pipe", [(0, 1), (1, 0)])


def dot(left, right):
    return jnp.dot(left, right, preferred_element_type=SINGLE)


def dot_back(left, right):
    return lax.dot_general(left, right, (((1,), (1,)), ((), ())), preferred_element_type=SINGLE)


def silu(value):
    return value * jax.nn.sigmoid(value)


def slope(value):
    gate = jax.nn.sigmoid(value)
    return gate * (1.0 + value * (1.0 - gate))


def put_sums(ref, values, first):
    for k, value in enumerate(values):
        for m in range(2):
            total = jnp.sum(value[m * HALF : (m + 1) * HALF], axis=0, keepdims=True)
            row = 2 * k + m
            ref[row : row + 1, :] = total if first else ref[row : row + 1, :] + total


def both(function):
    return jnp.concatenate([function(0), function(1)], axis=0)


def part(m):
    return slice(m * HALF, (m + 1) * HALF)


def moments(total_ref, inv_ref, m, scale=1.0):
    inv = inv_ref[m] * scale
    mean = total_ref[m : m + 1, :] * inv
    var = total_ref[2 + m : 3 + m, :] * inv - mean * mean
    return mean, lax.rsqrt(var + EPS)


def normed(a, total_ref, inv_ref, m, scale=1.0):
    mean, rstd = moments(total_ref, inv_ref, m, scale)
    return (a - mean) * rstd, rstd


def conv_grad(gz, xhat, rstd, gain, mask, sum_ref, inv_ref, m, scale=1.0, second=2):
    inv = inv_ref[m] * scale
    first_row = sum_ref[m : m + 1, :] * inv
    second_row = sum_ref[second + m : second + m + 1, :] * inv
    return (mask * ((rstd * gain) * (gz - first_row - xhat * second_row))).astype(BFLOAT)


def k_prep(core_ref, assign_ref, height_ref, width_ref, img_ref, perm_ref, out_ref, mask_ref, count_ref):
    slot = pl.program_id(0)
    image = assign_ref[core_ref[0] * SLOTS + slot]
    pixel = lax.broadcasted_iota(jnp.int32, (PIX, 1), 0)
    inside = ((pixel & (HB - 1)) < height_ref[image]) & (pixel < width_ref[image] * HB)
    mask = jnp.where(inside, 1.0, 0.0).astype(SINGLE)
    mask_ref[...] = mask
    planes = dot(perm_ref[...], img_ref[0])
    for k in range(4):
        out_ref[k] = (planes[k * PIX : (k + 1) * PIX] * mask).astype(BFLOAT)
    column = lax.broadcasted_iota(jnp.int32, count_ref.shape, 1)
    counts = jnp.zeros(count_ref.shape, jnp.int32)
    for m in range(4):
        pair = (assign_ref[2 * m], assign_ref[2 * m + 1])
        total = sum(height_ref[k] * width_ref[k] for k in pair)
        counts = jnp.where(column == m, total, counts)
    count_ref[...] = counts.astype(SINGLE)


def k_first(x_ref, w_ref, a_ref, sum_ref):
    a = dot(x_ref[0], w_ref[...])
    a_ref[0] = a

    @pl.when(pl.program_id(0) == 0)
    def _():
        sum_ref[...] = jnp.zeros_like(sum_ref)

    put_sums(sum_ref, [a, a * a], False)


def shift_mask(di, dj):
    if not di and not dj:
        return None
    pixel = lax.broadcasted_iota(jnp.int32, (SLOTS, PIX, 1), 1)
    inside = None
    if di:
        row = pixel & (HB - 1)
        inside = row >= -di if di < 0 else row < HB - di
    if dj:
        column = pixel >= -dj * HB if dj < 0 else pixel < PIX - dj * HB
        inside = column if inside is None else inside & column
    return jnp.where(inside, 1.0, 0.0).astype(SINGLE).reshape(ROWS, 1)


def rows_at(pad, di, dj):
    start = PAD + HB * dj + di
    rows = pad[start : start + ROWS, :]
    mask = shift_mask(di, dj)
    return rows if mask is None else rows * mask


def clear_pad(pad):
    pad[0:PAD, :] = jnp.zeros((PAD, pad.shape[1]), SINGLE)
    pad[PAD + ROWS : PAD + ROWS + PAD, :] = jnp.zeros((PAD, pad.shape[1]), SINGLE)


def body(pad, m):
    return pad.at[PAD + m * HALF : PAD + (m + 1) * HALF, :]


def carried(ref, fresh):
    return jnp.where(fresh, 0.0, ref[...])


def k_conv_two(inv_ref, total_ref, tab_ref, mask_ref, a_ref, w0, w1, w2, out_ref, h_ref, sum_ref, pad, moved):
    step = pl.program_id(0)
    gain, bias = tab_ref[0:1, :], tab_ref[1:2, :]

    @pl.when(step < 2)
    def _():
        for k in range(2):
            clear_pad(pad.at[k])
            clear_pad(moved.at[k])
            for m in range(2):
                xhat, _unused = normed(a_ref[k, part(m), :], total_ref, inv_ref, m, 0.25)
                h = (silu(xhat * gain + bias) * mask_ref[part(m), :]).astype(BFLOAT)
                h_ref[k, part(m), :] = h
                body(pad.at[k], m)[...] = h.astype(SINGLE)
                body(moved.at[k], m)[...] = h.astype(SINGLE)

    @pl.when(step == 2)
    def _():
        for k in range(2):
            moved[k, PAD : PAD + ROWS, :] = rows_at(pad.at[k], -1, 0)

    term = dot(rows_at(moved.at[0], 0, 0).astype(BFLOAT), w1[...])
    term += dot(rows_at(moved.at[1], 0, -1).astype(BFLOAT), w0[...])
    term += dot(rows_at(moved.at[1], 0, 0).astype(BFLOAT), w2[...])
    out_ref[...] = carried(out_ref, step == 0) + term

    @pl.when(step == 2)
    def _():
        a = out_ref[...]
        masked = a * mask_ref[...]
        put_sums(sum_ref, [masked, masked * a], True)


def k_conv_one(inv_ref, total_ref, tab_ref, mask_ref, a_ref, w0, w1, w2, out_ref, h_ref, sum_ref, pad, moved):
    step = pl.program_id(0)
    gain, bias = tab_ref[0:1, :], tab_ref[1:2, :]

    @pl.when(step == 0)
    def _():
        clear_pad(pad)
        clear_pad(moved)
        for m in range(2):
            xhat, _unused = normed(a_ref[part(m), :], total_ref, inv_ref, m)
            h = (silu(xhat * gain + bias) * mask_ref[part(m), :]).astype(BFLOAT)
            h_ref[part(m), :] = h
            body(pad, m)[...] = h.astype(SINGLE)

    for s in range(3):

        @pl.when(step == s)
        def _(s=s):
            moved[PAD : PAD + ROWS, :] = rows_at(pad, s - 1, 0)

    term = dot(rows_at(moved, 0, -1).astype(BFLOAT), w0[...])
    term += dot(rows_at(moved, 0, 0).astype(BFLOAT), w1[...])
    term += dot(rows_at(moved, 0, 1).astype(BFLOAT), w2[...])
    out_ref[...] = carried(out_ref, step == 0) + term

    @pl.when(step == 2)
    def _():
        a = out_ref[...]
        masked = a * mask_ref[...]
        put_sums(sum_ref, [masked, masked * a], True)


def k_expand(inv_ref, total_ref, tab_ref, mask_ref, a_ref, w_ref, h_ref, out_ref, sum_ref):
    @pl.when(pl.program_id(0) == 0)
    def _():
        gain, bias = tab_ref[0:1, :], tab_ref[1:2, :]
        for m in range(2):
            xhat, _unused = normed(a_ref[part(m), :], total_ref, inv_ref, m)
            h_ref[part(m), :] = (silu(xhat * gain + bias) * mask_ref[part(m), :]).astype(BFLOAT)

    a = dot(h_ref[...], w_ref[...])
    out_ref[...] = a
    put_sums(sum_ref, [a, a * a], True)


def k_short(x_ref, w0, w1, out_ref, sum_ref):
    a = dot(x_ref[0, :, :TILE], w0[...]) + dot(x_ref[0, :, TILE:], w1[...])
    out_ref[...] = a
    put_sums(sum_ref, [a, a * a], True)


def k_meet(inv_ref, t3_ref, ts_ref, tab3_ref, tabs_ref, mask_ref, a3_ref, as_ref, wa_ref, wb_ref, y_ref, out_ref, sum_ref):
    step = pl.program_id(0)
    for m in range(2):
        x3, _unused = normed(a3_ref[part(m), :], t3_ref, inv_ref, m)
        xs, _unused = normed(as_ref[part(m), :], ts_ref, inv_ref, m)
        joined = (x3 * tab3_ref[0:1, :] + tab3_ref[1:2, :]) + (xs * tabs_ref[0:1, :] + tabs_ref[1:2, :])
        y_ref[part(m), :] = (silu(joined) * mask_ref[part(m), :]).astype(BFLOAT)

    @pl.when(step == 0)
    def _():
        out_ref[...] = dot(y_ref[...], wa_ref[...])

    @pl.when(step > 0)
    def _():
        out_ref[...] += dot(y_ref[...], wb_ref[...])

    @pl.when(step == pl.num_programs(0) - 1)
    def _():
        a = out_ref[...]
        put_sums(sum_ref, [a, a * a], True)


def k_head(slot_ref, inv_ref, total_ref, tab_ref, mask_ref, a_ref, y_ref, c0, c1, c2, c3, blk_ref, gz_ref, sum_ref):
    cots = (c0, c1, c2, c3)
    gain, bias = tab_ref[0:1, :], tab_ref[1:2, :]
    for m in range(2):
        mask = mask_ref[part(m), :]
        xhat, _unused = normed(a_ref[part(m), :], total_ref, inv_ref, m)
        z = (xhat * gain + bias) + y_ref[part(m), :].astype(SINGLE)
        gate = jax.nn.sigmoid(z)
        blk_ref[0, part(m), :] = (z * gate * mask).astype(BFLOAT)
        cot = jnp.concatenate([cots[2 * m][0], cots[2 * m + 1][0]], axis=0).astype(SINGLE)
        gz = cot * mask * (gate * (1.0 + z * (1.0 - gate)))
        gz_ref[part(m), :] = gz
        sum_ref[m : m + 1, :] = jnp.sum(gz, axis=0, keepdims=True)
        sum_ref[2 + m : 3 + m, :] = jnp.sum(gz * xhat, axis=0, keepdims=True)


def finish_back(gz_ref, sum_ref, grad, a_ref, total_ref, tab_ref, inv_ref, mask_ref):
    gain, bias = tab_ref[0:1, :], tab_ref[1:2, :]
    for m in range(2):
        xhat, _unused = normed(a_ref[part(m), :], total_ref, inv_ref, m)
        gz = grad[part(m)] * mask_ref[part(m), :] * slope(xhat * gain + bias)
        gz_ref[part(m), :] = gz
        sum_ref[m : m + 1, :] = jnp.sum(gz, axis=0, keepdims=True)
        sum_ref[2 + m : 3 + m, :] = jnp.sum(gz * xhat, axis=0, keepdims=True)


def k_back_six(inv_ref, gz_ref, a_ref, total_ref, s_ref, tab_ref, mask_ref, w_ref, low_ref, low_total, low_tab, ga_ref, out_ref, sum_ref, acc):
    step = pl.program_id(0)
    for m in range(2):
        xhat, rstd = normed(a_ref[part(m), :], total_ref, inv_ref, m)
        ga_ref[part(m), :] = conv_grad(
            gz_ref[part(m), :], xhat, rstd, tab_ref[0:1, :], mask_ref[part(m), :], s_ref, inv_ref, m
        )
    term = dot_back(ga_ref[...], w_ref[...])

    @pl.when(step == 0)
    def _():
        acc[...] = term

    @pl.when(step > 0)
    def _():
        acc[...] += term

    @pl.when(step == pl.num_programs(0) - 1)
    def _():
        finish_back(out_ref, sum_ref, acc[...], low_ref, low_total, low_tab, inv_ref, mask_ref)


def k_back_conv_one(inv_ref, gz_ref, a_ref, total_ref, s_ref, tab_ref, mask_ref, w0, w1, w2, low_ref, low_total, low_tab, col_ref, out_ref, sum_ref, pad, moved, acc):
    step = pl.program_id(0)

    @pl.when(step == 0)
    def _():
        clear_pad(pad)
        clear_pad(moved)
        for m in range(2):
            xhat, rstd = normed(a_ref[part(m), :], total_ref, inv_ref, m)
            ga = conv_grad(gz_ref[part(m), :], xhat, rstd, tab_ref[0:1, :], mask_ref[part(m), :], s_ref, inv_ref, m)
            body(pad, m)[...] = ga.astype(SINGLE)

    for s in range(3):

        @pl.when(step == s)
        def _(s=s):
            moved[PAD : PAD + ROWS, :] = rows_at(pad, 1 - s, 0)

    term = None
    for kx, weight in enumerate((w0, w1, w2)):
        tap = rows_at(moved, 0, 1 - kx).astype(BFLOAT)
        col_ref[kx] = tap
        product = dot_back(tap, weight[...])
        term = product if term is None else term + product
    acc[...] = carried(acc, step == 0) + term

    @pl.when(step == 2)
    def _():
        finish_back(out_ref, sum_ref, acc[...], low_ref, low_total, low_tab, inv_ref, mask_ref)


def k_back_four(inv_ref, gz_ref, a_ref, total_ref, s_ref, tab_ref, mask_ref, wa_ref, wb_ref, up_ref, a3_ref, as_ref, t3_ref, ts_ref, tab3_ref, tabs_ref, ga_ref, gj_ref, sum_ref):
    @pl.when(pl.program_id(0) == 0)
    def _():
        for m in range(2):
            xhat, rstd = normed(a_ref[part(m), :], total_ref, inv_ref, m)
            ga_ref[part(m), :] = conv_grad(
                gz_ref[part(m), :], xhat, rstd, tab_ref[0:1, :], mask_ref[part(m), :], s_ref, inv_ref, m
            )

    weight = jnp.where(pl.program_id(0) == 0, wa_ref[...], wb_ref[...])
    grad = dot_back(ga_ref[...], weight) + up_ref[...]
    for m in range(2):
        x3, _unused = normed(a3_ref[part(m), :], t3_ref, inv_ref, m)
        xs, _unused = normed(as_ref[part(m), :], ts_ref, inv_ref, m)
        joined = (x3 * tab3_ref[0:1, :] + tab3_ref[1:2, :]) + (xs * tabs_ref[0:1, :] + tabs_ref[1:2, :])
        gj = grad[part(m)].astype(BFLOAT).astype(SINGLE) * mask_ref[part(m), :] * slope(joined)
        gj_ref[part(m), :] = gj
        for k, value in enumerate((gj, gj * x3, gj * xs)):
            row = 2 * k + m
            sum_ref[row : row + 1, :] = jnp.sum(value, axis=0, keepdims=True)


def k_back_three(inv_ref, gj_ref, a3_ref, as_ref, t3_ref, ts_ref, s_ref, tab3_ref, tabs_ref, mask_ref, w_ref, low_ref, low_total, low_tab, g3_ref, gs_ref, out_ref, sum_ref, acc):
    step = pl.program_id(0)
    for m in range(2):
        mask = mask_ref[part(m), :]
        gj = gj_ref[part(m), :]
        x3, r3 = normed(a3_ref[part(m), :], t3_ref, inv_ref, m)
        g3_ref[part(m), :] = conv_grad(gj, x3, r3, tab3_ref[0:1, :], mask, s_ref, inv_ref, m)
        xs, rs = normed(as_ref[part(m), :], ts_ref, inv_ref, m)
        gs_ref[part(m), :] = conv_grad(gj, xs, rs, tabs_ref[0:1, :], mask, s_ref, inv_ref, m, second=4)
    term = dot_back(g3_ref[...], w_ref[...])

    @pl.when(step == 0)
    def _():
        acc[...] = term

    @pl.when(step > 0)
    def _():
        acc[...] += term

    @pl.when(step == pl.num_programs(0) - 1)
    def _():
        finish_back(out_ref, sum_ref, acc[...], low_ref, low_total, low_tab, inv_ref, mask_ref)


def k_back_conv_two(inv_ref, gz_ref, a_ref, total_ref, s_ref, tab_ref, mask_ref, w0, w1, w2, low_ref, low_total, low_tab, col_ref, out_ref, sum_ref, pad, moved, acc):
    step = pl.program_id(0)
    gain, bias = low_tab[0:1, :], low_tab[1:2, :]

    @pl.when(step == 0)
    def _():
        clear_pad(pad)
        clear_pad(moved)
        for m in range(2):
            xhat, rstd = normed(a_ref[part(m), :], total_ref, inv_ref, m)
            ga = conv_grad(gz_ref[part(m), :], xhat, rstd, tab_ref[0:1, :], mask_ref[part(m), :], s_ref, inv_ref, m)
            body(pad, m)[...] = ga.astype(SINGLE)
            body(moved, m)[...] = ga.astype(SINGLE)
        sum_ref[...] = jnp.zeros_like(sum_ref)

    @pl.when(step == 2)
    def _():
        moved[PAD : PAD + ROWS, :] = rows_at(pad, 1, 0)

    plain = rows_at(moved, 0, 0).astype(BFLOAT)
    aside = rows_at(moved, 0, 1).astype(BFLOAT)
    col_ref[0], col_ref[1], col_ref[2] = aside, plain, plain
    acc[0] = carried(acc.at[0], step < 2) + dot_back(plain, w1[...])
    acc[1] = carried(acc.at[1], step < 2) + (dot_back(aside, w0[...]) + dot_back(plain, w2[...]))

    @pl.when(step != 1)
    def _():
        for k in range(2):
            for m in range(2):
                xhat, _unused = normed(low_ref[k, part(m), :], low_total, inv_ref, m, 0.25)
                gz = acc[k, part(m), :] * mask_ref[part(m), :] * slope(xhat * gain + bias)
                out_ref[k, part(m), :] = gz
                for q, value in enumerate((gz, gz * xhat)):
                    row = 2 * q + m
                    sum_ref[row : row + 1, :] += jnp.sum(value, axis=0, keepdims=True)


def k_wide_back(g_ref, w_ref, *refs):
    refs[-1][...] = dot_back(g_ref[...], w_ref[...])


def k_first_grad(inv_ref, gz_ref, a_ref, total_ref, s_ref, tab_ref, mask_ref, ga_ref):
    for m in range(2):
        xhat, rstd = normed(a_ref[0, part(m), :], total_ref, inv_ref, m, 0.25)
        ga_ref[0, part(m), :] = conv_grad(
            gz_ref[0, part(m), :], xhat, rstd, tab_ref[0:1, :], mask_ref[part(m), :], s_ref, inv_ref, m, 0.25
        )


def k_image_grad(slot_ref, ga_ref, mask_ref, w_ref, short_ref, perm_ref, *refs):
    out_ref = refs[-1]
    grads = dot_back(ga_ref[...].reshape(4 * PIX, C_MID), w_ref[...])
    mask = mask_ref[...]
    parts = []
    for k in range(4):
        grad = grads[k * PIX : (k + 1) * PIX]
        if k == 0:
            grad = grad + short_ref[...]
        parts.append((grad * mask).astype(BFLOAT))
    planes = jnp.concatenate(parts, axis=0)
    image = lax.dot_general(perm_ref[...], planes, (((0,), (0,)), ((), ())), preferred_element_type=SINGLE).astype(BFLOAT)
    core = slot_ref[SLOTS]
    out_ref[core, 0] = image[:, : C_IN // 2]
    out_ref[1 - core, 0] = image[:, C_IN // 2 :]


def k_place(slot_ref, own_ref, got_ref, *refs):
    out_ref = refs[-1]
    step = pl.program_id(0)

    @pl.when(step < SLOTS)
    def _():
        out_ref[0] = own_ref[0, 0]

    @pl.when(step >= SLOTS)
    def _():
        out_ref[0] = got_ref[0]


def k_turn(in_ref, *refs):
    refs[-1][...] = in_ref[...].reshape(in_ref.shape[-2:]).T


def k_grad(slot_ref, feature_ref, grad_ref, *refs):
    keep_ref, send_ref = refs[-2:]
    core = slot_ref[SLOTS]
    rows, half = feature_ref.shape[-2], grad_ref.shape[-1] // 2
    for k in range(grad_ref.shape[0]):
        feature = feature_ref[k % feature_ref.shape[0]]
        for ref, side in ((keep_ref, core), (send_ref, 1 - core)):
            columns = pl.ds(pl.multiple_of(side * half, half), half)
            ref[k * rows : (k + 1) * rows] = dot(feature, grad_ref[k, :, columns]).astype(BFLOAT)


def k_keep(in_ref, *refs):
    out_ref, sem = refs[-2:]
    copy = pltpu.make_async_copy(in_ref, out_ref, sem)
    copy.start()
    copy.wait()


def k_join(n_in, n_out, *refs):
    stayed, came = refs[:n_in], refs[n_in : 2 * n_in]
    outs, sems = refs[-1 - n_out : -1], refs[-1]
    copies = []
    for which in range(2):
        target = outs[0].at[which] if n_out == 1 else outs[which]
        for side, sources in enumerate((stayed, came)):
            source = sources[0].at[which] if n_in == 1 else sources[which]
            size = source.shape[0]
            copies.append(pltpu.make_async_copy(source, target.at[pl.ds(side * size, size)], sems.at[len(copies)]))
    for copy in copies:
        copy.start()
    for copy in copies:
        copy.wait()


def k_halve(*refs):
    for which in range(2):
        keep0, keep1, came0, came1 = refs[4 * which : 4 * which + 4]
        stay = (keep0[0].astype(SINGLE) + came0[0].astype(SINGLE)).astype(BFLOAT)
        sent = (keep1[0].astype(SINGLE) + came1[0].astype(SINGLE)).astype(BFLOAT)
        if len(refs) == 10:
            refs[8][which, 0], refs[9][which, 0] = stay, sent
        else:
            refs[8 + 2 * which][0], refs[9 + 2 * which][0] = stay, sent


def k_halve_both(keep_ref, came_ref, stay_ref, sent_ref):
    total = (keep_ref[...].astype(SINGLE) + came_ref[...].astype(SINGLE)).astype(BFLOAT)
    half = total.shape[1] // 2
    stay_ref[...], sent_ref[...] = total[:, :half], total[:, half:]


def k_gather(me_ref, *refs):
    ins, out_ref, sems = refs[:8], refs[8], refs[9]
    rows, cols = ins[0].shape[1:]
    copies = []
    for other in range(2):
        column = pl.multiple_of((1 - me_ref[1] if other else me_ref[1]) * cols, cols)
        for which in range(2):
            for came in range(2):
                source = ins[4 * other + 2 * which + came]
                for q in range(8):
                    third, low, high = q >> 2, (q >> 1) & 1, q & 1
                    pair = 2 * third + came if which == 0 else 2 * came + third
                    block = me_ref[0] ^ (8 * high + 4 * low + pair)
                    row = pl.multiple_of((2 * block + which) * rows, rows)
                    target = out_ref.at[pl.ds(row, rows), pl.ds(column, cols)]
                    copies.append(pltpu.make_async_copy(source.at[q], target, sems.at[len(copies)]))
    for copy in copies:
        copy.start()
    for copy in copies:
        copy.wait()


def k_split(me_ref, *refs):
    own, got, outs = refs[:4], refs[4:8], refs[8:]
    for own_ref, got_ref, out_ref in zip(own, got, outs):
        out_ref[0] = (own_ref[...].astype(SINGLE) + got_ref[...].astype(SINGLE)).astype(BFLOAT)


def group_of(rows, start, bounds):
    index = lax.broadcasted_iota(jnp.int32, (rows, 1), 0) + start
    return sum((index >= bound).astype(jnp.int32) for bound in bounds)


def k_squares(start_ref, *refs):
    out_ref = refs[-1]
    lane = lax.broadcasted_iota(jnp.int32, (1, 128), 1)
    out_ref[...] = jnp.zeros_like(out_ref)
    for k in range(2):
        squares = [jnp.sum(ref[...] * ref[...], axis=1, keepdims=True) for ref in refs[4 * k : 4 * k + 4]]
        total = jnp.zeros((1, 128), SINGLE)
        for which, bounds in enumerate((NARROW_BOUNDS, WIDE_BOUNDS)):
            group = group_of(squares[which].shape[0], start_ref[which], bounds)
            for g in range(len(bounds) + 1):
                part_sum = jnp.sum(jnp.where(group == g, squares[which], 0.0))
                total = total + jnp.where(lane == 4 * which + g, part_sum, 0.0)
        for rows, first in ((squares[2], 7), (squares[3], 15)):
            row = lax.broadcasted_iota(jnp.int32, (rows.shape[0], 128), 0)
            column = lax.broadcasted_iota(jnp.int32, (rows.shape[0], 128), 1)
            total = total + jnp.sum(jnp.where(column == row + first, rows, 0.0), axis=0, keepdims=True)
        out_ref[k : k + 1, :] = total


def k_update(start_ref, square_ref, *refs):
    step = pl.program_id(0)
    norms = jnp.sqrt(square_ref[...])
    weight_norm, grad_norm = norms[0:1], norms[1:2]
    ratio = TRUST * weight_norm / (grad_norm + DECAY * weight_norm)
    lane = lax.broadcasted_iota(jnp.int32, (1, 128), 1)
    for k in range(4):
        weight, grad = refs[k][...], refs[4 + k][...]
        rows = weight.shape[0]
        if k < 2:
            bounds = (NARROW_BOUNDS, WIDE_BOUNDS)[k]
            group = group_of(rows, start_ref[k] + step * rows, bounds)
            scale = jnp.zeros((rows, 1), SINGLE)
            for g in range(len(bounds) + 1):
                scale = jnp.where(group == g, jnp.sum(jnp.where(lane == 4 * k + g, ratio, 0.0)), scale)
        else:
            row = lax.broadcasted_iota(jnp.int32, (rows, 128), 0)
            column = lax.broadcasted_iota(jnp.int32, (rows, 128), 1)
            scale = jnp.sum(jnp.where(column == row + (7, 15)[k - 2], ratio, 0.0), axis=1, keepdims=True)
        moment = MOMENTUM * refs[8 + k][...] + RATE * scale * (grad + DECAY * weight)
        refs[12 + k][...] = moment
        refs[16 + k][...] = weight - moment


def full(shape):
    zeros = (0,) * len(shape)
    return pl.BlockSpec(tuple(shape), lambda *_: zeros, pipeline_mode=pl.Buffered(1))


SCALARS = pl.BlockSpec(memory_space=pltpu.SMEM)
ANYWHERE = pl.BlockSpec(memory_space=pl.ANY)


def spec(shape, index):
    return pl.BlockSpec(tuple(shape), index)


def call(kernel, name, grid, in_specs, out_specs, out_shape, scratch, args, prefetch=0, vmem=8, aliases=None):
    return pl.pallas_call(
        kernel,
        out_shape=out_shape,
        grid_spec=pltpu.PrefetchScalarGridSpec(
            num_scalar_prefetch=prefetch,
            grid=grid,
            in_specs=in_specs,
            out_specs=out_specs,
            scratch_shapes=scratch,
        ),
        input_output_aliases=aliases or {},
        compiler_params=pltpu.CompilerParams(vmem_limit_bytes=vmem * MIB),
        cost_estimate=pl.CostEstimate(flops=0, bytes_accessed=int(MICROSECONDS.get(name, 1) * BYTES_PER_US), transcendentals=0),
        name=name,
    )(*args)


def shape_of(shape, dtype=SINGLE):
    return jax.ShapeDtypeStruct(tuple(shape), dtype)


def vmem_of(shape, dtype=SINGLE):
    return pltpu.VMEM(tuple(shape), dtype)


def hbm_of(shape, dtype=SINGLE):
    return pltpu.HBM(tuple(shape), dtype)


def in_vmem(value):
    return pltpu.with_memory_space_constraint(value, pltpu.VMEM)


def in_hbm(value):
    return pltpu.with_memory_space_constraint(value, pltpu.HBM)


def permutation():
    table = np.zeros((4 * PIX, 4 * PIX), np.float32)
    for pi in range(2):
        for pj in range(2):
            for i in range(HB):
                for j in range(WB):
                    table[((2 * pi + pj) * WB + j) * HB + i, (2 * i + pi) * 2 * WB + 2 * j + pj] = 1.0
    return jnp.asarray(table, BFLOAT)


def rounded(value):
    return lax.reduce_precision(value, 8, 7)


def split_group(name, keep, got, rows, index):
    cols = keep.shape[1]

    def block(which, sent):
        def at(q, me):
            other, low, high = (q >> 2) & 1, (q >> 1) & 1, q & 1
            pair = other * 2 + sent if which == 0 else sent * 2 + other
            return (index(which, me[0] ^ (high * 8 + low * 4 + pair)), 0)

        return spec((rows, cols), at)

    blocks = [block(which, sent) for which in range(2) for sent in range(2)]
    return call(
        k_split, name, (8,), blocks + blocks,
        [spec((1, rows, cols), lambda q, me: (q, 0, 0))] * 4,
        [shape_of((8, rows, cols), BFLOAT)] * 4, [],
        (lax.axis_index("dp")[None].astype(jnp.int32),) + (keep,) * 4 + (got,) * 4, prefetch=1,
    )


def halved(state, came, merge):
    (keep0, _sent, keep1, _sent), (came0, came1) = state, came
    count, block = keep0.shape[0] // 2, keep0.shape[1:]
    low, high = (spec((1,) + block, lambda q, at=at: (q + at, 0, 0)) for at in (0, count))
    if merge:
        outs, out_spec = [vmem_of((2, count) + block, BFLOAT)] * 2, [spec((2, 1) + block, lambda q: (0, q, 0, 0))] * 2
    else:
        outs, out_spec = [vmem_of((count,) + block, BFLOAT)] * 4, [low] * 4
    return tuple(call(
        k_halve, "halve", (count,), [low, high] * 4, out_spec, outs, [], (keep0, keep0, came0, came0, keep1, keep1, came1, came1), vmem=4,
    ))


def halved_both(state, came):
    shape = state[0].shape
    half = (2, shape[1] // 2) + shape[2:]
    return tuple(call(
        k_halve_both, "halve", (1,), [full(shape)] * 2, [full(half)] * 2, [vmem_of(half, BFLOAT)] * 2, [], (state[0], came), vmem=4,
    ))


def added(state, came):
    total = state[0].astype(SINGLE) + came.astype(SINGLE)
    return total[0, 0], total[1, 0]


def scatter_plain(keep, got, block, by_rows):
    total = (keep.astype(SINGLE) + got.astype(SINGLE)).astype(BFLOAT)
    if by_rows:
        own = lax.psum_scatter(total, "dp", scatter_dimension=0, tiled=True).astype(SINGLE)
        return own[: block // 2], own[block // 2 :]
    middle = total.shape[0] // 2
    return tuple(lax.psum_scatter(p, "dp", scatter_dimension=0, tiled=True).astype(SINGLE) for p in (total[:middle], total[middle:]))


def joined(value, got):
    return jnp.concatenate([value, got], axis=0)


def gather_blocks(name, core, parts, others, out_shape):
    scalars = jnp.stack([lax.axis_index("dp"), core]).astype(jnp.int32)
    pieces = [a for pair in list(parts) + list(others) for a in pair]
    return call(
        k_gather, name, (), [ANYWHERE] * 8, ANYWHERE, vmem_of(out_shape, BFLOAT),
        [pltpu.SemaphoreType.DMA((64,))], (scalars, *pieces), prefetch=1, vmem=2,
    )


def swap_all(parts):
    return [tuple(swap_pipe(a) for a in pair) for pair in parts]


def join_parts(stayed, came, token, n_out):
    n_in = len(stayed)
    shape = stayed[0].shape[-3:]
    shape = (2 * shape[0],) + shape[1:]
    outs = [vmem_of(shape, BFLOAT)] * 2 if n_out == 2 else [vmem_of((2,) + shape, BFLOAT)]
    return call(
        functools.partial(k_join, n_in, n_out), "join", (), [ANYWHERE] * (2 * n_in + 1), [ANYWHERE] * n_out, outs,
        [pltpu.SemaphoreType.DMA((4,))], tuple(stayed) + tuple(came) + (token,), vmem=2,
    )


def keep_in_hbm(value):
    def filler(token):
        return call(
            k_keep, "keep", (), [ANYWHERE] * 2, ANYWHERE, hbm_of(value.shape, value.dtype),
            [pltpu.SemaphoreType.DMA], (in_vmem(value), token), vmem=2,
        )

    return filler


def nothing(token):
    return token


def both_of(*fillers):
    return lambda token: tuple(filler(token) for filler in fillers)


def on_device(images, cotangent, heights, widths, assign, w_narrow, w_wide, bn_mid, bn_wide, mom_narrow, mom_wide, mom_bn_mid, mom_bn_wide):
    core = lax.axis_index("pipe")
    shard = lax.axis_index(("pipe", "dp"))
    fast = lax.axis_size("dp") == 16

    own_narrow = w_narrow.astype(BFLOAT)
    own_wide = w_wide.astype(BFLOAT)
    rows_n, half_n = w_narrow.shape[0], C_MID // 2
    part_n = rows_n // 2
    whole_n = (R_N // 2, C_MID)
    if fast:
        sent = swap_pipe(jnp.where(core == 0, own_narrow[:, half_n:], own_narrow[:, :half_n]))
        kept = jnp.where(core == 0, own_narrow[:, :half_n], own_narrow[:, half_n:])
        mine_a, mine_b = jnp.where(core == 0, kept, sent), jnp.where(core == 0, sent, kept)
        a, b = (mine.reshape(2, 1, part_n, half_n) for mine in (mine_a, mine_b))
        (a,) = join_parts((a,), (exchange(a, 8),), a, 1)
        a0, a1 = join_parts((a,), (exchange(a, 4),), a, 2)
        b = pin(b, a1)
        got, got_b = lax.optimization_barrier(((exchange(a0, 2), exchange(a1, 1)), exchange(b, 8)))
        a0, a1 = join_parts((a0, a1), got, got[1], 2)
        (b,) = join_parts((b,), (got_b,), got_b, 1)
        stay_a = swap_all([(a0,), (a1,)])
        own_wide = pin(own_wide, a1)
        wide = lax.all_gather(own_wide, ("pipe", "dp"), axis=0, tiled=True)
    else:
        narrow = lax.all_gather(own_narrow, ("pipe", "dp"), axis=0, tiled=True)
        narrow_a, narrow_b = narrow[: R_N // 2], narrow[R_N // 2 :]
        wide = lax.all_gather(own_wide, ("pipe", "dp"), axis=0, tiled=True)

    perm = permutation()
    core_row = core[None].astype(jnp.int32)
    x, mask, count_rows = call(
        k_prep, "prep", (SLOTS,),
        [spec((1, 4 * PIX, C_IN), lambda s, core, order, *_: (order[core[0] * SLOTS + s], 0, 0)), full((4 * PIX, 4 * PIX))],
        [spec((4, PIX, C_IN), lambda s, *_: (0, s, 0)), spec((PIX, 1), lambda s, *_: (s, 0)), full((4, C_MID))],
        [vmem_of((4, ROWS, C_IN), BFLOAT), vmem_of((ROWS, 1)), shape_of((4, C_MID))], [],
        (core_row, assign[0], heights, widths, in_hbm(images.reshape(IMG_DEV, 4 * PIX, C_IN)), in_hbm(perm)), prefetch=4, vmem=7,
    )
    mask = in_vmem(mask)
    order = assign[0].reshape(2, SLOTS)
    own_slots = lax.dynamic_index_in_dim(order, core, 0, keepdims=False)
    other_slots = lax.dynamic_index_in_dim(order, 1 - core, 0, keepdims=False)
    slots = jnp.concatenate([own_slots, core_row, other_slots])

    mid_cols, wide_cols = bn_mid.shape[1], bn_wide.shape[1]
    tables = jnp.concatenate(
        [
            lax.dynamic_update_slice(jnp.zeros((8, C_MID), SINGLE), rounded(bn_mid), (0, shard * mid_cols)),
            lax.dynamic_update_slice(jnp.zeros((6, C_OUT), SINGLE), rounded(bn_wide), (0, shard * wide_cols)).reshape(24, C_MID),
        ]
    )
    tables = tables + swap_pipe(tables)
    tables = jnp.concatenate([tables, count_rows])

    held = {}
    if fast:
        last0, last1, got_b, x, tables = lax.optimization_barrier((exchange(a0, 1), exchange(a1, 2), exchange(b, 4), x, tables))
        came_a = swap_all([(last0,), (last1,)])
        part_b = join_parts((b,), (got_b,), got_b, 2)
        narrow_a = gather_blocks("wa", core, [(a0, last0), (a1, last1)], [u + v for u, v in zip(stay_a, came_a)], whole_n)

    def turn(feature, feature_spec, grid, shape, index):
        def filler(token):
            return call(
                k_turn, "turn", grid, [feature_spec, ANYWHERE],
                spec((C_MID, ROWS), index), hbm_of(shape, BFLOAT), [], (feature, token),
            )

        return filler

    def weight_grad(name, feature, feature_spec, grad, grad_spec, tiles, shape, rows, base, bufs, token, space):
        out_spec = spec((rows, shape[1]), lambda t, slot: (base + t, 0))
        hold = in_vmem if space is vmem_of else in_hbm
        extra = tuple(hold(b) for b in bufs or ()) + (() if token is None else (token,))
        return call(
            k_grad, name, (tiles,), [feature_spec, grad_spec] + [ANYWHERE] * len(extra),
            [out_spec] * 2, [space(shape, BFLOAT)] * 2, [], (slots, feature, grad) + extra,
            prefetch=1, vmem=7, aliases={3: 0, 4: 1} if bufs else {},
        )

    full_row = full((4, C_MID))
    full_tab = full((2, C_MID))
    full_mask = full((ROWS, 1))
    full_mid = full((ROWS, C_MID))
    plane_pair = spec((2, ROWS, C_MID), lambda s: (jnp.minimum(s, 1), 0, 0))

    def narrow_block(index):
        return spec((TILE, TILE), index)

    chunk = spec((ROWS, TILE), lambda k, *_: (0, k))
    chunk_sum = spec((4, TILE), lambda k, *_: (0, k))
    chunk_tab = spec((2, TILE), lambda k, *_: (0, k))
    four_a = narrow_block(lambda k: (11, 0))
    four_b = narrow_block(lambda k: (jnp.maximum(k - 1, 0), 0))

    a1, part1 = call(
        k_first, "a1", (4,),
        [spec((1, ROWS, C_IN), lambda k: (k, 0, 0)), full((C_IN, C_MID))],
        [spec((1, ROWS, C_MID), lambda k: (k, 0, 0)), full_row],
        [hbm_of((4, ROWS, C_MID)), shape_of((4, C_MID))], [],
        (in_vmem(x), in_vmem(narrow_a)), vmem=6,
    )

    a1 = in_hbm(a1)
    def second_part_b(token):
        if not fast:
            return token
        part = pin(part_b, token)
        held["got"] = exchange(part[0], 2), exchange(part[1], 1)
        return token

    first_sum, (a_kept, (x_kept, first_b), _unused) = dp_sum(jnp.concatenate([part1, tables]), [keep_in_hbm(narrow_a), lambda token: (keep_in_hbm(x)(token), part_b if fast else token), second_part_b])
    x_kept, a_kept = in_hbm(x_kept), in_hbm(a_kept)
    total1, tables = first_sum[:4], first_sum[4:]
    mid, table = tables[:8], tables[8:32].reshape(6, C_OUT)
    inv = lax.dynamic_slice(1.0 / tables[32, :4], (2 * core,), (2,))
    mid1, mid2, mid4, mid5 = (mid[2 * k : 2 * k + 2] for k in range(4))
    tab3, tabs, tab6 = (table[2 * k : 2 * k + 2] for k in range(3))

    a_s, part_s = call(
        k_short, "as", (4,),
        [spec((1, ROWS, C_IN), lambda k: (0, 0, 0)), spec((TILE, TILE), lambda k: (1, k)), spec((TILE, TILE), lambda k: (2, k))],
        [chunk, chunk_sum],
        [vmem_of((ROWS, C_OUT)), shape_of((4, C_OUT))], [],
        (in_vmem(x), in_hbm(wide), in_hbm(wide)), vmem=6,
    )

    def conv_weights(first, order_of):
        return [narrow_block(lambda s, kx=kx: (first + 3 * order_of(s) + kx, 0)) for kx in range(3)]

    turned = lambda s: lax.rem(s + 1, 3)
    straight = lambda s: s

    a2, h1, part2 = call(
        k_conv_two, "a2", (3,),
        [SCALARS, full_row, full_tab, full_mask, plane_pair] + conv_weights(2, turned),
        [full_mid, plane_pair, full_row],
        [vmem_of((ROWS, C_MID)), vmem_of((4, ROWS, C_MID), BFLOAT), shape_of((4, C_MID))],
        [pltpu.VMEM((2, PAD + ROWS + PAD, C_MID), SINGLE)] * 2,
        (inv, total1, mid1, mask, a1) + (a_kept,) * 3, vmem=11,
    )
    a2 = in_vmem(a2)

    def third_part_b(token):
        if not fast:
            return token
        held["big_b"] = join_parts(first_b, pin(held["got"], token), token, 2)
        return held["big_b"]

    def fourth_b(token):
        if fast:
            big = pin(held["big_b"], token)
            held["got"] = exchange(big[0], 1), exchange(big[1], 2)
        return token

    turn_h1 = turn(h1, spec((1, ROWS, C_MID), lambda k: (k, 0, 0)), (4,), (4 * C_MID, ROWS), lambda k: (k, 0))
    total2, (h1_t, big_b, _unused) = dp_sum(part2, [turn_h1, third_part_b, fourth_b])

    def expand(name, a, total, tab, row):
        return call(
            k_expand, name, (4,),
            [SCALARS, full_row, full_tab, full_mask, full_mid, spec((TILE, TILE), lambda k: (row, k))],
            [full_mid, chunk, chunk_sum],
            [vmem_of((ROWS, C_MID), BFLOAT), vmem_of((ROWS, C_OUT)), shape_of((4, C_OUT))], [],
            (inv, total, tab, mask, a, in_hbm(wide)), vmem=6,
        )

    h2, a3, part3 = expand("a3", a2, total2, mid2, 0)
    whole = spec((ROWS, C_MID), lambda k: (0, 0))

    def swap_b(token):
        if not fast:
            return token
        ready = pin(tuple(big_b) + held["got"], token)
        return [(ready[0], ready[2]), (ready[1], ready[3])]

    def gather_b(token):
        if not fast:
            return narrow_b
        others = pin(held["others"], token)
        return gather_blocks("wb", core, held["parts"], others, whole_n)

    def start_swap_b(token):
        if fast:
            held["parts"] = swap_b(token)
            held["others"] = swap_all(held["parts"])
        return token

    total3s, ((h2_t, as_kept), (_unused, a3_kept), _unused, narrow_b) = dp_sum(
        jnp.concatenate([part3, part_s]),
        [
            both_of(turn(h2, whole, (1,), (C_MID, ROWS), lambda k: (0, 0)), keep_in_hbm(a_s)),
            both_of(start_swap_b, keep_in_hbm(a3)),
            nothing,
            gather_b,
        ],
    )
    as_kept, a3_kept = in_hbm(as_kept), in_hbm(a3_kept)
    total3, total_s = total3s[:4], total3s[4:]

    y, a4, part4 = call(
        k_meet, "a4", (4,),
        [SCALARS, chunk_sum, chunk_sum, chunk_tab, chunk_tab, full_mask, chunk, chunk, four_a, four_b],
        [chunk, full_mid, full_row],
        [vmem_of((ROWS, C_OUT), BFLOAT), vmem_of((ROWS, C_MID)), shape_of((4, C_MID))], [],
        (inv, total3, total_s, tab3, tabs, mask, in_vmem(a3), in_vmem(a_s), a_kept, in_vmem(narrow_b)), vmem=8,
    )
    a4 = in_vmem(a4)
    def turn_x(q, start, into):
        def filler(token):
            extra = () if into is None else (in_hbm(into[-1]),)
            held["x_t"] = call(
                k_turn, "turn", (2,), [spec((1, ROWS, C_MID), lambda k: (start + k, 0, q))] + [ANYWHERE] * (1 + len(extra)),
                spec((C_MID, ROWS), lambda k: (q, start + k)), hbm_of((C_IN, 4 * ROWS), BFLOAT), [], (x_kept, *extra, token),
                aliases={1: 0} if extra else {},
            )
            return held["x_t"]

        return filler

    total4, (y_t, y_kept, x_t0, x_t1) = dp_sum(
        part4,
        [
            turn(in_vmem(y), spec((ROWS, C_MID), lambda k: (0, k)), (4,), (4 * C_MID, ROWS), lambda k: (k, 0)),
            keep_in_hbm(y),
            turn_x(0, 0, None),
            lambda token: turn_x(0, 2, [held["x_t"]])(token),
        ],
    )
    del x_t0

    a5, h4, part5 = call(
        k_conv_one, "a5", (3,),
        [SCALARS, full_row, full_tab, full_mask, full_mid] + conv_weights(3, straight),
        [full_mid, full_mid, full_row],
        [vmem_of((ROWS, C_MID)), vmem_of((ROWS, C_MID), BFLOAT), shape_of((4, C_MID))],
        [pltpu.VMEM((PAD + ROWS + PAD, C_MID), SINGLE)] * 2,
        (inv, total4, mid4, mask, a4) + (in_vmem(narrow_b),) * 3, vmem=8,
    )
    a5 = in_vmem(a5)
    total5, (h4_t, b_kept, _unused, x_t) = dp_sum(
        part5,
        [
            turn(h4, whole, (1,), (C_MID, ROWS), lambda k: (0, 0)),
            keep_in_hbm(narrow_b),
            turn_x(1, 0, [x_t1]),
            lambda token: turn_x(1, 2, [held["x_t"]])(token),
        ],
    )
    b_kept = in_hbm(b_kept)
    h5, a6, part6 = expand("a6", a5, total5, mid5, 3)
    total6, (h5_t, a6_kept) = dp_sum(part6, [turn(h5, whole, (1,), (C_MID, ROWS), lambda k: (0, 0)), keep_in_hbm(a6)])
    a6_kept = in_hbm(a6_kept)

    cot = in_hbm(cotangent.transpose(0, 2, 1, 3).reshape(IMG_DEV, PIX, C_OUT))
    blk, gz6, s6 = call(
        k_head, "head", (4,),
        [SCALARS, chunk_sum, chunk_tab, full_mask, chunk, chunk]
        + [spec((1, PIX, TILE), lambda k, slot, s=s: (slot[s], 0, k)) for s in range(SLOTS)],
        [
            spec((1, ROWS, TILE), lambda k, slot: ((k // 2) ^ slot[SLOTS], 0, lax.rem(k, 2))),
            chunk,
            chunk_sum,
        ],
        [shape_of((2, ROWS, C_OUT // 2), BFLOAT), vmem_of((ROWS, C_OUT)), shape_of((4, C_OUT))], [],
        (slots, inv, total6, tab6, mask, in_vmem(a6), in_hbm(y_kept), cot, cot, cot, cot), prefetch=1, vmem=9,
    )
    gz6 = in_vmem(gz6)

    def place(name, pair, got, token):
        block = (1,) + pair.shape[2:]
        return call(
            k_place, name, (IMG_DEV,),
            [
                spec((1,) + block, lambda t, slot: (0, jnp.minimum(t, SLOTS - 1), 0, 0)),
                spec(block, lambda t, slot: (jnp.maximum(t - SLOTS, 0), 0, 0)),
                ANYWHERE,
            ],
            spec(block, lambda t, slot: (slot[t + (t >= SLOTS)], 0, 0)),
            shape_of((IMG_DEV,) + pair.shape[2:], BFLOAT), [],
            (slots, pair, got, token), prefetch=1, vmem=9,
        )

    blk = blk.reshape(2, SLOTS, PIX, C_OUT // 2)
    sum6, (got_blk, _unused, _unused, block_local) = dp_sum(
        s6,
        [
            lambda token: swap_pipe(pin(blk[1], token)),
            lambda token: token,
            lambda token: token,
            lambda token: token,
        ],
    )

    ga6, gz5, s5 = call(
        k_back_six, "g5", (4,),
        [SCALARS, chunk, chunk, chunk_sum, chunk_sum, chunk_tab, full_mask, spec((TILE, TILE), lambda k: (3, k)), full_mid, full_row, full_tab],
        [chunk, full_mid, full_row],
        [vmem_of((ROWS, C_OUT), BFLOAT), vmem_of((ROWS, C_MID)), shape_of((4, C_MID))],
        [pltpu.VMEM((ROWS, C_MID), SINGLE)],
        (inv, gz6, a6_kept, total6, sum6, tab6, mask, in_hbm(wide), a5, total5, mid5), vmem=9,
    )
    gz5 = in_vmem(gz5)

    def wide_rows(k):
        return spec((1, 256, ROWS), lambda t, slot: (0, t + k, 0))

    def whole_wide(grad):
        return grad.reshape((1,) + grad.shape), full((1,) + grad.shape)

    wide_shape, narrow_shape = (R_W, C_OUT // 2), (R_N // 2, C_MID // 2)
    sum5, (bufs_w, block_local) = dp_sum(
        s5,
        [
            lambda token: weight_grad("dw6", h5_t[None], wide_rows(0), *whole_wide(ga6), 2, wide_shape, 256, 6, None, token, hbm_of),
            lambda token: place("place_out", blk, got_blk, token),
        ],
    )
    block_local = block_local.reshape(IMG_DEV, WB, HB, C_OUT // 2).transpose(0, 2, 1, 3)

    col5, gz4, s4 = call(
        k_back_conv_one, "g4", (3,),
        [SCALARS, full_mid, full_mid, full_row, full_row, full_tab, full_mask] + conv_weights(3, straight) + [full_mid, full_row, full_tab],
        [spec((3, ROWS, C_MID), lambda s: (s, 0, 0)), full_mid, full_row],
        [vmem_of((9, ROWS, C_MID), BFLOAT), vmem_of((ROWS, C_MID)), shape_of((4, C_MID))],
        [pltpu.VMEM((PAD + ROWS + PAD, C_MID), SINGLE)] * 2 + [pltpu.VMEM((ROWS, C_MID), SINGLE)],
        (inv, gz5, a5, total5, sum5, mid5, mask, b_kept, b_kept, b_kept, a4, total4, mid4), vmem=10,
    )
    gz4 = in_vmem(gz4)
    one_turned = spec((1, C_MID, ROWS), lambda t, slot: (0, 0, 0))
    held_b = []

    def grad_five(k):
        def filler(token):
            grad_spec = spec((3, ROWS, C_MID), lambda t, slot: (k, 0, 0))
            held_b[:] = weight_grad("dw5", h4_t[None], one_turned, in_vmem(col5), grad_spec, 1, narrow_shape, 3 * TILE, 1 + k, list(held_b), token, vmem_of)
            return tuple(held_b)

        return filler

    sum4, results4 = dp_sum(s4, [grad_five(k) for k in range(3)])
    bufs_b = results4[2]

    ga4, gj, s3 = call(
        k_back_four, "gy", (4,),
        [SCALARS, full_mid, full_mid, full_row, full_row, full_tab, full_mask, four_a, four_b,
         chunk, chunk, chunk, chunk_sum, chunk_sum, chunk_tab, chunk_tab],
        [full_mid, chunk, spec((6, TILE), lambda k: (0, k))],
        [vmem_of((ROWS, C_MID), BFLOAT), vmem_of((ROWS, C_OUT)), shape_of((6, C_OUT))], [],
        (inv, gz4, a4, total4, sum4, mid4, mask, a_kept, b_kept, gz6, a3_kept, as_kept, total3, total_s, tab3, tabs), vmem=12,
    )
    gj = in_vmem(gj)

    by_rows = lambda which, m: 2 * m + which

    def grad_four(token):
        y_tiles = y_t.reshape(4, C_MID, ROWS)
        one = full((1, ROWS, C_MID))
        grad = in_vmem(ga4.reshape(1, ROWS, C_MID))
        held["grad_b"] = weight_grad("dw4b", y_tiles, spec((1, C_MID, ROWS), lambda t, slot: (1 + t, 0, 0)), grad, one, 3, narrow_shape, TILE, 0, bufs_b, token, vmem_of)
        return held["grad_b"]

    def grad_four_first(token):
        return weight_grad(
            "dw4a", y_t.reshape(4, C_MID, ROWS), spec((1, C_MID, ROWS), lambda t, slot: (0, 0, 0)), in_vmem(ga4.reshape(1, ROWS, C_MID)),
            full((1, ROWS, C_MID)), 1, narrow_shape, TILE, 11, None, token, vmem_of,
        )

    def swap_grad_b(token):
        held["got_b"] = swap_pipe(pin(held["grad_b"][1], token))
        return token

    def split_b(token):
        if not fast:
            return token
        keep, got = pin((held["grad_b"][0], held["got_b"]), token)
        state = split_group("split_b", in_vmem(keep), got, part_n, by_rows)
        held["came_b"] = exchange(state[1], 1), exchange(state[3], 2)
        return state

    sum3, results3 = dp_sum(s3, [grad_four, both_of(swap_grad_b, grad_four_first), split_b])
    bufs_b, bufs_a = results3[0], results3[1][1]
    held["b"] = results3[2]

    ga3, gas, gz2, s2 = call(
        k_back_three, "g2", (4,),
        [SCALARS, chunk, chunk, chunk, chunk_sum, chunk_sum, spec((6, TILE), lambda k: (0, k)), chunk_tab, chunk_tab, full_mask,
         spec((TILE, TILE), lambda k: (0, k)), full_mid, full_row, full_tab],
        [chunk, chunk, full_mid, full_row],
        [hbm_of((ROWS, C_OUT), BFLOAT), hbm_of((ROWS, C_OUT), BFLOAT), vmem_of((ROWS, C_MID)), shape_of((4, C_MID))],
        [pltpu.VMEM((ROWS, C_MID), SINGLE)],
        (inv, gj, a3_kept, as_kept, total3, total_s, sum3, tab3, tabs, mask, in_hbm(wide), a2, total2, mid2), vmem=11,
    )
    gz2 = in_vmem(gz2)

    def second_b(token):
        if not fast:
            return token
        state = halved(held["b"], pin(held["came_b"], token), False)
        held["came_b"] = exchange(state[1], 2), exchange(state[3], 1)
        return state

    def third_exchange_b(token):
        if not fast:
            return token
        state = halved(held["b"], pin(held["came_b"], token), True)
        held["came_b"] = exchange(state[1], 4)
        return state

    def fourth_exchange_b(token):
        if not fast:
            return token
        state = halved_both(held["b"], pin(held["came_b"], token))
        held["came_b"] = exchange(state[1], 8)
        return state

    def grad_three(token):
        held["w"] = weight_grad("dw3", h2_t[None], wide_rows(0), *whole_wide(ga3), 2, wide_shape, 256, 0, bufs_w, token, hbm_of)
        return held["w"]

    def grad_short(q):
        def filler(token):
            held["w"] = weight_grad("dws", x_t[None], wide_rows(2 * q), *whole_wide(gas), 2, wide_shape, 256, 2 + 2 * q, held["w"], token, hbm_of)
            return held["w"]

        return filler

    def start_swap_w(token):
        held["got_w"] = swap_pipe(pin(held["w"][1], token))
        return token

    def two_grads(token):
        grad_three(token)
        return grad_short(0)(token)

    sum2, results2 = dp_sum(s2, [two_grads, both_of(second_b, grad_short(1)), start_swap_w])
    held["b"], bufs_w = results2[1]
    got_w = held["got_w"]
    if fast:
        split = split_group("split_w", bufs_w[0], pin(got_w, sum2), w_wide.shape[0], lambda which, m: 16 * which + m)
        sum2, split, held["b"] = lax.optimization_barrier((sum2, split, third_exchange_b(sum2)))
        held["came"] = exchange(split[1], 1), exchange(split[3], 2)

    col2, gz1, s1 = call(
        k_back_conv_two, "g1", (3,),
        [SCALARS, full_mid, full_mid, full_row, full_row, full_tab, full_mask] + conv_weights(2, turned)
        + [plane_pair, full_row, full_tab],
        [spec((3, ROWS, C_MID), lambda s: (turned(s), 0, 0)), plane_pair, full_row],
        [vmem_of((9, ROWS, C_MID), BFLOAT), vmem_of((4, ROWS, C_MID)), shape_of((4, C_MID))],
        [pltpu.VMEM((PAD + ROWS + PAD, C_MID), SINGLE)] * 2 + [pltpu.VMEM((2, ROWS, C_MID), SINGLE)],
        (inv, gz2, a2, total2, sum2, mid2, mask, a_kept, a_kept, a_kept, a1, total1, mid1), vmem=12,
    )
    gz1 = in_vmem(gz1)
    h1_planes = h1_t.reshape(4, C_MID, ROWS)

    def grad_two(row):
        def filler(token):
            first = 2 * (1 - (row & 1))
            held["a"] = weight_grad(
                "dw2", h1_planes, spec((1, C_MID, ROWS), lambda t, slot: (first + (1 - (t & 1)), 0, 0)), in_vmem(col2),
                spec((1, ROWS, C_MID), lambda t, slot: (3 * row + t, 0, 0)), 3, narrow_shape, TILE, 2 + 3 * row, held["a"], token, vmem_of,
            )
            return held["a"]

        return filler

    def wide_back(token):
        return call(
            k_wide_back, "dxs", (2,),
            [full((ROWS, C_OUT)), spec((TILE, C_OUT), lambda k: (1 + k, 0)), ANYWHERE],
            spec((ROWS, TILE), lambda k: (0, k)),
            hbm_of((ROWS, C_IN)), [],
            (in_hbm(gas), in_hbm(wide), token), vmem=8,
        )

    def first_w(token):
        if not fast:
            return token
        came = pin(held["came"], token)
        return halved(split, came, False)

    held["a"] = bufs_a
    sum1, results1 = dp_sum(s1, [grad_two(0), grad_two(1), both_of(fourth_exchange_b, grad_two(2)), first_w], 4)
    held["b"], bufs_a = results1[2]
    state_w = results1[3]
    state_b = held["b"]
    plane = spec((1, ROWS, C_MID), lambda k: (k, 0, 0))
    ga1 = call(
        k_first_grad, "g0", (4,), [SCALARS, plane, plane, full_row, full_row, full_tab, full_mask], plane,
        vmem_of((4, ROWS, C_MID), BFLOAT), [], (inv, gz1, a1, total1, sum1, mid1, mask),
    )
    flat_ga1 = in_vmem(ga1.reshape(1, 4 * ROWS, C_MID))
    bufs_a = weight_grad(
        "dw1", x_t.reshape(2, C_MID, 4 * ROWS), spec((1, C_MID, 4 * ROWS), lambda t, slot: (t, 0, 0)), flat_ga1, full((1, 4 * ROWS, C_MID)),
        2, narrow_shape, TILE, 0, bufs_a, None, vmem_of,
    )
    got_a = swap_pipe(bufs_a[1])
    dxs = wide_back(bufs_a[0])

    def image_grads(token):
        pair = call(
            k_image_grad, "gx", (SLOTS,),
            [spec((4, PIX, C_MID), lambda s, slot: (0, s, 0)), spec((PIX, 1), lambda s, slot: (s, 0)), full((C_IN, C_MID)),
             spec((PIX, C_IN), lambda s, slot: (s, 0)), full((4 * PIX, 4 * PIX)), ANYWHERE],
            spec((2, 1, 4 * PIX, C_IN // 2), lambda s, slot: (0, s, 0, 0)),
            shape_of((2, SLOTS, 4 * PIX, C_IN // 2), BFLOAT), [],
            (slots, in_vmem(ga1), mask, a_kept, in_hbm(dxs), in_hbm(perm), token), prefetch=1, vmem=9,
        )
        return pair, swap_pipe(pair[1])

    if fast:
        state_w = halved(state_w, (exchange(state_w[1], 2), exchange(state_w[3], 1)), True)
        got_a, dxs, state_w, came_b = lax.optimization_barrier((got_a, dxs, state_w, held["came_b"]))
        came_w = exchange(state_w[1], 4)
        state_a = split_group("split_a", in_vmem(bufs_a[0]), got_a, part_n, by_rows)
        came_a = exchange(state_a[1], 1), exchange(state_a[3], 2)
        pair, got_pair = image_grads(state_a[0])
        state_w = halved_both(state_w, came_w)
        came_a, state_w, pair = lax.optimization_barrier((came_a, state_w, pair))
        came_w = exchange(state_w[1], 8)
        state_a = halved(state_a, came_a, False)
        came_a = exchange(state_a[1], 2), exchange(state_a[3], 1)
        half_w0, half_w1 = added(state_w, came_w)
        half_b = jnp.concatenate(added(state_b, came_b), axis=0)
        came_a, half_w0, half_w1, half_b = lax.optimization_barrier((came_a, half_w0, half_w1, half_b))
        state_a = halved(state_a, came_a, True)
        came_a = exchange(state_a[1], 4)
        grad_local = place("place_grad", pair, got_pair, state_a[0])
        came_a, grad_local = lax.optimization_barrier((came_a, grad_local))
        state_a = halved_both(state_a, came_a)
        came_a = exchange(state_a[1], 8)
        sum1, sum2, sum3, sum4, sum5, sum6 = pin((sum1, sum2, sum3, sum4, sum5, sum6), state_a[0])
        half_a = jnp.concatenate(added(state_a, came_a), axis=0)
    else:
        half_a = jnp.concatenate(scatter_plain(bufs_a[0], got_a, rows_n, True), axis=0)
        half_w0, half_w1 = scatter_plain(bufs_w[0], got_w, w_wide.shape[0], False)
        half_b = jnp.concatenate(scatter_plain(bufs_b[0], held["got_b"], rows_n, True), axis=0)
        pair, got_pair = image_grads(ga1)
        grad_local = place("place_grad", pair, got_pair, ga1)
    grad_local = grad_local.reshape(IMG_DEV, 2 * HB, 2 * WB, C_IN // 2)

    def join_halves(first, second):
        mine = jnp.where(core == 0, first, second)
        got = swap_pipe(jnp.where(core == 0, second, first))
        return jnp.where(core == 0, jnp.concatenate([mine, got], axis=1), jnp.concatenate([got, mine], axis=1))

    grad_narrow = join_halves(half_a, half_b)
    grad_wide = join_halves(half_w0, half_w1)

    def pair_sum(rows):
        return rows[0] + rows[1]

    mid_rows = jnp.stack([pair_sum(v) for t in (sum1, sum2, sum4, sum5) for v in (t[2:4], t[0:2])])
    wide_rows = jnp.stack([pair_sum(v) for v in (sum3[2:4], sum3[0:2], sum3[4:6], sum3[0:2], sum6[2:4], sum6[0:2])])
    mid_rows = mid_rows + swap_pipe(mid_rows)
    wide_rows = wide_rows + swap_pipe(wide_rows)
    grad_mid = lax.dynamic_slice(mid_rows, (0, shard * mid_cols), (8, mid_cols))
    grad_table = lax.dynamic_slice(wide_rows, (0, shard * wide_cols), (6, wide_cols))

    starts = (shard * jnp.array([rows_n, w_wide.shape[0]])).astype(jnp.int32)
    weights, grads = (w_narrow, w_wide, bn_mid, bn_wide), (grad_narrow, grad_wide, grad_mid, grad_table)
    whole_specs = [full(v.shape) for v in weights]
    squares = call(
        k_squares, "squares", (1,), whole_specs * 2, full((8, 128)), shape_of((8, 128)), [], (starts, *weights, *grads), prefetch=1, vmem=10,
    )
    squares, _unused = dp_sum(squares + swap_pipe(squares))
    parts = 4 if rows_n % 64 == 0 and w_wide.shape[0] % 64 == 0 else 1
    specs = [spec((v.shape[0] // parts, v.shape[1]), lambda k, *_: (k, 0)) for v in weights[:2]] + whole_specs[2:]
    updated = call(
        k_update, "update", (parts,), [full((8, 128))] + specs * 3, specs * 2, [shape_of(v.shape) for v in weights] * 2, [],
        (starts, squares, *weights, *grads, mom_narrow, mom_wide, mom_bn_mid, mom_bn_wide), prefetch=1, vmem=12,
    )
    new_mom_narrow, new_mom_wide, new_mom_mid, new_mom_table, new_narrow, new_wide, new_mid, new_table = updated
    return (
        block_local, grad_local, grad_narrow, grad_wide, grad_mid, grad_table,
        new_mom_narrow, new_mom_wide, new_mom_mid, new_mom_table,
        new_narrow, new_wide, new_mid, new_table,
    )


def solution(mesh):
    rows = P(("pipe", "dp"), None)
    columns = P(None, ("pipe", "dp"))
    feature = P("dp", None, None, None)
    return jax.shard_map(
        on_device,
        mesh=mesh,
        in_specs=(feature, feature, P("dp"), P("dp"), P("dp", None), rows, rows, columns, columns, rows, rows, columns, columns),
        out_specs=(P("dp", None, None, "pipe"), P("dp", None, None, "pipe"), rows, rows, columns, columns, rows, rows, columns, columns, rows, rows, columns, columns),
        check_vma=False,
    )
```

```python
import functools

import jax
import jax.numpy as jnp
import numpy as np
from jax import lax
from jax.experimental import pallas as pl
from jax.experimental.pallas import tpu as pltpu
from jax.sharding import PartitionSpec as P

C_IN = 1024
C_MID = 512
C_OUT = 2048
R_N = 12288
R_W = 2048
HB = 8
WB = 12
IMG_DEV = 8
SLOTS = 4
PIX = HB * WB
ROWS = SLOTS * PIX
HALF = ROWS // 2
PAD = 16
TILE = 512

EPS = 1e-05
MOMENTUM = 0.9
DECAY = 5e-05
TRUST = 0.001
RATE = 29.0
NARROW_BOUNDS = (C_IN, C_IN + 9 * C_MID, C_IN + 9 * C_MID + C_OUT)
WIDE_BOUNDS = (C_MID, C_MID + C_IN)
BFLOAT = jnp.bfloat16
SINGLE = jnp.float32
MIB = 1024 * 1024
BYTES_PER_US = 600000
MICROSECONDS = {
    "prep": 5, "a1": 3, "a2": 5, "as": 4.5, "a3": 4, "a4": 4.7, "a5": 4, "a6": 3.7, "head": 5.3, "g5": 5.2, "g4": 5.4, "gy": 7,
    "g2": 7.3, "g1": 8, "g0": 3, "gx": 6.4, "dxs": 5, "dw1": 3.4, "dw2": 2.1, "dw3": 2.9, "dws": 2.9, "dw4a": 1.7, "dw4b": 1.9,
    "dw5": 1.5, "dw6": 2.8, "place_out": 3.4, "place_grad": 5, "wa": 3, "wb": 3, "turn": 1.7, "keep": 1.7, "halve": 1, "squares": 2, "update": 3,
}


def pairs(bit):
    return [(i, i ^ bit) for i in range(lax.axis_size("dp"))]


def exchange(value, bit):
    return lax.ppermute(value, "dp", pairs(bit))


def pin(value, after):
    return lax.optimization_barrier((value, after))[0]


class Total:
    def __init__(self, *parts):
        self.parts = parts

    @property
    def sum(self):
        return self.parts[0] + self.parts[1]


def dp_sum(value, fillers=(), first=None):
    size = lax.axis_size("dp")
    bits = [1 << k for k in range(size.bit_length() - 1)]
    if first in bits:
        at = bits.index(first)
        bits = bits[at:] + bits[:at]
    results = []
    for bit in bits:
        got = exchange(value, bit)
        if len(results) < len(fillers):
            result = fillers[len(results)](value)
            got, result = lax.optimization_barrier((got, result))
            results.append(result)
        if bit == bits[-1]:
            break
        value = value + got
    for filler in fillers[len(results) :]:
        results.append(filler(got))
    return Total(value, got), results


def swap_pipe(value):
    return lax.ppermute(value, "pipe", [(0, 1), (1, 0)])


def dot(left, right):
    return jnp.dot(left, right, preferred_element_type=SINGLE)


def dot_back(left, right):
    return lax.dot_general(left, right, (((1,), (1,)), ((), ())), preferred_element_type=SINGLE)


def silu(value):
    return value * jax.nn.sigmoid(value)


def slope(value):
    gate = jax.nn.sigmoid(value)
    return gate * (1.0 + value * (1.0 - gate))


def put_sums(ref, values, first):
    for k, value in enumerate(values):
        for m in range(2):
            total = jnp.sum(value[m * HALF : (m + 1) * HALF], axis=0, keepdims=True)
            row = 2 * k + m
            ref[row : row + 1, :] = total if first else ref[row : row + 1, :] + total


def both(function):
    return jnp.concatenate([function(0), function(1)], axis=0)


def part(m):
    return slice(m * HALF, (m + 1) * HALF)


def moments(total_ref, inv_ref, m, scale=1.0):
    inv = inv_ref[m] * scale
    mean = total_ref[m : m + 1, :] * inv
    var = total_ref[2 + m : 3 + m, :] * inv - mean * mean
    return mean, lax.rsqrt(var + EPS)


def normed(a, total_ref, inv_ref, m, scale=1.0):
    mean, rstd = moments(total_ref, inv_ref, m, scale)
    return (a - mean) * rstd, rstd


def conv_grad(gz, xhat, rstd, gain, mask, sum_ref, inv_ref, m, scale=1.0, second=2):
    inv = inv_ref[m] * scale
    first_row = sum_ref[m : m + 1, :] * inv
    second_row = sum_ref[second + m : second + m + 1, :] * inv
    return (mask * ((rstd * gain) * (gz - first_row - xhat * second_row))).astype(BFLOAT)


class Both:
    def __init__(self, refs, start=0):
        self.refs, self.start = refs, start

    def __getitem__(self, index):
        rows, columns = index
        rows = slice(rows.start + self.start, rows.stop + self.start)
        return sum(ref[rows, columns] for ref in self.refs)


class Chunk:
    def __init__(self, refs, which, step):
        self.refs, self.first = refs, WIDE_ROW + 8 * which + step

    def __getitem__(self, index):
        rows, columns = index
        return sum(ref[pl.ds(self.first + 4 * rows.start, 1), columns] for ref in self.refs)


class Inverse:
    def __init__(self, refs, core):
        self.refs, self.core = refs, core

    def __getitem__(self, m):
        row = sum(ref[COUNT_ROW : COUNT_ROW + 1, 0:128] for ref in self.refs)
        lane = lax.broadcasted_iota(jnp.int32, (1, 128), 1)
        return 1.0 / jnp.sum(jnp.where(lane == 2 * self.core + m, row, 0.0), axis=1, keepdims=True)


ONE = (0,)
MID_ROW, WIDE_ROW, COUNT_ROW, TABLE_ROWS = 4, 12, 36, 40


def paired(kernel, views, tabs=None, inv=None, tables=1, lead=0):
    def run(*refs):
        fixed, refs = {}, list(refs)
        if inv is not None:
            core = refs.pop(0)[0]
            table, refs[lead : lead + tables] = refs[lead : lead + tables], []
            step = pl.program_id(0)
            fixed[inv] = Inverse(table, core)
            for at, (kind, which) in (tabs or {}).items():
                if kind == "wide":
                    fixed[at] = Chunk(table, which, step)
                else:
                    fixed[at] = Both(table, MID_ROW + 2 * which if kind == "mid" else 0)
        given, at = [], 0
        while at < len(refs) or len(given) in fixed:
            if len(given) in fixed:
                given.append(fixed[len(given)])
            elif len(given) in views:
                given.extend([Both(refs[at : at + 2], start) for start in views[len(given)]])
                at += 2
            else:
                given.append(refs[at])
                at += 1
        return kernel(*given)

    return run


def k_prep(core_ref, assign_ref, height_ref, width_ref, img_ref, perm_ref, out_ref, mask_ref, count_ref):
    slot = pl.program_id(0)
    image = assign_ref[0, core_ref[0] * SLOTS + slot]
    pixel = lax.broadcasted_iota(jnp.int32, (PIX, 1), 0)
    inside = ((pixel & (HB - 1)) < height_ref[image]) & (pixel < width_ref[image] * HB)
    mask = jnp.where(inside, 1.0, 0.0).astype(SINGLE)
    mask_ref[...] = mask
    planes = dot(perm_ref[...], img_ref[0])
    for k in range(4):
        out_ref[k] = (planes[k * PIX : (k + 1) * PIX] * mask).astype(BFLOAT)
    column = lax.broadcasted_iota(jnp.int32, count_ref.shape, 1)
    counts = jnp.zeros(count_ref.shape, jnp.int32)
    for m in range(4):
        pair = (assign_ref[0, 2 * m], assign_ref[0, 2 * m + 1])
        total = sum(height_ref[k] * width_ref[k] for k in pair)
        counts = jnp.where(column == m, total, counts)
    count_ref[...] = counts.astype(SINGLE)


def k_first(x_ref, w_ref, a_ref, sum_ref):
    a = dot(x_ref[0], w_ref[...])
    a_ref[0] = a

    @pl.when(pl.program_id(0) == 0)
    def _():
        sum_ref[...] = jnp.zeros_like(sum_ref)

    put_sums(sum_ref, [a, a * a], False)


def shift_mask(di, dj):
    if not di and not dj:
        return None
    pixel = lax.broadcasted_iota(jnp.int32, (SLOTS, PIX, 1), 1)
    inside = None
    if di:
        row = pixel & (HB - 1)
        inside = row >= -di if di < 0 else row < HB - di
    if dj:
        column = pixel >= -dj * HB if dj < 0 else pixel < PIX - dj * HB
        inside = column if inside is None else inside & column
    return jnp.where(inside, 1.0, 0.0).astype(SINGLE).reshape(ROWS, 1)


def rows_at(pad, di, dj):
    start = PAD + HB * dj + di
    rows = pad[start : start + ROWS, :]
    mask = shift_mask(di, dj)
    return rows if mask is None else rows * mask


def clear_pad(pad):
    pad[0:PAD, :] = jnp.zeros((PAD, pad.shape[1]), SINGLE)
    pad[PAD + ROWS : PAD + ROWS + PAD, :] = jnp.zeros((PAD, pad.shape[1]), SINGLE)


def body(pad, m):
    return pad.at[PAD + m * HALF : PAD + (m + 1) * HALF, :]


def carried(ref, fresh):
    return jnp.where(fresh, 0.0, ref[...])


def k_conv_two(inv_ref, total_ref, tab_ref, mask_ref, a_ref, w0, w1, w2, out_ref, h_ref, sum_ref, pad, moved):
    step = pl.program_id(0)
    gain, bias = tab_ref[0:1, :], tab_ref[1:2, :]

    @pl.when(step < 2)
    def _():
        for k in range(2):
            clear_pad(pad.at[k])
            clear_pad(moved.at[k])
            for m in range(2):
                xhat, _unused = normed(a_ref[k, part(m), :], total_ref, inv_ref, m, 0.25)
                h = (silu(xhat * gain + bias) * mask_ref[part(m), :]).astype(BFLOAT)
                h_ref[k, part(m), :] = h
                body(pad.at[k], m)[...] = h.astype(SINGLE)
                body(moved.at[k], m)[...] = h.astype(SINGLE)

    @pl.when(step == 2)
    def _():
        for k in range(2):
            moved[k, PAD : PAD + ROWS, :] = rows_at(pad.at[k], -1, 0)

    term = dot(rows_at(moved.at[0], 0, 0).astype(BFLOAT), w1[...])
    term += dot(rows_at(moved.at[1], 0, -1).astype(BFLOAT), w0[...])
    term += dot(rows_at(moved.at[1], 0, 0).astype(BFLOAT), w2[...])
    out_ref[...] = carried(out_ref, step == 0) + term

    @pl.when(step == 2)
    def _():
        a = out_ref[...]
        masked = a * mask_ref[...]
        put_sums(sum_ref, [masked, masked * a], True)


def k_conv_one(inv_ref, total_ref, tab_ref, mask_ref, a_ref, w0, w1, w2, out_ref, h_ref, sum_ref, pad, moved):
    step = pl.program_id(0)
    gain, bias = tab_ref[0:1, :], tab_ref[1:2, :]

    @pl.when(step == 0)
    def _():
        clear_pad(pad)
        clear_pad(moved)
        for m in range(2):
            xhat, _unused = normed(a_ref[part(m), :], total_ref, inv_ref, m)
            h = (silu(xhat * gain + bias) * mask_ref[part(m), :]).astype(BFLOAT)
            h_ref[part(m), :] = h
            body(pad, m)[...] = h.astype(SINGLE)

    for s in range(3):

        @pl.when(step == s)
        def _(s=s):
            moved[PAD : PAD + ROWS, :] = rows_at(pad, s - 1, 0)

    term = dot(rows_at(moved, 0, -1).astype(BFLOAT), w0[...])
    term += dot(rows_at(moved, 0, 0).astype(BFLOAT), w1[...])
    term += dot(rows_at(moved, 0, 1).astype(BFLOAT), w2[...])
    out_ref[...] = carried(out_ref, step == 0) + term

    @pl.when(step == 2)
    def _():
        a = out_ref[...]
        masked = a * mask_ref[...]
        put_sums(sum_ref, [masked, masked * a], True)


def k_expand(inv_ref, total_ref, tab_ref, mask_ref, a_ref, w_ref, h_ref, out_ref, sum_ref):
    @pl.when(pl.program_id(0) == 0)
    def _():
        gain, bias = tab_ref[0:1, :], tab_ref[1:2, :]
        for m in range(2):
            xhat, _unused = normed(a_ref[part(m), :], total_ref, inv_ref, m)
            h_ref[part(m), :] = (silu(xhat * gain + bias) * mask_ref[part(m), :]).astype(BFLOAT)

    a = dot(h_ref[...], w_ref[...])
    out_ref[...] = a
    put_sums(sum_ref, [a, a * a], True)


def k_short(x_ref, w0, w1, out_ref, sum_ref):
    a = dot(x_ref[0, :, :TILE], w0[...]) + dot(x_ref[0, :, TILE:], w1[...])
    out_ref[...] = a
    put_sums(sum_ref, [a, a * a], True)


def k_meet(inv_ref, t3_ref, ts_ref, tab3_ref, tabs_ref, mask_ref, a3_ref, as_ref, wa_ref, wb_ref, y_ref, out_ref, sum_ref):
    step = pl.program_id(0)
    for m in range(2):
        x3, _unused = normed(a3_ref[part(m), :], t3_ref, inv_ref, m)
        xs, _unused = normed(as_ref[part(m), :], ts_ref, inv_ref, m)
        joined = (x3 * tab3_ref[0:1, :] + tab3_ref[1:2, :]) + (xs * tabs_ref[0:1, :] + tabs_ref[1:2, :])
        y_ref[part(m), :] = (silu(joined) * mask_ref[part(m), :]).astype(BFLOAT)

    @pl.when(step == 0)
    def _():
        out_ref[...] = dot(y_ref[...], wa_ref[...])

    @pl.when(step > 0)
    def _():
        out_ref[...] += dot(y_ref[...], wb_ref[...])

    @pl.when(step == pl.num_programs(0) - 1)
    def _():
        a = out_ref[...]
        put_sums(sum_ref, [a, a * a], True)


def k_head(order_ref, inv_ref, total_ref, tab_ref, mask_ref, a_ref, y_ref, c0, c1, c2, c3, blk_ref, gz_ref, sum_ref):
    cots = (c0, c1, c2, c3)
    gain, bias = tab_ref[0:1, :], tab_ref[1:2, :]
    for m in range(2):
        mask = mask_ref[part(m), :]
        xhat, _unused = normed(a_ref[part(m), :], total_ref, inv_ref, m)
        z = (xhat * gain + bias) + y_ref[part(m), :].astype(SINGLE)
        gate = jax.nn.sigmoid(z)
        blk_ref[0, part(m), :] = (z * gate * mask).astype(BFLOAT)
        cot = jnp.concatenate([cots[2 * m][0], cots[2 * m + 1][0]], axis=0).astype(SINGLE)
        gz = cot * mask * (gate * (1.0 + z * (1.0 - gate)))
        gz_ref[part(m), :] = gz
        sum_ref[m : m + 1, :] = jnp.sum(gz, axis=0, keepdims=True)
        sum_ref[2 + m : 3 + m, :] = jnp.sum(gz * xhat, axis=0, keepdims=True)


def finish_back(gz_ref, sum_ref, grad, a_ref, total_ref, tab_ref, inv_ref, mask_ref):
    gain, bias = tab_ref[0:1, :], tab_ref[1:2, :]
    for m in range(2):
        xhat, _unused = normed(a_ref[part(m), :], total_ref, inv_ref, m)
        gz = grad[part(m)] * mask_ref[part(m), :] * slope(xhat * gain + bias)
        gz_ref[part(m), :] = gz
        sum_ref[m : m + 1, :] = jnp.sum(gz, axis=0, keepdims=True)
        sum_ref[2 + m : 3 + m, :] = jnp.sum(gz * xhat, axis=0, keepdims=True)


def k_back_six(inv_ref, gz_ref, a_ref, total_ref, s_ref, tab_ref, mask_ref, w_ref, low_ref, low_total, low_tab, ga_ref, out_ref, sum_ref, acc):
    step = pl.program_id(0)
    for m in range(2):
        xhat, rstd = normed(a_ref[part(m), :], total_ref, inv_ref, m)
        ga_ref[part(m), :] = conv_grad(
            gz_ref[part(m), :], xhat, rstd, tab_ref[0:1, :], mask_ref[part(m), :], s_ref, inv_ref, m
        )
    term = dot_back(ga_ref[...], w_ref[...])

    @pl.when(step == 0)
    def _():
        acc[...] = term

    @pl.when(step > 0)
    def _():
        acc[...] += term

    @pl.when(step == pl.num_programs(0) - 1)
    def _():
        finish_back(out_ref, sum_ref, acc[...], low_ref, low_total, low_tab, inv_ref, mask_ref)


def k_back_conv_one(inv_ref, gz_ref, a_ref, total_ref, s_ref, tab_ref, mask_ref, w0, w1, w2, low_ref, low_total, low_tab, col_ref, out_ref, sum_ref, pad, moved, acc):
    step = pl.program_id(0)

    @pl.when(step == 0)
    def _():
        clear_pad(pad)
        clear_pad(moved)
        for m in range(2):
            xhat, rstd = normed(a_ref[part(m), :], total_ref, inv_ref, m)
            ga = conv_grad(gz_ref[part(m), :], xhat, rstd, tab_ref[0:1, :], mask_ref[part(m), :], s_ref, inv_ref, m)
            body(pad, m)[...] = ga.astype(SINGLE)

    for s in range(3):

        @pl.when(step == s)
        def _(s=s):
            moved[PAD : PAD + ROWS, :] = rows_at(pad, 1 - s, 0)

    term = None
    for kx, weight in enumerate((w0, w1, w2)):
        tap = rows_at(moved, 0, 1 - kx).astype(BFLOAT)
        col_ref[kx] = tap
        product = dot_back(tap, weight[...])
        term = product if term is None else term + product
    acc[...] = carried(acc, step == 0) + term

    @pl.when(step == 2)
    def _():
        finish_back(out_ref, sum_ref, acc[...], low_ref, low_total, low_tab, inv_ref, mask_ref)


def k_back_four(inv_ref, gz_ref, a_ref, total_ref, s_ref, tab_ref, mask_ref, wa_ref, wb_ref, up_ref, a3_ref, as_ref, t3_ref, ts_ref, tab3_ref, tabs_ref, ga_ref, gj_ref, sum_ref):
    @pl.when(pl.program_id(0) == 0)
    def _():
        for m in range(2):
            xhat, rstd = normed(a_ref[part(m), :], total_ref, inv_ref, m)
            ga_ref[part(m), :] = conv_grad(
                gz_ref[part(m), :], xhat, rstd, tab_ref[0:1, :], mask_ref[part(m), :], s_ref, inv_ref, m
            )

    weight = jnp.where(pl.program_id(0) == 0, wa_ref[...], wb_ref[...])
    grad = dot_back(ga_ref[...], weight) + up_ref[...]
    for m in range(2):
        x3, _unused = normed(a3_ref[part(m), :], t3_ref, inv_ref, m)
        xs, _unused = normed(as_ref[part(m), :], ts_ref, inv_ref, m)
        joined = (x3 * tab3_ref[0:1, :] + tab3_ref[1:2, :]) + (xs * tabs_ref[0:1, :] + tabs_ref[1:2, :])
        gj = grad[part(m)].astype(BFLOAT).astype(SINGLE) * mask_ref[part(m), :] * slope(joined)
        gj_ref[part(m), :] = gj
        for k, value in enumerate((gj, gj * x3, gj * xs)):
            row = 2 * k + m
            sum_ref[row : row + 1, :] = jnp.sum(value, axis=0, keepdims=True)


def k_back_three(inv_ref, gj_ref, a3_ref, as_ref, t3_ref, ts_ref, s_ref, tab3_ref, tabs_ref, mask_ref, w_ref, low_ref, low_total, low_tab, g3_ref, gs_ref, out_ref, sum_ref, acc):
    step = pl.program_id(0)
    for m in range(2):
        mask = mask_ref[part(m), :]
        gj = gj_ref[part(m), :]
        x3, r3 = normed(a3_ref[part(m), :], t3_ref, inv_ref, m)
        g3_ref[part(m), :] = conv_grad(gj, x3, r3, tab3_ref[0:1, :], mask, s_ref, inv_ref, m)
        xs, rs = normed(as_ref[part(m), :], ts_ref, inv_ref, m)
        gs_ref[part(m), :] = conv_grad(gj, xs, rs, tabs_ref[0:1, :], mask, s_ref, inv_ref, m, second=4)
    term = dot_back(g3_ref[...], w_ref[...])

    @pl.when(step == 0)
    def _():
        acc[...] = term

    @pl.when(step > 0)
    def _():
        acc[...] += term

    @pl.when(step == pl.num_programs(0) - 1)
    def _():
        finish_back(out_ref, sum_ref, acc[...], low_ref, low_total, low_tab, inv_ref, mask_ref)


def k_back_conv_two(inv_ref, gz_ref, a_ref, total_ref, s_ref, tab_ref, mask_ref, w0, w1, w2, low_ref, low_total, low_tab, col_ref, out_ref, sum_ref, pad, moved, acc):
    step = pl.program_id(0)
    gain, bias = low_tab[0:1, :], low_tab[1:2, :]

    @pl.when(step == 0)
    def _():
        clear_pad(pad)
        clear_pad(moved)
        for m in range(2):
            xhat, rstd = normed(a_ref[part(m), :], total_ref, inv_ref, m)
            ga = conv_grad(gz_ref[part(m), :], xhat, rstd, tab_ref[0:1, :], mask_ref[part(m), :], s_ref, inv_ref, m)
            body(pad, m)[...] = ga.astype(SINGLE)
            body(moved, m)[...] = ga.astype(SINGLE)
        sum_ref[...] = jnp.zeros_like(sum_ref)

    @pl.when(step == 2)
    def _():
        moved[PAD : PAD + ROWS, :] = rows_at(pad, 1, 0)

    plain = rows_at(moved, 0, 0).astype(BFLOAT)
    aside = rows_at(moved, 0, 1).astype(BFLOAT)
    col_ref[0], col_ref[1], col_ref[2] = aside, plain, plain
    acc[0] = carried(acc.at[0], step < 2) + dot_back(plain, w1[...])
    acc[1] = carried(acc.at[1], step < 2) + (dot_back(aside, w0[...]) + dot_back(plain, w2[...]))

    @pl.when(step != 1)
    def _():
        for k in range(2):
            for m in range(2):
                xhat, _unused = normed(low_ref[k, part(m), :], low_total, inv_ref, m, 0.25)
                gz = acc[k, part(m), :] * mask_ref[part(m), :] * slope(xhat * gain + bias)
                out_ref[k, part(m), :] = gz
                for q, value in enumerate((gz, gz * xhat)):
                    row = 2 * q + m
                    sum_ref[row : row + 1, :] += jnp.sum(value, axis=0, keepdims=True)


def k_wide_back(g_ref, w_ref, *refs):
    refs[-1][...] = dot_back(g_ref[...], w_ref[...])


def k_first_grad(inv_ref, gz_ref, a_ref, total_ref, s_ref, tab_ref, mask_ref, ga_ref):
    for m in range(2):
        xhat, rstd = normed(a_ref[0, part(m), :], total_ref, inv_ref, m, 0.25)
        ga_ref[0, part(m), :] = conv_grad(
            gz_ref[0, part(m), :], xhat, rstd, tab_ref[0:1, :], mask_ref[part(m), :], s_ref, inv_ref, m, 0.25
        )


def k_image_grad(core_ref, ga_ref, mask_ref, w_ref, short_ref, perm_ref, *refs):
    out_ref = refs[-1]
    grads = dot_back(ga_ref[...].reshape(4 * PIX, C_MID), w_ref[...])
    mask = mask_ref[...]
    parts = []
    for k in range(4):
        grad = grads[k * PIX : (k + 1) * PIX]
        if k == 0:
            grad = grad + short_ref[...]
        parts.append((grad * mask).astype(BFLOAT))
    planes = jnp.concatenate(parts, axis=0)
    image = lax.dot_general(perm_ref[...], planes, (((0,), (0,)), ((), ())), preferred_element_type=SINGLE).astype(BFLOAT)
    core = core_ref[0]
    out_ref[core, 0] = image[:, : C_IN // 2]
    out_ref[1 - core, 0] = image[:, C_IN // 2 :]


def k_place(core_ref, order_ref, own_ref, got_ref, *refs):
    out_ref = refs[-1]
    step = pl.program_id(0)

    @pl.when(step < SLOTS)
    def _():
        out_ref[0] = own_ref[0, 0]

    @pl.when(step >= SLOTS)
    def _():
        out_ref[0] = got_ref[0]


def k_turn(in_ref, *refs):
    refs[-1][...] = in_ref[...].reshape(in_ref.shape[-2:]).T


def k_grad(core_ref, feature_ref, grad_ref, *refs):
    keep_ref, send_ref = refs[-2:]
    core = core_ref[0]
    rows, half = feature_ref.shape[-2], grad_ref.shape[-1] // 2
    for k in range(grad_ref.shape[0]):
        feature = feature_ref[k % feature_ref.shape[0]]
        for ref, side in ((keep_ref, core), (send_ref, 1 - core)):
            columns = pl.ds(pl.multiple_of(side * half, half), half)
            ref[k * rows : (k + 1) * rows] = dot(feature, grad_ref[k, :, columns]).astype(BFLOAT)


def k_keep(in_ref, *refs):
    out_ref, sem = refs[-2:]
    copy = pltpu.make_async_copy(in_ref, out_ref, sem)
    copy.start()
    copy.wait()


def k_join(n_in, n_out, *refs):
    stayed, came = refs[:n_in], refs[n_in : 2 * n_in]
    outs, sems = refs[-1 - n_out : -1], refs[-1]
    copies = []
    for which in range(2):
        target = outs[0].at[which] if n_out == 1 else outs[which]
        for side, sources in enumerate((stayed, came)):
            source = sources[0].at[which] if n_in == 1 else sources[which]
            size = source.shape[0]
            copies.append(pltpu.make_async_copy(source, target.at[pl.ds(side * size, size)], sems.at[len(copies)]))
    for copy in copies:
        copy.start()
    for copy in copies:
        copy.wait()


def k_halve(*refs):
    for which in range(2):
        keep0, keep1, came0, came1 = refs[4 * which : 4 * which + 4]
        stay = (keep0[0].astype(SINGLE) + came0[0].astype(SINGLE)).astype(BFLOAT)
        sent = (keep1[0].astype(SINGLE) + came1[0].astype(SINGLE)).astype(BFLOAT)
        if len(refs) == 10:
            refs[8][which, 0], refs[9][which, 0] = stay, sent
        else:
            refs[8 + 2 * which][0], refs[9 + 2 * which][0] = stay, sent


def k_halve_both(keep_ref, came_ref, stay_ref, sent_ref):
    total = (keep_ref[...].astype(SINGLE) + came_ref[...].astype(SINGLE)).astype(BFLOAT)
    half = total.shape[1] // 2
    stay_ref[...], sent_ref[...] = total[:, :half], total[:, half:]


def k_gather(me_ref, *refs):
    ins, out_ref, sems = refs[:8], refs[8], refs[9]
    rows, cols = ins[0].shape[1:]
    copies = []
    for other in range(2):
        column = pl.multiple_of((1 - me_ref[1] if other else me_ref[1]) * cols, cols)
        for which in range(2):
            for came in range(2):
                source = ins[4 * other + 2 * which + came]
                for q in range(8):
                    third, low, high = q >> 2, (q >> 1) & 1, q & 1
                    pair = 2 * third + came if which == 0 else 2 * came + third
                    block = me_ref[0] ^ (8 * high + 4 * low + pair)
                    row = pl.multiple_of((2 * block + which) * rows, rows)
                    target = out_ref.at[pl.ds(row, rows), pl.ds(column, cols)]
                    copies.append(pltpu.make_async_copy(source.at[q], target, sems.at[len(copies)]))
    for copy in copies:
        copy.start()
    for copy in copies:
        copy.wait()


def k_split(me_ref, *refs):
    own, got, outs = refs[:4], refs[4:8], refs[8:]
    for own_ref, got_ref, out_ref in zip(own, got, outs):
        out_ref[0] = (own_ref[...].astype(SINGLE) + got_ref[...].astype(SINGLE)).astype(BFLOAT)


def group_of(rows, start, bounds):
    index = lax.broadcasted_iota(jnp.int32, (rows, 1), 0) + start
    return sum((index >= bound).astype(jnp.int32) for bound in bounds)


def k_squares(start_ref, *refs):
    out_ref = refs[-1]
    lane = lax.broadcasted_iota(jnp.int32, (1, 128), 1)
    out_ref[...] = jnp.zeros_like(out_ref)
    for k in range(2):
        squares = [jnp.sum(ref[...] * ref[...], axis=1, keepdims=True) for ref in refs[4 * k : 4 * k + 4]]
        total = jnp.zeros((1, 128), SINGLE)
        for which, bounds in enumerate((NARROW_BOUNDS, WIDE_BOUNDS)):
            group = group_of(squares[which].shape[0], start_ref[which], bounds)
            for g in range(len(bounds) + 1):
                part_sum = jnp.sum(jnp.where(group == g, squares[which], 0.0))
                total = total + jnp.where(lane == 4 * which + g, part_sum, 0.0)
        for rows, first in ((squares[2], 7), (squares[3], 15)):
            row = lax.broadcasted_iota(jnp.int32, (rows.shape[0], 128), 0)
            column = lax.broadcasted_iota(jnp.int32, (rows.shape[0], 128), 1)
            total = total + jnp.sum(jnp.where(column == row + first, rows, 0.0), axis=0, keepdims=True)
        out_ref[k : k + 1, :] = total


def k_update(start_ref, square_ref, *refs):
    step = pl.program_id(0)
    norms = jnp.sqrt(square_ref[0:8, :])
    weight_norm, grad_norm = norms[0:1], norms[1:2]
    ratio = TRUST * weight_norm / (grad_norm + DECAY * weight_norm)
    lane = lax.broadcasted_iota(jnp.int32, (1, 128), 1)
    for k in range(4):
        weight, grad = refs[k][...], refs[4 + k][...]
        rows = weight.shape[0]
        if k < 2:
            bounds = (NARROW_BOUNDS, WIDE_BOUNDS)[k]
            group = group_of(rows, start_ref[k] + step * rows, bounds)
            scale = jnp.zeros((rows, 1), SINGLE)
            for g in range(len(bounds) + 1):
                scale = jnp.where(group == g, jnp.sum(jnp.where(lane == 4 * k + g, ratio, 0.0)), scale)
        else:
            row = lax.broadcasted_iota(jnp.int32, (rows, 128), 0)
            column = lax.broadcasted_iota(jnp.int32, (rows, 128), 1)
            scale = jnp.sum(jnp.where(column == row + (7, 15)[k - 2], ratio, 0.0), axis=1, keepdims=True)
        moment = MOMENTUM * refs[8 + k][...] + RATE * scale * (grad + DECAY * weight)
        refs[12 + k][...] = moment
        refs[16 + k][...] = weight - moment


def full(shape):
    zeros = (0,) * len(shape)
    return pl.BlockSpec(tuple(shape), lambda *_: zeros, pipeline_mode=pl.Buffered(1))


SCALARS = pl.BlockSpec(memory_space=pltpu.SMEM)
ANYWHERE = pl.BlockSpec(memory_space=pl.ANY)


def spec(shape, index):
    return pl.BlockSpec(tuple(shape), index)


def call(kernel, name, grid, in_specs, out_specs, out_shape, scratch, args, prefetch=0, vmem=8, aliases=None):
    return pl.pallas_call(
        kernel,
        out_shape=out_shape,
        grid_spec=pltpu.PrefetchScalarGridSpec(
            num_scalar_prefetch=prefetch,
            grid=grid,
            in_specs=in_specs,
            out_specs=out_specs,
            scratch_shapes=scratch,
        ),
        input_output_aliases=aliases or {},
        compiler_params=pltpu.CompilerParams(vmem_limit_bytes=vmem * MIB),
        cost_estimate=pl.CostEstimate(flops=0, bytes_accessed=int(MICROSECONDS.get(name, 1) * BYTES_PER_US), transcendentals=0),
        name=name,
    )(*args)


def shape_of(shape, dtype=SINGLE):
    return jax.ShapeDtypeStruct(tuple(shape), dtype)


def vmem_of(shape, dtype=SINGLE):
    return pltpu.VMEM(tuple(shape), dtype)


def hbm_of(shape, dtype=SINGLE):
    return pltpu.HBM(tuple(shape), dtype)


def in_vmem(value):
    return pltpu.with_memory_space_constraint(value, pltpu.VMEM)


def in_hbm(value):
    return pltpu.with_memory_space_constraint(value, pltpu.HBM)


def permutation():
    table = np.zeros((4 * PIX, 4 * PIX), np.float32)
    for pi in range(2):
        for pj in range(2):
            for i in range(HB):
                for j in range(WB):
                    table[((2 * pi + pj) * WB + j) * HB + i, (2 * i + pi) * 2 * WB + 2 * j + pj] = 1.0
    return jnp.asarray(table, BFLOAT)


def rounded(value):
    return lax.reduce_precision(value, 8, 7)


def split_group(name, keep, got, rows, index):
    cols = keep.shape[1]

    def block(which, sent):
        def at(q, me):
            other, low, high = (q >> 2) & 1, (q >> 1) & 1, q & 1
            pair = other * 2 + sent if which == 0 else sent * 2 + other
            return (index(which, me[0] ^ (high * 8 + low * 4 + pair)), 0)

        return spec((rows, cols), at)

    blocks = [block(which, sent) for which in range(2) for sent in range(2)]
    return call(
        k_split, name, (8,), blocks + blocks,
        [spec((1, rows, cols), lambda q, me: (q, 0, 0))] * 4,
        [shape_of((8, rows, cols), BFLOAT)] * 4, [],
        (lax.axis_index("dp")[None].astype(jnp.int32),) + (keep,) * 4 + (got,) * 4, prefetch=1,
    )


def halved(state, came, merge):
    (keep0, _sent, keep1, _sent), (came0, came1) = state, came
    count, block = keep0.shape[0] // 2, keep0.shape[1:]
    low, high = (spec((1,) + block, lambda q, at=at: (q + at, 0, 0)) for at in (0, count))
    if merge:
        outs, out_spec = [vmem_of((2, count) + block, BFLOAT)] * 2, [spec((2, 1) + block, lambda q: (0, q, 0, 0))] * 2
    else:
        outs, out_spec = [vmem_of((count,) + block, BFLOAT)] * 4, [low] * 4
    return tuple(call(
        k_halve, "halve", (count,), [low, high] * 4, out_spec, outs, [], (keep0, keep0, came0, came0, keep1, keep1, came1, came1), vmem=4,
    ))


def halved_both(state, came):
    shape = state[0].shape
    half = (2, shape[1] // 2) + shape[2:]
    return tuple(call(
        k_halve_both, "halve", (1,), [full(shape)] * 2, [full(half)] * 2, [vmem_of(half, BFLOAT)] * 2, [], (state[0], came), vmem=4,
    ))


def added(state, came):
    total = state[0].astype(SINGLE) + came.astype(SINGLE)
    return total[0, 0], total[1, 0]


def scatter_plain(keep, got, block, by_rows):
    total = (keep.astype(SINGLE) + got.astype(SINGLE)).astype(BFLOAT)
    if by_rows:
        own = lax.psum_scatter(total, "dp", scatter_dimension=0, tiled=True).astype(SINGLE)
        return own[: block // 2], own[block // 2 :]
    middle = total.shape[0] // 2
    return tuple(lax.psum_scatter(p, "dp", scatter_dimension=0, tiled=True).astype(SINGLE) for p in (total[:middle], total[middle:]))


def joined(value, got):
    return jnp.concatenate([value, got], axis=0)


def gather_blocks(name, core, parts, others, out_shape):
    scalars = jnp.stack([lax.axis_index("dp"), core]).astype(jnp.int32)
    pieces = [a for pair in list(parts) + list(others) for a in pair]
    return call(
        k_gather, name, (), [ANYWHERE] * 8, ANYWHERE, vmem_of(out_shape, BFLOAT),
        [pltpu.SemaphoreType.DMA((64,))], (scalars, *pieces), prefetch=1, vmem=2,
    )


def swap_all(parts):
    return [tuple(swap_pipe(a) for a in pair) for pair in parts]


def join_parts(stayed, came, token, n_out):
    n_in = len(stayed)
    shape = stayed[0].shape[-3:]
    shape = (2 * shape[0],) + shape[1:]
    outs = [vmem_of(shape, BFLOAT)] * 2 if n_out == 2 else [vmem_of((2,) + shape, BFLOAT)]
    return call(
        functools.partial(k_join, n_in, n_out), "join", (), [ANYWHERE] * (2 * n_in + 1), [ANYWHERE] * n_out, outs,
        [pltpu.SemaphoreType.DMA((4,))], tuple(stayed) + tuple(came) + (token,), vmem=2,
    )


def keep_in_hbm(value):
    def filler(token):
        return call(
            k_keep, "keep", (), [ANYWHERE] * 2, ANYWHERE, hbm_of(value.shape, value.dtype),
            [pltpu.SemaphoreType.DMA], (in_vmem(value), token), vmem=2,
        )

    return filler


def nothing(token):
    return token


def both_of(*fillers):
    return lambda token: tuple(filler(token) for filler in fillers)


def on_device(images, cotangent, heights, widths, assign, w_narrow, w_wide, bn_mid, bn_wide, mom_narrow, mom_wide, mom_bn_mid, mom_bn_wide):
    core = lax.axis_index("pipe")
    shard = lax.axis_index(("pipe", "dp"))
    fast = lax.axis_size("dp") == 16

    own_narrow = w_narrow.astype(BFLOAT)
    own_wide = w_wide.astype(BFLOAT)
    rows_n, half_n = w_narrow.shape[0], C_MID // 2
    part_n = rows_n // 2
    whole_n = (R_N // 2, C_MID)
    if fast:
        sent = swap_pipe(jnp.where(core == 0, own_narrow[:, half_n:], own_narrow[:, :half_n]))
        kept = jnp.where(core == 0, own_narrow[:, :half_n], own_narrow[:, half_n:])
        mine_a, mine_b = jnp.where(core == 0, kept, sent), jnp.where(core == 0, sent, kept)
        a, b = (mine.reshape(2, 1, part_n, half_n) for mine in (mine_a, mine_b))
        (a,) = join_parts((a,), (exchange(a, 8),), a, 1)
        a0, a1 = join_parts((a,), (exchange(a, 4),), a, 2)
        b = pin(b, a1)
        got, got_b = lax.optimization_barrier(((exchange(a0, 2), exchange(a1, 1)), exchange(b, 8)))
        a0, a1 = join_parts((a0, a1), got, got[1], 2)
        (b,) = join_parts((b,), (got_b,), got_b, 1)
        stay_a = swap_all([(a0,), (a1,)])
        own_wide = pin(own_wide, a1)
        wide = lax.all_gather(own_wide, ("pipe", "dp"), axis=0, tiled=True)
    else:
        narrow = lax.all_gather(own_narrow, ("pipe", "dp"), axis=0, tiled=True)
        narrow_a, narrow_b = narrow[: R_N // 2], narrow[R_N // 2 :]
        wide = lax.all_gather(own_wide, ("pipe", "dp"), axis=0, tiled=True)

    perm = permutation()
    core_row = core[None].astype(jnp.int32)
    x, mask, count_rows = call(
        k_prep, "prep", (SLOTS,),
        [spec((1, 4 * PIX, C_IN), lambda s, core, order, *_: (order[0, core[0] * SLOTS + s], 0, 0)), full((4 * PIX, 4 * PIX))],
        [spec((4, PIX, C_IN), lambda s, *_: (0, s, 0)), spec((PIX, 1), lambda s, *_: (s, 0)), full((4, C_MID))],
        [vmem_of((4, ROWS, C_IN), BFLOAT), vmem_of((ROWS, 1)), shape_of((4, C_MID))], [],
        (core_row, assign, heights, widths, in_hbm(images.reshape(IMG_DEV, 4 * PIX, C_IN)), in_hbm(perm)), prefetch=4, vmem=7,
    )
    mask = in_vmem(mask)
    mid_cols, wide_cols = bn_mid.shape[1], bn_wide.shape[1]
    tables = jnp.concatenate(
        [
            lax.dynamic_update_slice(jnp.zeros((8, C_MID), SINGLE), rounded(bn_mid), (0, shard * mid_cols)),
            lax.dynamic_update_slice(jnp.zeros((6, C_OUT), SINGLE), rounded(bn_wide), (0, shard * wide_cols)).reshape(24, C_MID),
        ]
    )
    tables = tables + swap_pipe(tables)
    tables = jnp.concatenate([tables, count_rows])

    held = {}
    if fast:
        last0, last1, got_b, x, tables = lax.optimization_barrier((exchange(a0, 1), exchange(a1, 2), exchange(b, 4), x, tables))
        came_a = swap_all([(last0,), (last1,)])
        part_b = join_parts((b,), (got_b,), got_b, 2)
        narrow_a = gather_blocks("wa", core, [(a0, last0), (a1, last1)], [u + v for u, v in zip(stay_a, came_a)], whole_n)

    def turn(feature, feature_spec, grid, shape, index):
        def filler(token):
            return call(
                k_turn, "turn", grid, [feature_spec, ANYWHERE],
                spec((C_MID, ROWS), index), hbm_of(shape, BFLOAT), [], (feature, token),
            )

        return filler

    def weight_grad(name, feature, feature_spec, grad, grad_spec, tiles, shape, rows, base, bufs, token, space):
        out_spec = spec((rows, shape[1]), lambda t, slot: (base + t, 0))
        hold = in_vmem if space is vmem_of else in_hbm
        extra = tuple(hold(b) for b in bufs or ()) + (() if token is None else (token,))
        return call(
            k_grad, name, (tiles,), [feature_spec, grad_spec] + [ANYWHERE] * len(extra),
            [out_spec] * 2, [space(shape, BFLOAT)] * 2, [], (core_row, feature, grad) + extra,
            prefetch=1, vmem=7, aliases={3: 0, 4: 1} if bufs else {},
        )

    full_row = full((4, C_MID))
    full_table = full((TABLE_ROWS, C_MID))
    full_mask = full((ROWS, 1))
    full_mid = full((ROWS, C_MID))
    plane_pair = spec((2, ROWS, C_MID), lambda s: (jnp.minimum(s, 1), 0, 0))

    def narrow_block(index):
        return spec((TILE, TILE), index)

    chunk = spec((ROWS, TILE), lambda k, *_: (0, k))
    chunk_sum = spec((4, TILE), lambda k, *_: (0, k))
    chunk_eight = spec((8, TILE), lambda k, *_: (0, k))
    four_a = narrow_block(lambda k: (11, 0))
    four_b = narrow_block(lambda k: (jnp.maximum(k - 1, 0), 0))

    a1, part1 = call(
        k_first, "a1", (4,),
        [spec((1, ROWS, C_IN), lambda k: (k, 0, 0)), full((C_IN, C_MID))],
        [spec((1, ROWS, C_MID), lambda k: (k, 0, 0)), full_row],
        [hbm_of((4, ROWS, C_MID)), shape_of((4, C_MID))], [],
        (in_vmem(x), in_vmem(narrow_a)), vmem=6,
    )

    a1 = in_hbm(a1)
    def second_part_b(token):
        if not fast:
            return token
        part = pin(part_b, token)
        held["got"] = exchange(part[0], 2), exchange(part[1], 1)
        return token

    first_sum, (a_kept, (x_kept, first_b), _unused) = dp_sum(jnp.concatenate([part1, tables]), [keep_in_hbm(narrow_a), lambda token: (keep_in_hbm(x)(token), part_b if fast else token), second_part_b])
    x_kept, a_kept = in_hbm(x_kept), in_hbm(a_kept)
    base = in_vmem(first_sum.sum)

    a_s, part_s = call(
        k_short, "as", (4,),
        [spec((1, ROWS, C_IN), lambda k: (0, 0, 0)), spec((TILE, TILE), lambda k: (1, k)), spec((TILE, TILE), lambda k: (2, k))],
        [chunk, chunk_sum],
        [vmem_of((ROWS, C_OUT)), shape_of((4, C_OUT))], [],
        (in_vmem(x), in_hbm(wide), in_hbm(wide)), vmem=6,
    )

    def conv_weights(first, order_of):
        return [narrow_block(lambda s, kx=kx: (first + 3 * order_of(s) + kx, 0)) for kx in range(3)]

    turned = lambda s: lax.rem(s + 1, 3)
    straight = lambda s: s

    a2, h1, part2 = call(
        paired(k_conv_two, {}, {1: ("base", 0), 2: ("mid", 0)}, 0, 2), "a2", (3,),
        [SCALARS, full_table, full_table, full_mask, plane_pair] + conv_weights(2, turned),
        [full_mid, plane_pair, full_row],
        [vmem_of((ROWS, C_MID)), vmem_of((4, ROWS, C_MID), BFLOAT), shape_of((4, C_MID))],
        [pltpu.VMEM((2, PAD + ROWS + PAD, C_MID), SINGLE)] * 2,
        (core_row, *first_sum.parts, mask, a1) + (a_kept,) * 3, vmem=11,
    )
    a2 = in_vmem(a2)

    def third_part_b(token):
        if not fast:
            return token
        held["big_b"] = join_parts(first_b, pin(held["got"], token), token, 2)
        return held["big_b"]

    def fourth_b(token):
        if fast:
            big = pin(held["big_b"], token)
            held["got"] = exchange(big[0], 1), exchange(big[1], 2)
        return token

    turn_h1 = turn(h1, spec((1, ROWS, C_MID), lambda k: (k, 0, 0)), (4,), (4 * C_MID, ROWS), lambda k: (k, 0))
    total2, (h1_t, big_b, _unused) = dp_sum(part2, [turn_h1, third_part_b, fourth_b])

    def expand(name, a, total, which, row):
        return call(
            paired(k_expand, {1: ONE}, {2: ("mid", which)}, 0), name, (4,),
            [SCALARS, full_table, full_row, full_row, full_mask, full_mid, spec((TILE, TILE), lambda k: (row, k))],
            [full_mid, chunk, chunk_sum],
            [vmem_of((ROWS, C_MID), BFLOAT), vmem_of((ROWS, C_OUT)), shape_of((4, C_OUT))], [],
            (core_row, base, *total.parts, mask, a, in_hbm(wide)), vmem=6,
        )

    h2, a3, part3 = expand("a3", a2, total2, 1, 0)
    whole = spec((ROWS, C_MID), lambda k: (0, 0))

    def swap_b(token):
        if not fast:
            return token
        ready = pin(tuple(big_b) + held["got"], token)
        return [(ready[0], ready[2]), (ready[1], ready[3])]

    def gather_b(token):
        if not fast:
            return narrow_b
        others = pin(held["others"], token)
        return gather_blocks("wb", core, held["parts"], others, whole_n)

    def start_swap_b(token):
        if fast:
            held["parts"] = swap_b(token)
            held["others"] = swap_all(held["parts"])
        return token

    total3s, ((h2_t, as_kept), (_unused, a3_kept), _unused, narrow_b) = dp_sum(
        jnp.concatenate([part3, part_s]),
        [
            both_of(turn(h2, whole, (1,), (C_MID, ROWS), lambda k: (0, 0)), keep_in_hbm(a_s)),
            both_of(start_swap_b, keep_in_hbm(a3)),
            nothing,
            gather_b,
        ],
    )
    as_kept, a3_kept = in_hbm(as_kept), in_hbm(a3_kept)

    y, a4, part4 = call(
        paired(k_meet, {1: (0, 4)}, {3: ("wide", 0), 4: ("wide", 1)}, 0), "a4", (4,),
        [SCALARS, full_table, chunk_eight, chunk_eight, full_mask, chunk, chunk, four_a, four_b],
        [chunk, full_mid, full_row],
        [vmem_of((ROWS, C_OUT), BFLOAT), vmem_of((ROWS, C_MID)), shape_of((4, C_MID))], [],
        (core_row, base, *total3s.parts, mask, in_vmem(a3), in_vmem(a_s), a_kept, in_vmem(narrow_b)), vmem=8,
    )
    a4 = in_vmem(a4)
    def turn_x(q, start, into):
        def filler(token):
            extra = () if into is None else (in_hbm(into[-1]),)
            held["x_t"] = call(
                k_turn, "turn", (2,), [spec((1, ROWS, C_MID), lambda k: (start + k, 0, q))] + [ANYWHERE] * (1 + len(extra)),
                spec((C_MID, ROWS), lambda k: (q, start + k)), hbm_of((C_IN, 4 * ROWS), BFLOAT), [], (x_kept, *extra, token),
                aliases={1: 0} if extra else {},
            )
            return held["x_t"]

        return filler

    total4, (y_t, y_kept, x_t0, x_t1) = dp_sum(
        part4,
        [
            turn(in_vmem(y), spec((ROWS, C_MID), lambda k: (0, k)), (4,), (4 * C_MID, ROWS), lambda k: (k, 0)),
            keep_in_hbm(y),
            turn_x(0, 0, None),
            lambda token: turn_x(0, 2, [held["x_t"]])(token),
        ],
    )
    del x_t0

    a5, h4, part5 = call(
        paired(k_conv_one, {1: ONE}, {2: ("mid", 2)}, 0), "a5", (3,),
        [SCALARS, full_table, full_row, full_row, full_mask, full_mid] + conv_weights(3, straight),
        [full_mid, full_mid, full_row],
        [vmem_of((ROWS, C_MID)), vmem_of((ROWS, C_MID), BFLOAT), shape_of((4, C_MID))],
        [pltpu.VMEM((PAD + ROWS + PAD, C_MID), SINGLE)] * 2,
        (core_row, base, *total4.parts, mask, a4) + (in_vmem(narrow_b),) * 3, vmem=8,
    )
    a5 = in_vmem(a5)
    total5, (h4_t, b_kept, _unused, x_t) = dp_sum(
        part5,
        [
            turn(h4, whole, (1,), (C_MID, ROWS), lambda k: (0, 0)),
            keep_in_hbm(narrow_b),
            turn_x(1, 0, [x_t1]),
            lambda token: turn_x(1, 2, [held["x_t"]])(token),
        ],
    )
    b_kept = in_hbm(b_kept)
    h5, a6, part6 = expand("a6", a5, total5, 3, 3)
    total6, (h5_t, a6_kept) = dp_sum(part6, [turn(h5, whole, (1,), (C_MID, ROWS), lambda k: (0, 0)), keep_in_hbm(a6)])
    a6_kept = in_hbm(a6_kept)

    cot = in_hbm(cotangent.transpose(0, 2, 1, 3).reshape(IMG_DEV, PIX, C_OUT))
    blk, gz6, s6 = call(
        paired(k_head, {2: ONE}, {3: ("wide", 2)}, 1, lead=1), "head", (4,),
        [full_table, chunk_sum, chunk_sum, full_mask, chunk, chunk]
        + [spec((1, PIX, TILE), lambda k, core, order, s=s: (order[0, core[0] * SLOTS + s], 0, k)) for s in range(SLOTS)],
        [
            spec((1, ROWS, TILE), lambda k, core, _order: ((k // 2) ^ core[0], 0, lax.rem(k, 2))),
            chunk,
            chunk_sum,
        ],
        [shape_of((2, ROWS, C_OUT // 2), BFLOAT), vmem_of((ROWS, C_OUT)), shape_of((4, C_OUT))], [],
        (core_row, assign, base, *total6.parts, mask, in_vmem(a6), in_hbm(y_kept), cot, cot, cot, cot), prefetch=2, vmem=9,
    )
    gz6 = in_vmem(gz6)

    def place(name, pair, got, token):
        block = (1,) + pair.shape[2:]
        return call(
            k_place, name, (IMG_DEV,),
            [
                spec((1,) + block, lambda t, *_: (0, jnp.minimum(t, SLOTS - 1), 0, 0)),
                spec(block, lambda t, *_: (jnp.maximum(t - SLOTS, 0), 0, 0)),
                ANYWHERE,
            ],
            spec(block, lambda t, core, order: (order[0, (core[0] * SLOTS + t) & (IMG_DEV - 1)], 0, 0)),
            shape_of((IMG_DEV,) + pair.shape[2:], BFLOAT), [],
            (core_row, assign, pair, got, token), prefetch=2, vmem=9,
        )

    blk = blk.reshape(2, SLOTS, PIX, C_OUT // 2)
    sum6, (got_blk, _unused, _unused, block_local) = dp_sum(
        s6,
        [
            lambda token: swap_pipe(pin(blk[1], token)),
            lambda token: token,
            lambda token: token,
            lambda token: token,
        ],
    )

    ga6, gz5, s5 = call(
        paired(k_back_six, {3: ONE, 4: ONE, 9: ONE}, {5: ("wide", 2), 10: ("mid", 3)}, 0), "g5", (4,),
        [SCALARS, full_table, chunk, chunk, chunk_sum, chunk_sum, chunk_sum, chunk_sum, full_mask, spec((TILE, TILE), lambda k: (3, k)), full_mid,
         full_row, full_row],
        [chunk, full_mid, full_row],
        [vmem_of((ROWS, C_OUT), BFLOAT), vmem_of((ROWS, C_MID)), shape_of((4, C_MID))],
        [pltpu.VMEM((ROWS, C_MID), SINGLE)],
        (core_row, base, gz6, a6_kept, *total6.parts, *sum6.parts, mask, in_hbm(wide), a5, *total5.parts), vmem=9,
    )
    gz5 = in_vmem(gz5)

    def wide_rows(k):
        return spec((1, 256, ROWS), lambda t, slot: (0, t + k, 0))

    def whole_wide(grad):
        return grad.reshape((1,) + grad.shape), full((1,) + grad.shape)

    wide_shape, narrow_shape = (R_W, C_OUT // 2), (R_N // 2, C_MID // 2)
    sum5, (bufs_w, block_local) = dp_sum(
        s5,
        [
            lambda token: weight_grad("dw6", h5_t[None], wide_rows(0), *whole_wide(ga6), 2, wide_shape, 256, 6, None, token, vmem_of),
            lambda token: place("place_out", blk, got_blk, token),
        ],
    )
    block_local = block_local.reshape(IMG_DEV, WB, HB, C_OUT // 2).transpose(0, 2, 1, 3)

    col5, gz4, s4 = call(
        paired(k_back_conv_one, {3: ONE, 4: ONE, 11: ONE}, {5: ("mid", 3), 12: ("mid", 2)}, 0), "g4", (3,),
        [SCALARS, full_table, full_mid, full_mid, full_row, full_row, full_row, full_row, full_mask] + conv_weights(3, straight)
        + [full_mid, full_row, full_row],
        [spec((3, ROWS, C_MID), lambda s: (s, 0, 0)), full_mid, full_row],
        [vmem_of((9, ROWS, C_MID), BFLOAT), vmem_of((ROWS, C_MID)), shape_of((4, C_MID))],
        [pltpu.VMEM((PAD + ROWS + PAD, C_MID), SINGLE)] * 2 + [pltpu.VMEM((ROWS, C_MID), SINGLE)],
        (core_row, base, gz5, a5, *total5.parts, *sum5.parts, mask, b_kept, b_kept, b_kept, a4, *total4.parts), vmem=10,
    )
    gz4 = in_vmem(gz4)
    one_turned = spec((1, C_MID, ROWS), lambda t, slot: (0, 0, 0))
    held_b = []

    def grad_five(k):
        def filler(token):
            grad_spec = spec((3, ROWS, C_MID), lambda t, slot: (k, 0, 0))
            held_b[:] = weight_grad("dw5", h4_t[None], one_turned, in_vmem(col5), grad_spec, 1, narrow_shape, 3 * TILE, 1 + k, list(held_b), token, vmem_of)
            return tuple(held_b)

        return filler

    sum4, results4 = dp_sum(s4, [grad_five(k) for k in range(3)])
    bufs_b = results4[2]

    ga4, gj, s3 = call(
        paired(k_back_four, {3: ONE, 4: ONE, 12: (0, 4)}, {5: ("mid", 2), 14: ("wide", 0), 15: ("wide", 1)}, 0), "gy", (4,),
        [SCALARS, full_table, full_mid, full_mid, full_row, full_row, full_row, full_row, full_mask, four_a, four_b,
         chunk, chunk, chunk, chunk_eight, chunk_eight],
        [full_mid, chunk, spec((6, TILE), lambda k: (0, k))],
        [vmem_of((ROWS, C_MID), BFLOAT), vmem_of((ROWS, C_OUT)), shape_of((6, C_OUT))], [],
        (core_row, base, gz4, a4, *total4.parts, *sum4.parts, mask, a_kept, b_kept, gz6, a3_kept, as_kept, *total3s.parts), vmem=12,
    )
    gj = in_vmem(gj)

    by_rows = lambda which, m: 2 * m + which

    def grad_four(token):
        y_tiles = y_t.reshape(4, C_MID, ROWS)
        one = full((1, ROWS, C_MID))
        grad = in_vmem(ga4.reshape(1, ROWS, C_MID))
        held["grad_b"] = weight_grad("dw4b", y_tiles, spec((1, C_MID, ROWS), lambda t, slot: (1 + t, 0, 0)), grad, one, 3, narrow_shape, TILE, 0, bufs_b, token, vmem_of)
        return held["grad_b"]

    def grad_four_first(token):
        return weight_grad(
            "dw4a", y_t.reshape(4, C_MID, ROWS), spec((1, C_MID, ROWS), lambda t, slot: (0, 0, 0)), in_vmem(ga4.reshape(1, ROWS, C_MID)),
            full((1, ROWS, C_MID)), 1, narrow_shape, TILE, 11, None, token, vmem_of,
        )

    def swap_grad_b(token):
        held["got_b"] = swap_pipe(pin(held["grad_b"][1], token))
        return token

    def split_b(token):
        if not fast:
            return token
        keep, got = pin((held["grad_b"][0], held["got_b"]), token)
        state = split_group("split_b", in_vmem(keep), got, part_n, by_rows)
        held["came_b"] = exchange(state[1], 1), exchange(state[3], 2)
        return state

    sum3, results3 = dp_sum(s3, [grad_four, both_of(swap_grad_b, grad_four_first), split_b])
    bufs_b, bufs_a = results3[0], results3[1][1]
    held["b"] = results3[2]

    ga3, gas, gz2, s2 = call(
        paired(k_back_three, {4: (0, 4), 6: ONE, 12: ONE}, {7: ("wide", 0), 8: ("wide", 1), 13: ("mid", 1)}, 0), "g2", (4,),
        [SCALARS, full_table, chunk, chunk, chunk, chunk_eight, chunk_eight, spec((6, TILE), lambda k: (0, k)), spec((6, TILE), lambda k: (0, k)), full_mask,
         spec((TILE, TILE), lambda k: (0, k)), full_mid, full_row, full_row],
        [chunk, chunk, full_mid, full_row],
        [hbm_of((ROWS, C_OUT), BFLOAT), hbm_of((ROWS, C_OUT), BFLOAT), vmem_of((ROWS, C_MID)), shape_of((4, C_MID))],
        [pltpu.VMEM((ROWS, C_MID), SINGLE)],
        (core_row, base, gj, a3_kept, as_kept, *total3s.parts, *sum3.parts, mask, in_hbm(wide), a2, *total2.parts), vmem=11,
    )
    gz2 = in_vmem(gz2)

    def second_b(token):
        if not fast:
            return token
        state = halved(held["b"], pin(held["came_b"], token), False)
        held["came_b"] = exchange(state[1], 2), exchange(state[3], 1)
        return state

    def third_exchange_b(token):
        if not fast:
            return token
        state = halved(held["b"], pin(held["came_b"], token), True)
        held["came_b"] = exchange(state[1], 4)
        return state

    def fourth_exchange_b(token):
        if not fast:
            return token
        state = halved_both(held["b"], pin(held["came_b"], token))
        held["came_b"] = exchange(state[1], 8)
        return state

    def grad_three(token):
        held["w"] = weight_grad("dw3", h2_t[None], wide_rows(0), *whole_wide(ga3), 2, wide_shape, 256, 0, bufs_w, token, vmem_of)
        return held["w"]

    def grad_short(q):
        def filler(token):
            held["w"] = weight_grad("dws", x_t[None], wide_rows(2 * q), *whole_wide(gas), 2, wide_shape, 256, 2 + 2 * q, held["w"], token, vmem_of)
            return held["w"]

        return filler

    def start_swap_w(token):
        held["got_w"] = swap_pipe(pin(held["w"][1], token))
        return token

    def two_grads(token):
        grad_three(token)
        return grad_short(0)(token)

    sum2, results2 = dp_sum(s2, [two_grads, both_of(second_b, grad_short(1)), start_swap_w])
    held["b"], bufs_w = results2[1]
    got_w = held["got_w"]
    if fast:
        split = split_group("split_w", bufs_w[0], pin(got_w, sum2.parts[1]), w_wide.shape[0], lambda which, m: 16 * which + m)
        last, split, held["b"] = lax.optimization_barrier((sum2.parts[1], split, third_exchange_b(sum2.parts[1])))
        sum2 = Total(sum2.parts[0], last)
        held["came"] = exchange(split[1], 1), exchange(split[3], 2)

    col2, gz1, s1 = call(
        paired(k_back_conv_two, {3: ONE, 4: ONE}, {5: ("mid", 1), 11: ("base", 0), 12: ("mid", 0)}, 0), "g1", (3,),
        [SCALARS, full_table, full_mid, full_mid, full_row, full_row, full_row, full_row, full_mask] + conv_weights(2, turned)
        + [plane_pair],
        [spec((3, ROWS, C_MID), lambda s: (turned(s), 0, 0)), plane_pair, full_row],
        [vmem_of((9, ROWS, C_MID), BFLOAT), vmem_of((4, ROWS, C_MID)), shape_of((4, C_MID))],
        [pltpu.VMEM((PAD + ROWS + PAD, C_MID), SINGLE)] * 2 + [pltpu.VMEM((2, ROWS, C_MID), SINGLE)],
        (core_row, base, gz2, a2, *total2.parts, *sum2.parts, mask, a_kept, a_kept, a_kept, a1), vmem=12,
    )
    gz1 = in_vmem(gz1)
    h1_planes = h1_t.reshape(4, C_MID, ROWS)

    def grad_two(row):
        def filler(token):
            first = 2 * (1 - (row & 1))
            held["a"] = weight_grad(
                "dw2", h1_planes, spec((1, C_MID, ROWS), lambda t, slot: (first + (1 - (t & 1)), 0, 0)), in_vmem(col2),
                spec((1, ROWS, C_MID), lambda t, slot: (3 * row + t, 0, 0)), 3, narrow_shape, TILE, 2 + 3 * row, held["a"], token, vmem_of,
            )
            return held["a"]

        return filler

    def wide_back(token):
        return call(
            k_wide_back, "dxs", (2,),
            [full((ROWS, C_OUT)), spec((TILE, C_OUT), lambda k: (1 + k, 0)), ANYWHERE],
            spec((ROWS, TILE), lambda k: (0, k)),
            hbm_of((ROWS, C_IN)), [],
            (in_hbm(gas), in_hbm(wide), token), vmem=8,
        )

    def first_w(token):
        if not fast:
            return token
        came = pin(held["came"], token)
        return halved(split, came, False)

    held["a"] = bufs_a
    sum1, results1 = dp_sum(s1, [grad_two(0), grad_two(1), both_of(fourth_exchange_b, grad_two(2)), first_w], 4)
    held["b"], bufs_a = results1[2]
    state_w = results1[3]
    state_b = held["b"]
    plane = spec((1, ROWS, C_MID), lambda k: (k, 0, 0))
    ga1 = call(
        paired(k_first_grad, {4: ONE}, {3: ("base", 0), 5: ("mid", 0)}, 0), "g0", (4,),
        [SCALARS, full_table, plane, plane, full_row, full_row, full_mask], plane,
        vmem_of((4, ROWS, C_MID), BFLOAT), [], (core_row, base, gz1, a1, *sum1.parts, mask),
    )
    flat_ga1 = in_vmem(ga1.reshape(1, 4 * ROWS, C_MID))
    bufs_a = weight_grad(
        "dw1", x_t.reshape(2, C_MID, 4 * ROWS), spec((1, C_MID, 4 * ROWS), lambda t, slot: (t, 0, 0)), flat_ga1, full((1, 4 * ROWS, C_MID)),
        2, narrow_shape, TILE, 0, bufs_a, None, vmem_of,
    )
    got_a = swap_pipe(bufs_a[1])
    sums = [sum1, sum2, sum3, sum4, sum5, sum6]

    def image_grads(token, dxs):
        pair = call(
            k_image_grad, "gx", (SLOTS,),
            [spec((4, PIX, C_MID), lambda s, slot: (0, s, 0)), spec((PIX, 1), lambda s, slot: (s, 0)), full((C_IN, C_MID)),
             spec((PIX, C_IN), lambda s, slot: (s, 0)), full((4 * PIX, 4 * PIX)), ANYWHERE],
            spec((2, 1, 4 * PIX, C_IN // 2), lambda s, slot: (0, s, 0, 0)),
            shape_of((2, SLOTS, 4 * PIX, C_IN // 2), BFLOAT), [],
            (core_row, in_vmem(ga1), mask, a_kept, in_hbm(dxs), in_hbm(perm), token), prefetch=1, vmem=9,
        )
        return pair, swap_pipe(pair[1])

    if fast:
        state_w = halved(state_w, (exchange(state_w[1], 2), exchange(state_w[3], 1)), True)
        got_a, state_w, came_b = lax.optimization_barrier((got_a, state_w, held["came_b"]))
        came_w = exchange(state_w[1], 4)
        state_a = split_group("split_a", in_vmem(bufs_a[0]), got_a, part_n, by_rows)
        came_a = exchange(state_a[1], 1), exchange(state_a[3], 2)
        dxs = wide_back(state_a[0])
        state_w = halved_both(state_w, came_w)
        pair, got_pair = image_grads(state_w[0], dxs)
        came_a, state_w, pair = lax.optimization_barrier((came_a, state_w, pair))
        came_w = exchange(state_w[1], 8)
        state_a = halved(state_a, came_a, False)
        came_a = exchange(state_a[1], 2), exchange(state_a[3], 1)
        half_w0, half_w1 = added(state_w, came_w)
        half_b = jnp.concatenate(added(state_b, came_b), axis=0)
        came_a, half_w0, half_w1, half_b = lax.optimization_barrier((came_a, half_w0, half_w1, half_b))
        state_a = halved(state_a, came_a, True)
        came_a = exchange(state_a[1], 4)
        grad_local = place("place_grad", pair, got_pair, state_a[0])
        came_a, grad_local = lax.optimization_barrier((came_a, grad_local))
        state_a = halved_both(state_a, came_a)
        came_a = exchange(state_a[1], 8)
        sums = pin(tuple(t.parts for t in sums), state_a[0])
        sums = [Total(*parts) for parts in sums]
        half_a = jnp.concatenate(added(state_a, came_a), axis=0)
    else:
        half_a = jnp.concatenate(scatter_plain(bufs_a[0], got_a, rows_n, True), axis=0)
        half_w0, half_w1 = scatter_plain(bufs_w[0], got_w, w_wide.shape[0], False)
        half_b = jnp.concatenate(scatter_plain(bufs_b[0], held["got_b"], rows_n, True), axis=0)
        pair, got_pair = image_grads(ga1, wide_back(ga1))
        grad_local = place("place_grad", pair, got_pair, ga1)
    grad_local = grad_local.reshape(IMG_DEV, 2 * HB, 2 * WB, C_IN // 2)

    def join_halves(first, second):
        mine = jnp.where(core == 0, first, second)
        got = swap_pipe(jnp.where(core == 0, second, first))
        return jnp.where(core == 0, jnp.concatenate([mine, got], axis=1), jnp.concatenate([got, mine], axis=1))

    grad_narrow = join_halves(half_a, half_b)
    grad_wide = join_halves(half_w0, half_w1)

    sum1, sum2, sum3, sum4, sum5, sum6 = (t.sum for t in sums)

    def pair_sum(rows):
        return rows[0] + rows[1]

    mid_rows = jnp.stack([pair_sum(v) for t in (sum1, sum2, sum4, sum5) for v in (t[2:4], t[0:2])])
    wide_rows = jnp.stack([pair_sum(v) for v in (sum3[2:4], sum3[0:2], sum3[4:6], sum3[0:2], sum6[2:4], sum6[0:2])])
    mid_rows = mid_rows + swap_pipe(mid_rows)
    wide_rows = wide_rows + swap_pipe(wide_rows)
    grad_mid = lax.dynamic_slice(mid_rows, (0, shard * mid_cols), (8, mid_cols))
    grad_table = lax.dynamic_slice(wide_rows, (0, shard * wide_cols), (6, wide_cols))

    starts = (shard * jnp.array([rows_n, w_wide.shape[0]])).astype(jnp.int32)
    weights, grads = (w_narrow, w_wide, bn_mid, bn_wide), (grad_narrow, grad_wide, grad_mid, grad_table)
    whole_specs = [full(v.shape) for v in weights]
    squares = call(
        k_squares, "squares", (1,), whole_specs * 2, full((8, 128)), shape_of((8, 128)), [], (starts, *weights, *grads), prefetch=1, vmem=10,
    )
    squares, _unused = dp_sum(squares + swap_pipe(squares))
    parts = 4 if rows_n % 64 == 0 and w_wide.shape[0] % 64 == 0 else 1
    specs = [spec((v.shape[0] // parts, v.shape[1]), lambda k, *_: (k, 0)) for v in weights[:2]] + whole_specs[2:]
    updated = call(
        paired(k_update, {1: ONE}), "update", (parts,), [full((8, 128))] * 2 + specs * 3, specs * 2, [shape_of(v.shape) for v in weights] * 2, [],
        (starts, *squares.parts, *weights, *grads, mom_narrow, mom_wide, mom_bn_mid, mom_bn_wide), prefetch=1, vmem=12,
    )
    new_mom_narrow, new_mom_wide, new_mom_mid, new_mom_table, new_narrow, new_wide, new_mid, new_table = updated
    return (
        block_local, grad_local, grad_narrow, grad_wide, grad_mid, grad_table,
        new_mom_narrow, new_mom_wide, new_mom_mid, new_mom_table,
        new_narrow, new_wide, new_mid, new_table,
    )


def solution(mesh):
    rows = P(("pipe", "dp"), None)
    columns = P(None, ("pipe", "dp"))
    feature = P("dp", None, None, None)
    return jax.shard_map(
        on_device,
        mesh=mesh,
        in_specs=(feature, feature, P("dp"), P("dp"), P("dp", None), rows, rows, columns, columns, rows, rows, columns, columns),
        out_specs=(P("dp", None, None, "pipe"), P("dp", None, None, "pipe"), rows, rows, columns, columns, rows, rows, columns, columns, rows, rows, columns, columns),
        check_vma=False,
    )
```

```python
import functools

import jax
import jax.numpy as jnp
import numpy as np
from jax import lax
from jax.experimental import pallas as pl
from jax.experimental.pallas import tpu as pltpu
from jax.sharding import PartitionSpec as P

C_IN = 1024
C_MID = 512
C_OUT = 2048
R_N = 12288
R_W = 2048
HB = 8
WB = 12
IMG_DEV = 8
SLOTS = 4
PIX = HB * WB
ROWS = SLOTS * PIX
HALF = ROWS // 2
PAD = 16
TILE = 512

EPS = 1e-05
MOMENTUM = 0.9
DECAY = 5e-05
TRUST = 0.001
RATE = 29.0
NARROW_BOUNDS = (C_IN, C_IN + 9 * C_MID, C_IN + 9 * C_MID + C_OUT)
WIDE_BOUNDS = (C_MID, C_MID + C_IN)
BFLOAT = jnp.bfloat16
SINGLE = jnp.float32
MIB = 1024 * 1024
BYTES_PER_US = 600000
MICROSECONDS = {
    "prep": 5, "a1": 3, "a2": 5, "as": 4.5, "a3": 4, "a4": 4.7, "a5": 4, "a6": 3.7, "head": 5.3, "g5": 5.2, "g4": 5.4, "gy": 7,
    "g2": 7.3, "g1": 8, "g0": 3, "gx": 6.4, "dxs": 5, "dw1": 3.4, "dw2": 2.1, "dw3": 2.9, "dws": 2.9, "dw4a": 1.7, "dw4b": 1.9,
    "dw5": 1.5, "dw6": 2.8, "place_out": 3.4, "place_grad": 5, "wa": 3, "wb": 3, "turn": 1.7, "keep": 1.7, "halve": 1, "squares": 2, "update": 3,
}


def pairs(bit):
    return [(i, i ^ bit) for i in range(lax.axis_size("dp"))]


def exchange(value, bit):
    return lax.ppermute(value, "dp", pairs(bit))


def pin(value, after):
    return lax.optimization_barrier((value, after))[0]


class Total:
    def __init__(self, *parts):
        self.parts = parts

    @property
    def sum(self):
        return self.parts[0] + self.parts[1]


def dp_sum(value, fillers=(), first=None):
    size = lax.axis_size("dp")
    bits = [1 << k for k in range(size.bit_length() - 1)]
    if first in bits:
        at = bits.index(first)
        bits = bits[at:] + bits[:at]
    results = []
    for bit in bits:
        got = exchange(value, bit)
        if len(results) < len(fillers):
            result = fillers[len(results)](value)
            got, result = lax.optimization_barrier((got, result))
            results.append(result)
        if bit == bits[-1]:
            break
        value = value + got
    for filler in fillers[len(results) :]:
        results.append(filler(got))
    return Total(value, got), results


def swap_pipe(value):
    return lax.ppermute(value, "pipe", [(0, 1), (1, 0)])


def dot(left, right):
    return jnp.dot(left, right, preferred_element_type=SINGLE)


def dot_back(left, right):
    return lax.dot_general(left, right, (((1,), (1,)), ((), ())), preferred_element_type=SINGLE)


def silu(value):
    return value * jax.nn.sigmoid(value)


def slope(value):
    gate = jax.nn.sigmoid(value)
    return gate * (1.0 + value * (1.0 - gate))


def put_sums(ref, values, first):
    for k, value in enumerate(values):
        for m in range(2):
            total = jnp.sum(value[m * HALF : (m + 1) * HALF], axis=0, keepdims=True)
            row = 2 * k + m
            ref[row : row + 1, :] = total if first else ref[row : row + 1, :] + total


def both(function):
    return jnp.concatenate([function(0), function(1)], axis=0)


def part(m):
    return slice(m * HALF, (m + 1) * HALF)


def moments(total_ref, inv_ref, m, scale=1.0):
    inv = inv_ref[m] * scale
    mean = total_ref[m : m + 1, :] * inv
    var = total_ref[2 + m : 3 + m, :] * inv - mean * mean
    return mean, lax.rsqrt(var + EPS)


def normed(a, total_ref, inv_ref, m, scale=1.0):
    mean, rstd = moments(total_ref, inv_ref, m, scale)
    return (a - mean) * rstd, rstd


def conv_grad(gz, xhat, rstd, gain, mask, sum_ref, inv_ref, m, scale=1.0, second=2):
    inv = inv_ref[m] * scale
    first_row = sum_ref[m : m + 1, :] * inv
    second_row = sum_ref[second + m : second + m + 1, :] * inv
    return (mask * ((rstd * gain) * (gz - first_row - xhat * second_row))).astype(BFLOAT)


class Both:
    def __init__(self, refs, start=0):
        self.refs, self.start = refs, start

    def __getitem__(self, index):
        rows, columns = index
        rows = slice(rows.start + self.start, rows.stop + self.start)
        return sum(ref[rows, columns] for ref in self.refs)


class Chunk:
    def __init__(self, refs, which, step):
        self.refs, self.first = refs, WIDE_ROW + 8 * which + step

    def __getitem__(self, index):
        rows, columns = index
        return sum(ref[pl.ds(self.first + 4 * rows.start, 1), columns] for ref in self.refs)


class Inverse:
    def __init__(self, refs, core):
        self.refs, self.core = refs, core

    def __getitem__(self, m):
        row = sum(ref[COUNT_ROW : COUNT_ROW + 1, 0:128] for ref in self.refs)
        lane = lax.broadcasted_iota(jnp.int32, (1, 128), 1)
        return 1.0 / jnp.sum(jnp.where(lane == 2 * self.core + m, row, 0.0), axis=1, keepdims=True)


ONE = (0,)
MID_ROW, WIDE_ROW, COUNT_ROW, TABLE_ROWS = 4, 12, 36, 40


def paired(kernel, views, tabs=None, inv=None, tables=1, lead=0):
    def run(*refs):
        fixed, refs = {}, list(refs)
        if inv is not None:
            core = refs.pop(0)[0]
            table, refs[lead : lead + tables] = refs[lead : lead + tables], []
            step = pl.program_id(0)
            fixed[inv] = Inverse(table, core)
            for at, (kind, which) in (tabs or {}).items():
                if kind == "wide":
                    fixed[at] = Chunk(table, which, step)
                else:
                    fixed[at] = Both(table, MID_ROW + 2 * which if kind == "mid" else 0)
        given, at = [], 0
        while at < len(refs) or len(given) in fixed:
            if len(given) in fixed:
                given.append(fixed[len(given)])
            elif len(given) in views:
                given.extend([Both(refs[at : at + 2], start) for start in views[len(given)]])
                at += 2
            else:
                given.append(refs[at])
                at += 1
        return kernel(*given)

    return run


def k_prep(core_ref, assign_ref, height_ref, width_ref, img_ref, perm_ref, out_ref, mask_ref, count_ref):
    slot = pl.program_id(0)
    image = assign_ref[0, core_ref[0] * SLOTS + slot]
    pixel = lax.broadcasted_iota(jnp.int32, (PIX, 1), 0)
    inside = ((pixel & (HB - 1)) < height_ref[image]) & (pixel < width_ref[image] * HB)
    mask = jnp.where(inside, 1.0, 0.0).astype(SINGLE)
    mask_ref[...] = mask
    planes = dot(perm_ref[...], img_ref[0])
    for k in range(4):
        out_ref[k] = (planes[k * PIX : (k + 1) * PIX] * mask).astype(BFLOAT)
    column = lax.broadcasted_iota(jnp.int32, count_ref.shape, 1)
    counts = jnp.zeros(count_ref.shape, jnp.int32)
    for m in range(4):
        pair = (assign_ref[0, 2 * m], assign_ref[0, 2 * m + 1])
        total = sum(height_ref[k] * width_ref[k] for k in pair)
        counts = jnp.where(column == m, total, counts)
    count_ref[...] = counts.astype(SINGLE)


def k_first(x_ref, w_ref, a_ref, sum_ref):
    a = dot(x_ref[0], w_ref[...])
    a_ref[0] = a

    @pl.when(pl.program_id(0) == 0)
    def _():
        sum_ref[...] = jnp.zeros_like(sum_ref)

    put_sums(sum_ref, [a, a * a], False)


def shift_mask(di, dj):
    if not di and not dj:
        return None
    pixel = lax.broadcasted_iota(jnp.int32, (SLOTS, PIX, 1), 1)
    inside = None
    if di:
        row = pixel & (HB - 1)
        inside = row >= -di if di < 0 else row < HB - di
    if dj:
        column = pixel >= -dj * HB if dj < 0 else pixel < PIX - dj * HB
        inside = column if inside is None else inside & column
    return jnp.where(inside, 1.0, 0.0).astype(SINGLE).reshape(ROWS, 1)


def rows_at(pad, di, dj):
    start = PAD + HB * dj + di
    rows = pad[start : start + ROWS, :]
    mask = shift_mask(di, dj)
    return rows if mask is None else rows * mask


def clear_pad(pad):
    pad[0:PAD, :] = jnp.zeros((PAD, pad.shape[1]), SINGLE)
    pad[PAD + ROWS : PAD + ROWS + PAD, :] = jnp.zeros((PAD, pad.shape[1]), SINGLE)


def body(pad, m):
    return pad.at[PAD + m * HALF : PAD + (m + 1) * HALF, :]


def carried(ref, fresh):
    return jnp.where(fresh, 0.0, ref[...])


def k_conv_two(inv_ref, total_ref, tab_ref, mask_ref, a_ref, w0, w1, w2, out_ref, h_ref, sum_ref, pad, moved):
    step = pl.program_id(0)
    gain, bias = tab_ref[0:1, :], tab_ref[1:2, :]

    @pl.when(step < 2)
    def _():
        for k in range(2):
            clear_pad(pad.at[k])
            clear_pad(moved.at[k])
            for m in range(2):
                xhat, _unused = normed(a_ref[k, part(m), :], total_ref, inv_ref, m, 0.25)
                h = (silu(xhat * gain + bias) * mask_ref[part(m), :]).astype(BFLOAT)
                h_ref[k, part(m), :] = h
                body(pad.at[k], m)[...] = h.astype(SINGLE)
                body(moved.at[k], m)[...] = h.astype(SINGLE)

    @pl.when(step == 2)
    def _():
        for k in range(2):
            moved[k, PAD : PAD + ROWS, :] = rows_at(pad.at[k], -1, 0)

    term = dot(rows_at(moved.at[0], 0, 0).astype(BFLOAT), w1[...])
    term += dot(rows_at(moved.at[1], 0, -1).astype(BFLOAT), w0[...])
    term += dot(rows_at(moved.at[1], 0, 0).astype(BFLOAT), w2[...])
    out_ref[...] = carried(out_ref, step == 0) + term

    @pl.when(step == 2)
    def _():
        a = out_ref[...]
        masked = a * mask_ref[...]
        put_sums(sum_ref, [masked, masked * a], True)


def k_conv_one(inv_ref, total_ref, tab_ref, mask_ref, a_ref, w0, w1, w2, out_ref, h_ref, sum_ref, pad, moved):
    step = pl.program_id(0)
    gain, bias = tab_ref[0:1, :], tab_ref[1:2, :]

    @pl.when(step == 0)
    def _():
        clear_pad(pad)
        clear_pad(moved)
        for m in range(2):
            xhat, _unused = normed(a_ref[part(m), :], total_ref, inv_ref, m)
            h = (silu(xhat * gain + bias) * mask_ref[part(m), :]).astype(BFLOAT)
            h_ref[part(m), :] = h
            body(pad, m)[...] = h.astype(SINGLE)

    for s in range(3):

        @pl.when(step == s)
        def _(s=s):
            moved[PAD : PAD + ROWS, :] = rows_at(pad, s - 1, 0)

    term = dot(rows_at(moved, 0, -1).astype(BFLOAT), w0[...])
    term += dot(rows_at(moved, 0, 0).astype(BFLOAT), w1[...])
    term += dot(rows_at(moved, 0, 1).astype(BFLOAT), w2[...])
    out_ref[...] = carried(out_ref, step == 0) + term

    @pl.when(step == 2)
    def _():
        a = out_ref[...]
        masked = a * mask_ref[...]
        put_sums(sum_ref, [masked, masked * a], True)


def k_expand(inv_ref, total_ref, tab_ref, mask_ref, a_ref, w_ref, h_ref, out_ref, sum_ref):
    @pl.when(pl.program_id(0) == 0)
    def _():
        gain, bias = tab_ref[0:1, :], tab_ref[1:2, :]
        for m in range(2):
            xhat, _unused = normed(a_ref[part(m), :], total_ref, inv_ref, m)
            h_ref[part(m), :] = (silu(xhat * gain + bias) * mask_ref[part(m), :]).astype(BFLOAT)

    a = dot(h_ref[...], w_ref[...])
    out_ref[...] = a
    put_sums(sum_ref, [a, a * a], True)


def k_short(x_ref, w0, w1, out_ref, sum_ref):
    a = dot(x_ref[0, :, :TILE], w0[...]) + dot(x_ref[0, :, TILE:], w1[...])
    out_ref[...] = a
    put_sums(sum_ref, [a, a * a], True)


def k_meet(inv_ref, t3_ref, ts_ref, tab3_ref, tabs_ref, mask_ref, a3_ref, as_ref, wa_ref, wb_ref, y_ref, out_ref, sum_ref):
    step = pl.program_id(0)
    for m in range(2):
        x3, _unused = normed(a3_ref[part(m), :], t3_ref, inv_ref, m)
        xs, _unused = normed(as_ref[part(m), :], ts_ref, inv_ref, m)
        joined = (x3 * tab3_ref[0:1, :] + tab3_ref[1:2, :]) + (xs * tabs_ref[0:1, :] + tabs_ref[1:2, :])
        y_ref[part(m), :] = (silu(joined) * mask_ref[part(m), :]).astype(BFLOAT)

    @pl.when(step == 0)
    def _():
        out_ref[...] = dot(y_ref[...], wa_ref[...])

    @pl.when(step > 0)
    def _():
        out_ref[...] += dot(y_ref[...], wb_ref[...])

    @pl.when(step == pl.num_programs(0) - 1)
    def _():
        a = out_ref[...]
        put_sums(sum_ref, [a, a * a], True)


def k_head(order_ref, inv_ref, total_ref, tab_ref, mask_ref, a_ref, y_ref, c0, c1, c2, c3, blk_ref, gz_ref, sum_ref):
    cots = (c0, c1, c2, c3)
    gain, bias = tab_ref[0:1, :], tab_ref[1:2, :]
    for m in range(2):
        mask = mask_ref[part(m), :]
        xhat, _unused = normed(a_ref[part(m), :], total_ref, inv_ref, m)
        z = (xhat * gain + bias) + y_ref[part(m), :].astype(SINGLE)
        gate = jax.nn.sigmoid(z)
        blk_ref[0, part(m), :] = (z * gate * mask).astype(BFLOAT)
        cot = jnp.concatenate([cots[2 * m][0], cots[2 * m + 1][0]], axis=0).astype(SINGLE)
        gz = cot * mask * (gate * (1.0 + z * (1.0 - gate)))
        gz_ref[part(m), :] = gz
        sum_ref[m : m + 1, :] = jnp.sum(gz, axis=0, keepdims=True)
        sum_ref[2 + m : 3 + m, :] = jnp.sum(gz * xhat, axis=0, keepdims=True)


def finish_back(gz_ref, sum_ref, grad, a_ref, total_ref, tab_ref, inv_ref, mask_ref):
    gain, bias = tab_ref[0:1, :], tab_ref[1:2, :]
    for m in range(2):
        xhat, _unused = normed(a_ref[part(m), :], total_ref, inv_ref, m)
        gz = grad[part(m)] * mask_ref[part(m), :] * slope(xhat * gain + bias)
        gz_ref[part(m), :] = gz
        sum_ref[m : m + 1, :] = jnp.sum(gz, axis=0, keepdims=True)
        sum_ref[2 + m : 3 + m, :] = jnp.sum(gz * xhat, axis=0, keepdims=True)


def k_back_six(inv_ref, gz_ref, a_ref, total_ref, s_ref, tab_ref, mask_ref, w_ref, low_ref, low_total, low_tab, ga_ref, out_ref, sum_ref, acc):
    step = pl.program_id(0)
    for m in range(2):
        xhat, rstd = normed(a_ref[part(m), :], total_ref, inv_ref, m)
        ga_ref[part(m), :] = conv_grad(
            gz_ref[part(m), :], xhat, rstd, tab_ref[0:1, :], mask_ref[part(m), :], s_ref, inv_ref, m
        )
    term = dot_back(ga_ref[...], w_ref[...])

    @pl.when(step == 0)
    def _():
        acc[...] = term

    @pl.when(step > 0)
    def _():
        acc[...] += term

    @pl.when(step == pl.num_programs(0) - 1)
    def _():
        finish_back(out_ref, sum_ref, acc[...], low_ref, low_total, low_tab, inv_ref, mask_ref)


def k_back_conv_one(inv_ref, gz_ref, a_ref, total_ref, s_ref, tab_ref, mask_ref, w0, w1, w2, low_ref, low_total, low_tab, col_ref, out_ref, sum_ref, pad, moved, acc):
    step = pl.program_id(0)

    @pl.when(step == 0)
    def _():
        clear_pad(pad)
        clear_pad(moved)
        for m in range(2):
            xhat, rstd = normed(a_ref[part(m), :], total_ref, inv_ref, m)
            ga = conv_grad(gz_ref[part(m), :], xhat, rstd, tab_ref[0:1, :], mask_ref[part(m), :], s_ref, inv_ref, m)
            body(pad, m)[...] = ga.astype(SINGLE)

    for s in range(3):

        @pl.when(step == s)
        def _(s=s):
            moved[PAD : PAD + ROWS, :] = rows_at(pad, 1 - s, 0)

    term = None
    for kx, weight in enumerate((w0, w1, w2)):
        tap = rows_at(moved, 0, 1 - kx).astype(BFLOAT)
        col_ref[kx] = tap
        product = dot_back(tap, weight[...])
        term = product if term is None else term + product
    acc[...] = carried(acc, step == 0) + term

    @pl.when(step == 2)
    def _():
        finish_back(out_ref, sum_ref, acc[...], low_ref, low_total, low_tab, inv_ref, mask_ref)


def k_back_four(inv_ref, gz_ref, a_ref, total_ref, s_ref, tab_ref, mask_ref, wa_ref, wb_ref, up_ref, a3_ref, as_ref, t3_ref, ts_ref, tab3_ref, tabs_ref, ga_ref, gj_ref, sum_ref):
    @pl.when(pl.program_id(0) == 0)
    def _():
        for m in range(2):
            xhat, rstd = normed(a_ref[part(m), :], total_ref, inv_ref, m)
            ga_ref[part(m), :] = conv_grad(
                gz_ref[part(m), :], xhat, rstd, tab_ref[0:1, :], mask_ref[part(m), :], s_ref, inv_ref, m
            )

    weight = jnp.where(pl.program_id(0) == 0, wa_ref[...], wb_ref[...])
    grad = dot_back(ga_ref[...], weight) + up_ref[...]
    for m in range(2):
        x3, _unused = normed(a3_ref[part(m), :], t3_ref, inv_ref, m)
        xs, _unused = normed(as_ref[part(m), :], ts_ref, inv_ref, m)
        joined = (x3 * tab3_ref[0:1, :] + tab3_ref[1:2, :]) + (xs * tabs_ref[0:1, :] + tabs_ref[1:2, :])
        gj = grad[part(m)].astype(BFLOAT).astype(SINGLE) * mask_ref[part(m), :] * slope(joined)
        gj_ref[part(m), :] = gj
        for k, value in enumerate((gj, gj * x3, gj * xs)):
            row = 2 * k + m
            sum_ref[row : row + 1, :] = jnp.sum(value, axis=0, keepdims=True)


def k_back_three(inv_ref, gj_ref, a3_ref, as_ref, t3_ref, ts_ref, s_ref, tab3_ref, tabs_ref, mask_ref, w_ref, low_ref, low_total, low_tab, g3_ref, gs_ref, out_ref, sum_ref, acc):
    step = pl.program_id(0)
    for m in range(2):
        mask = mask_ref[part(m), :]
        gj = gj_ref[part(m), :]
        x3, r3 = normed(a3_ref[part(m), :], t3_ref, inv_ref, m)
        g3_ref[part(m), :] = conv_grad(gj, x3, r3, tab3_ref[0:1, :], mask, s_ref, inv_ref, m)
        xs, rs = normed(as_ref[part(m), :], ts_ref, inv_ref, m)
        gs_ref[part(m), :] = conv_grad(gj, xs, rs, tabs_ref[0:1, :], mask, s_ref, inv_ref, m, second=4)
    term = dot_back(g3_ref[...], w_ref[...])

    @pl.when(step == 0)
    def _():
        acc[...] = term

    @pl.when(step > 0)
    def _():
        acc[...] += term

    @pl.when(step == pl.num_programs(0) - 1)
    def _():
        finish_back(out_ref, sum_ref, acc[...], low_ref, low_total, low_tab, inv_ref, mask_ref)


def k_back_conv_two(inv_ref, gz_ref, a_ref, total_ref, s_ref, tab_ref, mask_ref, w0, w1, w2, low_ref, low_total, low_tab, col_ref, out_ref, sum_ref, pad, moved, acc):
    step = pl.program_id(0)
    gain, bias = low_tab[0:1, :], low_tab[1:2, :]

    @pl.when(step == 0)
    def _():
        clear_pad(pad)
        clear_pad(moved)
        for m in range(2):
            xhat, rstd = normed(a_ref[part(m), :], total_ref, inv_ref, m)
            ga = conv_grad(gz_ref[part(m), :], xhat, rstd, tab_ref[0:1, :], mask_ref[part(m), :], s_ref, inv_ref, m)
            body(pad, m)[...] = ga.astype(SINGLE)
            body(moved, m)[...] = ga.astype(SINGLE)
        sum_ref[...] = jnp.zeros_like(sum_ref)

    @pl.when(step == 2)
    def _():
        moved[PAD : PAD + ROWS, :] = rows_at(pad, 1, 0)

    plain = rows_at(moved, 0, 0).astype(BFLOAT)
    aside = rows_at(moved, 0, 1).astype(BFLOAT)
    col_ref[0], col_ref[1], col_ref[2] = aside, plain, plain
    acc[0] = carried(acc.at[0], step < 2) + dot_back(plain, w1[...])
    acc[1] = carried(acc.at[1], step < 2) + (dot_back(aside, w0[...]) + dot_back(plain, w2[...]))

    @pl.when(step != 1)
    def _():
        for k in range(2):
            for m in range(2):
                xhat, _unused = normed(low_ref[k, part(m), :], low_total, inv_ref, m, 0.25)
                gz = acc[k, part(m), :] * mask_ref[part(m), :] * slope(xhat * gain + bias)
                out_ref[k, part(m), :] = gz
                for q, value in enumerate((gz, gz * xhat)):
                    row = 2 * q + m
                    sum_ref[row : row + 1, :] += jnp.sum(value, axis=0, keepdims=True)


def k_wide_back(g_ref, w_ref, *refs):
    refs[-1][...] = dot_back(g_ref[...], w_ref[...])


def k_first_grad(inv_ref, gz_ref, a_ref, total_ref, s_ref, tab_ref, mask_ref, ga_ref):
    for m in range(2):
        xhat, rstd = normed(a_ref[0, part(m), :], total_ref, inv_ref, m, 0.25)
        ga_ref[0, part(m), :] = conv_grad(
            gz_ref[0, part(m), :], xhat, rstd, tab_ref[0:1, :], mask_ref[part(m), :], s_ref, inv_ref, m, 0.25
        )


def k_image_grad(core_ref, ga_ref, mask_ref, w_ref, short_ref, perm_ref, *refs):
    out_ref = refs[-1]
    grads = dot_back(ga_ref[...].reshape(4 * PIX, C_MID), w_ref[...])
    mask = mask_ref[...]
    parts = []
    for k in range(4):
        grad = grads[k * PIX : (k + 1) * PIX]
        if k == 0:
            grad = grad + short_ref[...]
        parts.append((grad * mask).astype(BFLOAT))
    planes = jnp.concatenate(parts, axis=0)
    image = lax.dot_general(perm_ref[...], planes, (((0,), (0,)), ((), ())), preferred_element_type=SINGLE).astype(BFLOAT)
    core = core_ref[0]
    out_ref[core, 0] = image[:, : C_IN // 2]
    out_ref[1 - core, 0] = image[:, C_IN // 2 :]


def k_place(core_ref, order_ref, own_ref, got_ref, *refs):
    out_ref = refs[-1]
    step = pl.program_id(0)

    @pl.when(step < SLOTS)
    def _():
        out_ref[0] = own_ref[0, 0]

    @pl.when(step >= SLOTS)
    def _():
        out_ref[0] = got_ref[0]


def k_turn(in_ref, *refs):
    refs[-1][...] = in_ref[...].reshape(in_ref.shape[-2:]).T


def k_grad(core_ref, feature_ref, grad_ref, *refs):
    keep_ref, send_ref = refs[-2:]
    core = core_ref[0]
    rows, half = feature_ref.shape[-2], grad_ref.shape[-1] // 2
    for k in range(grad_ref.shape[0]):
        feature = feature_ref[k % feature_ref.shape[0]]
        for ref, side in ((keep_ref, core), (send_ref, 1 - core)):
            columns = pl.ds(pl.multiple_of(side * half, half), half)
            ref[k * rows : (k + 1) * rows] = dot(feature, grad_ref[k, :, columns]).astype(BFLOAT)


def k_keep(in_ref, *refs):
    out_ref, sem = refs[-2:]
    copy = pltpu.make_async_copy(in_ref, out_ref, sem)
    copy.start()
    copy.wait()


def k_join(n_in, n_out, *refs):
    stayed, came = refs[:n_in], refs[n_in : 2 * n_in]
    outs, sems = refs[-1 - n_out : -1], refs[-1]
    copies = []
    for which in range(2):
        target = outs[0].at[which] if n_out == 1 else outs[which]
        for side, sources in enumerate((stayed, came)):
            source = sources[0].at[which] if n_in == 1 else sources[which]
            size = source.shape[0]
            copies.append(pltpu.make_async_copy(source, target.at[pl.ds(side * size, size)], sems.at[len(copies)]))
    for copy in copies:
        copy.start()
    for copy in copies:
        copy.wait()


def k_halve(*refs):
    for which in range(2):
        keep0, keep1, came0, came1 = refs[4 * which : 4 * which + 4]
        stay = (keep0[0].astype(SINGLE) + came0[0].astype(SINGLE)).astype(BFLOAT)
        sent = (keep1[0].astype(SINGLE) + came1[0].astype(SINGLE)).astype(BFLOAT)
        if len(refs) == 10:
            refs[8][which, 0], refs[9][which, 0] = stay, sent
        else:
            refs[8 + 2 * which][0], refs[9 + 2 * which][0] = stay, sent


def k_halve_both(keep_ref, came_ref, stay_ref, sent_ref):
    total = (keep_ref[...].astype(SINGLE) + came_ref[...].astype(SINGLE)).astype(BFLOAT)
    half = total.shape[1] // 2
    stay_ref[...], sent_ref[...] = total[:, :half], total[:, half:]


def k_gather(me_ref, *refs):
    ins, out_ref, sems = refs[:8], refs[8], refs[9]
    rows, cols = ins[0].shape[1:]
    copies = []
    for other in range(2):
        column = pl.multiple_of((1 - me_ref[1] if other else me_ref[1]) * cols, cols)
        for which in range(2):
            for came in range(2):
                source = ins[4 * other + 2 * which + came]
                for q in range(8):
                    third, low, high = q >> 2, (q >> 1) & 1, q & 1
                    pair = 2 * third + came if which == 0 else 2 * came + third
                    block = me_ref[0] ^ (8 * high + 4 * low + pair)
                    row = pl.multiple_of((2 * block + which) * rows, rows)
                    target = out_ref.at[pl.ds(row, rows), pl.ds(column, cols)]
                    copies.append(pltpu.make_async_copy(source.at[q], target, sems.at[len(copies)]))
    for copy in copies:
        copy.start()
    for copy in copies:
        copy.wait()


def k_split(me_ref, *refs):
    own, got, outs = refs[:4], refs[4:8], refs[8:]
    for own_ref, got_ref, out_ref in zip(own, got, outs):
        out_ref[0] = (own_ref[...].astype(SINGLE) + got_ref[...].astype(SINGLE)).astype(BFLOAT)


def group_of(rows, start, bounds):
    index = lax.broadcasted_iota(jnp.int32, (rows, 1), 0) + start
    return sum((index >= bound).astype(jnp.int32) for bound in bounds)


def k_squares(start_ref, *refs):
    out_ref = refs[-1]
    lane = lax.broadcasted_iota(jnp.int32, (1, 128), 1)
    out_ref[...] = jnp.zeros_like(out_ref)
    for k in range(2):
        squares = [jnp.sum(ref[...] * ref[...], axis=1, keepdims=True) for ref in refs[4 * k : 4 * k + 4]]
        total = jnp.zeros((1, 128), SINGLE)
        for which, bounds in enumerate((NARROW_BOUNDS, WIDE_BOUNDS)):
            group = group_of(squares[which].shape[0], start_ref[which], bounds)
            for g in range(len(bounds) + 1):
                part_sum = jnp.sum(jnp.where(group == g, squares[which], 0.0))
                total = total + jnp.where(lane == 4 * which + g, part_sum, 0.0)
        for rows, first in ((squares[2], 7), (squares[3], 15)):
            row = lax.broadcasted_iota(jnp.int32, (rows.shape[0], 128), 0)
            column = lax.broadcasted_iota(jnp.int32, (rows.shape[0], 128), 1)
            total = total + jnp.sum(jnp.where(column == row + first, rows, 0.0), axis=0, keepdims=True)
        out_ref[k : k + 1, :] = total


def k_update(start_ref, square_ref, *refs):
    step = pl.program_id(0)
    norms = jnp.sqrt(square_ref[0:8, :])
    weight_norm, grad_norm = norms[0:1], norms[1:2]
    ratio = TRUST * weight_norm / (grad_norm + DECAY * weight_norm)
    lane = lax.broadcasted_iota(jnp.int32, (1, 128), 1)
    for k in range(4):
        weight, grad = refs[k][...], refs[4 + k][...]
        rows = weight.shape[0]
        if k < 2:
            bounds = (NARROW_BOUNDS, WIDE_BOUNDS)[k]
            group = group_of(rows, start_ref[k] + step * rows, bounds)
            scale = jnp.zeros((rows, 1), SINGLE)
            for g in range(len(bounds) + 1):
                scale = jnp.where(group == g, jnp.sum(jnp.where(lane == 4 * k + g, ratio, 0.0)), scale)
        else:
            row = lax.broadcasted_iota(jnp.int32, (rows, 128), 0)
            column = lax.broadcasted_iota(jnp.int32, (rows, 128), 1)
            scale = jnp.sum(jnp.where(column == row + (7, 15)[k - 2], ratio, 0.0), axis=1, keepdims=True)
        moment = MOMENTUM * refs[8 + k][...] + RATE * scale * (grad + DECAY * weight)
        refs[12 + k][...] = moment
        refs[16 + k][...] = weight - moment


def full(shape):
    zeros = (0,) * len(shape)
    return pl.BlockSpec(tuple(shape), lambda *_: zeros, pipeline_mode=pl.Buffered(1))


SCALARS = pl.BlockSpec(memory_space=pltpu.SMEM)
ANYWHERE = pl.BlockSpec(memory_space=pl.ANY)


def spec(shape, index):
    return pl.BlockSpec(tuple(shape), index)


def call(kernel, name, grid, in_specs, out_specs, out_shape, scratch, args, prefetch=0, vmem=8, aliases=None):
    return pl.pallas_call(
        kernel,
        out_shape=out_shape,
        grid_spec=pltpu.PrefetchScalarGridSpec(
            num_scalar_prefetch=prefetch,
            grid=grid,
            in_specs=in_specs,
            out_specs=out_specs,
            scratch_shapes=scratch,
        ),
        input_output_aliases=aliases or {},
        compiler_params=pltpu.CompilerParams(vmem_limit_bytes=vmem * MIB),
        cost_estimate=pl.CostEstimate(flops=0, bytes_accessed=int(MICROSECONDS.get(name, 1) * BYTES_PER_US), transcendentals=0),
        name=name,
    )(*args)


def shape_of(shape, dtype=SINGLE):
    return jax.ShapeDtypeStruct(tuple(shape), dtype)


def vmem_of(shape, dtype=SINGLE):
    return pltpu.VMEM(tuple(shape), dtype)


def hbm_of(shape, dtype=SINGLE):
    return pltpu.HBM(tuple(shape), dtype)


def in_vmem(value):
    return pltpu.with_memory_space_constraint(value, pltpu.VMEM)


def in_hbm(value):
    return pltpu.with_memory_space_constraint(value, pltpu.HBM)


def permutation():
    table = np.zeros((4 * PIX, 4 * PIX), np.float32)
    for pi in range(2):
        for pj in range(2):
            for i in range(HB):
                for j in range(WB):
                    table[((2 * pi + pj) * WB + j) * HB + i, (2 * i + pi) * 2 * WB + 2 * j + pj] = 1.0
    return jnp.asarray(table, BFLOAT)


def rounded(value):
    return lax.reduce_precision(value, 8, 7)


def split_group(name, keep, got, rows, index):
    cols = keep.shape[1]

    def block(which, sent):
        def at(q, me):
            other, low, high = (q >> 2) & 1, (q >> 1) & 1, q & 1
            pair = other * 2 + sent if which == 0 else sent * 2 + other
            return (index(which, me[0] ^ (high * 8 + low * 4 + pair)), 0)

        return spec((rows, cols), at)

    blocks = [block(which, sent) for which in range(2) for sent in range(2)]
    return call(
        k_split, name, (8,), blocks + blocks,
        [spec((1, rows, cols), lambda q, me: (q, 0, 0))] * 4,
        [shape_of((8, rows, cols), BFLOAT)] * 4, [],
        (lax.axis_index("dp")[None].astype(jnp.int32),) + (keep,) * 4 + (got,) * 4, prefetch=1,
    )


def halved(state, came, merge):
    (keep0, _sent, keep1, _sent), (came0, came1) = state, came
    count, block = keep0.shape[0] // 2, keep0.shape[1:]
    low, high = (spec((1,) + block, lambda q, at=at: (q + at, 0, 0)) for at in (0, count))
    if merge:
        outs, out_spec = [vmem_of((2, count) + block, BFLOAT)] * 2, [spec((2, 1) + block, lambda q: (0, q, 0, 0))] * 2
    else:
        outs, out_spec = [vmem_of((count,) + block, BFLOAT)] * 4, [low] * 4
    return tuple(call(
        k_halve, "halve", (count,), [low, high] * 4, out_spec, outs, [], (keep0, keep0, came0, came0, keep1, keep1, came1, came1), vmem=4,
    ))


def halved_both(state, came):
    shape = state[0].shape
    half = (2, shape[1] // 2) + shape[2:]
    return tuple(call(
        k_halve_both, "halve", (1,), [full(shape)] * 2, [full(half)] * 2, [vmem_of(half, BFLOAT)] * 2, [], (state[0], came), vmem=4,
    ))


def added(state, came):
    total = state[0].astype(SINGLE) + came.astype(SINGLE)
    return total[0, 0], total[1, 0]


def scatter_plain(keep, got, block, by_rows):
    total = (keep.astype(SINGLE) + got.astype(SINGLE)).astype(BFLOAT)
    if by_rows:
        own = lax.psum_scatter(total, "dp", scatter_dimension=0, tiled=True).astype(SINGLE)
        return own[: block // 2], own[block // 2 :]
    middle = total.shape[0] // 2
    return tuple(lax.psum_scatter(p, "dp", scatter_dimension=0, tiled=True).astype(SINGLE) for p in (total[:middle], total[middle:]))


def joined(value, got):
    return jnp.concatenate([value, got], axis=0)


def gather_blocks(name, core, parts, others, out_shape):
    scalars = jnp.stack([lax.axis_index("dp"), core]).astype(jnp.int32)
    pieces = [a for pair in list(parts) + list(others) for a in pair]
    return call(
        k_gather, name, (), [ANYWHERE] * 8, ANYWHERE, vmem_of(out_shape, BFLOAT),
        [pltpu.SemaphoreType.DMA((64,))], (scalars, *pieces), prefetch=1, vmem=2,
    )


def swap_all(parts):
    return [tuple(swap_pipe(a) for a in pair) for pair in parts]


def join_parts(stayed, came, token, n_out):
    n_in = len(stayed)
    shape = stayed[0].shape[-3:]
    shape = (2 * shape[0],) + shape[1:]
    outs = [vmem_of(shape, BFLOAT)] * 2 if n_out == 2 else [vmem_of((2,) + shape, BFLOAT)]
    return call(
        functools.partial(k_join, n_in, n_out), "join", (), [ANYWHERE] * (2 * n_in + 1), [ANYWHERE] * n_out, outs,
        [pltpu.SemaphoreType.DMA((4,))], tuple(stayed) + tuple(came) + (token,), vmem=2,
    )


def keep_in_hbm(value):
    def filler(token):
        return call(
            k_keep, "keep", (), [ANYWHERE] * 2, ANYWHERE, hbm_of(value.shape, value.dtype),
            [pltpu.SemaphoreType.DMA], (in_vmem(value), token), vmem=2,
        )

    return filler


def nothing(token):
    return token


def both_of(*fillers):
    return lambda token: tuple(filler(token) for filler in fillers)


def on_device(images, cotangent, heights, widths, assign, w_narrow, w_wide, bn_mid, bn_wide, mom_narrow, mom_wide, mom_bn_mid, mom_bn_wide):
    core = lax.axis_index("pipe")
    shard = lax.axis_index(("pipe", "dp"))
    fast = lax.axis_size("dp") == 16

    own_narrow = w_narrow.astype(BFLOAT)
    own_wide = w_wide.astype(BFLOAT)
    rows_n, half_n = w_narrow.shape[0], C_MID // 2
    part_n = rows_n // 2
    whole_n = (R_N // 2, C_MID)
    if fast:
        sent = swap_pipe(jnp.where(core == 0, own_narrow[:, half_n:], own_narrow[:, :half_n]))
        kept = jnp.where(core == 0, own_narrow[:, :half_n], own_narrow[:, half_n:])
        mine_a, mine_b = jnp.where(core == 0, kept, sent), jnp.where(core == 0, sent, kept)
        a, b = (mine.reshape(2, 1, part_n, half_n) for mine in (mine_a, mine_b))
        (a,) = join_parts((a,), (exchange(a, 8),), a, 1)
        a0, a1 = join_parts((a,), (exchange(a, 4),), a, 2)
        b = pin(b, a1)
        got, got_b = lax.optimization_barrier(((exchange(a0, 2), exchange(a1, 1)), exchange(b, 8)))
        a0, a1 = join_parts((a0, a1), got, got[1], 2)
        (b,) = join_parts((b,), (got_b,), got_b, 1)
        stay_a = swap_all([(a0,), (a1,)])
        own_wide = pin(own_wide, a1)
        wide = lax.all_gather(own_wide, ("pipe", "dp"), axis=0, tiled=True)
    else:
        narrow = lax.all_gather(own_narrow, ("pipe", "dp"), axis=0, tiled=True)
        narrow_a, narrow_b = narrow[: R_N // 2], narrow[R_N // 2 :]
        wide = lax.all_gather(own_wide, ("pipe", "dp"), axis=0, tiled=True)

    perm = permutation()
    core_row = core[None].astype(jnp.int32)
    x, mask, count_rows = call(
        k_prep, "prep", (SLOTS,),
        [spec((1, 4 * PIX, C_IN), lambda s, core, order, *_: (order[0, core[0] * SLOTS + s], 0, 0)), full((4 * PIX, 4 * PIX))],
        [spec((4, PIX, C_IN), lambda s, *_: (0, s, 0)), spec((PIX, 1), lambda s, *_: (s, 0)), full((4, C_MID))],
        [vmem_of((4, ROWS, C_IN), BFLOAT), vmem_of((ROWS, 1)), shape_of((4, C_MID))], [],
        (core_row, assign, heights, widths, in_hbm(images.reshape(IMG_DEV, 4 * PIX, C_IN)), in_hbm(perm)), prefetch=4, vmem=7,
    )
    mask = in_vmem(mask)
    mid_cols, wide_cols = bn_mid.shape[1], bn_wide.shape[1]
    tables = jnp.concatenate(
        [
            lax.dynamic_update_slice(jnp.zeros((8, C_MID), SINGLE), rounded(bn_mid), (0, shard * mid_cols)),
            lax.dynamic_update_slice(jnp.zeros((6, C_OUT), SINGLE), rounded(bn_wide), (0, shard * wide_cols)).reshape(24, C_MID),
        ]
    )
    tables = tables + swap_pipe(tables)
    tables = jnp.concatenate([tables, count_rows])

    held = {}
    if fast:
        last0, last1, got_b, x, tables = lax.optimization_barrier((exchange(a0, 1), exchange(a1, 2), exchange(b, 4), x, tables))
        came_a = swap_all([(last0,), (last1,)])
        part_b = join_parts((b,), (got_b,), got_b, 2)
        narrow_a = gather_blocks("wa", core, [(a0, last0), (a1, last1)], [u + v for u, v in zip(stay_a, came_a)], whole_n)

    def turn(feature, feature_spec, grid, shape, index):
        def filler(token):
            return call(
                k_turn, "turn", grid, [feature_spec, ANYWHERE],
                spec((C_MID, ROWS), index), hbm_of(shape, BFLOAT), [], (feature, token),
            )

        return filler

    def weight_grad(name, feature, feature_spec, grad, grad_spec, tiles, shape, rows, base, bufs, token, space):
        out_spec = spec((rows, shape[1]), lambda t, slot: (base + t, 0))
        hold = in_vmem if space is vmem_of else in_hbm
        extra = tuple(hold(b) for b in bufs or ()) + (() if token is None else (token,))
        return call(
            k_grad, name, (tiles,), [feature_spec, grad_spec] + [ANYWHERE] * len(extra),
            [out_spec] * 2, [space(shape, BFLOAT)] * 2, [], (core_row, feature, grad) + extra,
            prefetch=1, vmem=7, aliases={3: 0, 4: 1} if bufs else {},
        )

    full_row = full((4, C_MID))
    full_table = full((TABLE_ROWS, C_MID))
    full_mask = full((ROWS, 1))
    full_mid = full((ROWS, C_MID))
    plane_pair = spec((2, ROWS, C_MID), lambda s: (jnp.minimum(s, 1), 0, 0))

    def narrow_block(index):
        return spec((TILE, TILE), index)

    chunk = spec((ROWS, TILE), lambda k, *_: (0, k))
    chunk_sum = spec((4, TILE), lambda k, *_: (0, k))
    chunk_eight = spec((8, TILE), lambda k, *_: (0, k))
    four_a = narrow_block(lambda k: (11, 0))
    four_b = narrow_block(lambda k: (jnp.maximum(k - 1, 0), 0))

    a1, part1 = call(
        k_first, "a1", (4,),
        [spec((1, ROWS, C_IN), lambda k: (k, 0, 0)), full((C_IN, C_MID))],
        [spec((1, ROWS, C_MID), lambda k: (k, 0, 0)), full_row],
        [hbm_of((4, ROWS, C_MID)), shape_of((4, C_MID))], [],
        (in_vmem(x), in_vmem(narrow_a)), vmem=6,
    )

    a1 = in_hbm(a1)
    def second_part_b(token):
        if not fast:
            return token
        part = pin(part_b, token)
        held["got"] = exchange(part[0], 2), exchange(part[1], 1)
        return token

    first_sum, (a_kept, (x_kept, first_b), _unused) = dp_sum(jnp.concatenate([part1, tables]), [keep_in_hbm(narrow_a), lambda token: (keep_in_hbm(x)(token), part_b if fast else token), second_part_b])
    x_kept, a_kept = in_hbm(x_kept), in_hbm(a_kept)
    base = in_vmem(first_sum.sum)

    a_s, part_s = call(
        k_short, "as", (4,),
        [spec((1, ROWS, C_IN), lambda k: (0, 0, 0)), spec((TILE, TILE), lambda k: (1, k)), spec((TILE, TILE), lambda k: (2, k))],
        [chunk, chunk_sum],
        [vmem_of((ROWS, C_OUT)), shape_of((4, C_OUT))], [],
        (in_vmem(x), in_hbm(wide), in_hbm(wide)), vmem=6,
    )

    def conv_weights(first, order_of):
        return [narrow_block(lambda s, kx=kx: (first + 3 * order_of(s) + kx, 0)) for kx in range(3)]

    turned = lambda s: lax.rem(s + 1, 3)
    straight = lambda s: s

    a2, h1, part2 = call(
        paired(k_conv_two, {}, {1: ("base", 0), 2: ("mid", 0)}, 0, 2), "a2", (3,),
        [SCALARS, full_table, full_table, full_mask, plane_pair] + conv_weights(2, turned),
        [full_mid, plane_pair, full_row],
        [vmem_of((ROWS, C_MID)), vmem_of((4, ROWS, C_MID), BFLOAT), shape_of((4, C_MID))],
        [pltpu.VMEM((2, PAD + ROWS + PAD, C_MID), SINGLE)] * 2,
        (core_row, *first_sum.parts, mask, a1) + (a_kept,) * 3, vmem=11,
    )
    a2 = in_vmem(a2)

    def third_part_b(token):
        if not fast:
            return token
        held["big_b"] = join_parts(first_b, pin(held["got"], token), token, 2)
        return held["big_b"]

    def fourth_b(token):
        if fast:
            big = pin(held["big_b"], token)
            held["got"] = exchange(big[0], 1), exchange(big[1], 2)
        return token

    turn_h1 = turn(h1, spec((1, ROWS, C_MID), lambda k: (k, 0, 0)), (4,), (4 * C_MID, ROWS), lambda k: (k, 0))
    total2, (h1_t, big_b, _unused) = dp_sum(part2, [turn_h1, third_part_b, fourth_b])

    def expand(name, a, total, which, row):
        return call(
            paired(k_expand, {1: ONE}, {2: ("mid", which)}, 0), name, (4,),
            [SCALARS, full_table, full_row, full_row, full_mask, full_mid, spec((TILE, TILE), lambda k: (row, k))],
            [full_mid, chunk, chunk_sum],
            [vmem_of((ROWS, C_MID), BFLOAT), vmem_of((ROWS, C_OUT)), shape_of((4, C_OUT))], [],
            (core_row, base, *total.parts, mask, a, in_hbm(wide)), vmem=6,
        )

    h2, a3, part3 = expand("a3", a2, total2, 1, 0)
    whole = spec((ROWS, C_MID), lambda k: (0, 0))

    def swap_b(token):
        if not fast:
            return token
        ready = pin(tuple(big_b) + held["got"], token)
        return [(ready[0], ready[2]), (ready[1], ready[3])]

    def gather_b(token):
        if not fast:
            return narrow_b
        others = pin(held["others"], token)
        return gather_blocks("wb", core, held["parts"], others, whole_n)

    def start_swap_b(token):
        if fast:
            held["parts"] = swap_b(token)
            held["others"] = swap_all(held["parts"])
        return token

    total3s, ((h2_t, as_kept), (_unused, a3_kept), _unused, narrow_b) = dp_sum(
        jnp.concatenate([part3, part_s]),
        [
            both_of(turn(h2, whole, (1,), (C_MID, ROWS), lambda k: (0, 0)), keep_in_hbm(a_s)),
            both_of(start_swap_b, keep_in_hbm(a3)),
            nothing,
            gather_b,
        ],
    )
    as_kept, a3_kept = in_hbm(as_kept), in_hbm(a3_kept)

    y, a4, part4 = call(
        paired(k_meet, {1: (0, 4)}, {3: ("wide", 0), 4: ("wide", 1)}, 0), "a4", (4,),
        [SCALARS, full_table, chunk_eight, chunk_eight, full_mask, chunk, chunk, four_a, four_b],
        [chunk, full_mid, full_row],
        [vmem_of((ROWS, C_OUT), BFLOAT), vmem_of((ROWS, C_MID)), shape_of((4, C_MID))], [],
        (core_row, base, *total3s.parts, mask, in_vmem(a3), in_vmem(a_s), a_kept, in_vmem(narrow_b)), vmem=8,
    )
    a4 = in_vmem(a4)
    def turn_x(q, start, into):
        def filler(token):
            extra = () if into is None else (in_hbm(into[-1]),)
            held["x_t"] = call(
                k_turn, "turn", (2,), [spec((1, ROWS, C_MID), lambda k: (start + k, 0, q))] + [ANYWHERE] * (1 + len(extra)),
                spec((C_MID, ROWS), lambda k: (q, start + k)), hbm_of((C_IN, 4 * ROWS), BFLOAT), [], (x_kept, *extra, token),
                aliases={1: 0} if extra else {},
            )
            return held["x_t"]

        return filler

    total4, (y_t, y_kept, x_t0, x_t1) = dp_sum(
        part4,
        [
            turn(in_vmem(y), spec((ROWS, C_MID), lambda k: (0, k)), (4,), (4 * C_MID, ROWS), lambda k: (k, 0)),
            keep_in_hbm(y),
            turn_x(0, 0, None),
            lambda token: turn_x(0, 2, [held["x_t"]])(token),
        ],
    )
    del x_t0

    a5, h4, part5 = call(
        paired(k_conv_one, {1: ONE}, {2: ("mid", 2)}, 0), "a5", (3,),
        [SCALARS, full_table, full_row, full_row, full_mask, full_mid] + conv_weights(3, straight),
        [full_mid, full_mid, full_row],
        [vmem_of((ROWS, C_MID)), vmem_of((ROWS, C_MID), BFLOAT), shape_of((4, C_MID))],
        [pltpu.VMEM((PAD + ROWS + PAD, C_MID), SINGLE)] * 2,
        (core_row, base, *total4.parts, mask, a4) + (in_vmem(narrow_b),) * 3, vmem=8,
    )
    a5 = in_vmem(a5)
    total5, (h4_t, b_kept, _unused, x_t) = dp_sum(
        part5,
        [
            turn(h4, whole, (1,), (C_MID, ROWS), lambda k: (0, 0)),
            keep_in_hbm(narrow_b),
            turn_x(1, 0, [x_t1]),
            lambda token: turn_x(1, 2, [held["x_t"]])(token),
        ],
    )
    b_kept = in_hbm(b_kept)
    h5, a6, part6 = expand("a6", a5, total5, 3, 3)
    total6, (h5_t, a6_kept) = dp_sum(part6, [turn(h5, whole, (1,), (C_MID, ROWS), lambda k: (0, 0)), keep_in_hbm(a6)])
    a6_kept = in_hbm(a6_kept)

    cot = in_hbm(cotangent.transpose(0, 2, 1, 3).reshape(IMG_DEV, PIX, C_OUT))
    blk, gz6, s6 = call(
        paired(k_head, {2: ONE}, {3: ("wide", 2)}, 1, lead=1), "head", (4,),
        [full_table, chunk_sum, chunk_sum, full_mask, chunk, chunk]
        + [spec((1, PIX, TILE), lambda k, core, order, s=s: (order[0, core[0] * SLOTS + s], 0, k)) for s in range(SLOTS)],
        [
            spec((1, ROWS, TILE), lambda k, core, _order: ((k // 2) ^ core[0], 0, lax.rem(k, 2))),
            chunk,
            chunk_sum,
        ],
        [shape_of((2, ROWS, C_OUT // 2), BFLOAT), vmem_of((ROWS, C_OUT)), shape_of((4, C_OUT))], [],
        (core_row, assign, base, *total6.parts, mask, in_vmem(a6), in_hbm(y_kept), cot, cot, cot, cot), prefetch=2, vmem=9,
    )
    gz6 = in_vmem(gz6)

    def place(name, pair, got, token):
        block = (1,) + pair.shape[2:]
        return call(
            k_place, name, (IMG_DEV,),
            [
                spec((1,) + block, lambda t, *_: (0, jnp.minimum(t, SLOTS - 1), 0, 0)),
                spec(block, lambda t, *_: (jnp.maximum(t - SLOTS, 0), 0, 0)),
                ANYWHERE,
            ],
            spec(block, lambda t, core, order: (order[0, (core[0] * SLOTS + t) & (IMG_DEV - 1)], 0, 0)),
            shape_of((IMG_DEV,) + pair.shape[2:], BFLOAT), [],
            (core_row, assign, pair, got, token), prefetch=2, vmem=9,
        )

    blk = blk.reshape(2, SLOTS, PIX, C_OUT // 2)
    sum6, (got_blk, _unused, _unused, block_local) = dp_sum(
        s6,
        [
            lambda token: swap_pipe(pin(blk[1], token)),
            lambda token: token,
            lambda token: token,
            lambda token: token,
        ],
    )

    ga6, gz5, s5 = call(
        paired(k_back_six, {3: ONE, 4: ONE, 9: ONE}, {5: ("wide", 2), 10: ("mid", 3)}, 0), "g5", (4,),
        [SCALARS, full_table, chunk, chunk, chunk_sum, chunk_sum, chunk_sum, chunk_sum, full_mask, spec((TILE, TILE), lambda k: (3, k)), full_mid,
         full_row, full_row],
        [chunk, full_mid, full_row],
        [vmem_of((ROWS, C_OUT), BFLOAT), vmem_of((ROWS, C_MID)), shape_of((4, C_MID))],
        [pltpu.VMEM((ROWS, C_MID), SINGLE)],
        (core_row, base, gz6, a6_kept, *total6.parts, *sum6.parts, mask, in_hbm(wide), a5, *total5.parts), vmem=9,
    )
    gz5 = in_vmem(gz5)

    def wide_rows(k):
        return spec((1, 256, ROWS), lambda t, slot: (0, t + k, 0))

    def whole_wide(grad):
        return grad.reshape((1,) + grad.shape), full((1,) + grad.shape)

    wide_shape, narrow_shape = (R_W, C_OUT // 2), (R_N // 2, C_MID // 2)
    sum5, (bufs_w, block_local) = dp_sum(
        s5,
        [
            lambda token: weight_grad("dw6", h5_t[None], wide_rows(0), *whole_wide(ga6), 2, wide_shape, 256, 6, None, token, vmem_of),
            lambda token: place("place_out", blk, got_blk, token),
        ],
    )
    block_local = block_local.reshape(IMG_DEV, WB, HB, C_OUT // 2).transpose(0, 2, 1, 3)

    col5, gz4, s4 = call(
        paired(k_back_conv_one, {3: ONE, 4: ONE, 11: ONE}, {5: ("mid", 3), 12: ("mid", 2)}, 0), "g4", (3,),
        [SCALARS, full_table, full_mid, full_mid, full_row, full_row, full_row, full_row, full_mask] + conv_weights(3, straight)
        + [full_mid, full_row, full_row],
        [spec((3, ROWS, C_MID), lambda s: (s, 0, 0)), full_mid, full_row],
        [vmem_of((9, ROWS, C_MID), BFLOAT), vmem_of((ROWS, C_MID)), shape_of((4, C_MID))],
        [pltpu.VMEM((PAD + ROWS + PAD, C_MID), SINGLE)] * 2 + [pltpu.VMEM((ROWS, C_MID), SINGLE)],
        (core_row, base, gz5, a5, *total5.parts, *sum5.parts, mask, b_kept, b_kept, b_kept, a4, *total4.parts), vmem=10,
    )
    gz4 = in_vmem(gz4)
    one_turned = spec((1, C_MID, ROWS), lambda t, slot: (0, 0, 0))
    held_b = []

    def grad_five(k):
        def filler(token):
            grad_spec = spec((3, ROWS, C_MID), lambda t, slot: (k, 0, 0))
            held_b[:] = weight_grad("dw5", h4_t[None], one_turned, in_vmem(col5), grad_spec, 1, narrow_shape, 3 * TILE, 1 + k, list(held_b), token, vmem_of)
            return tuple(held_b)

        return filler

    sum4, results4 = dp_sum(s4, [grad_five(k) for k in range(3)])
    bufs_b = results4[2]

    ga4, gj, s3 = call(
        paired(k_back_four, {3: ONE, 4: ONE, 12: (0, 4)}, {5: ("mid", 2), 14: ("wide", 0), 15: ("wide", 1)}, 0), "gy", (4,),
        [SCALARS, full_table, full_mid, full_mid, full_row, full_row, full_row, full_row, full_mask, four_a, four_b,
         chunk, chunk, chunk, chunk_eight, chunk_eight],
        [full_mid, chunk, spec((6, TILE), lambda k: (0, k))],
        [vmem_of((ROWS, C_MID), BFLOAT), vmem_of((ROWS, C_OUT)), shape_of((6, C_OUT))], [],
        (core_row, base, gz4, a4, *total4.parts, *sum4.parts, mask, a_kept, b_kept, gz6, a3_kept, as_kept, *total3s.parts), vmem=12,
    )
    gj = in_vmem(gj)

    by_rows = lambda which, m: 2 * m + which

    def grad_four(token):
        y_tiles = y_t.reshape(4, C_MID, ROWS)
        one = full((1, ROWS, C_MID))
        grad = in_vmem(ga4.reshape(1, ROWS, C_MID))
        held["grad_b"] = weight_grad("dw4b", y_tiles, spec((1, C_MID, ROWS), lambda t, slot: (1 + t, 0, 0)), grad, one, 3, narrow_shape, TILE, 0, bufs_b, token, vmem_of)
        return held["grad_b"]

    def grad_four_first(token):
        return weight_grad(
            "dw4a", y_t.reshape(4, C_MID, ROWS), spec((1, C_MID, ROWS), lambda t, slot: (0, 0, 0)), in_vmem(ga4.reshape(1, ROWS, C_MID)),
            full((1, ROWS, C_MID)), 1, narrow_shape, TILE, 11, None, token, vmem_of,
        )

    def swap_grad_b(token):
        held["got_b"] = swap_pipe(pin(held["grad_b"][1], token))
        return token

    def split_b(token):
        if not fast:
            return token
        keep, got = pin((held["grad_b"][0], held["got_b"]), token)
        state = split_group("split_b", in_vmem(keep), got, part_n, by_rows)
        held["came_b"] = exchange(state[1], 1), exchange(state[3], 2)
        return state

    sum3, results3 = dp_sum(s3, [grad_four, both_of(swap_grad_b, grad_four_first), split_b])
    bufs_b, bufs_a = results3[0], results3[1][1]
    held["b"] = results3[2]

    ga3, gas, gz2, s2 = call(
        paired(k_back_three, {4: (0, 4), 6: ONE, 12: ONE}, {7: ("wide", 0), 8: ("wide", 1), 13: ("mid", 1)}, 0), "g2", (4,),
        [SCALARS, full_table, chunk, chunk, chunk, chunk_eight, chunk_eight, spec((6, TILE), lambda k: (0, k)), spec((6, TILE), lambda k: (0, k)), full_mask,
         spec((TILE, TILE), lambda k: (0, k)), full_mid, full_row, full_row],
        [chunk, chunk, full_mid, full_row],
        [vmem_of((ROWS, C_OUT), BFLOAT), vmem_of((ROWS, C_OUT), BFLOAT), vmem_of((ROWS, C_MID)), shape_of((4, C_MID))],
        [pltpu.VMEM((ROWS, C_MID), SINGLE)],
        (core_row, base, gj, a3_kept, as_kept, *total3s.parts, *sum3.parts, mask, in_hbm(wide), a2, *total2.parts), vmem=11,
    )
    gz2 = in_vmem(gz2)

    def second_b(token):
        if not fast:
            return token
        state = halved(held["b"], pin(held["came_b"], token), False)
        held["came_b"] = exchange(state[1], 2), exchange(state[3], 1)
        return state

    def third_exchange_b(token):
        if not fast:
            return token
        state = halved(held["b"], pin(held["came_b"], token), True)
        held["came_b"] = exchange(state[1], 4)
        return state

    def fourth_exchange_b(token):
        if not fast:
            return token
        state = halved_both(held["b"], pin(held["came_b"], token))
        held["came_b"] = exchange(state[1], 8)
        return state

    def grad_three(token):
        held["w"] = weight_grad("dw3", h2_t[None], wide_rows(0), *whole_wide(ga3), 2, wide_shape, 256, 0, bufs_w, token, vmem_of)
        return held["w"]

    def grad_short(q):
        def filler(token):
            held["w"] = weight_grad("dws", x_t[None], wide_rows(2 * q), *whole_wide(gas), 2, wide_shape, 256, 2 + 2 * q, held["w"], token, vmem_of)
            return held["w"]

        return filler

    def start_swap_w(token):
        held["got_w"] = swap_pipe(pin(held["w"][1], token))
        return token

    def two_grads(token):
        grad_three(token)
        return grad_short(0)(token)

    sum2, results2 = dp_sum(s2, [two_grads, both_of(second_b, grad_short(1)), start_swap_w])
    held["b"], bufs_w = results2[1]
    got_w = held["got_w"]
    if fast:
        split = split_group("split_w", bufs_w[0], pin(got_w, sum2.parts[1]), w_wide.shape[0], lambda which, m: 16 * which + m)
        last, split, held["b"] = lax.optimization_barrier((sum2.parts[1], split, third_exchange_b(sum2.parts[1])))
        sum2 = Total(sum2.parts[0], last)
        held["came"] = exchange(split[1], 1), exchange(split[3], 2)

    col2, gz1, s1 = call(
        paired(k_back_conv_two, {3: ONE, 4: ONE}, {5: ("mid", 1), 11: ("base", 0), 12: ("mid", 0)}, 0), "g1", (3,),
        [SCALARS, full_table, full_mid, full_mid, full_row, full_row, full_row, full_row, full_mask] + conv_weights(2, turned)
        + [plane_pair],
        [spec((3, ROWS, C_MID), lambda s: (turned(s), 0, 0)), plane_pair, full_row],
        [vmem_of((9, ROWS, C_MID), BFLOAT), vmem_of((4, ROWS, C_MID)), shape_of((4, C_MID))],
        [pltpu.VMEM((PAD + ROWS + PAD, C_MID), SINGLE)] * 2 + [pltpu.VMEM((2, ROWS, C_MID), SINGLE)],
        (core_row, base, gz2, a2, *total2.parts, *sum2.parts, mask, a_kept, a_kept, a_kept, a1), vmem=12,
    )
    gz1 = in_vmem(gz1)
    h1_planes = h1_t.reshape(4, C_MID, ROWS)

    def grad_two(row):
        def filler(token):
            first = 2 * (1 - (row & 1))
            held["a"] = weight_grad(
                "dw2", h1_planes, spec((1, C_MID, ROWS), lambda t, slot: (first + (1 - (t & 1)), 0, 0)), in_vmem(col2),
                spec((1, ROWS, C_MID), lambda t, slot: (3 * row + t, 0, 0)), 3, narrow_shape, TILE, 2 + 3 * row, held["a"], token, vmem_of,
            )
            return held["a"]

        return filler

    def wide_back(token):
        return call(
            k_wide_back, "dxs", (2,),
            [full((ROWS, C_OUT)), spec((TILE, C_OUT), lambda k: (1 + k, 0)), ANYWHERE],
            spec((ROWS, TILE), lambda k: (0, k)),
            hbm_of((ROWS, C_IN)), [],
            (gas, in_hbm(wide), token), vmem=8,
        )

    def first_w(token):
        if not fast:
            return token
        came = pin(held["came"], token)
        state = halved(split, came, False)
        held["came_w"] = exchange(state[1], 2), exchange(state[3], 1)
        return state

    held["a"] = bufs_a
    sum1, results1 = dp_sum(s1, [grad_two(0), grad_two(1), both_of(fourth_exchange_b, grad_two(2)), first_w], 4)
    held["b"], bufs_a = results1[2]
    state_w = results1[3]
    state_b = held["b"]
    plane = spec((1, ROWS, C_MID), lambda k: (k, 0, 0))
    ga1 = call(
        paired(k_first_grad, {4: ONE}, {3: ("base", 0), 5: ("mid", 0)}, 0), "g0", (4,),
        [SCALARS, full_table, plane, plane, full_row, full_row, full_mask], plane,
        vmem_of((4, ROWS, C_MID), BFLOAT), [], (core_row, base, gz1, a1, *sum1.parts, mask),
    )
    flat_ga1 = in_vmem(ga1.reshape(1, 4 * ROWS, C_MID))
    bufs_a = weight_grad(
        "dw1", x_t.reshape(2, C_MID, 4 * ROWS), spec((1, C_MID, 4 * ROWS), lambda t, slot: (t, 0, 0)), flat_ga1, full((1, 4 * ROWS, C_MID)),
        2, narrow_shape, TILE, 0, bufs_a, None, vmem_of,
    )
    got_a = swap_pipe(bufs_a[1])
    sums = [sum1, sum2, sum3, sum4, sum5, sum6]

    def image_grads(token, dxs):
        pair = call(
            k_image_grad, "gx", (SLOTS,),
            [spec((4, PIX, C_MID), lambda s, slot: (0, s, 0)), spec((PIX, 1), lambda s, slot: (s, 0)), full((C_IN, C_MID)),
             spec((PIX, C_IN), lambda s, slot: (s, 0)), full((4 * PIX, 4 * PIX)), ANYWHERE],
            spec((2, 1, 4 * PIX, C_IN // 2), lambda s, slot: (0, s, 0, 0)),
            shape_of((2, SLOTS, 4 * PIX, C_IN // 2), BFLOAT), [],
            (core_row, in_vmem(ga1), mask, a_kept, in_hbm(dxs), in_hbm(perm), token), prefetch=1, vmem=9,
        )
        return pair, swap_pipe(pair[1])

    if fast:
        state_w = halved(state_w, held["came_w"], True)
        got_a, state_w, came_b = lax.optimization_barrier((got_a, state_w, held["came_b"]))
        came_w = exchange(state_w[1], 4)
        state_a = split_group("split_a", in_vmem(bufs_a[0]), got_a, part_n, by_rows)
        came_a = exchange(state_a[1], 1), exchange(state_a[3], 2)
        dxs = wide_back(state_a[0])
        state_w = halved_both(state_w, came_w)
        pair, got_pair = image_grads(state_w[0], dxs)
        came_a, state_w, pair = lax.optimization_barrier((came_a, state_w, pair))
        came_w = exchange(state_w[1], 8)
        state_a = halved(state_a, came_a, False)
        came_a = exchange(state_a[1], 2), exchange(state_a[3], 1)
        half_w0, half_w1 = added(state_w, came_w)
        half_b = jnp.concatenate(added(state_b, came_b), axis=0)
        came_a, half_w0, half_w1, half_b = lax.optimization_barrier((came_a, half_w0, half_w1, half_b))
        state_a = halved(state_a, came_a, True)
        came_a = exchange(state_a[1], 4)
        grad_local = place("place_grad", pair, got_pair, state_a[0])
        came_a, grad_local = lax.optimization_barrier((came_a, grad_local))
        state_a = halved_both(state_a, came_a)
        came_a = exchange(state_a[1], 8)
        sums = pin(tuple(t.parts for t in sums), state_a[0])
        sums = [Total(*parts) for parts in sums]
        half_a = jnp.concatenate(added(state_a, came_a), axis=0)
    else:
        half_a = jnp.concatenate(scatter_plain(bufs_a[0], got_a, rows_n, True), axis=0)
        half_w0, half_w1 = scatter_plain(bufs_w[0], got_w, w_wide.shape[0], False)
        half_b = jnp.concatenate(scatter_plain(bufs_b[0], held["got_b"], rows_n, True), axis=0)
        pair, got_pair = image_grads(ga1, wide_back(ga1))
        grad_local = place("place_grad", pair, got_pair, ga1)
    grad_local = grad_local.reshape(IMG_DEV, 2 * HB, 2 * WB, C_IN // 2)

    def join_halves(first, second):
        mine = jnp.where(core == 0, first, second)
        got = swap_pipe(jnp.where(core == 0, second, first))
        return jnp.where(core == 0, jnp.concatenate([mine, got], axis=1), jnp.concatenate([got, mine], axis=1))

    grad_narrow = join_halves(half_a, half_b)
    grad_wide = join_halves(half_w0, half_w1)

    sum1, sum2, sum3, sum4, sum5, sum6 = (t.sum for t in sums)

    def pair_sum(rows):
        return rows[0] + rows[1]

    mid_rows = jnp.stack([pair_sum(v) for t in (sum1, sum2, sum4, sum5) for v in (t[2:4], t[0:2])])
    wide_rows = jnp.stack([pair_sum(v) for v in (sum3[2:4], sum3[0:2], sum3[4:6], sum3[0:2], sum6[2:4], sum6[0:2])])
    mid_rows = mid_rows + swap_pipe(mid_rows)
    wide_rows = wide_rows + swap_pipe(wide_rows)
    grad_mid = lax.dynamic_slice(mid_rows, (0, shard * mid_cols), (8, mid_cols))
    grad_table = lax.dynamic_slice(wide_rows, (0, shard * wide_cols), (6, wide_cols))

    starts = (shard * jnp.array([rows_n, w_wide.shape[0]])).astype(jnp.int32)
    weights, grads = (w_narrow, w_wide, bn_mid, bn_wide), (grad_narrow, grad_wide, grad_mid, grad_table)
    whole_specs = [full(v.shape) for v in weights]
    squares = call(
        k_squares, "squares", (1,), whole_specs * 2, full((8, 128)), shape_of((8, 128)), [], (starts, *weights, *grads), prefetch=1, vmem=10,
    )
    squares, _unused = dp_sum(squares + swap_pipe(squares))
    parts = 4 if rows_n % 64 == 0 and w_wide.shape[0] % 64 == 0 else 1
    specs = [spec((v.shape[0] // parts, v.shape[1]), lambda k, *_: (k, 0)) for v in weights[:2]] + whole_specs[2:]
    updated = call(
        paired(k_update, {1: ONE}), "update", (parts,), [full((8, 128))] * 2 + specs * 3, specs * 2, [shape_of(v.shape) for v in weights] * 2, [],
        (starts, *squares.parts, *weights, *grads, mom_narrow, mom_wide, mom_bn_mid, mom_bn_wide), prefetch=1, vmem=12,
    )
    new_mom_narrow, new_mom_wide, new_mom_mid, new_mom_table, new_narrow, new_wide, new_mid, new_table = updated
    return (
        block_local, grad_local, grad_narrow, grad_wide, grad_mid, grad_table,
        new_mom_narrow, new_mom_wide, new_mom_mid, new_mom_table,
        new_narrow, new_wide, new_mid, new_table,
    )


def solution(mesh):
    rows = P(("pipe", "dp"), None)
    columns = P(None, ("pipe", "dp"))
    feature = P("dp", None, None, None)
    return jax.shard_map(
        on_device,
        mesh=mesh,
        in_specs=(feature, feature, P("dp"), P("dp"), P("dp", None), rows, rows, columns, columns, rows, rows, columns, columns),
        out_specs=(P("dp", None, None, "pipe"), P("dp", None, None, "pipe"), rows, rows, columns, columns, rows, rows, columns, columns, rows, rows, columns, columns),
        check_vma=False,
    )
```

```python
import functools

import jax
import jax.numpy as jnp
import numpy as np
from jax import lax
from jax.experimental import pallas as pl
from jax.experimental.pallas import tpu as pltpu
from jax.sharding import PartitionSpec as P

C_IN = 1024
C_MID = 512
C_OUT = 2048
R_N = 12288
R_W = 2048
HB = 8
WB = 12
IMG_DEV = 8
SLOTS = 4
PIX = HB * WB
ROWS = SLOTS * PIX
HALF = ROWS // 2
PAD = 16
TILE = 512

EPS = 1e-05
MOMENTUM = 0.9
DECAY = 5e-05
TRUST = 0.001
RATE = 29.0
NARROW_BOUNDS = (C_IN, C_IN + 9 * C_MID, C_IN + 9 * C_MID + C_OUT)
WIDE_BOUNDS = (C_MID, C_MID + C_IN)
BFLOAT = jnp.bfloat16
SINGLE = jnp.float32
MIB = 1024 * 1024
BYTES_PER_US = 600000
MICROSECONDS = {
    "prep": 5, "a1": 3, "a2": 5, "as": 4.5, "a3": 4, "a4": 4.7, "a5": 4, "a6": 3.7, "head": 5.3, "g5": 5.2, "g4": 5.4, "gy": 7,
    "g2": 7.3, "g1": 8, "g0": 3, "gx": 6.4, "dxs": 5, "dw1": 3.4, "dw2": 2.1, "dw3": 2.9, "dws": 2.9, "dw4a": 1.7, "dw4b": 1.9,
    "dw5": 1.5, "dw6": 2.8, "place_out": 3.4, "place_grad": 5, "wa": 3, "wb": 3, "turn": 1.7, "keep": 1.7, "halve": 1, "squares": 2, "update": 3,
}


def pairs(bit):
    return [(i, i ^ bit) for i in range(lax.axis_size("dp"))]


def exchange(value, bit):
    return lax.ppermute(value, "dp", pairs(bit))


def pin(value, after):
    return lax.optimization_barrier((value, after))[0]


class Total:
    def __init__(self, *parts):
        self.parts = parts

    @property
    def sum(self):
        return self.parts[0] + self.parts[1]


def dp_sum(value, fillers=(), first=None):
    size = lax.axis_size("dp")
    bits = [1 << k for k in range(size.bit_length() - 1)]
    if first in bits:
        at = bits.index(first)
        bits = bits[at:] + bits[:at]
    results = []
    for bit in bits:
        got = exchange(value, bit)
        if len(results) < len(fillers):
            result = fillers[len(results)](value)
            got, result = lax.optimization_barrier((got, result))
            results.append(result)
        if bit == bits[-1]:
            break
        value = value + got
    for filler in fillers[len(results) :]:
        results.append(filler(got))
    return Total(value, got), results


def swap_pipe(value):
    return lax.ppermute(value, "pipe", [(0, 1), (1, 0)])


def dot(left, right):
    return jnp.dot(left, right, preferred_element_type=SINGLE)


def dot_back(left, right):
    return lax.dot_general(left, right, (((1,), (1,)), ((), ())), preferred_element_type=SINGLE)


def silu(value):
    return value * jax.nn.sigmoid(value)


def slope(value):
    gate = jax.nn.sigmoid(value)
    return gate * (1.0 + value * (1.0 - gate))


def put_sums(ref, values, first):
    for k, value in enumerate(values):
        for m in range(2):
            total = jnp.sum(value[m * HALF : (m + 1) * HALF], axis=0, keepdims=True)
            row = 2 * k + m
            ref[row : row + 1, :] = total if first else ref[row : row + 1, :] + total


def both(function):
    return jnp.concatenate([function(0), function(1)], axis=0)


def part(m):
    return slice(m * HALF, (m + 1) * HALF)


def moments(total_ref, inv_ref, m, scale=1.0):
    inv = inv_ref[m] * scale
    mean = total_ref[m : m + 1, :] * inv
    var = total_ref[2 + m : 3 + m, :] * inv - mean * mean
    return mean, lax.rsqrt(var + EPS)


def normed(a, total_ref, inv_ref, m, scale=1.0):
    mean, rstd = moments(total_ref, inv_ref, m, scale)
    return (a - mean) * rstd, rstd


def conv_grad(gz, xhat, rstd, gain, mask, sum_ref, inv_ref, m, scale=1.0, second=2):
    inv = inv_ref[m] * scale
    first_row = sum_ref[m : m + 1, :] * inv
    second_row = sum_ref[second + m : second + m + 1, :] * inv
    return (mask * ((rstd * gain) * (gz - first_row - xhat * second_row))).astype(BFLOAT)


class Both:
    def __init__(self, refs, start=0):
        self.refs, self.start = refs, start

    def __getitem__(self, index):
        rows, columns = index
        rows = slice(rows.start + self.start, rows.stop + self.start)
        return sum(ref[rows, columns] for ref in self.refs)


class Chunk:
    def __init__(self, refs, which, step):
        self.refs, self.first = refs, WIDE_ROW + 8 * which + step

    def __getitem__(self, index):
        rows, columns = index
        return sum(ref[pl.ds(self.first + 4 * rows.start, 1), columns] for ref in self.refs)


class Inverse:
    def __init__(self, refs, core):
        self.refs, self.core = refs, core

    def __getitem__(self, m):
        row = sum(ref[COUNT_ROW : COUNT_ROW + 1, 0:128] for ref in self.refs)
        lane = lax.broadcasted_iota(jnp.int32, (1, 128), 1)
        return 1.0 / jnp.sum(jnp.where(lane == 2 * self.core + m, row, 0.0), axis=1, keepdims=True)


ONE = (0,)
MID_ROW, WIDE_ROW, COUNT_ROW, TABLE_ROWS = 4, 12, 36, 40


def paired(kernel, views, tabs=None, inv=None, tables=1, lead=0):
    def run(*refs):
        fixed, refs = {}, list(refs)
        if inv is not None:
            core = refs.pop(0)[0]
            table, refs[lead : lead + tables] = refs[lead : lead + tables], []
            step = pl.program_id(0)
            fixed[inv] = Inverse(table, core)
            for at, (kind, which) in (tabs or {}).items():
                if kind == "wide":
                    fixed[at] = Chunk(table, which, step)
                else:
                    fixed[at] = Both(table, MID_ROW + 2 * which if kind == "mid" else 0)
        given, at = [], 0
        while at < len(refs) or len(given) in fixed:
            if len(given) in fixed:
                given.append(fixed[len(given)])
            elif len(given) in views:
                given.extend([Both(refs[at : at + 2], start) for start in views[len(given)]])
                at += 2
            else:
                given.append(refs[at])
                at += 1
        return kernel(*given)

    return run


def k_prep(core_ref, assign_ref, height_ref, width_ref, img_ref, perm_ref, out_ref, mask_ref, count_ref):
    slot = pl.program_id(0)
    image = assign_ref[0, core_ref[0] * SLOTS + slot]
    pixel = lax.broadcasted_iota(jnp.int32, (PIX, 1), 0)
    inside = ((pixel & (HB - 1)) < height_ref[image]) & (pixel < width_ref[image] * HB)
    mask = jnp.where(inside, 1.0, 0.0).astype(SINGLE)
    mask_ref[...] = mask
    planes = dot(perm_ref[...], img_ref[0])
    for k in range(4):
        out_ref[k] = (planes[k * PIX : (k + 1) * PIX] * mask).astype(BFLOAT)
    column = lax.broadcasted_iota(jnp.int32, count_ref.shape, 1)
    counts = jnp.zeros(count_ref.shape, jnp.int32)
    for m in range(4):
        pair = (assign_ref[0, 2 * m], assign_ref[0, 2 * m + 1])
        total = sum(height_ref[k] * width_ref[k] for k in pair)
        counts = jnp.where(column == m, total, counts)
    count_ref[...] = counts.astype(SINGLE)


def k_first(x_ref, w_ref, a_ref, sum_ref):
    a = dot(x_ref[0], w_ref[...])
    a_ref[0] = a

    @pl.when(pl.program_id(0) == 0)
    def _():
        sum_ref[...] = jnp.zeros_like(sum_ref)

    put_sums(sum_ref, [a, a * a], False)


def shift_mask(di, dj):
    if not di and not dj:
        return None
    pixel = lax.broadcasted_iota(jnp.int32, (SLOTS, PIX, 1), 1)
    inside = None
    if di:
        row = pixel & (HB - 1)
        inside = row >= -di if di < 0 else row < HB - di
    if dj:
        column = pixel >= -dj * HB if dj < 0 else pixel < PIX - dj * HB
        inside = column if inside is None else inside & column
    return jnp.where(inside, 1.0, 0.0).astype(SINGLE).reshape(ROWS, 1)


def rows_at(pad, di, dj):
    start = PAD + HB * dj + di
    rows = pad[start : start + ROWS, :]
    mask = shift_mask(di, dj)
    return rows if mask is None else rows * mask


def clear_pad(pad):
    pad[0:PAD, :] = jnp.zeros((PAD, pad.shape[1]), SINGLE)
    pad[PAD + ROWS : PAD + ROWS + PAD, :] = jnp.zeros((PAD, pad.shape[1]), SINGLE)


def body(pad, m):
    return pad.at[PAD + m * HALF : PAD + (m + 1) * HALF, :]


def carried(ref, fresh):
    return jnp.where(fresh, 0.0, ref[...])


def k_conv_two(inv_ref, total_ref, tab_ref, mask_ref, a_ref, w0, w1, w2, out_ref, h_ref, sum_ref, pad, moved):
    step = pl.program_id(0)
    gain, bias = tab_ref[0:1, :], tab_ref[1:2, :]

    @pl.when(step < 2)
    def _():
        for k in range(2):
            clear_pad(pad.at[k])
            clear_pad(moved.at[k])
            for m in range(2):
                xhat, _unused = normed(a_ref[k, part(m), :], total_ref, inv_ref, m, 0.25)
                h = (silu(xhat * gain + bias) * mask_ref[part(m), :]).astype(BFLOAT)
                h_ref[k, part(m), :] = h
                body(pad.at[k], m)[...] = h.astype(SINGLE)
                body(moved.at[k], m)[...] = h.astype(SINGLE)

    @pl.when(step == 2)
    def _():
        for k in range(2):
            moved[k, PAD : PAD + ROWS, :] = rows_at(pad.at[k], -1, 0)

    term = dot(rows_at(moved.at[0], 0, 0).astype(BFLOAT), w1[...])
    term += dot(rows_at(moved.at[1], 0, -1).astype(BFLOAT), w0[...])
    term += dot(rows_at(moved.at[1], 0, 0).astype(BFLOAT), w2[...])
    out_ref[...] = carried(out_ref, step == 0) + term

    @pl.when(step == 2)
    def _():
        a = out_ref[...]
        masked = a * mask_ref[...]
        put_sums(sum_ref, [masked, masked * a], True)


def k_conv_one(inv_ref, total_ref, tab_ref, mask_ref, a_ref, w0, w1, w2, out_ref, h_ref, sum_ref, pad, moved):
    step = pl.program_id(0)
    gain, bias = tab_ref[0:1, :], tab_ref[1:2, :]

    @pl.when(step == 0)
    def _():
        clear_pad(pad)
        clear_pad(moved)
        for m in range(2):
            xhat, _unused = normed(a_ref[part(m), :], total_ref, inv_ref, m)
            h = (silu(xhat * gain + bias) * mask_ref[part(m), :]).astype(BFLOAT)
            h_ref[part(m), :] = h
            body(pad, m)[...] = h.astype(SINGLE)

    for s in range(3):

        @pl.when(step == s)
        def _(s=s):
            moved[PAD : PAD + ROWS, :] = rows_at(pad, s - 1, 0)

    term = dot(rows_at(moved, 0, -1).astype(BFLOAT), w0[...])
    term += dot(rows_at(moved, 0, 0).astype(BFLOAT), w1[...])
    term += dot(rows_at(moved, 0, 1).astype(BFLOAT), w2[...])
    out_ref[...] = carried(out_ref, step == 0) + term

    @pl.when(step == 2)
    def _():
        a = out_ref[...]
        masked = a * mask_ref[...]
        put_sums(sum_ref, [masked, masked * a], True)


def k_expand(inv_ref, total_ref, tab_ref, mask_ref, a_ref, w_ref, h_ref, out_ref, sum_ref):
    @pl.when(pl.program_id(0) == 0)
    def _():
        gain, bias = tab_ref[0:1, :], tab_ref[1:2, :]
        for m in range(2):
            xhat, _unused = normed(a_ref[part(m), :], total_ref, inv_ref, m)
            h_ref[part(m), :] = (silu(xhat * gain + bias) * mask_ref[part(m), :]).astype(BFLOAT)

    a = dot(h_ref[...], w_ref[...])
    out_ref[...] = a
    put_sums(sum_ref, [a, a * a], True)


def k_short(x_ref, w0, w1, out_ref, sum_ref):
    a = dot(x_ref[0, :, :TILE], w0[...]) + dot(x_ref[0, :, TILE:], w1[...])
    out_ref[...] = a
    put_sums(sum_ref, [a, a * a], True)


def k_meet(inv_ref, t3_ref, ts_ref, tab3_ref, tabs_ref, mask_ref, a3_ref, as_ref, wa_ref, wb_ref, y_ref, out_ref, sum_ref):
    step = pl.program_id(0)
    for m in range(2):
        x3, _unused = normed(a3_ref[part(m), :], t3_ref, inv_ref, m)
        xs, _unused = normed(as_ref[part(m), :], ts_ref, inv_ref, m)
        joined = (x3 * tab3_ref[0:1, :] + tab3_ref[1:2, :]) + (xs * tabs_ref[0:1, :] + tabs_ref[1:2, :])
        y_ref[part(m), :] = (silu(joined) * mask_ref[part(m), :]).astype(BFLOAT)

    @pl.when(step == 0)
    def _():
        out_ref[...] = dot(y_ref[...], wa_ref[...])

    @pl.when(step > 0)
    def _():
        out_ref[...] += dot(y_ref[...], wb_ref[...])

    @pl.when(step == pl.num_programs(0) - 1)
    def _():
        a = out_ref[...]
        put_sums(sum_ref, [a, a * a], True)


def k_head(order_ref, inv_ref, total_ref, tab_ref, mask_ref, a_ref, y_ref, c0, c1, c2, c3, blk_ref, gz_ref, sum_ref):
    cots = (c0, c1, c2, c3)
    gain, bias = tab_ref[0:1, :], tab_ref[1:2, :]
    for m in range(2):
        mask = mask_ref[part(m), :]
        xhat, _unused = normed(a_ref[part(m), :], total_ref, inv_ref, m)
        z = (xhat * gain + bias) + y_ref[part(m), :].astype(SINGLE)
        gate = jax.nn.sigmoid(z)
        blk_ref[0, part(m), :] = (z * gate * mask).astype(BFLOAT)
        cot = jnp.concatenate([cots[2 * m][0], cots[2 * m + 1][0]], axis=0).astype(SINGLE)
        gz = cot * mask * (gate * (1.0 + z * (1.0 - gate)))
        gz_ref[part(m), :] = gz
        sum_ref[m : m + 1, :] = jnp.sum(gz, axis=0, keepdims=True)
        sum_ref[2 + m : 3 + m, :] = jnp.sum(gz * xhat, axis=0, keepdims=True)


def finish_back(gz_ref, sum_ref, grad, a_ref, total_ref, tab_ref, inv_ref, mask_ref):
    gain, bias = tab_ref[0:1, :], tab_ref[1:2, :]
    for m in range(2):
        xhat, _unused = normed(a_ref[part(m), :], total_ref, inv_ref, m)
        gz = grad[part(m)] * mask_ref[part(m), :] * slope(xhat * gain + bias)
        gz_ref[part(m), :] = gz
        sum_ref[m : m + 1, :] = jnp.sum(gz, axis=0, keepdims=True)
        sum_ref[2 + m : 3 + m, :] = jnp.sum(gz * xhat, axis=0, keepdims=True)


def k_back_six(inv_ref, gz_ref, a_ref, total_ref, s_ref, tab_ref, mask_ref, w_ref, low_ref, low_total, low_tab, ga_ref, out_ref, sum_ref, acc):
    step = pl.program_id(0)
    for m in range(2):
        xhat, rstd = normed(a_ref[part(m), :], total_ref, inv_ref, m)
        ga_ref[part(m), :] = conv_grad(
            gz_ref[part(m), :], xhat, rstd, tab_ref[0:1, :], mask_ref[part(m), :], s_ref, inv_ref, m
        )
    term = dot_back(ga_ref[...], w_ref[...])

    @pl.when(step == 0)
    def _():
        acc[...] = term

    @pl.when(step > 0)
    def _():
        acc[...] += term

    @pl.when(step == pl.num_programs(0) - 1)
    def _():
        finish_back(out_ref, sum_ref, acc[...], low_ref, low_total, low_tab, inv_ref, mask_ref)


def k_back_conv_one(inv_ref, gz_ref, a_ref, total_ref, s_ref, tab_ref, mask_ref, w0, w1, w2, low_ref, low_total, low_tab, col_ref, out_ref, sum_ref, pad, moved, acc):
    step = pl.program_id(0)

    @pl.when(step == 0)
    def _():
        clear_pad(pad)
        clear_pad(moved)
        for m in range(2):
            xhat, rstd = normed(a_ref[part(m), :], total_ref, inv_ref, m)
            ga = conv_grad(gz_ref[part(m), :], xhat, rstd, tab_ref[0:1, :], mask_ref[part(m), :], s_ref, inv_ref, m)
            body(pad, m)[...] = ga.astype(SINGLE)

    for s in range(3):

        @pl.when(step == s)
        def _(s=s):
            moved[PAD : PAD + ROWS, :] = rows_at(pad, 1 - s, 0)

    term = None
    for kx, weight in enumerate((w0, w1, w2)):
        tap = rows_at(moved, 0, 1 - kx).astype(BFLOAT)
        col_ref[kx] = tap
        product = dot_back(tap, weight[...])
        term = product if term is None else term + product
    acc[...] = carried(acc, step == 0) + term

    @pl.when(step == 2)
    def _():
        finish_back(out_ref, sum_ref, acc[...], low_ref, low_total, low_tab, inv_ref, mask_ref)


def k_back_four(inv_ref, gz_ref, a_ref, total_ref, s_ref, tab_ref, mask_ref, wa_ref, wb_ref, up_ref, a3_ref, as_ref, t3_ref, ts_ref, tab3_ref, tabs_ref, ga_ref, gj_ref, sum_ref):
    @pl.when(pl.program_id(0) == 0)
    def _():
        for m in range(2):
            xhat, rstd = normed(a_ref[part(m), :], total_ref, inv_ref, m)
            ga_ref[part(m), :] = conv_grad(
                gz_ref[part(m), :], xhat, rstd, tab_ref[0:1, :], mask_ref[part(m), :], s_ref, inv_ref, m
            )

    weight = jnp.where(pl.program_id(0) == 0, wa_ref[...], wb_ref[...])
    grad = dot_back(ga_ref[...], weight) + up_ref[...]
    for m in range(2):
        x3, _unused = normed(a3_ref[part(m), :], t3_ref, inv_ref, m)
        xs, _unused = normed(as_ref[part(m), :], ts_ref, inv_ref, m)
        joined = (x3 * tab3_ref[0:1, :] + tab3_ref[1:2, :]) + (xs * tabs_ref[0:1, :] + tabs_ref[1:2, :])
        gj = grad[part(m)].astype(BFLOAT).astype(SINGLE) * mask_ref[part(m), :] * slope(joined)
        gj_ref[part(m), :] = gj
        for k, value in enumerate((gj, gj * x3, gj * xs)):
            row = 2 * k + m
            sum_ref[row : row + 1, :] = jnp.sum(value, axis=0, keepdims=True)


def k_back_three(inv_ref, gj_ref, a3_ref, as_ref, t3_ref, ts_ref, s_ref, tab3_ref, tabs_ref, mask_ref, w_ref, low_ref, low_total, low_tab, g3_ref, gs_ref, out_ref, sum_ref, acc):
    step = pl.program_id(0)
    for m in range(2):
        mask = mask_ref[part(m), :]
        gj = gj_ref[part(m), :]
        x3, r3 = normed(a3_ref[part(m), :], t3_ref, inv_ref, m)
        g3_ref[part(m), :] = conv_grad(gj, x3, r3, tab3_ref[0:1, :], mask, s_ref, inv_ref, m)
        xs, rs = normed(as_ref[part(m), :], ts_ref, inv_ref, m)
        gs_ref[part(m), :] = conv_grad(gj, xs, rs, tabs_ref[0:1, :], mask, s_ref, inv_ref, m, second=4)
    term = dot_back(g3_ref[...], w_ref[...])

    @pl.when(step == 0)
    def _():
        acc[...] = term

    @pl.when(step > 0)
    def _():
        acc[...] += term

    @pl.when(step == pl.num_programs(0) - 1)
    def _():
        finish_back(out_ref, sum_ref, acc[...], low_ref, low_total, low_tab, inv_ref, mask_ref)


def k_back_conv_two(inv_ref, gz_ref, a_ref, total_ref, s_ref, tab_ref, mask_ref, w0, w1, w2, low_ref, low_total, low_tab, col_ref, out_ref, sum_ref, pad, moved, acc):
    step = pl.program_id(0)
    gain, bias = low_tab[0:1, :], low_tab[1:2, :]

    @pl.when(step == 0)
    def _():
        clear_pad(pad)
        clear_pad(moved)
        for m in range(2):
            xhat, rstd = normed(a_ref[part(m), :], total_ref, inv_ref, m)
            ga = conv_grad(gz_ref[part(m), :], xhat, rstd, tab_ref[0:1, :], mask_ref[part(m), :], s_ref, inv_ref, m)
            body(pad, m)[...] = ga.astype(SINGLE)
            body(moved, m)[...] = ga.astype(SINGLE)
        sum_ref[...] = jnp.zeros_like(sum_ref)

    @pl.when(step == 2)
    def _():
        moved[PAD : PAD + ROWS, :] = rows_at(pad, 1, 0)

    plain = rows_at(moved, 0, 0).astype(BFLOAT)
    aside = rows_at(moved, 0, 1).astype(BFLOAT)
    col_ref[0], col_ref[1], col_ref[2] = aside, plain, plain
    acc[0] = carried(acc.at[0], step < 2) + dot_back(plain, w1[...])
    acc[1] = carried(acc.at[1], step < 2) + (dot_back(aside, w0[...]) + dot_back(plain, w2[...]))

    @pl.when(step != 1)
    def _():
        for k in range(2):
            for m in range(2):
                xhat, _unused = normed(low_ref[k, part(m), :], low_total, inv_ref, m, 0.25)
                gz = acc[k, part(m), :] * mask_ref[part(m), :] * slope(xhat * gain + bias)
                out_ref[k, part(m), :] = gz
                for q, value in enumerate((gz, gz * xhat)):
                    row = 2 * q + m
                    sum_ref[row : row + 1, :] += jnp.sum(value, axis=0, keepdims=True)


def k_wide_back(g_ref, w_ref, *refs):
    refs[-1][...] = dot_back(g_ref[...], w_ref[...])


def k_first_grad(inv_ref, gz_ref, a_ref, total_ref, s_ref, tab_ref, mask_ref, ga_ref):
    for m in range(2):
        xhat, rstd = normed(a_ref[0, part(m), :], total_ref, inv_ref, m, 0.25)
        ga_ref[0, part(m), :] = conv_grad(
            gz_ref[0, part(m), :], xhat, rstd, tab_ref[0:1, :], mask_ref[part(m), :], s_ref, inv_ref, m, 0.25
        )


def k_image_grad(core_ref, ga_ref, mask_ref, w_ref, short_ref, perm_ref, *refs):
    out_ref = refs[-1]
    grads = dot_back(ga_ref[...].reshape(4 * PIX, C_MID), w_ref[...])
    mask = mask_ref[...]
    parts = []
    for k in range(4):
        grad = grads[k * PIX : (k + 1) * PIX]
        if k == 0:
            grad = grad + short_ref[...]
        parts.append((grad * mask).astype(BFLOAT))
    planes = jnp.concatenate(parts, axis=0)
    image = lax.dot_general(perm_ref[...], planes, (((0,), (0,)), ((), ())), preferred_element_type=SINGLE).astype(BFLOAT)
    core = core_ref[0]
    out_ref[core, 0] = image[:, : C_IN // 2]
    out_ref[1 - core, 0] = image[:, C_IN // 2 :]


def k_place(core_ref, order_ref, own_ref, got_ref, *refs):
    out_ref = refs[-1]
    step = pl.program_id(0)

    @pl.when(step < SLOTS)
    def _():
        out_ref[0] = own_ref[0, 0]

    @pl.when(step >= SLOTS)
    def _():
        out_ref[0] = got_ref[0]


def k_turn(in_ref, *refs):
    refs[-1][...] = in_ref[...].reshape(in_ref.shape[-2:]).T


def k_grad(core_ref, feature_ref, grad_ref, *refs):
    keep_ref, send_ref = refs[-2:]
    core = core_ref[0]
    rows, half = feature_ref.shape[-2], grad_ref.shape[-1] // 2
    for k in range(grad_ref.shape[0]):
        feature = feature_ref[k % feature_ref.shape[0]]
        for ref, side in ((keep_ref, core), (send_ref, 1 - core)):
            columns = pl.ds(pl.multiple_of(side * half, half), half)
            ref[k * rows : (k + 1) * rows] = dot(feature, grad_ref[k, :, columns]).astype(BFLOAT)


def k_keep(in_ref, *refs):
    out_ref, sem = refs[-2:]
    copy = pltpu.make_async_copy(in_ref, out_ref, sem)
    copy.start()
    copy.wait()


def k_join(n_in, n_out, *refs):
    stayed, came = refs[:n_in], refs[n_in : 2 * n_in]
    outs, sems = refs[-1 - n_out : -1], refs[-1]
    copies = []
    for which in range(2):
        target = outs[0].at[which] if n_out == 1 else outs[which]
        for side, sources in enumerate((stayed, came)):
            source = sources[0].at[which] if n_in == 1 else sources[which]
            size = source.shape[0]
            copies.append(pltpu.make_async_copy(source, target.at[pl.ds(side * size, size)], sems.at[len(copies)]))
    for copy in copies:
        copy.start()
    for copy in copies:
        copy.wait()


def k_halve(*refs):
    for which in range(2):
        keep0, keep1, came0, came1 = refs[4 * which : 4 * which + 4]
        stay = (keep0[0].astype(SINGLE) + came0[0].astype(SINGLE)).astype(BFLOAT)
        sent = (keep1[0].astype(SINGLE) + came1[0].astype(SINGLE)).astype(BFLOAT)
        if len(refs) == 10:
            refs[8][which, 0], refs[9][which, 0] = stay, sent
        else:
            refs[8 + 2 * which][0], refs[9 + 2 * which][0] = stay, sent


def k_halve_both(keep_ref, came_ref, stay_ref, sent_ref):
    total = (keep_ref[...].astype(SINGLE) + came_ref[...].astype(SINGLE)).astype(BFLOAT)
    half = total.shape[1] // 2
    stay_ref[...], sent_ref[...] = total[:, :half], total[:, half:]


def k_gather(me_ref, *refs):
    ins, out_ref, sems = refs[:8], refs[8], refs[9]
    rows, cols = ins[0].shape[1:]
    copies = []
    for other in range(2):
        column = pl.multiple_of((1 - me_ref[1] if other else me_ref[1]) * cols, cols)
        for which in range(2):
            for came in range(2):
                source = ins[4 * other + 2 * which + came]
                for q in range(8):
                    third, low, high = q >> 2, (q >> 1) & 1, q & 1
                    pair = 2 * third + came if which == 0 else 2 * came + third
                    block = me_ref[0] ^ (8 * high + 4 * low + pair)
                    row = pl.multiple_of((2 * block + which) * rows, rows)
                    target = out_ref.at[pl.ds(row, rows), pl.ds(column, cols)]
                    copies.append(pltpu.make_async_copy(source.at[q], target, sems.at[len(copies)]))
    for copy in copies:
        copy.start()
    for copy in copies:
        copy.wait()


def k_split(me_ref, *refs):
    own, got, outs = refs[:4], refs[4:8], refs[8:]
    for own_ref, got_ref, out_ref in zip(own, got, outs):
        out_ref[0] = (own_ref[...].astype(SINGLE) + got_ref[...].astype(SINGLE)).astype(BFLOAT)


def group_of(rows, start, bounds):
    index = lax.broadcasted_iota(jnp.int32, (rows, 1), 0) + start
    return sum((index >= bound).astype(jnp.int32) for bound in bounds)


def k_squares(start_ref, *refs):
    out_ref = refs[-1]
    lane = lax.broadcasted_iota(jnp.int32, (1, 128), 1)
    out_ref[...] = jnp.zeros_like(out_ref)
    for k in range(2):
        squares = [jnp.sum(ref[...] * ref[...], axis=1, keepdims=True) for ref in refs[4 * k : 4 * k + 4]]
        total = jnp.zeros((1, 128), SINGLE)
        for which, bounds in enumerate((NARROW_BOUNDS, WIDE_BOUNDS)):
            group = group_of(squares[which].shape[0], start_ref[which], bounds)
            for g in range(len(bounds) + 1):
                part_sum = jnp.sum(jnp.where(group == g, squares[which], 0.0))
                total = total + jnp.where(lane == 4 * which + g, part_sum, 0.0)
        for rows, first in ((squares[2], 7), (squares[3], 15)):
            row = lax.broadcasted_iota(jnp.int32, (rows.shape[0], 128), 0)
            column = lax.broadcasted_iota(jnp.int32, (rows.shape[0], 128), 1)
            total = total + jnp.sum(jnp.where(column == row + first, rows, 0.0), axis=0, keepdims=True)
        out_ref[k : k + 1, :] = total


def k_update(start_ref, square_ref, *refs):
    step = pl.program_id(0)
    norms = jnp.sqrt(square_ref[0:8, :])
    weight_norm, grad_norm = norms[0:1], norms[1:2]
    ratio = TRUST * weight_norm / (grad_norm + DECAY * weight_norm)
    lane = lax.broadcasted_iota(jnp.int32, (1, 128), 1)
    for k in range(4):
        weight, grad = refs[k][...], refs[4 + k][...]
        rows = weight.shape[0]
        if k < 2:
            bounds = (NARROW_BOUNDS, WIDE_BOUNDS)[k]
            group = group_of(rows, start_ref[k] + step * rows, bounds)
            scale = jnp.zeros((rows, 1), SINGLE)
            for g in range(len(bounds) + 1):
                scale = jnp.where(group == g, jnp.sum(jnp.where(lane == 4 * k + g, ratio, 0.0)), scale)
        else:
            row = lax.broadcasted_iota(jnp.int32, (rows, 128), 0)
            column = lax.broadcasted_iota(jnp.int32, (rows, 128), 1)
            scale = jnp.sum(jnp.where(column == row + (7, 15)[k - 2], ratio, 0.0), axis=1, keepdims=True)
        moment = MOMENTUM * refs[8 + k][...] + RATE * scale * (grad + DECAY * weight)
        refs[12 + k][...] = moment
        refs[16 + k][...] = weight - moment


def full(shape):
    zeros = (0,) * len(shape)
    return pl.BlockSpec(tuple(shape), lambda *_: zeros, pipeline_mode=pl.Buffered(1))


SCALARS = pl.BlockSpec(memory_space=pltpu.SMEM)
ANYWHERE = pl.BlockSpec(memory_space=pl.ANY)


def spec(shape, index):
    return pl.BlockSpec(tuple(shape), index)


def call(kernel, name, grid, in_specs, out_specs, out_shape, scratch, args, prefetch=0, vmem=8, aliases=None):
    return pl.pallas_call(
        kernel,
        out_shape=out_shape,
        grid_spec=pltpu.PrefetchScalarGridSpec(
            num_scalar_prefetch=prefetch,
            grid=grid,
            in_specs=in_specs,
            out_specs=out_specs,
            scratch_shapes=scratch,
        ),
        input_output_aliases=aliases or {},
        compiler_params=pltpu.CompilerParams(vmem_limit_bytes=vmem * MIB),
        cost_estimate=pl.CostEstimate(flops=0, bytes_accessed=int(MICROSECONDS.get(name, 1) * BYTES_PER_US), transcendentals=0),
        name=name,
    )(*args)


def shape_of(shape, dtype=SINGLE):
    return jax.ShapeDtypeStruct(tuple(shape), dtype)


def vmem_of(shape, dtype=SINGLE):
    return pltpu.VMEM(tuple(shape), dtype)


def hbm_of(shape, dtype=SINGLE):
    return pltpu.HBM(tuple(shape), dtype)


def in_vmem(value):
    return pltpu.with_memory_space_constraint(value, pltpu.VMEM)


def in_hbm(value):
    return pltpu.with_memory_space_constraint(value, pltpu.HBM)


def permutation():
    table = np.zeros((4 * PIX, 4 * PIX), np.float32)
    for pi in range(2):
        for pj in range(2):
            for i in range(HB):
                for j in range(WB):
                    table[((2 * pi + pj) * WB + j) * HB + i, (2 * i + pi) * 2 * WB + 2 * j + pj] = 1.0
    return jnp.asarray(table, BFLOAT)


def rounded(value):
    return lax.reduce_precision(value, 8, 7)


def split_group(name, keep, got, rows, index):
    cols = keep.shape[1]

    def block(which, sent):
        def at(q, me):
            other, low, high = (q >> 2) & 1, (q >> 1) & 1, q & 1
            pair = other * 2 + sent if which == 0 else sent * 2 + other
            return (index(which, me[0] ^ (high * 8 + low * 4 + pair)), 0)

        return spec((rows, cols), at)

    blocks = [block(which, sent) for which in range(2) for sent in range(2)]
    return call(
        k_split, name, (8,), blocks + blocks,
        [spec((1, rows, cols), lambda q, me: (q, 0, 0))] * 4,
        [shape_of((8, rows, cols), BFLOAT)] * 4, [],
        (lax.axis_index("dp")[None].astype(jnp.int32),) + (keep,) * 4 + (got,) * 4, prefetch=1,
    )


def halved(state, came, merge):
    (keep0, _sent, keep1, _sent), (came0, came1) = state, came
    count, block = keep0.shape[0] // 2, keep0.shape[1:]
    low, high = (spec((1,) + block, lambda q, at=at: (q + at, 0, 0)) for at in (0, count))
    if merge:
        outs, out_spec = [vmem_of((2, count) + block, BFLOAT)] * 2, [spec((2, 1) + block, lambda q: (0, q, 0, 0))] * 2
    else:
        outs, out_spec = [vmem_of((count,) + block, BFLOAT)] * 4, [low] * 4
    return tuple(call(
        k_halve, "halve", (count,), [low, high] * 4, out_spec, outs, [], (keep0, keep0, came0, came0, keep1, keep1, came1, came1), vmem=4,
    ))


def halved_both(state, came):
    shape = state[0].shape
    half = (2, shape[1] // 2) + shape[2:]
    return tuple(call(
        k_halve_both, "halve", (1,), [full(shape)] * 2, [full(half)] * 2, [vmem_of(half, BFLOAT)] * 2, [], (state[0], came), vmem=4,
    ))


def added(state, came):
    total = state[0].astype(SINGLE) + came.astype(SINGLE)
    return total[0, 0], total[1, 0]


def scatter_plain(keep, got, block, by_rows):
    total = (keep.astype(SINGLE) + got.astype(SINGLE)).astype(BFLOAT)
    if by_rows:
        own = lax.psum_scatter(total, "dp", scatter_dimension=0, tiled=True).astype(SINGLE)
        return own[: block // 2], own[block // 2 :]
    middle = total.shape[0] // 2
    return tuple(lax.psum_scatter(p, "dp", scatter_dimension=0, tiled=True).astype(SINGLE) for p in (total[:middle], total[middle:]))


def joined(value, got):
    return jnp.concatenate([value, got], axis=0)


def gather_blocks(name, core, parts, others, out_shape):
    scalars = jnp.stack([lax.axis_index("dp"), core]).astype(jnp.int32)
    pieces = [a for pair in list(parts) + list(others) for a in pair]
    return call(
        k_gather, name, (), [ANYWHERE] * 8, ANYWHERE, vmem_of(out_shape, BFLOAT),
        [pltpu.SemaphoreType.DMA((64,))], (scalars, *pieces), prefetch=1, vmem=2,
    )


def swap_all(parts):
    return [tuple(swap_pipe(a) for a in pair) for pair in parts]


def join_parts(stayed, came, token, n_out):
    n_in = len(stayed)
    shape = stayed[0].shape[-3:]
    shape = (2 * shape[0],) + shape[1:]
    outs = [vmem_of(shape, BFLOAT)] * 2 if n_out == 2 else [vmem_of((2,) + shape, BFLOAT)]
    return call(
        functools.partial(k_join, n_in, n_out), "join", (), [ANYWHERE] * (2 * n_in + 1), [ANYWHERE] * n_out, outs,
        [pltpu.SemaphoreType.DMA((4,))], tuple(stayed) + tuple(came) + (token,), vmem=2,
    )


def keep_in_hbm(value):
    def filler(token):
        return call(
            k_keep, "keep", (), [ANYWHERE] * 2, ANYWHERE, hbm_of(value.shape, value.dtype),
            [pltpu.SemaphoreType.DMA], (in_vmem(value), token), vmem=2,
        )

    return filler


def nothing(token):
    return token


def both_of(*fillers):
    return lambda token: tuple(filler(token) for filler in fillers)


def on_device(images, cotangent, heights, widths, assign, w_narrow, w_wide, bn_mid, bn_wide, mom_narrow, mom_wide, mom_bn_mid, mom_bn_wide):
    core = lax.axis_index("pipe")
    shard = lax.axis_index(("pipe", "dp"))
    fast = lax.axis_size("dp") == 16

    own_narrow = w_narrow.astype(BFLOAT)
    own_wide = w_wide.astype(BFLOAT)
    rows_n, half_n = w_narrow.shape[0], C_MID // 2
    part_n = rows_n // 2
    whole_n = (R_N // 2, C_MID)
    if fast:
        sent = swap_pipe(jnp.where(core == 0, own_narrow[:, half_n:], own_narrow[:, :half_n]))
        kept = jnp.where(core == 0, own_narrow[:, :half_n], own_narrow[:, half_n:])
        mine_a, mine_b = jnp.where(core == 0, kept, sent), jnp.where(core == 0, sent, kept)
        a, b = (mine.reshape(2, 1, part_n, half_n) for mine in (mine_a, mine_b))
        (a,) = join_parts((a,), (exchange(a, 8),), a, 1)
        a0, a1 = join_parts((a,), (exchange(a, 4),), a, 2)
        b = pin(b, a1)
        got, got_b = lax.optimization_barrier(((exchange(a0, 2), exchange(a1, 1)), exchange(b, 8)))
        a0, a1 = join_parts((a0, a1), got, got[1], 2)
        (b,) = join_parts((b,), (got_b,), got_b, 1)
        stay_a = swap_all([(a0,), (a1,)])
        own_wide = pin(own_wide, a1)
        wide = lax.all_gather(own_wide, ("pipe", "dp"), axis=0, tiled=True)
    else:
        narrow = lax.all_gather(own_narrow, ("pipe", "dp"), axis=0, tiled=True)
        narrow_a, narrow_b = narrow[: R_N // 2], narrow[R_N // 2 :]
        wide = lax.all_gather(own_wide, ("pipe", "dp"), axis=0, tiled=True)

    perm = permutation()
    core_row = core[None].astype(jnp.int32)
    x, mask, count_rows = call(
        k_prep, "prep", (SLOTS,),
        [spec((1, 4 * PIX, C_IN), lambda s, core, order, *_: (order[0, core[0] * SLOTS + s], 0, 0)), full((4 * PIX, 4 * PIX))],
        [spec((4, PIX, C_IN), lambda s, *_: (0, s, 0)), spec((PIX, 1), lambda s, *_: (s, 0)), full((4, C_MID))],
        [vmem_of((4, ROWS, C_IN), BFLOAT), vmem_of((ROWS, 1)), shape_of((4, C_MID))], [],
        (core_row, assign, heights, widths, in_hbm(images.reshape(IMG_DEV, 4 * PIX, C_IN)), in_hbm(perm)), prefetch=4, vmem=7,
    )
    mask = in_vmem(mask)
    mid_cols, wide_cols = bn_mid.shape[1], bn_wide.shape[1]
    tables = jnp.concatenate(
        [
            lax.dynamic_update_slice(jnp.zeros((8, C_MID), SINGLE), rounded(bn_mid), (0, shard * mid_cols)),
            lax.dynamic_update_slice(jnp.zeros((6, C_OUT), SINGLE), rounded(bn_wide), (0, shard * wide_cols)).reshape(24, C_MID),
        ]
    )
    tables = tables + swap_pipe(tables)
    tables = jnp.concatenate([tables, count_rows])

    held = {}
    if fast:
        last0, last1, got_b, x, tables = lax.optimization_barrier((exchange(a0, 1), exchange(a1, 2), exchange(b, 4), x, tables))
        came_a = swap_all([(last0,), (last1,)])
        part_b = join_parts((b,), (got_b,), got_b, 2)
        narrow_a = gather_blocks("wa", core, [(a0, last0), (a1, last1)], [u + v for u, v in zip(stay_a, came_a)], whole_n)

    def turn(feature, feature_spec, grid, shape, index):
        def filler(token):
            return call(
                k_turn, "turn", grid, [feature_spec, ANYWHERE],
                spec((C_MID, ROWS), index), hbm_of(shape, BFLOAT), [], (feature, token),
            )

        return filler

    def weight_grad(name, feature, feature_spec, grad, grad_spec, tiles, shape, rows, base, bufs, token, space):
        out_spec = spec((rows, shape[1]), lambda t, slot: (base + t, 0))
        hold = in_vmem if space is vmem_of else in_hbm
        extra = tuple(hold(b) for b in bufs or ()) + (() if token is None else (token,))
        return call(
            k_grad, name, (tiles,), [feature_spec, grad_spec] + [ANYWHERE] * len(extra),
            [out_spec] * 2, [space(shape, BFLOAT)] * 2, [], (core_row, feature, grad) + extra,
            prefetch=1, vmem=7, aliases={3: 0, 4: 1} if bufs else {},
        )

    full_row = full((4, C_MID))
    full_table = full((TABLE_ROWS, C_MID))
    full_mask = full((ROWS, 1))
    full_mid = full((ROWS, C_MID))
    plane_pair = spec((2, ROWS, C_MID), lambda s: (jnp.minimum(s, 1), 0, 0))

    def narrow_block(index):
        return spec((TILE, TILE), index)

    chunk = spec((ROWS, TILE), lambda k, *_: (0, k))
    chunk_sum = spec((4, TILE), lambda k, *_: (0, k))
    chunk_eight = spec((8, TILE), lambda k, *_: (0, k))
    four_a = narrow_block(lambda k: (11, 0))
    four_b = narrow_block(lambda k: (jnp.maximum(k - 1, 0), 0))

    a1, part1 = call(
        k_first, "a1", (4,),
        [spec((1, ROWS, C_IN), lambda k: (k, 0, 0)), full((C_IN, C_MID))],
        [spec((1, ROWS, C_MID), lambda k: (k, 0, 0)), full_row],
        [hbm_of((4, ROWS, C_MID)), shape_of((4, C_MID))], [],
        (in_vmem(x), in_vmem(narrow_a)), vmem=6,
    )

    a1 = in_hbm(a1)
    def second_part_b(token):
        if not fast:
            return token
        part = pin(part_b, token)
        held["got"] = exchange(part[0], 2), exchange(part[1], 1)
        return token

    first_sum, (a_kept, (x_kept, first_b), _unused) = dp_sum(jnp.concatenate([part1, tables]), [keep_in_hbm(narrow_a), lambda token: (keep_in_hbm(x)(token), part_b if fast else token), second_part_b])
    x_kept, a_kept = in_hbm(x_kept), in_hbm(a_kept)
    base = in_vmem(first_sum.sum)

    a_s, part_s = call(
        k_short, "as", (4,),
        [spec((1, ROWS, C_IN), lambda k: (0, 0, 0)), spec((TILE, TILE), lambda k: (1, k)), spec((TILE, TILE), lambda k: (2, k))],
        [chunk, chunk_sum],
        [vmem_of((ROWS, C_OUT)), shape_of((4, C_OUT))], [],
        (in_vmem(x), in_hbm(wide), in_hbm(wide)), vmem=6,
    )

    def conv_weights(first, order_of):
        return [narrow_block(lambda s, kx=kx: (first + 3 * order_of(s) + kx, 0)) for kx in range(3)]

    turned = lambda s: lax.rem(s + 1, 3)
    straight = lambda s: s

    a2, h1, part2 = call(
        paired(k_conv_two, {}, {1: ("base", 0), 2: ("mid", 0)}, 0, 2), "a2", (3,),
        [SCALARS, full_table, full_table, full_mask, plane_pair] + conv_weights(2, turned),
        [full_mid, plane_pair, full_row],
        [vmem_of((ROWS, C_MID)), vmem_of((4, ROWS, C_MID), BFLOAT), shape_of((4, C_MID))],
        [pltpu.VMEM((2, PAD + ROWS + PAD, C_MID), SINGLE)] * 2,
        (core_row, *first_sum.parts, mask, a1) + (a_kept,) * 3, vmem=11,
    )
    a2 = in_vmem(a2)

    def third_part_b(token):
        if not fast:
            return token
        held["big_b"] = join_parts(first_b, pin(held["got"], token), token, 2)
        return held["big_b"]

    def fourth_b(token):
        if fast:
            big = pin(held["big_b"], token)
            held["got"] = exchange(big[0], 1), exchange(big[1], 2)
        return token

    turn_h1 = turn(h1, spec((1, ROWS, C_MID), lambda k: (k, 0, 0)), (4,), (4 * C_MID, ROWS), lambda k: (k, 0))
    total2, (h1_t, big_b, _unused) = dp_sum(part2, [turn_h1, third_part_b, fourth_b])

    def expand(name, a, total, which, row):
        return call(
            paired(k_expand, {1: ONE}, {2: ("mid", which)}, 0), name, (4,),
            [SCALARS, full_table, full_row, full_row, full_mask, full_mid, spec((TILE, TILE), lambda k: (row, k))],
            [full_mid, chunk, chunk_sum],
            [vmem_of((ROWS, C_MID), BFLOAT), vmem_of((ROWS, C_OUT)), shape_of((4, C_OUT))], [],
            (core_row, base, *total.parts, mask, a, in_hbm(wide)), vmem=6,
        )

    h2, a3, part3 = expand("a3", a2, total2, 1, 0)
    whole = spec((ROWS, C_MID), lambda k: (0, 0))

    def swap_b(token):
        if not fast:
            return token
        ready = pin(tuple(big_b) + held["got"], token)
        return [(ready[0], ready[2]), (ready[1], ready[3])]

    def gather_b(token):
        if not fast:
            return narrow_b
        others = pin(held["others"], token)
        return gather_blocks("wb", core, held["parts"], others, whole_n)

    def start_swap_b(token):
        if fast:
            held["parts"] = swap_b(token)
            held["others"] = swap_all(held["parts"])
        return token

    total3s, ((h2_t, as_kept), (_unused, a3_kept), _unused, narrow_b) = dp_sum(
        jnp.concatenate([part3, part_s]),
        [
            both_of(turn(h2, whole, (1,), (C_MID, ROWS), lambda k: (0, 0)), keep_in_hbm(a_s)),
            both_of(start_swap_b, keep_in_hbm(a3)),
            nothing,
            gather_b,
        ],
    )
    as_kept, a3_kept = in_hbm(as_kept), in_hbm(a3_kept)

    y, a4, part4 = call(
        paired(k_meet, {1: (0, 4)}, {3: ("wide", 0), 4: ("wide", 1)}, 0), "a4", (4,),
        [SCALARS, full_table, chunk_eight, chunk_eight, full_mask, chunk, chunk, four_a, four_b],
        [chunk, full_mid, full_row],
        [vmem_of((ROWS, C_OUT), BFLOAT), vmem_of((ROWS, C_MID)), shape_of((4, C_MID))], [],
        (core_row, base, *total3s.parts, mask, in_vmem(a3), in_vmem(a_s), a_kept, in_vmem(narrow_b)), vmem=8,
    )
    a4 = in_vmem(a4)
    def turn_x(q, start, into):
        def filler(token):
            extra = () if into is None else (in_hbm(into[-1]),)
            held["x_t"] = call(
                k_turn, "turn", (2,), [spec((1, ROWS, C_MID), lambda k: (start + k, 0, q))] + [ANYWHERE] * (1 + len(extra)),
                spec((C_MID, ROWS), lambda k: (q, start + k)), hbm_of((C_IN, 4 * ROWS), BFLOAT), [], (x_kept, *extra, token),
                aliases={1: 0} if extra else {},
            )
            return held["x_t"]

        return filler

    total4, (y_t, y_kept, x_t0, x_t1) = dp_sum(
        part4,
        [
            turn(in_vmem(y), spec((ROWS, C_MID), lambda k: (0, k)), (4,), (4 * C_MID, ROWS), lambda k: (k, 0)),
            keep_in_hbm(y),
            turn_x(0, 0, None),
            lambda token: turn_x(0, 2, [held["x_t"]])(token),
        ],
    )
    del x_t0

    a5, h4, part5 = call(
        paired(k_conv_one, {1: ONE}, {2: ("mid", 2)}, 0), "a5", (3,),
        [SCALARS, full_table, full_row, full_row, full_mask, full_mid] + conv_weights(3, straight),
        [full_mid, full_mid, full_row],
        [vmem_of((ROWS, C_MID)), vmem_of((ROWS, C_MID), BFLOAT), shape_of((4, C_MID))],
        [pltpu.VMEM((PAD + ROWS + PAD, C_MID), SINGLE)] * 2,
        (core_row, base, *total4.parts, mask, a4) + (in_vmem(narrow_b),) * 3, vmem=8,
    )
    a5 = in_vmem(a5)
    total5, (h4_t, b_kept, _unused, x_t) = dp_sum(
        part5,
        [
            turn(h4, whole, (1,), (C_MID, ROWS), lambda k: (0, 0)),
            keep_in_hbm(narrow_b),
            turn_x(1, 0, [x_t1]),
            lambda token: turn_x(1, 2, [held["x_t"]])(token),
        ],
    )
    b_kept = in_hbm(b_kept)
    h5, a6, part6 = expand("a6", a5, total5, 3, 3)
    total6, (h5_t, a6_kept) = dp_sum(part6, [turn(h5, whole, (1,), (C_MID, ROWS), lambda k: (0, 0)), keep_in_hbm(a6)])
    a6_kept = in_hbm(a6_kept)

    cot = in_hbm(cotangent.transpose(0, 2, 1, 3).reshape(IMG_DEV, PIX, C_OUT))
    blk, gz6, s6 = call(
        paired(k_head, {2: ONE}, {3: ("wide", 2)}, 1, lead=1), "head", (4,),
        [full_table, chunk_sum, chunk_sum, full_mask, chunk, chunk]
        + [spec((1, PIX, TILE), lambda k, core, order, s=s: (order[0, core[0] * SLOTS + s], 0, k)) for s in range(SLOTS)],
        [
            spec((1, ROWS, TILE), lambda k, core, _order: ((k // 2) ^ core[0], 0, lax.rem(k, 2))),
            chunk,
            chunk_sum,
        ],
        [shape_of((2, ROWS, C_OUT // 2), BFLOAT), vmem_of((ROWS, C_OUT)), shape_of((4, C_OUT))], [],
        (core_row, assign, base, *total6.parts, mask, in_vmem(a6), in_hbm(y_kept), cot, cot, cot, cot), prefetch=2, vmem=9,
    )
    gz6 = in_vmem(gz6)

    def place(name, pair, got, token):
        block = (1,) + pair.shape[2:]
        return call(
            k_place, name, (IMG_DEV,),
            [
                spec((1,) + block, lambda t, *_: (0, jnp.minimum(t, SLOTS - 1), 0, 0)),
                spec(block, lambda t, *_: (jnp.maximum(t - SLOTS, 0), 0, 0)),
                ANYWHERE,
            ],
            spec(block, lambda t, core, order: (order[0, (core[0] * SLOTS + t) & (IMG_DEV - 1)], 0, 0)),
            shape_of((IMG_DEV,) + pair.shape[2:], BFLOAT), [],
            (core_row, assign, pair, got, token), prefetch=2, vmem=9,
        )

    blk = blk.reshape(2, SLOTS, PIX, C_OUT // 2)
    sum6, (got_blk, _unused, _unused, block_local) = dp_sum(
        s6,
        [
            lambda token: swap_pipe(pin(blk[1], token)),
            lambda token: token,
            lambda token: token,
            lambda token: token,
        ],
    )

    ga6, gz5, s5 = call(
        paired(k_back_six, {3: ONE, 4: ONE, 9: ONE}, {5: ("wide", 2), 10: ("mid", 3)}, 0), "g5", (4,),
        [SCALARS, full_table, chunk, chunk, chunk_sum, chunk_sum, chunk_sum, chunk_sum, full_mask, spec((TILE, TILE), lambda k: (3, k)), full_mid,
         full_row, full_row],
        [chunk, full_mid, full_row],
        [vmem_of((ROWS, C_OUT), BFLOAT), vmem_of((ROWS, C_MID)), shape_of((4, C_MID))],
        [pltpu.VMEM((ROWS, C_MID), SINGLE)],
        (core_row, base, gz6, a6_kept, *total6.parts, *sum6.parts, mask, in_hbm(wide), a5, *total5.parts), vmem=9,
    )
    gz5 = in_vmem(gz5)

    def wide_rows(k):
        return spec((1, 256, ROWS), lambda t, slot: (0, t + k, 0))

    def whole_wide(grad):
        return grad.reshape((1,) + grad.shape), full((1,) + grad.shape)

    wide_shape, narrow_shape = (R_W, C_OUT // 2), (R_N // 2, C_MID // 2)
    sum5, (bufs_w, block_local) = dp_sum(
        s5,
        [
            lambda token: weight_grad("dw6", h5_t[None], wide_rows(0), *whole_wide(ga6), 2, wide_shape, 256, 6, None, token, vmem_of),
            lambda token: place("place_out", blk, got_blk, token),
        ],
    )
    block_local = block_local.reshape(IMG_DEV, WB, HB, C_OUT // 2).transpose(0, 2, 1, 3)

    col5, gz4, s4 = call(
        paired(k_back_conv_one, {3: ONE, 4: ONE, 11: ONE}, {5: ("mid", 3), 12: ("mid", 2)}, 0), "g4", (3,),
        [SCALARS, full_table, full_mid, full_mid, full_row, full_row, full_row, full_row, full_mask] + conv_weights(3, straight)
        + [full_mid, full_row, full_row],
        [spec((3, ROWS, C_MID), lambda s: (s, 0, 0)), full_mid, full_row],
        [vmem_of((9, ROWS, C_MID), BFLOAT), vmem_of((ROWS, C_MID)), shape_of((4, C_MID))],
        [pltpu.VMEM((PAD + ROWS + PAD, C_MID), SINGLE)] * 2 + [pltpu.VMEM((ROWS, C_MID), SINGLE)],
        (core_row, base, gz5, a5, *total5.parts, *sum5.parts, mask, b_kept, b_kept, b_kept, a4, *total4.parts), vmem=10,
    )
    gz4 = in_vmem(gz4)
    one_turned = spec((1, C_MID, ROWS), lambda t, slot: (0, 0, 0))
    held_b = []

    def grad_five(k):
        def filler(token):
            grad_spec = spec((3, ROWS, C_MID), lambda t, slot: (k, 0, 0))
            held_b[:] = weight_grad("dw5", h4_t[None], one_turned, in_vmem(col5), grad_spec, 1, narrow_shape, 3 * TILE, 1 + k, list(held_b), token, vmem_of)
            return tuple(held_b)

        return filler

    sum4, results4 = dp_sum(s4, [grad_five(k) for k in range(3)])
    bufs_b = results4[2]

    ga4, gj, s3 = call(
        paired(k_back_four, {3: ONE, 4: ONE, 12: (0, 4)}, {5: ("mid", 2), 14: ("wide", 0), 15: ("wide", 1)}, 0), "gy", (4,),
        [SCALARS, full_table, full_mid, full_mid, full_row, full_row, full_row, full_row, full_mask, four_a, four_b,
         chunk, chunk, chunk, chunk_eight, chunk_eight],
        [full_mid, chunk, spec((6, TILE), lambda k: (0, k))],
        [vmem_of((ROWS, C_MID), BFLOAT), vmem_of((ROWS, C_OUT)), shape_of((6, C_OUT))], [],
        (core_row, base, gz4, a4, *total4.parts, *sum4.parts, mask, a_kept, b_kept, gz6, a3_kept, as_kept, *total3s.parts), vmem=12,
    )
    gj = in_vmem(gj)

    by_rows = lambda which, m: 2 * m + which

    def grad_four(token):
        y_tiles = y_t.reshape(4, C_MID, ROWS)
        one = full((1, ROWS, C_MID))
        grad = in_vmem(ga4.reshape(1, ROWS, C_MID))
        held["grad_b"] = weight_grad("dw4b", y_tiles, spec((1, C_MID, ROWS), lambda t, slot: (1 + t, 0, 0)), grad, one, 3, narrow_shape, TILE, 0, bufs_b, token, vmem_of)
        return held["grad_b"]

    def grad_four_first(token):
        return weight_grad(
            "dw4a", y_t.reshape(4, C_MID, ROWS), spec((1, C_MID, ROWS), lambda t, slot: (0, 0, 0)), in_vmem(ga4.reshape(1, ROWS, C_MID)),
            full((1, ROWS, C_MID)), 1, narrow_shape, TILE, 11, None, token, vmem_of,
        )

    def swap_grad_b(token):
        held["got_b"] = swap_pipe(pin(held["grad_b"][1], token))
        return token

    def split_b(token):
        if not fast:
            return token
        keep, got = pin((held["grad_b"][0], held["got_b"]), token)
        state = split_group("split_b", in_vmem(keep), got, part_n, by_rows)
        held["came_b"] = exchange(state[1], 1), exchange(state[3], 2)
        return state

    sum3, results3 = dp_sum(s3, [grad_four, both_of(swap_grad_b, grad_four_first), split_b])
    bufs_b, bufs_a = results3[0], results3[1][1]
    held["b"] = results3[2]

    ga3, gas, gz2, s2 = call(
        paired(k_back_three, {4: (0, 4), 6: ONE, 12: ONE}, {7: ("wide", 0), 8: ("wide", 1), 13: ("mid", 1)}, 0), "g2", (4,),
        [SCALARS, full_table, chunk, chunk, chunk, chunk_eight, chunk_eight, spec((6, TILE), lambda k: (0, k)), spec((6, TILE), lambda k: (0, k)), full_mask,
         spec((TILE, TILE), lambda k: (0, k)), full_mid, full_row, full_row],
        [chunk, chunk, full_mid, full_row],
        [vmem_of((ROWS, C_OUT), BFLOAT), vmem_of((ROWS, C_OUT), BFLOAT), vmem_of((ROWS, C_MID)), shape_of((4, C_MID))],
        [pltpu.VMEM((ROWS, C_MID), SINGLE)],
        (core_row, base, gj, a3_kept, as_kept, *total3s.parts, *sum3.parts, mask, in_hbm(wide), a2, *total2.parts), vmem=11,
    )
    gz2 = in_vmem(gz2)

    def second_b(token):
        if not fast:
            return token
        state = halved(held["b"], pin(held["came_b"], token), False)
        held["came_b"] = exchange(state[1], 2), exchange(state[3], 1)
        return state

    def third_exchange_b(token):
        if not fast:
            return token
        state = halved(held["b"], pin(held["came_b"], token), True)
        held["came_b"] = exchange(state[1], 4)
        return state

    def fourth_exchange_b(token):
        if not fast:
            return token
        state = halved_both(held["b"], pin(held["came_b"], token))
        held["came_b"] = exchange(state[1], 8)
        return state

    def grad_three(token):
        held["w"] = weight_grad("dw3", h2_t[None], wide_rows(0), *whole_wide(ga3), 2, wide_shape, 256, 0, bufs_w, token, vmem_of)
        return held["w"]

    def grad_short(q):
        def filler(token):
            held["w"] = weight_grad("dws", x_t[None], wide_rows(2 * q), *whole_wide(gas), 2, wide_shape, 256, 2 + 2 * q, held["w"], token, vmem_of)
            return held["w"]

        return filler

    def start_swap_w(token):
        held["got_w"] = swap_pipe(pin(held["w"][1], token))
        return token

    def two_grads(token):
        grad_three(token)
        return grad_short(0)(token)

    sum2, results2 = dp_sum(s2, [two_grads, both_of(second_b, grad_short(1)), start_swap_w])
    held["b"], bufs_w = results2[1]
    got_w = held["got_w"]
    if fast:
        split = split_group("split_w", bufs_w[0], pin(got_w, sum2.parts[1]), w_wide.shape[0], lambda which, m: 16 * which + m)
        last, split, held["b"] = lax.optimization_barrier((sum2.parts[1], split, third_exchange_b(sum2.parts[1])))
        sum2 = Total(sum2.parts[0], last)
        held["came"] = exchange(split[1], 1), exchange(split[3], 2)

    col2, gz1, s1 = call(
        paired(k_back_conv_two, {3: ONE, 4: ONE}, {5: ("mid", 1), 11: ("base", 0), 12: ("mid", 0)}, 0), "g1", (3,),
        [SCALARS, full_table, full_mid, full_mid, full_row, full_row, full_row, full_row, full_mask] + conv_weights(2, turned)
        + [plane_pair],
        [spec((3, ROWS, C_MID), lambda s: (turned(s), 0, 0)), plane_pair, full_row],
        [vmem_of((9, ROWS, C_MID), BFLOAT), vmem_of((4, ROWS, C_MID)), shape_of((4, C_MID))],
        [pltpu.VMEM((PAD + ROWS + PAD, C_MID), SINGLE)] * 2 + [pltpu.VMEM((2, ROWS, C_MID), SINGLE)],
        (core_row, base, gz2, a2, *total2.parts, *sum2.parts, mask, a_kept, a_kept, a_kept, a1), vmem=12,
    )
    gz1 = in_vmem(gz1)
    h1_planes = h1_t.reshape(4, C_MID, ROWS)

    def grad_two(row):
        def filler(token):
            first = 2 * (1 - (row & 1))
            held["a"] = weight_grad(
                "dw2", h1_planes, spec((1, C_MID, ROWS), lambda t, slot: (first + (1 - (t & 1)), 0, 0)), in_vmem(col2),
                spec((1, ROWS, C_MID), lambda t, slot: (3 * row + t, 0, 0)), 3, narrow_shape, TILE, 2 + 3 * row, held["a"], token, vmem_of,
            )
            return held["a"]

        return filler

    def wide_back(token):
        return call(
            k_wide_back, "dxs", (2,),
            [full((ROWS, C_OUT)), spec((TILE, C_OUT), lambda k: (1 + k, 0)), ANYWHERE],
            spec((ROWS, TILE), lambda k: (0, k)),
            hbm_of((ROWS, C_IN)), [],
            (gas, in_hbm(wide), token), vmem=8,
        )

    def first_w(token):
        if not fast:
            return token
        came = pin(held["came"], token)
        state = halved(split, came, False)
        held["came_w"] = exchange(state[1], 2), exchange(state[3], 1)
        return state

    held["a"] = bufs_a
    sum1, results1 = dp_sum(s1, [grad_two(0), grad_two(1), both_of(fourth_exchange_b, grad_two(2)), first_w], 4)
    held["b"], bufs_a = results1[2]
    state_w = results1[3]
    state_b = held["b"]
    plane = spec((1, ROWS, C_MID), lambda k: (k, 0, 0))
    ga1 = call(
        paired(k_first_grad, {4: ONE}, {3: ("base", 0), 5: ("mid", 0)}, 0), "g0", (4,),
        [SCALARS, full_table, plane, plane, full_row, full_row, full_mask], plane,
        vmem_of((4, ROWS, C_MID), BFLOAT), [], (core_row, base, gz1, a1, *sum1.parts, mask),
    )
    flat_ga1 = in_vmem(ga1.reshape(1, 4 * ROWS, C_MID))
    bufs_a = weight_grad(
        "dw1", x_t.reshape(2, C_MID, 4 * ROWS), spec((1, C_MID, 4 * ROWS), lambda t, slot: (t, 0, 0)), flat_ga1, full((1, 4 * ROWS, C_MID)),
        2, narrow_shape, TILE, 0, bufs_a, None, vmem_of,
    )
    got_a = swap_pipe(bufs_a[1])
    sums = [sum1, sum2, sum3, sum4, sum5, sum6]

    def image_grads(token, dxs):
        pair = call(
            k_image_grad, "gx", (SLOTS,),
            [spec((4, PIX, C_MID), lambda s, slot: (0, s, 0)), spec((PIX, 1), lambda s, slot: (s, 0)), full((C_IN, C_MID)),
             spec((PIX, C_IN), lambda s, slot: (s, 0)), full((4 * PIX, 4 * PIX)), ANYWHERE],
            spec((2, 1, 4 * PIX, C_IN // 2), lambda s, slot: (0, s, 0, 0)),
            shape_of((2, SLOTS, 4 * PIX, C_IN // 2), BFLOAT), [],
            (core_row, in_vmem(ga1), mask, a_kept, in_hbm(dxs), in_hbm(perm), token), prefetch=1, vmem=9,
        )
        return pair, swap_pipe(pair[1])

    def table_grads(sums):
        sum1, sum2, sum3, sum4, sum5, sum6 = (t.sum for t in sums)

        def pair_sum(rows):
            return rows[0] + rows[1]

        mid_rows = jnp.stack([pair_sum(v) for t in (sum1, sum2, sum4, sum5) for v in (t[2:4], t[0:2])])
        wide_rows = jnp.stack([pair_sum(v) for v in (sum3[2:4], sum3[0:2], sum3[4:6], sum3[0:2], sum6[2:4], sum6[0:2])])
        mid_rows = mid_rows + swap_pipe(mid_rows)
        wide_rows = wide_rows + swap_pipe(wide_rows)
        return lax.dynamic_slice(mid_rows, (0, shard * mid_cols), (8, mid_cols)), lax.dynamic_slice(wide_rows, (0, shard * wide_cols), (6, wide_cols))

    if fast:
        state_w = halved(state_w, held["came_w"], True)
        got_a, state_w, came_b = lax.optimization_barrier((got_a, state_w, held["came_b"]))
        came_w = exchange(state_w[1], 4)
        state_a = split_group("split_a", in_vmem(bufs_a[0]), got_a, part_n, by_rows)
        came_a = exchange(state_a[1], 1), exchange(state_a[3], 2)
        dxs = wide_back(state_a[0])
        state_w = halved_both(state_w, came_w)
        pair, got_pair = image_grads(state_w[0], dxs)
        came_a, state_w, pair = lax.optimization_barrier((came_a, state_w, pair))
        came_w = exchange(state_w[1], 8)
        state_a = halved(state_a, came_a, False)
        came_a = exchange(state_a[1], 2), exchange(state_a[3], 1)
        half_w0, half_w1 = added(state_w, came_w)
        half_b = jnp.concatenate(added(state_b, came_b), axis=0)
        came_a, half_w0, half_w1, half_b = lax.optimization_barrier((came_a, half_w0, half_w1, half_b))
        state_a = halved(state_a, came_a, True)
        came_a = exchange(state_a[1], 4)
        grad_local = place("place_grad", pair, got_pair, state_a[0])
        came_a, grad_local = lax.optimization_barrier((came_a, grad_local))
        state_a = halved_both(state_a, came_a)
        came_a = exchange(state_a[1], 8)
        sums = pin(tuple(t.parts for t in sums), state_a[0])
        grad_mid, grad_table = table_grads([Total(*parts) for parts in sums])
        came_a, grad_mid, grad_table = lax.optimization_barrier((came_a, grad_mid, grad_table))
        half_a = jnp.concatenate(added(state_a, came_a), axis=0)
    else:
        half_a = jnp.concatenate(scatter_plain(bufs_a[0], got_a, rows_n, True), axis=0)
        half_w0, half_w1 = scatter_plain(bufs_w[0], got_w, w_wide.shape[0], False)
        half_b = jnp.concatenate(scatter_plain(bufs_b[0], held["got_b"], rows_n, True), axis=0)
        pair, got_pair = image_grads(ga1, wide_back(ga1))
        grad_local = place("place_grad", pair, got_pair, ga1)
        grad_mid, grad_table = table_grads(sums)
    grad_local = grad_local.reshape(IMG_DEV, 2 * HB, 2 * WB, C_IN // 2)

    def join_halves(first, second):
        mine = jnp.where(core == 0, first, second)
        got = swap_pipe(jnp.where(core == 0, second, first))
        return jnp.where(core == 0, jnp.concatenate([mine, got], axis=1), jnp.concatenate([got, mine], axis=1))

    grad_narrow = join_halves(half_a, half_b)
    grad_wide = join_halves(half_w0, half_w1)

    starts = (shard * jnp.array([rows_n, w_wide.shape[0]])).astype(jnp.int32)
    weights, grads = (w_narrow, w_wide, bn_mid, bn_wide), (grad_narrow, grad_wide, grad_mid, grad_table)
    whole_specs = [full(v.shape) for v in weights]
    squares = call(
        k_squares, "squares", (1,), whole_specs * 2, full((8, 128)), shape_of((8, 128)), [], (starts, *weights, *grads), prefetch=1, vmem=10,
    )
    squares, _unused = dp_sum(squares + swap_pipe(squares))
    parts = 4 if rows_n % 64 == 0 and w_wide.shape[0] % 64 == 0 else 1
    specs = [spec((v.shape[0] // parts, v.shape[1]), lambda k, *_: (k, 0)) for v in weights[:2]] + whole_specs[2:]
    updated = call(
        paired(k_update, {1: ONE}), "update", (parts,), [full((8, 128))] * 2 + specs * 3, specs * 2, [shape_of(v.shape) for v in weights] * 2, [],
        (starts, *squares.parts, *weights, *grads, mom_narrow, mom_wide, mom_bn_mid, mom_bn_wide), prefetch=1, vmem=12,
    )
    new_mom_narrow, new_mom_wide, new_mom_mid, new_mom_table, new_narrow, new_wide, new_mid, new_table = updated
    return (
        block_local, grad_local, grad_narrow, grad_wide, grad_mid, grad_table,
        new_mom_narrow, new_mom_wide, new_mom_mid, new_mom_table,
        new_narrow, new_wide, new_mid, new_table,
    )


def solution(mesh):
    rows = P(("pipe", "dp"), None)
    columns = P(None, ("pipe", "dp"))
    feature = P("dp", None, None, None)
    return jax.shard_map(
        on_device,
        mesh=mesh,
        in_specs=(feature, feature, P("dp"), P("dp"), P("dp", None), rows, rows, columns, columns, rows, rows, columns, columns),
        out_specs=(P("dp", None, None, "pipe"), P("dp", None, None, "pipe"), rows, rows, columns, columns, rows, rows, columns, columns, rows, rows, columns, columns),
        check_vma=False,
    )
```

```python
import functools

import jax
import jax.numpy as jnp
import numpy as np
from jax import lax
from jax.experimental import pallas as pl
from jax.experimental.pallas import tpu as pltpu
from jax.sharding import PartitionSpec as P

C_IN = 1024
C_MID = 512
C_OUT = 2048
R_N = 12288
R_W = 2048
HB = 8
WB = 12
IMG_DEV = 8
SLOTS = 4
PIX = HB * WB
ROWS = SLOTS * PIX
HALF = ROWS // 2
PAD = 16
TILE = 512

EPS = 1e-05
MOMENTUM = 0.9
DECAY = 5e-05
TRUST = 0.001
RATE = 29.0
NARROW_BOUNDS = (C_IN, C_IN + 9 * C_MID, C_IN + 9 * C_MID + C_OUT)
WIDE_BOUNDS = (C_MID, C_MID + C_IN)
BFLOAT = jnp.bfloat16
SINGLE = jnp.float32
MIB = 1024 * 1024
BYTES_PER_US = 600000
MICROSECONDS = {
    "prep": 5, "a1": 3, "a2": 5, "as": 4.5, "a3": 4, "a4": 4.7, "a5": 4, "a6": 3.7, "head": 5.3, "g5": 5.2, "g4": 5.4, "gy": 7,
    "g2": 7.3, "g1": 8, "g0": 3, "gx": 6.4, "dxs": 5, "dw1": 3.4, "dw2": 2.1, "dw3": 2.9, "dws": 2.9, "dw4a": 1.7, "dw4b": 1.9,
    "dw5": 1.5, "dw6": 2.8, "place_out": 3.4, "place_grad": 5, "wa": 3, "wb": 3, "turn": 1.7, "keep": 1.7, "halve": 1, "squares": 2, "update": 3,
}


def pairs(bit):
    return [(i, i ^ bit) for i in range(lax.axis_size("dp"))]


def exchange(value, bit):
    return lax.ppermute(value, "dp", pairs(bit))


def pin(value, after):
    return lax.optimization_barrier((value, after))[0]


class Total:
    def __init__(self, *parts):
        self.parts = parts

    @property
    def sum(self):
        return self.parts[0] + self.parts[1]


def dp_sum(value, fillers=(), first=None):
    size = lax.axis_size("dp")
    bits = [1 << k for k in range(size.bit_length() - 1)]
    if first in bits:
        at = bits.index(first)
        bits = bits[at:] + bits[:at]
    results = []
    for bit in bits:
        got = exchange(value, bit)
        if len(results) < len(fillers):
            result = fillers[len(results)](value)
            got, result = lax.optimization_barrier((got, result))
            results.append(result)
        if bit == bits[-1]:
            break
        value = value + got
    for filler in fillers[len(results) :]:
        results.append(filler(got))
    return Total(value, got), results


def swap_pipe(value):
    return lax.ppermute(value, "pipe", [(0, 1), (1, 0)])


def dot(left, right):
    return jnp.dot(left, right, preferred_element_type=SINGLE)


def dot_back(left, right):
    return lax.dot_general(left, right, (((1,), (1,)), ((), ())), preferred_element_type=SINGLE)


def silu(value):
    return value * jax.nn.sigmoid(value)


def slope(value):
    gate = jax.nn.sigmoid(value)
    return gate * (1.0 + value * (1.0 - gate))


def put_sums(ref, values, first):
    for k, value in enumerate(values):
        for m in range(2):
            total = jnp.sum(value[m * HALF : (m + 1) * HALF], axis=0, keepdims=True)
            row = 2 * k + m
            ref[row : row + 1, :] = total if first else ref[row : row + 1, :] + total


def both(function):
    return jnp.concatenate([function(0), function(1)], axis=0)


def part(m):
    return slice(m * HALF, (m + 1) * HALF)


def moments(total_ref, inv_ref, m, scale=1.0):
    inv = inv_ref[m] * scale
    mean = total_ref[m : m + 1, :] * inv
    var = total_ref[2 + m : 3 + m, :] * inv - mean * mean
    return mean, lax.rsqrt(var + EPS)


def normed(a, total_ref, inv_ref, m, scale=1.0):
    mean, rstd = moments(total_ref, inv_ref, m, scale)
    return (a - mean) * rstd, rstd


def conv_grad(gz, xhat, rstd, gain, mask, sum_ref, inv_ref, m, scale=1.0, second=2):
    inv = inv_ref[m] * scale
    first_row = sum_ref[m : m + 1, :] * inv
    second_row = sum_ref[second + m : second + m + 1, :] * inv
    return (mask * ((rstd * gain) * (gz - first_row - xhat * second_row))).astype(BFLOAT)


class Both:
    def __init__(self, refs, start=0):
        self.refs, self.start = refs, start

    def __getitem__(self, index):
        rows, columns = index
        rows = slice(rows.start + self.start, rows.stop + self.start)
        return sum(ref[rows, columns] for ref in self.refs)


class Chunk:
    def __init__(self, refs, which, step):
        self.refs, self.first = refs, WIDE_ROW + 8 * which + step

    def __getitem__(self, index):
        rows, columns = index
        return sum(ref[pl.ds(self.first + 4 * rows.start, 1), columns] for ref in self.refs)


class Inverse:
    def __init__(self, refs, core):
        self.refs, self.core = refs, core

    def __getitem__(self, m):
        row = sum(ref[COUNT_ROW : COUNT_ROW + 1, 0:128] for ref in self.refs)
        lane = lax.broadcasted_iota(jnp.int32, (1, 128), 1)
        return 1.0 / jnp.sum(jnp.where(lane == 2 * self.core + m, row, 0.0), axis=1, keepdims=True)


ONE = (0,)
MID_ROW, WIDE_ROW, COUNT_ROW, TABLE_ROWS = 4, 12, 36, 40


def paired(kernel, views, tabs=None, inv=None, tables=1, lead=0):
    def run(*refs):
        fixed, refs = {}, list(refs)
        if inv is not None:
            core = refs.pop(0)[0]
            table, refs[lead : lead + tables] = refs[lead : lead + tables], []
            step = pl.program_id(0)
            fixed[inv] = Inverse(table, core)
            for at, (kind, which) in (tabs or {}).items():
                if kind == "wide":
                    fixed[at] = Chunk(table, which, step)
                else:
                    fixed[at] = Both(table, MID_ROW + 2 * which if kind == "mid" else 0)
        given, at = [], 0
        while at < len(refs) or len(given) in fixed:
            if len(given) in fixed:
                given.append(fixed[len(given)])
            elif len(given) in views:
                given.extend([Both(refs[at : at + 2], start) for start in views[len(given)]])
                at += 2
            else:
                given.append(refs[at])
                at += 1
        return kernel(*given)

    return run


def k_prep(core_ref, assign_ref, height_ref, width_ref, img_ref, perm_ref, out_ref, mask_ref, count_ref):
    slot = pl.program_id(0)
    image = assign_ref[0, core_ref[0] * SLOTS + slot]
    pixel = lax.broadcasted_iota(jnp.int32, (PIX, 1), 0)
    inside = ((pixel & (HB - 1)) < height_ref[image]) & (pixel < width_ref[image] * HB)
    mask = jnp.where(inside, 1.0, 0.0).astype(SINGLE)
    mask_ref[...] = mask
    planes = dot(perm_ref[...], img_ref[0])
    for k in range(4):
        out_ref[k] = (planes[k * PIX : (k + 1) * PIX] * mask).astype(BFLOAT)
    column = lax.broadcasted_iota(jnp.int32, count_ref.shape, 1)
    counts = jnp.zeros(count_ref.shape, jnp.int32)
    for m in range(4):
        pair = (assign_ref[0, 2 * m], assign_ref[0, 2 * m + 1])
        total = sum(height_ref[k] * width_ref[k] for k in pair)
        counts = jnp.where(column == m, total, counts)
    count_ref[...] = counts.astype(SINGLE)


def k_first(x_ref, w_ref, a_ref, sum_ref):
    a = dot(x_ref[0], w_ref[...])
    a_ref[0] = a

    @pl.when(pl.program_id(0) == 0)
    def _():
        sum_ref[...] = jnp.zeros_like(sum_ref)

    put_sums(sum_ref, [a, a * a], False)


def shift_mask(di, dj):
    if not di and not dj:
        return None
    pixel = lax.broadcasted_iota(jnp.int32, (SLOTS, PIX, 1), 1)
    inside = None
    if di:
        row = pixel & (HB - 1)
        inside = row >= -di if di < 0 else row < HB - di
    if dj:
        column = pixel >= -dj * HB if dj < 0 else pixel < PIX - dj * HB
        inside = column if inside is None else inside & column
    return jnp.where(inside, 1.0, 0.0).astype(SINGLE).reshape(ROWS, 1)


def rows_at(pad, di, dj):
    start = PAD + HB * dj + di
    rows = pad[start : start + ROWS, :]
    mask = shift_mask(di, dj)
    return rows if mask is None else rows * mask


def clear_pad(pad):
    pad[0:PAD, :] = jnp.zeros((PAD, pad.shape[1]), SINGLE)
    pad[PAD + ROWS : PAD + ROWS + PAD, :] = jnp.zeros((PAD, pad.shape[1]), SINGLE)


def body(pad, m):
    return pad.at[PAD + m * HALF : PAD + (m + 1) * HALF, :]


def carried(ref, fresh):
    return jnp.where(fresh, 0.0, ref[...])


def k_conv_two(inv_ref, total_ref, tab_ref, mask_ref, a_ref, w0, w1, w2, out_ref, h_ref, sum_ref, pad, moved):
    step = pl.program_id(0)
    gain, bias = tab_ref[0:1, :], tab_ref[1:2, :]

    @pl.when(step < 2)
    def _():
        for k in range(2):
            clear_pad(pad.at[k])
            clear_pad(moved.at[k])
            for m in range(2):
                xhat, _unused = normed(a_ref[k, part(m), :], total_ref, inv_ref, m, 0.25)
                h = (silu(xhat * gain + bias) * mask_ref[part(m), :]).astype(BFLOAT)
                h_ref[k, part(m), :] = h
                body(pad.at[k], m)[...] = h.astype(SINGLE)
                body(moved.at[k], m)[...] = h.astype(SINGLE)

    @pl.when(step == 2)
    def _():
        for k in range(2):
            moved[k, PAD : PAD + ROWS, :] = rows_at(pad.at[k], -1, 0)

    term = dot(rows_at(moved.at[0], 0, 0).astype(BFLOAT), w1[...])
    term += dot(rows_at(moved.at[1], 0, -1).astype(BFLOAT), w0[...])
    term += dot(rows_at(moved.at[1], 0, 0).astype(BFLOAT), w2[...])
    out_ref[...] = carried(out_ref, step == 0) + term

    @pl.when(step == 2)
    def _():
        a = out_ref[...]
        masked = a * mask_ref[...]
        put_sums(sum_ref, [masked, masked * a], True)


def k_conv_one(inv_ref, total_ref, tab_ref, mask_ref, a_ref, w0, w1, w2, out_ref, h_ref, sum_ref, pad, moved):
    step = pl.program_id(0)
    gain, bias = tab_ref[0:1, :], tab_ref[1:2, :]

    @pl.when(step == 0)
    def _():
        clear_pad(pad)
        clear_pad(moved)
        for m in range(2):
            xhat, _unused = normed(a_ref[part(m), :], total_ref, inv_ref, m)
            h = (silu(xhat * gain + bias) * mask_ref[part(m), :]).astype(BFLOAT)
            h_ref[part(m), :] = h
            body(pad, m)[...] = h.astype(SINGLE)

    for s in range(3):

        @pl.when(step == s)
        def _(s=s):
            moved[PAD : PAD + ROWS, :] = rows_at(pad, s - 1, 0)

    term = dot(rows_at(moved, 0, -1).astype(BFLOAT), w0[...])
    term += dot(rows_at(moved, 0, 0).astype(BFLOAT), w1[...])
    term += dot(rows_at(moved, 0, 1).astype(BFLOAT), w2[...])
    out_ref[...] = carried(out_ref, step == 0) + term

    @pl.when(step == 2)
    def _():
        a = out_ref[...]
        masked = a * mask_ref[...]
        put_sums(sum_ref, [masked, masked * a], True)


def k_expand(inv_ref, total_ref, tab_ref, mask_ref, a_ref, w_ref, h_ref, out_ref, sum_ref):
    @pl.when(pl.program_id(0) == 0)
    def _():
        gain, bias = tab_ref[0:1, :], tab_ref[1:2, :]
        for m in range(2):
            xhat, _unused = normed(a_ref[part(m), :], total_ref, inv_ref, m)
            h_ref[part(m), :] = (silu(xhat * gain + bias) * mask_ref[part(m), :]).astype(BFLOAT)

    a = dot(h_ref[...], w_ref[...])
    out_ref[...] = a
    put_sums(sum_ref, [a, a * a], True)


def k_short(x_ref, w0, w1, out_ref, sum_ref):
    a = dot(x_ref[0, :, :TILE], w0[...]) + dot(x_ref[0, :, TILE:], w1[...])
    out_ref[...] = a
    put_sums(sum_ref, [a, a * a], True)


def k_meet(inv_ref, t3_ref, ts_ref, tab3_ref, tabs_ref, mask_ref, a3_ref, as_ref, wa_ref, wb_ref, y_ref, out_ref, sum_ref):
    step = pl.program_id(0)
    for m in range(2):
        x3, _unused = normed(a3_ref[part(m), :], t3_ref, inv_ref, m)
        xs, _unused = normed(as_ref[part(m), :], ts_ref, inv_ref, m)
        joined = (x3 * tab3_ref[0:1, :] + tab3_ref[1:2, :]) + (xs * tabs_ref[0:1, :] + tabs_ref[1:2, :])
        y_ref[part(m), :] = (silu(joined) * mask_ref[part(m), :]).astype(BFLOAT)

    @pl.when(step == 0)
    def _():
        out_ref[...] = dot(y_ref[...], wa_ref[...])

    @pl.when(step > 0)
    def _():
        out_ref[...] += dot(y_ref[...], wb_ref[...])

    @pl.when(step == pl.num_programs(0) - 1)
    def _():
        a = out_ref[...]
        put_sums(sum_ref, [a, a * a], True)


def k_head(order_ref, inv_ref, total_ref, tab_ref, mask_ref, a_ref, y_ref, c0, c1, c2, c3, blk_ref, gz_ref, sum_ref):
    cots = (c0, c1, c2, c3)
    gain, bias = tab_ref[0:1, :], tab_ref[1:2, :]
    for m in range(2):
        mask = mask_ref[part(m), :]
        xhat, _unused = normed(a_ref[part(m), :], total_ref, inv_ref, m)
        z = (xhat * gain + bias) + y_ref[part(m), :].astype(SINGLE)
        gate = jax.nn.sigmoid(z)
        blk_ref[0, part(m), :] = (z * gate * mask).astype(BFLOAT)
        cot = jnp.concatenate([cots[2 * m][0], cots[2 * m + 1][0]], axis=0).astype(SINGLE)
        gz = cot * mask * (gate * (1.0 + z * (1.0 - gate)))
        gz_ref[part(m), :] = gz
        sum_ref[m : m + 1, :] = jnp.sum(gz, axis=0, keepdims=True)
        sum_ref[2 + m : 3 + m, :] = jnp.sum(gz * xhat, axis=0, keepdims=True)


def finish_back(gz_ref, sum_ref, grad, a_ref, total_ref, tab_ref, inv_ref, mask_ref):
    gain, bias = tab_ref[0:1, :], tab_ref[1:2, :]
    for m in range(2):
        xhat, _unused = normed(a_ref[part(m), :], total_ref, inv_ref, m)
        gz = grad[part(m)] * mask_ref[part(m), :] * slope(xhat * gain + bias)
        gz_ref[part(m), :] = gz
        sum_ref[m : m + 1, :] = jnp.sum(gz, axis=0, keepdims=True)
        sum_ref[2 + m : 3 + m, :] = jnp.sum(gz * xhat, axis=0, keepdims=True)


def k_back_six(inv_ref, gz_ref, a_ref, total_ref, s_ref, tab_ref, mask_ref, w_ref, low_ref, low_total, low_tab, ga_ref, out_ref, sum_ref, acc):
    step = pl.program_id(0)
    for m in range(2):
        xhat, rstd = normed(a_ref[part(m), :], total_ref, inv_ref, m)
        ga_ref[part(m), :] = conv_grad(
            gz_ref[part(m), :], xhat, rstd, tab_ref[0:1, :], mask_ref[part(m), :], s_ref, inv_ref, m
        )
    term = dot_back(ga_ref[...], w_ref[...])

    @pl.when(step == 0)
    def _():
        acc[...] = term

    @pl.when(step > 0)
    def _():
        acc[...] += term

    @pl.when(step == pl.num_programs(0) - 1)
    def _():
        finish_back(out_ref, sum_ref, acc[...], low_ref, low_total, low_tab, inv_ref, mask_ref)


def k_back_conv_one(inv_ref, gz_ref, a_ref, total_ref, s_ref, tab_ref, mask_ref, w0, w1, w2, low_ref, low_total, low_tab, col_ref, out_ref, sum_ref, pad, moved, acc):
    step = pl.program_id(0)

    @pl.when(step == 0)
    def _():
        clear_pad(pad)
        clear_pad(moved)
        for m in range(2):
            xhat, rstd = normed(a_ref[part(m), :], total_ref, inv_ref, m)
            ga = conv_grad(gz_ref[part(m), :], xhat, rstd, tab_ref[0:1, :], mask_ref[part(m), :], s_ref, inv_ref, m)
            body(pad, m)[...] = ga.astype(SINGLE)

    for s in range(3):

        @pl.when(step == s)
        def _(s=s):
            moved[PAD : PAD + ROWS, :] = rows_at(pad, 1 - s, 0)

    term = None
    for kx, weight in enumerate((w0, w1, w2)):
        tap = rows_at(moved, 0, 1 - kx).astype(BFLOAT)
        col_ref[kx] = tap
        product = dot_back(tap, weight[...])
        term = product if term is None else term + product
    acc[...] = carried(acc, step == 0) + term

    @pl.when(step == 2)
    def _():
        finish_back(out_ref, sum_ref, acc[...], low_ref, low_total, low_tab, inv_ref, mask_ref)


def k_back_four(inv_ref, gz_ref, a_ref, total_ref, s_ref, tab_ref, mask_ref, wa_ref, wb_ref, up_ref, a3_ref, as_ref, t3_ref, ts_ref, tab3_ref, tabs_ref, ga_ref, gj_ref, sum_ref):
    @pl.when(pl.program_id(0) == 0)
    def _():
        for m in range(2):
            xhat, rstd = normed(a_ref[part(m), :], total_ref, inv_ref, m)
            ga_ref[part(m), :] = conv_grad(
                gz_ref[part(m), :], xhat, rstd, tab_ref[0:1, :], mask_ref[part(m), :], s_ref, inv_ref, m
            )

    weight = jnp.where(pl.program_id(0) == 0, wa_ref[...], wb_ref[...])
    grad = dot_back(ga_ref[...], weight) + up_ref[...]
    for m in range(2):
        x3, _unused = normed(a3_ref[part(m), :], t3_ref, inv_ref, m)
        xs, _unused = normed(as_ref[part(m), :], ts_ref, inv_ref, m)
        joined = (x3 * tab3_ref[0:1, :] + tab3_ref[1:2, :]) + (xs * tabs_ref[0:1, :] + tabs_ref[1:2, :])
        gj = grad[part(m)].astype(BFLOAT).astype(SINGLE) * mask_ref[part(m), :] * slope(joined)
        gj_ref[part(m), :] = gj
        for k, value in enumerate((gj, gj * x3, gj * xs)):
            row = 2 * k + m
            sum_ref[row : row + 1, :] = jnp.sum(value, axis=0, keepdims=True)


def k_back_three(inv_ref, gj_ref, a3_ref, as_ref, t3_ref, ts_ref, s_ref, tab3_ref, tabs_ref, mask_ref, w_ref, low_ref, low_total, low_tab, g3_ref, gs_ref, out_ref, sum_ref, acc):
    step = pl.program_id(0)
    for m in range(2):
        mask = mask_ref[part(m), :]
        gj = gj_ref[part(m), :]
        x3, r3 = normed(a3_ref[part(m), :], t3_ref, inv_ref, m)
        g3_ref[part(m), :] = conv_grad(gj, x3, r3, tab3_ref[0:1, :], mask, s_ref, inv_ref, m)
        xs, rs = normed(as_ref[part(m), :], ts_ref, inv_ref, m)
        gs_ref[part(m), :] = conv_grad(gj, xs, rs, tabs_ref[0:1, :], mask, s_ref, inv_ref, m, second=4)
    term = dot_back(g3_ref[...], w_ref[...])

    @pl.when(step == 0)
    def _():
        acc[...] = term

    @pl.when(step > 0)
    def _():
        acc[...] += term

    @pl.when(step == pl.num_programs(0) - 1)
    def _():
        finish_back(out_ref, sum_ref, acc[...], low_ref, low_total, low_tab, inv_ref, mask_ref)


def k_back_conv_two(inv_ref, gz_ref, a_ref, total_ref, s_ref, tab_ref, mask_ref, w0, w1, w2, low_ref, low_total, low_tab, col_ref, out_ref, sum_ref, pad, moved, acc):
    step = pl.program_id(0)
    gain, bias = low_tab[0:1, :], low_tab[1:2, :]

    @pl.when(step == 0)
    def _():
        clear_pad(pad)
        clear_pad(moved)
        for m in range(2):
            xhat, rstd = normed(a_ref[part(m), :], total_ref, inv_ref, m)
            ga = conv_grad(gz_ref[part(m), :], xhat, rstd, tab_ref[0:1, :], mask_ref[part(m), :], s_ref, inv_ref, m)
            body(pad, m)[...] = ga.astype(SINGLE)
            body(moved, m)[...] = ga.astype(SINGLE)
        sum_ref[...] = jnp.zeros_like(sum_ref)

    @pl.when(step == 2)
    def _():
        moved[PAD : PAD + ROWS, :] = rows_at(pad, 1, 0)

    plain = rows_at(moved, 0, 0).astype(BFLOAT)
    aside = rows_at(moved, 0, 1).astype(BFLOAT)
    col_ref[0], col_ref[1], col_ref[2] = aside, plain, plain
    acc[0] = carried(acc.at[0], step < 2) + dot_back(plain, w1[...])
    acc[1] = carried(acc.at[1], step < 2) + (dot_back(aside, w0[...]) + dot_back(plain, w2[...]))

    @pl.when(step != 1)
    def _():
        for k in range(2):
            for m in range(2):
                xhat, _unused = normed(low_ref[k, part(m), :], low_total, inv_ref, m, 0.25)
                gz = acc[k, part(m), :] * mask_ref[part(m), :] * slope(xhat * gain + bias)
                out_ref[k, part(m), :] = gz
                for q, value in enumerate((gz, gz * xhat)):
                    row = 2 * q + m
                    sum_ref[row : row + 1, :] += jnp.sum(value, axis=0, keepdims=True)


def k_wide_back(g_ref, w_ref, *refs):
    refs[-1][...] = dot_back(g_ref[...], w_ref[...])


def k_first_grad(inv_ref, gz_ref, a_ref, total_ref, s_ref, tab_ref, mask_ref, ga_ref):
    for m in range(2):
        xhat, rstd = normed(a_ref[0, part(m), :], total_ref, inv_ref, m, 0.25)
        ga_ref[0, part(m), :] = conv_grad(
            gz_ref[0, part(m), :], xhat, rstd, tab_ref[0:1, :], mask_ref[part(m), :], s_ref, inv_ref, m, 0.25
        )


def k_image_grad(core_ref, ga_ref, mask_ref, w_ref, short_ref, perm_ref, *refs):
    out_ref = refs[-1]
    grads = dot_back(ga_ref[...].reshape(4 * PIX, C_MID), w_ref[...])
    mask = mask_ref[...]
    parts = []
    for k in range(4):
        grad = grads[k * PIX : (k + 1) * PIX]
        if k == 0:
            grad = grad + short_ref[...]
        parts.append((grad * mask).astype(BFLOAT))
    planes = jnp.concatenate(parts, axis=0)
    image = lax.dot_general(perm_ref[...], planes, (((0,), (0,)), ((), ())), preferred_element_type=SINGLE).astype(BFLOAT)
    core = core_ref[0]
    out_ref[core, 0] = image[:, : C_IN // 2]
    out_ref[1 - core, 0] = image[:, C_IN // 2 :]


def k_place(core_ref, order_ref, own_ref, got_ref, *refs):
    out_ref = refs[-1]
    step = pl.program_id(0)

    @pl.when(step < SLOTS)
    def _():
        out_ref[0] = own_ref[0, 0]

    @pl.when(step >= SLOTS)
    def _():
        out_ref[0] = got_ref[0]


def k_turn(in_ref, *refs):
    refs[-1][...] = in_ref[...].reshape(in_ref.shape[-2:]).T


def k_grad(core_ref, feature_ref, grad_ref, *refs):
    keep_ref, send_ref = refs[-2:]
    core = core_ref[0]
    rows, half = feature_ref.shape[-2], grad_ref.shape[-1] // 2
    for k in range(grad_ref.shape[0]):
        feature = feature_ref[k % feature_ref.shape[0]]
        for ref, side in ((keep_ref, core), (send_ref, 1 - core)):
            columns = pl.ds(pl.multiple_of(side * half, half), half)
            ref[k * rows : (k + 1) * rows] = dot(feature, grad_ref[k, :, columns]).astype(BFLOAT)


def k_keep(in_ref, *refs):
    out_ref, sem = refs[-2:]
    copy = pltpu.make_async_copy(in_ref, out_ref, sem)
    copy.start()
    copy.wait()


def k_join(n_in, n_out, *refs):
    stayed, came = refs[:n_in], refs[n_in : 2 * n_in]
    outs, sems = refs[-1 - n_out : -1], refs[-1]
    copies = []
    for which in range(2):
        target = outs[0].at[which] if n_out == 1 else outs[which]
        for side, sources in enumerate((stayed, came)):
            source = sources[0].at[which] if n_in == 1 else sources[which]
            size = source.shape[0]
            copies.append(pltpu.make_async_copy(source, target.at[pl.ds(side * size, size)], sems.at[len(copies)]))
    for copy in copies:
        copy.start()
    for copy in copies:
        copy.wait()


def k_halve(*refs):
    for which in range(2):
        keep0, keep1, came0, came1 = refs[4 * which : 4 * which + 4]
        stay = (keep0[0].astype(SINGLE) + came0[0].astype(SINGLE)).astype(BFLOAT)
        sent = (keep1[0].astype(SINGLE) + came1[0].astype(SINGLE)).astype(BFLOAT)
        if len(refs) == 10:
            refs[8][which, 0], refs[9][which, 0] = stay, sent
        else:
            refs[8 + 2 * which][0], refs[9 + 2 * which][0] = stay, sent


def k_halve_both(keep_ref, came_ref, stay_ref, sent_ref):
    total = (keep_ref[...].astype(SINGLE) + came_ref[...].astype(SINGLE)).astype(BFLOAT)
    half = total.shape[1] // 2
    stay_ref[...], sent_ref[...] = total[:, :half], total[:, half:]


def k_gather(me_ref, *refs):
    ins, out_ref, sems = refs[:8], refs[8], refs[9]
    rows, cols = ins[0].shape[1:]
    copies = []
    for other in range(2):
        column = pl.multiple_of((1 - me_ref[1] if other else me_ref[1]) * cols, cols)
        for which in range(2):
            for came in range(2):
                source = ins[4 * other + 2 * which + came]
                for q in range(8):
                    third, low, high = q >> 2, (q >> 1) & 1, q & 1
                    pair = 2 * third + came if which == 0 else 2 * came + third
                    block = me_ref[0] ^ (8 * high + 4 * low + pair)
                    row = pl.multiple_of((2 * block + which) * rows, rows)
                    target = out_ref.at[pl.ds(row, rows), pl.ds(column, cols)]
                    copies.append(pltpu.make_async_copy(source.at[q], target, sems.at[len(copies)]))
    for copy in copies:
        copy.start()
    for copy in copies:
        copy.wait()


def k_split(me_ref, *refs):
    own, got, outs = refs[:4], refs[4:8], refs[8:]
    for own_ref, got_ref, out_ref in zip(own, got, outs):
        out_ref[0] = (own_ref[...].astype(SINGLE) + got_ref[...].astype(SINGLE)).astype(BFLOAT)


def group_of(rows, start, bounds):
    index = lax.broadcasted_iota(jnp.int32, (rows, 1), 0) + start
    return sum((index >= bound).astype(jnp.int32) for bound in bounds)


def k_load(*refs):
    count = (len(refs) - 2) // 2
    ins, outs, sems = refs[:count], refs[count + 1 : -1], refs[-1]
    copies = [pltpu.make_async_copy(source, target, sems.at[k]) for k, (source, target) in enumerate(zip(ins, outs))]
    for copy in copies:
        copy.start()
    for copy in copies:
        copy.wait()


def k_squares(start_ref, *refs):
    out_ref = refs[-1]
    lane = lax.broadcasted_iota(jnp.int32, (1, 128), 1)
    out_ref[...] = jnp.zeros_like(out_ref)
    for k in range(2):
        squares = [jnp.sum(ref[...] * ref[...], axis=1, keepdims=True) for ref in refs[4 * k : 4 * k + 4]]
        total = jnp.zeros((1, 128), SINGLE)
        for which, bounds in enumerate((NARROW_BOUNDS, WIDE_BOUNDS)):
            group = group_of(squares[which].shape[0], start_ref[which], bounds)
            for g in range(len(bounds) + 1):
                part_sum = jnp.sum(jnp.where(group == g, squares[which], 0.0))
                total = total + jnp.where(lane == 4 * which + g, part_sum, 0.0)
        for rows, first in ((squares[2], 7), (squares[3], 15)):
            row = lax.broadcasted_iota(jnp.int32, (rows.shape[0], 128), 0)
            column = lax.broadcasted_iota(jnp.int32, (rows.shape[0], 128), 1)
            total = total + jnp.sum(jnp.where(column == row + first, rows, 0.0), axis=0, keepdims=True)
        out_ref[k : k + 1, :] = total


def k_update(start_ref, square_ref, *refs):
    step = pl.program_id(0)
    norms = jnp.sqrt(square_ref[0:8, :])
    weight_norm, grad_norm = norms[0:1], norms[1:2]
    ratio = TRUST * weight_norm / (grad_norm + DECAY * weight_norm)
    lane = lax.broadcasted_iota(jnp.int32, (1, 128), 1)
    for k in range(4):
        weight, grad = refs[k][...], refs[4 + k][...]
        rows = weight.shape[0]
        if k < 2:
            bounds = (NARROW_BOUNDS, WIDE_BOUNDS)[k]
            group = group_of(rows, start_ref[k] + step * rows, bounds)
            scale = jnp.zeros((rows, 1), SINGLE)
            for g in range(len(bounds) + 1):
                scale = jnp.where(group == g, jnp.sum(jnp.where(lane == 4 * k + g, ratio, 0.0)), scale)
        else:
            row = lax.broadcasted_iota(jnp.int32, (rows, 128), 0)
            column = lax.broadcasted_iota(jnp.int32, (rows, 128), 1)
            scale = jnp.sum(jnp.where(column == row + (7, 15)[k - 2], ratio, 0.0), axis=1, keepdims=True)
        moment = MOMENTUM * refs[8 + k][...] + RATE * scale * (grad + DECAY * weight)
        refs[12 + k][...] = moment
        refs[16 + k][...] = weight - moment


def full(shape):
    zeros = (0,) * len(shape)
    return pl.BlockSpec(tuple(shape), lambda *_: zeros, pipeline_mode=pl.Buffered(1))


SCALARS = pl.BlockSpec(memory_space=pltpu.SMEM)
ANYWHERE = pl.BlockSpec(memory_space=pl.ANY)


def spec(shape, index):
    return pl.BlockSpec(tuple(shape), index)


def call(kernel, name, grid, in_specs, out_specs, out_shape, scratch, args, prefetch=0, vmem=8, aliases=None):
    return pl.pallas_call(
        kernel,
        out_shape=out_shape,
        grid_spec=pltpu.PrefetchScalarGridSpec(
            num_scalar_prefetch=prefetch,
            grid=grid,
            in_specs=in_specs,
            out_specs=out_specs,
            scratch_shapes=scratch,
        ),
        input_output_aliases=aliases or {},
        compiler_params=pltpu.CompilerParams(vmem_limit_bytes=vmem * MIB),
        cost_estimate=pl.CostEstimate(flops=0, bytes_accessed=int(MICROSECONDS.get(name, 1) * BYTES_PER_US), transcendentals=0),
        name=name,
    )(*args)


def shape_of(shape, dtype=SINGLE):
    return jax.ShapeDtypeStruct(tuple(shape), dtype)


def vmem_of(shape, dtype=SINGLE):
    return pltpu.VMEM(tuple(shape), dtype)


def hbm_of(shape, dtype=SINGLE):
    return pltpu.HBM(tuple(shape), dtype)


def in_vmem(value):
    return pltpu.with_memory_space_constraint(value, pltpu.VMEM)


def in_hbm(value):
    return pltpu.with_memory_space_constraint(value, pltpu.HBM)


def permutation():
    table = np.zeros((4 * PIX, 4 * PIX), np.float32)
    for pi in range(2):
        for pj in range(2):
            for i in range(HB):
                for j in range(WB):
                    table[((2 * pi + pj) * WB + j) * HB + i, (2 * i + pi) * 2 * WB + 2 * j + pj] = 1.0
    return jnp.asarray(table, BFLOAT)


def rounded(value):
    return lax.reduce_precision(value, 8, 7)


def split_group(name, keep, got, rows, index):
    cols = keep.shape[1]

    def block(which, sent):
        def at(q, me):
            other, low, high = (q >> 2) & 1, (q >> 1) & 1, q & 1
            pair = other * 2 + sent if which == 0 else sent * 2 + other
            return (index(which, me[0] ^ (high * 8 + low * 4 + pair)), 0)

        return spec((rows, cols), at)

    blocks = [block(which, sent) for which in range(2) for sent in range(2)]
    return call(
        k_split, name, (8,), blocks + blocks,
        [spec((1, rows, cols), lambda q, me: (q, 0, 0))] * 4,
        [shape_of((8, rows, cols), BFLOAT)] * 4, [],
        (lax.axis_index("dp")[None].astype(jnp.int32),) + (keep,) * 4 + (got,) * 4, prefetch=1,
    )


def halved(state, came, merge):
    (keep0, _sent, keep1, _sent), (came0, came1) = state, came
    count, block = keep0.shape[0] // 2, keep0.shape[1:]
    low, high = (spec((1,) + block, lambda q, at=at: (q + at, 0, 0)) for at in (0, count))
    if merge:
        outs, out_spec = [vmem_of((2, count) + block, BFLOAT)] * 2, [spec((2, 1) + block, lambda q: (0, q, 0, 0))] * 2
    else:
        outs, out_spec = [vmem_of((count,) + block, BFLOAT)] * 4, [low] * 4
    return tuple(call(
        k_halve, "halve", (count,), [low, high] * 4, out_spec, outs, [], (keep0, keep0, came0, came0, keep1, keep1, came1, came1), vmem=4,
    ))


def halved_both(state, came):
    shape = state[0].shape
    half = (2, shape[1] // 2) + shape[2:]
    return tuple(call(
        k_halve_both, "halve", (1,), [full(shape)] * 2, [full(half)] * 2, [vmem_of(half, BFLOAT)] * 2, [], (state[0], came), vmem=4,
    ))


def added(state, came):
    total = state[0].astype(SINGLE) + came.astype(SINGLE)
    return total[0, 0], total[1, 0]


def scatter_plain(keep, got, block, by_rows):
    total = (keep.astype(SINGLE) + got.astype(SINGLE)).astype(BFLOAT)
    if by_rows:
        own = lax.psum_scatter(total, "dp", scatter_dimension=0, tiled=True).astype(SINGLE)
        return own[: block // 2], own[block // 2 :]
    middle = total.shape[0] // 2
    return tuple(lax.psum_scatter(p, "dp", scatter_dimension=0, tiled=True).astype(SINGLE) for p in (total[:middle], total[middle:]))


def joined(value, got):
    return jnp.concatenate([value, got], axis=0)


def gather_blocks(name, core, parts, others, out_shape):
    scalars = jnp.stack([lax.axis_index("dp"), core]).astype(jnp.int32)
    pieces = [a for pair in list(parts) + list(others) for a in pair]
    return call(
        k_gather, name, (), [ANYWHERE] * 8, ANYWHERE, vmem_of(out_shape, BFLOAT),
        [pltpu.SemaphoreType.DMA((64,))], (scalars, *pieces), prefetch=1, vmem=2,
    )


def swap_all(parts):
    return [tuple(swap_pipe(a) for a in pair) for pair in parts]


def join_parts(stayed, came, token, n_out):
    n_in = len(stayed)
    shape = stayed[0].shape[-3:]
    shape = (2 * shape[0],) + shape[1:]
    outs = [vmem_of(shape, BFLOAT)] * 2 if n_out == 2 else [vmem_of((2,) + shape, BFLOAT)]
    return call(
        functools.partial(k_join, n_in, n_out), "join", (), [ANYWHERE] * (2 * n_in + 1), [ANYWHERE] * n_out, outs,
        [pltpu.SemaphoreType.DMA((4,))], tuple(stayed) + tuple(came) + (token,), vmem=2,
    )


def keep_in_hbm(value):
    def filler(token):
        return call(
            k_keep, "keep", (), [ANYWHERE] * 2, ANYWHERE, hbm_of(value.shape, value.dtype),
            [pltpu.SemaphoreType.DMA], (in_vmem(value), token), vmem=2,
        )

    return filler


def nothing(token):
    return token


def both_of(*fillers):
    return lambda token: tuple(filler(token) for filler in fillers)


def on_device(images, cotangent, heights, widths, assign, w_narrow, w_wide, bn_mid, bn_wide, mom_narrow, mom_wide, mom_bn_mid, mom_bn_wide):
    core = lax.axis_index("pipe")
    shard = lax.axis_index(("pipe", "dp"))
    fast = lax.axis_size("dp") == 16

    own_narrow = w_narrow.astype(BFLOAT)
    own_wide = w_wide.astype(BFLOAT)
    rows_n, half_n = w_narrow.shape[0], C_MID // 2
    part_n = rows_n // 2
    whole_n = (R_N // 2, C_MID)
    if fast:
        sent = swap_pipe(jnp.where(core == 0, own_narrow[:, half_n:], own_narrow[:, :half_n]))
        kept = jnp.where(core == 0, own_narrow[:, :half_n], own_narrow[:, half_n:])
        mine_a, mine_b = jnp.where(core == 0, kept, sent), jnp.where(core == 0, sent, kept)
        a, b = (mine.reshape(2, 1, part_n, half_n) for mine in (mine_a, mine_b))
        (a,) = join_parts((a,), (exchange(a, 8),), a, 1)
        a0, a1 = join_parts((a,), (exchange(a, 4),), a, 2)
        b = pin(b, a1)
        got, got_b = lax.optimization_barrier(((exchange(a0, 2), exchange(a1, 1)), exchange(b, 8)))
        a0, a1 = join_parts((a0, a1), got, got[1], 2)
        (b,) = join_parts((b,), (got_b,), got_b, 1)
        stay_a = swap_all([(a0,), (a1,)])
        own_wide = pin(own_wide, a1)
        wide = lax.all_gather(own_wide, ("pipe", "dp"), axis=0, tiled=True)
    else:
        narrow = lax.all_gather(own_narrow, ("pipe", "dp"), axis=0, tiled=True)
        narrow_a, narrow_b = narrow[: R_N // 2], narrow[R_N // 2 :]
        wide = lax.all_gather(own_wide, ("pipe", "dp"), axis=0, tiled=True)

    perm = permutation()
    core_row = core[None].astype(jnp.int32)
    x, mask, count_rows = call(
        k_prep, "prep", (SLOTS,),
        [spec((1, 4 * PIX, C_IN), lambda s, core, order, *_: (order[0, core[0] * SLOTS + s], 0, 0)), full((4 * PIX, 4 * PIX))],
        [spec((4, PIX, C_IN), lambda s, *_: (0, s, 0)), spec((PIX, 1), lambda s, *_: (s, 0)), full((4, C_MID))],
        [vmem_of((4, ROWS, C_IN), BFLOAT), vmem_of((ROWS, 1)), shape_of((4, C_MID))], [],
        (core_row, assign, heights, widths, in_hbm(images.reshape(IMG_DEV, 4 * PIX, C_IN)), in_hbm(perm)), prefetch=4, vmem=7,
    )
    mask = in_vmem(mask)
    mid_cols, wide_cols = bn_mid.shape[1], bn_wide.shape[1]
    tables = jnp.concatenate(
        [
            lax.dynamic_update_slice(jnp.zeros((8, C_MID), SINGLE), rounded(bn_mid), (0, shard * mid_cols)),
            lax.dynamic_update_slice(jnp.zeros((6, C_OUT), SINGLE), rounded(bn_wide), (0, shard * wide_cols)).reshape(24, C_MID),
        ]
    )
    tables = tables + swap_pipe(tables)
    tables = jnp.concatenate([tables, count_rows])

    held = {}
    if fast:
        last0, last1, got_b, x, tables = lax.optimization_barrier((exchange(a0, 1), exchange(a1, 2), exchange(b, 4), x, tables))
        came_a = swap_all([(last0,), (last1,)])
        part_b = join_parts((b,), (got_b,), got_b, 2)
        narrow_a = gather_blocks("wa", core, [(a0, last0), (a1, last1)], [u + v for u, v in zip(stay_a, came_a)], whole_n)

    def turn(feature, feature_spec, grid, shape, index):
        def filler(token):
            return call(
                k_turn, "turn", grid, [feature_spec, ANYWHERE],
                spec((C_MID, ROWS), index), hbm_of(shape, BFLOAT), [], (feature, token),
            )

        return filler

    def weight_grad(name, feature, feature_spec, grad, grad_spec, tiles, shape, rows, base, bufs, token, space):
        out_spec = spec((rows, shape[1]), lambda t, slot: (base + t, 0))
        hold = in_vmem if space is vmem_of else in_hbm
        extra = tuple(hold(b) for b in bufs or ()) + (() if token is None else (token,))
        return call(
            k_grad, name, (tiles,), [feature_spec, grad_spec] + [ANYWHERE] * len(extra),
            [out_spec] * 2, [space(shape, BFLOAT)] * 2, [], (core_row, feature, grad) + extra,
            prefetch=1, vmem=7, aliases={3: 0, 4: 1} if bufs else {},
        )

    full_row = full((4, C_MID))
    full_table = full((TABLE_ROWS, C_MID))
    full_mask = full((ROWS, 1))
    full_mid = full((ROWS, C_MID))
    plane_pair = spec((2, ROWS, C_MID), lambda s: (jnp.minimum(s, 1), 0, 0))

    def narrow_block(index):
        return spec((TILE, TILE), index)

    chunk = spec((ROWS, TILE), lambda k, *_: (0, k))
    chunk_sum = spec((4, TILE), lambda k, *_: (0, k))
    chunk_eight = spec((8, TILE), lambda k, *_: (0, k))
    four_a = narrow_block(lambda k: (11, 0))
    four_b = narrow_block(lambda k: (jnp.maximum(k - 1, 0), 0))

    a1, part1 = call(
        k_first, "a1", (4,),
        [spec((1, ROWS, C_IN), lambda k: (k, 0, 0)), full((C_IN, C_MID))],
        [spec((1, ROWS, C_MID), lambda k: (k, 0, 0)), full_row],
        [hbm_of((4, ROWS, C_MID)), shape_of((4, C_MID))], [],
        (in_vmem(x), in_vmem(narrow_a)), vmem=6,
    )

    a1 = in_hbm(a1)
    def second_part_b(token):
        if not fast:
            return token
        part = pin(part_b, token)
        held["got"] = exchange(part[0], 2), exchange(part[1], 1)
        return token

    first_sum, (a_kept, (x_kept, first_b), _unused) = dp_sum(jnp.concatenate([part1, tables]), [keep_in_hbm(narrow_a), lambda token: (keep_in_hbm(x)(token), part_b if fast else token), second_part_b])
    x_kept, a_kept = in_hbm(x_kept), in_hbm(a_kept)
    base = in_vmem(first_sum.sum)

    a_s, part_s = call(
        k_short, "as", (4,),
        [spec((1, ROWS, C_IN), lambda k: (0, 0, 0)), spec((TILE, TILE), lambda k: (1, k)), spec((TILE, TILE), lambda k: (2, k))],
        [chunk, chunk_sum],
        [vmem_of((ROWS, C_OUT)), shape_of((4, C_OUT))], [],
        (in_vmem(x), in_hbm(wide), in_hbm(wide)), vmem=6,
    )

    def conv_weights(first, order_of):
        return [narrow_block(lambda s, kx=kx: (first + 3 * order_of(s) + kx, 0)) for kx in range(3)]

    turned = lambda s: lax.rem(s + 1, 3)
    straight = lambda s: s

    a2, h1, part2 = call(
        paired(k_conv_two, {}, {1: ("base", 0), 2: ("mid", 0)}, 0, 2), "a2", (3,),
        [SCALARS, full_table, full_table, full_mask, plane_pair] + conv_weights(2, turned),
        [full_mid, plane_pair, full_row],
        [vmem_of((ROWS, C_MID)), vmem_of((4, ROWS, C_MID), BFLOAT), shape_of((4, C_MID))],
        [pltpu.VMEM((2, PAD + ROWS + PAD, C_MID), SINGLE)] * 2,
        (core_row, *first_sum.parts, mask, a1) + (a_kept,) * 3, vmem=11,
    )
    a2 = in_vmem(a2)

    def third_part_b(token):
        if not fast:
            return token
        held["big_b"] = join_parts(first_b, pin(held["got"], token), token, 2)
        return held["big_b"]

    def fourth_b(token):
        if fast:
            big = pin(held["big_b"], token)
            held["got"] = exchange(big[0], 1), exchange(big[1], 2)
        return token

    turn_h1 = turn(h1, spec((1, ROWS, C_MID), lambda k: (k, 0, 0)), (4,), (4 * C_MID, ROWS), lambda k: (k, 0))
    total2, (h1_t, big_b, _unused) = dp_sum(part2, [turn_h1, third_part_b, fourth_b])

    def expand(name, a, total, which, row):
        return call(
            paired(k_expand, {1: ONE}, {2: ("mid", which)}, 0), name, (4,),
            [SCALARS, full_table, full_row, full_row, full_mask, full_mid, spec((TILE, TILE), lambda k: (row, k))],
            [full_mid, chunk, chunk_sum],
            [vmem_of((ROWS, C_MID), BFLOAT), vmem_of((ROWS, C_OUT)), shape_of((4, C_OUT))], [],
            (core_row, base, *total.parts, mask, a, in_hbm(wide)), vmem=6,
        )

    h2, a3, part3 = expand("a3", a2, total2, 1, 0)
    whole = spec((ROWS, C_MID), lambda k: (0, 0))

    def swap_b(token):
        if not fast:
            return token
        ready = pin(tuple(big_b) + held["got"], token)
        return [(ready[0], ready[2]), (ready[1], ready[3])]

    def gather_b(token):
        if not fast:
            return narrow_b
        others = pin(held["others"], token)
        return gather_blocks("wb", core, held["parts"], others, whole_n)

    def start_swap_b(token):
        if fast:
            held["parts"] = swap_b(token)
            held["others"] = swap_all(held["parts"])
        return token

    total3s, ((h2_t, as_kept), (_unused, a3_kept), _unused, narrow_b) = dp_sum(
        jnp.concatenate([part3, part_s]),
        [
            both_of(turn(h2, whole, (1,), (C_MID, ROWS), lambda k: (0, 0)), keep_in_hbm(a_s)),
            both_of(start_swap_b, keep_in_hbm(a3)),
            nothing,
            gather_b,
        ],
    )
    as_kept, a3_kept = in_hbm(as_kept), in_hbm(a3_kept)

    y, a4, part4 = call(
        paired(k_meet, {1: (0, 4)}, {3: ("wide", 0), 4: ("wide", 1)}, 0), "a4", (4,),
        [SCALARS, full_table, chunk_eight, chunk_eight, full_mask, chunk, chunk, four_a, four_b],
        [chunk, full_mid, full_row],
        [vmem_of((ROWS, C_OUT), BFLOAT), vmem_of((ROWS, C_MID)), shape_of((4, C_MID))], [],
        (core_row, base, *total3s.parts, mask, in_vmem(a3), in_vmem(a_s), a_kept, in_vmem(narrow_b)), vmem=8,
    )
    a4 = in_vmem(a4)
    def turn_x(q, start, into):
        def filler(token):
            extra = () if into is None else (in_hbm(into[-1]),)
            held["x_t"] = call(
                k_turn, "turn", (2,), [spec((1, ROWS, C_MID), lambda k: (start + k, 0, q))] + [ANYWHERE] * (1 + len(extra)),
                spec((C_MID, ROWS), lambda k: (q, start + k)), hbm_of((C_IN, 4 * ROWS), BFLOAT), [], (x_kept, *extra, token),
                aliases={1: 0} if extra else {},
            )
            return held["x_t"]

        return filler

    total4, (y_t, y_kept, x_t0, x_t1) = dp_sum(
        part4,
        [
            turn(in_vmem(y), spec((ROWS, C_MID), lambda k: (0, k)), (4,), (4 * C_MID, ROWS), lambda k: (k, 0)),
            keep_in_hbm(y),
            turn_x(0, 0, None),
            lambda token: turn_x(0, 2, [held["x_t"]])(token),
        ],
    )
    del x_t0

    a5, h4, part5 = call(
        paired(k_conv_one, {1: ONE}, {2: ("mid", 2)}, 0), "a5", (3,),
        [SCALARS, full_table, full_row, full_row, full_mask, full_mid] + conv_weights(3, straight),
        [full_mid, full_mid, full_row],
        [vmem_of((ROWS, C_MID)), vmem_of((ROWS, C_MID), BFLOAT), shape_of((4, C_MID))],
        [pltpu.VMEM((PAD + ROWS + PAD, C_MID), SINGLE)] * 2,
        (core_row, base, *total4.parts, mask, a4) + (in_vmem(narrow_b),) * 3, vmem=8,
    )
    a5 = in_vmem(a5)
    total5, (h4_t, b_kept, _unused, x_t) = dp_sum(
        part5,
        [
            turn(h4, whole, (1,), (C_MID, ROWS), lambda k: (0, 0)),
            keep_in_hbm(narrow_b),
            turn_x(1, 0, [x_t1]),
            lambda token: turn_x(1, 2, [held["x_t"]])(token),
        ],
    )
    b_kept = in_hbm(b_kept)
    h5, a6, part6 = expand("a6", a5, total5, 3, 3)
    total6, (h5_t, a6_kept) = dp_sum(part6, [turn(h5, whole, (1,), (C_MID, ROWS), lambda k: (0, 0)), keep_in_hbm(a6)])
    a6_kept = in_hbm(a6_kept)

    cot = in_hbm(cotangent.transpose(0, 2, 1, 3).reshape(IMG_DEV, PIX, C_OUT))
    blk, gz6, s6 = call(
        paired(k_head, {2: ONE}, {3: ("wide", 2)}, 1, lead=1), "head", (4,),
        [full_table, chunk_sum, chunk_sum, full_mask, chunk, chunk]
        + [spec((1, PIX, TILE), lambda k, core, order, s=s: (order[0, core[0] * SLOTS + s], 0, k)) for s in range(SLOTS)],
        [
            spec((1, ROWS, TILE), lambda k, core, _order: ((k // 2) ^ core[0], 0, lax.rem(k, 2))),
            chunk,
            chunk_sum,
        ],
        [shape_of((2, ROWS, C_OUT // 2), BFLOAT), vmem_of((ROWS, C_OUT)), shape_of((4, C_OUT))], [],
        (core_row, assign, base, *total6.parts, mask, in_vmem(a6), in_hbm(y_kept), cot, cot, cot, cot), prefetch=2, vmem=9,
    )
    gz6 = in_vmem(gz6)

    def place(name, pair, got, token):
        block = (1,) + pair.shape[2:]
        return call(
            k_place, name, (IMG_DEV,),
            [
                spec((1,) + block, lambda t, *_: (0, jnp.minimum(t, SLOTS - 1), 0, 0)),
                spec(block, lambda t, *_: (jnp.maximum(t - SLOTS, 0), 0, 0)),
                ANYWHERE,
            ],
            spec(block, lambda t, core, order: (order[0, (core[0] * SLOTS + t) & (IMG_DEV - 1)], 0, 0)),
            shape_of((IMG_DEV,) + pair.shape[2:], BFLOAT), [],
            (core_row, assign, pair, got, token), prefetch=2, vmem=9,
        )

    blk = blk.reshape(2, SLOTS, PIX, C_OUT // 2)
    sum6, (got_blk, _unused, _unused, block_local) = dp_sum(
        s6,
        [
            lambda token: swap_pipe(pin(blk[1], token)),
            lambda token: token,
            lambda token: token,
            lambda token: token,
        ],
    )

    ga6, gz5, s5 = call(
        paired(k_back_six, {3: ONE, 4: ONE, 9: ONE}, {5: ("wide", 2), 10: ("mid", 3)}, 0), "g5", (4,),
        [SCALARS, full_table, chunk, chunk, chunk_sum, chunk_sum, chunk_sum, chunk_sum, full_mask, spec((TILE, TILE), lambda k: (3, k)), full_mid,
         full_row, full_row],
        [chunk, full_mid, full_row],
        [vmem_of((ROWS, C_OUT), BFLOAT), vmem_of((ROWS, C_MID)), shape_of((4, C_MID))],
        [pltpu.VMEM((ROWS, C_MID), SINGLE)],
        (core_row, base, gz6, a6_kept, *total6.parts, *sum6.parts, mask, in_hbm(wide), a5, *total5.parts), vmem=9,
    )
    gz5 = in_vmem(gz5)

    def wide_rows(k):
        return spec((1, 256, ROWS), lambda t, slot: (0, t + k, 0))

    def whole_wide(grad):
        return grad.reshape((1,) + grad.shape), full((1,) + grad.shape)

    wide_shape, narrow_shape = (R_W, C_OUT // 2), (R_N // 2, C_MID // 2)
    sum5, (bufs_w, block_local) = dp_sum(
        s5,
        [
            lambda token: weight_grad("dw6", h5_t[None], wide_rows(0), *whole_wide(ga6), 2, wide_shape, 256, 6, None, token, vmem_of),
            lambda token: place("place_out", blk, got_blk, token),
        ],
    )
    block_local = block_local.reshape(IMG_DEV, WB, HB, C_OUT // 2).transpose(0, 2, 1, 3)

    col5, gz4, s4 = call(
        paired(k_back_conv_one, {3: ONE, 4: ONE, 11: ONE}, {5: ("mid", 3), 12: ("mid", 2)}, 0), "g4", (3,),
        [SCALARS, full_table, full_mid, full_mid, full_row, full_row, full_row, full_row, full_mask] + conv_weights(3, straight)
        + [full_mid, full_row, full_row],
        [spec((3, ROWS, C_MID), lambda s: (s, 0, 0)), full_mid, full_row],
        [vmem_of((9, ROWS, C_MID), BFLOAT), vmem_of((ROWS, C_MID)), shape_of((4, C_MID))],
        [pltpu.VMEM((PAD + ROWS + PAD, C_MID), SINGLE)] * 2 + [pltpu.VMEM((ROWS, C_MID), SINGLE)],
        (core_row, base, gz5, a5, *total5.parts, *sum5.parts, mask, b_kept, b_kept, b_kept, a4, *total4.parts), vmem=10,
    )
    gz4 = in_vmem(gz4)
    one_turned = spec((1, C_MID, ROWS), lambda t, slot: (0, 0, 0))
    held_b = []

    def grad_five(k):
        def filler(token):
            grad_spec = spec((3, ROWS, C_MID), lambda t, slot: (k, 0, 0))
            held_b[:] = weight_grad("dw5", h4_t[None], one_turned, in_vmem(col5), grad_spec, 1, narrow_shape, 3 * TILE, 1 + k, list(held_b), token, vmem_of)
            return tuple(held_b)

        return filler

    sum4, results4 = dp_sum(s4, [grad_five(k) for k in range(3)])
    bufs_b = results4[2]

    ga4, gj, s3 = call(
        paired(k_back_four, {3: ONE, 4: ONE, 12: (0, 4)}, {5: ("mid", 2), 14: ("wide", 0), 15: ("wide", 1)}, 0), "gy", (4,),
        [SCALARS, full_table, full_mid, full_mid, full_row, full_row, full_row, full_row, full_mask, four_a, four_b,
         chunk, chunk, chunk, chunk_eight, chunk_eight],
        [full_mid, chunk, spec((6, TILE), lambda k: (0, k))],
        [vmem_of((ROWS, C_MID), BFLOAT), vmem_of((ROWS, C_OUT)), shape_of((6, C_OUT))], [],
        (core_row, base, gz4, a4, *total4.parts, *sum4.parts, mask, a_kept, b_kept, gz6, a3_kept, as_kept, *total3s.parts), vmem=12,
    )
    gj = in_vmem(gj)

    by_rows = lambda which, m: 2 * m + which

    def grad_four(token):
        y_tiles = y_t.reshape(4, C_MID, ROWS)
        one = full((1, ROWS, C_MID))
        grad = in_vmem(ga4.reshape(1, ROWS, C_MID))
        held["grad_b"] = weight_grad("dw4b", y_tiles, spec((1, C_MID, ROWS), lambda t, slot: (1 + t, 0, 0)), grad, one, 3, narrow_shape, TILE, 0, bufs_b, token, vmem_of)
        return held["grad_b"]

    def grad_four_first(token):
        return weight_grad(
            "dw4a", y_t.reshape(4, C_MID, ROWS), spec((1, C_MID, ROWS), lambda t, slot: (0, 0, 0)), in_vmem(ga4.reshape(1, ROWS, C_MID)),
            full((1, ROWS, C_MID)), 1, narrow_shape, TILE, 11, None, token, vmem_of,
        )

    def swap_grad_b(token):
        held["got_b"] = swap_pipe(pin(held["grad_b"][1], token))
        return token

    def split_b(token):
        if not fast:
            return token
        keep, got = pin((held["grad_b"][0], held["got_b"]), token)
        state = split_group("split_b", in_vmem(keep), got, part_n, by_rows)
        held["came_b"] = exchange(state[1], 1), exchange(state[3], 2)
        return state

    sum3, results3 = dp_sum(s3, [grad_four, both_of(swap_grad_b, grad_four_first), split_b])
    bufs_b, bufs_a = results3[0], results3[1][1]
    held["b"] = results3[2]

    ga3, gas, gz2, s2 = call(
        paired(k_back_three, {4: (0, 4), 6: ONE, 12: ONE}, {7: ("wide", 0), 8: ("wide", 1), 13: ("mid", 1)}, 0), "g2", (4,),
        [SCALARS, full_table, chunk, chunk, chunk, chunk_eight, chunk_eight, spec((6, TILE), lambda k: (0, k)), spec((6, TILE), lambda k: (0, k)), full_mask,
         spec((TILE, TILE), lambda k: (0, k)), full_mid, full_row, full_row],
        [chunk, chunk, full_mid, full_row],
        [vmem_of((ROWS, C_OUT), BFLOAT), vmem_of((ROWS, C_OUT), BFLOAT), vmem_of((ROWS, C_MID)), shape_of((4, C_MID))],
        [pltpu.VMEM((ROWS, C_MID), SINGLE)],
        (core_row, base, gj, a3_kept, as_kept, *total3s.parts, *sum3.parts, mask, in_hbm(wide), a2, *total2.parts), vmem=11,
    )
    gz2 = in_vmem(gz2)

    def second_b(token):
        if not fast:
            return token
        state = halved(held["b"], pin(held["came_b"], token), False)
        held["came_b"] = exchange(state[1], 2), exchange(state[3], 1)
        return state

    def third_exchange_b(token):
        if not fast:
            return token
        state = halved(held["b"], pin(held["came_b"], token), True)
        held["came_b"] = exchange(state[1], 4)
        return state

    def fourth_exchange_b(token):
        if not fast:
            return token
        state = halved_both(held["b"], pin(held["came_b"], token))
        held["came_b"] = exchange(state[1], 8)
        return state

    def grad_three(token):
        held["w"] = weight_grad("dw3", h2_t[None], wide_rows(0), *whole_wide(ga3), 2, wide_shape, 256, 0, bufs_w, token, vmem_of)
        return held["w"]

    def grad_short(q):
        def filler(token):
            held["w"] = weight_grad("dws", x_t[None], wide_rows(2 * q), *whole_wide(gas), 2, wide_shape, 256, 2 + 2 * q, held["w"], token, vmem_of)
            return held["w"]

        return filler

    def start_swap_w(token):
        held["got_w"] = swap_pipe(pin(held["w"][1], token))
        return token

    def two_grads(token):
        grad_three(token)
        return grad_short(0)(token)

    sum2, results2 = dp_sum(s2, [two_grads, both_of(second_b, grad_short(1)), start_swap_w])
    held["b"], bufs_w = results2[1]
    got_w = held["got_w"]
    if fast:
        split = split_group("split_w", bufs_w[0], pin(got_w, sum2.parts[1]), w_wide.shape[0], lambda which, m: 16 * which + m)
        last, split, held["b"] = lax.optimization_barrier((sum2.parts[1], split, third_exchange_b(sum2.parts[1])))
        sum2 = Total(sum2.parts[0], last)
        held["came"] = exchange(split[1], 1), exchange(split[3], 2)

    col2, gz1, s1 = call(
        paired(k_back_conv_two, {3: ONE, 4: ONE}, {5: ("mid", 1), 11: ("base", 0), 12: ("mid", 0)}, 0), "g1", (3,),
        [SCALARS, full_table, full_mid, full_mid, full_row, full_row, full_row, full_row, full_mask] + conv_weights(2, turned)
        + [plane_pair],
        [spec((3, ROWS, C_MID), lambda s: (turned(s), 0, 0)), plane_pair, full_row],
        [vmem_of((9, ROWS, C_MID), BFLOAT), vmem_of((4, ROWS, C_MID)), shape_of((4, C_MID))],
        [pltpu.VMEM((PAD + ROWS + PAD, C_MID), SINGLE)] * 2 + [pltpu.VMEM((2, ROWS, C_MID), SINGLE)],
        (core_row, base, gz2, a2, *total2.parts, *sum2.parts, mask, a_kept, a_kept, a_kept, a1), vmem=12,
    )
    gz1 = in_vmem(gz1)
    h1_planes = h1_t.reshape(4, C_MID, ROWS)

    def grad_two(row):
        def filler(token):
            first = 2 * (1 - (row & 1))
            held["a"] = weight_grad(
                "dw2", h1_planes, spec((1, C_MID, ROWS), lambda t, slot: (first + (1 - (t & 1)), 0, 0)), in_vmem(col2),
                spec((1, ROWS, C_MID), lambda t, slot: (3 * row + t, 0, 0)), 3, narrow_shape, TILE, 2 + 3 * row, held["a"], token, vmem_of,
            )
            return held["a"]

        return filler

    def wide_back(token):
        return call(
            k_wide_back, "dxs", (2,),
            [full((ROWS, C_OUT)), spec((TILE, C_OUT), lambda k: (1 + k, 0)), ANYWHERE],
            spec((ROWS, TILE), lambda k: (0, k)),
            hbm_of((ROWS, C_IN)), [],
            (gas, in_hbm(wide), token), vmem=8,
        )

    def first_w(token):
        if not fast:
            return token
        came = pin(held["came"], token)
        state = halved(split, came, False)
        held["came_w"] = exchange(state[1], 2), exchange(state[3], 1)
        return state

    held["a"] = bufs_a
    sum1, results1 = dp_sum(s1, [grad_two(0), grad_two(1), both_of(fourth_exchange_b, grad_two(2)), first_w], 4)
    held["b"], bufs_a = results1[2]
    state_w = results1[3]
    state_b = held["b"]
    plane = spec((1, ROWS, C_MID), lambda k: (k, 0, 0))
    ga1 = call(
        paired(k_first_grad, {4: ONE}, {3: ("base", 0), 5: ("mid", 0)}, 0), "g0", (4,),
        [SCALARS, full_table, plane, plane, full_row, full_row, full_mask], plane,
        vmem_of((4, ROWS, C_MID), BFLOAT), [], (core_row, base, gz1, a1, *sum1.parts, mask),
    )
    flat_ga1 = in_vmem(ga1.reshape(1, 4 * ROWS, C_MID))
    bufs_a = weight_grad(
        "dw1", x_t.reshape(2, C_MID, 4 * ROWS), spec((1, C_MID, 4 * ROWS), lambda t, slot: (t, 0, 0)), flat_ga1, full((1, 4 * ROWS, C_MID)),
        2, narrow_shape, TILE, 0, bufs_a, None, vmem_of,
    )
    got_a = swap_pipe(bufs_a[1])
    sums = [sum1, sum2, sum3, sum4, sum5, sum6]

    def image_grads(token, dxs):
        pair = call(
            k_image_grad, "gx", (SLOTS,),
            [spec((4, PIX, C_MID), lambda s, slot: (0, s, 0)), spec((PIX, 1), lambda s, slot: (s, 0)), full((C_IN, C_MID)),
             spec((PIX, C_IN), lambda s, slot: (s, 0)), full((4 * PIX, 4 * PIX)), ANYWHERE],
            spec((2, 1, 4 * PIX, C_IN // 2), lambda s, slot: (0, s, 0, 0)),
            shape_of((2, SLOTS, 4 * PIX, C_IN // 2), BFLOAT), [],
            (core_row, in_vmem(ga1), mask, a_kept, in_hbm(dxs), in_hbm(perm), token), prefetch=1, vmem=9,
        )
        return pair, swap_pipe(pair[1])

    def table_grads(sums):
        sum1, sum2, sum3, sum4, sum5, sum6 = (t.sum for t in sums)

        def pair_sum(rows):
            return rows[0] + rows[1]

        mid_rows = jnp.stack([pair_sum(v) for t in (sum1, sum2, sum4, sum5) for v in (t[2:4], t[0:2])])
        wide_rows = jnp.stack([pair_sum(v) for v in (sum3[2:4], sum3[0:2], sum3[4:6], sum3[0:2], sum6[2:4], sum6[0:2])])
        mid_rows = mid_rows + swap_pipe(mid_rows)
        wide_rows = wide_rows + swap_pipe(wide_rows)
        return lax.dynamic_slice(mid_rows, (0, shard * mid_cols), (8, mid_cols)), lax.dynamic_slice(wide_rows, (0, shard * wide_cols), (6, wide_cols))

    if fast:
        state_w = halved(state_w, held["came_w"], True)
        got_a, state_w, came_b = lax.optimization_barrier((got_a, state_w, held["came_b"]))
        came_w = exchange(state_w[1], 4)
        state_a = split_group("split_a", in_vmem(bufs_a[0]), got_a, part_n, by_rows)
        came_a = exchange(state_a[1], 1), exchange(state_a[3], 2)
        dxs = wide_back(state_a[0])
        state_w = halved_both(state_w, came_w)
        pair, got_pair = image_grads(state_w[0], dxs)
        came_a, state_w, pair = lax.optimization_barrier((came_a, state_w, pair))
        came_w = exchange(state_w[1], 8)
        state_a = halved(state_a, came_a, False)
        came_a = exchange(state_a[1], 2), exchange(state_a[3], 1)
        half_w0, half_w1 = added(state_w, came_w)
        half_b = jnp.concatenate(added(state_b, came_b), axis=0)
        came_a, half_w0, half_w1, half_b = lax.optimization_barrier((came_a, half_w0, half_w1, half_b))
        state_a = halved(state_a, came_a, True)
        came_a = exchange(state_a[1], 4)
        grad_local = place("place_grad", pair, got_pair, state_a[0])
        came_a, grad_local = lax.optimization_barrier((came_a, grad_local))
        state_a = halved_both(state_a, came_a)
        came_a = exchange(state_a[1], 8)
        sums = pin(tuple(t.parts for t in sums), state_a[0])
        grad_mid, grad_table = table_grads([Total(*parts) for parts in sums])
        came_a, grad_mid, grad_table = lax.optimization_barrier((came_a, grad_mid, grad_table))
        half_a = jnp.concatenate(added(state_a, came_a), axis=0)
    else:
        half_a = jnp.concatenate(scatter_plain(bufs_a[0], got_a, rows_n, True), axis=0)
        half_w0, half_w1 = scatter_plain(bufs_w[0], got_w, w_wide.shape[0], False)
        half_b = jnp.concatenate(scatter_plain(bufs_b[0], held["got_b"], rows_n, True), axis=0)
        pair, got_pair = image_grads(ga1, wide_back(ga1))
        grad_local = place("place_grad", pair, got_pair, ga1)
        grad_mid, grad_table = table_grads(sums)
    grad_local = grad_local.reshape(IMG_DEV, 2 * HB, 2 * WB, C_IN // 2)

    def join_halves(first, second):
        mine = jnp.where(core == 0, first, second)
        got = swap_pipe(jnp.where(core == 0, second, first))
        return jnp.where(core == 0, jnp.concatenate([mine, got], axis=1), jnp.concatenate([got, mine], axis=1))

    grad_narrow = join_halves(half_a, half_b)
    grad_wide = join_halves(half_w0, half_w1)

    starts = (shard * jnp.array([rows_n, w_wide.shape[0]])).astype(jnp.int32)
    weights, grads = (w_narrow, w_wide, bn_mid, bn_wide), (grad_narrow, grad_wide, grad_mid, grad_table)
    whole_specs = [full(v.shape) for v in weights]
    squares = call(
        k_squares, "squares", (1,), whole_specs * 2, full((8, 128)), shape_of((8, 128)), [], (starts, *weights, *grads), prefetch=1, vmem=10,
    )
    big = (w_narrow, w_wide, mom_narrow, mom_wide)

    def load(token):
        return call(
            k_load, "load", (), [ANYWHERE] * 5, [ANYWHERE] * 4, [vmem_of(v.shape) for v in big], [pltpu.SemaphoreType.DMA((4,))],
            (*(in_hbm(v) for v in big), token), vmem=2,
        )

    squares, (loaded,) = dp_sum(squares + swap_pipe(squares), [load])
    near_narrow, near_wide, near_mom_narrow, near_mom_wide = (in_vmem(v) for v in loaded)
    parts = 4 if rows_n % 64 == 0 and w_wide.shape[0] % 64 == 0 else 1
    specs = [spec((v.shape[0] // parts, v.shape[1]), lambda k, *_: (k, 0)) for v in weights[:2]] + whole_specs[2:]
    updated = call(
        paired(k_update, {1: ONE}), "update", (parts,), [full((8, 128))] * 2 + specs * 3, specs * 2, [shape_of(v.shape) for v in weights] * 2, [],
        (starts, *squares.parts, near_narrow, near_wide, bn_mid, bn_wide, *grads, near_mom_narrow, near_mom_wide, mom_bn_mid, mom_bn_wide), prefetch=1, vmem=12,
    )
    new_mom_narrow, new_mom_wide, new_mom_mid, new_mom_table, new_narrow, new_wide, new_mid, new_table = updated
    return (
        block_local, grad_local, grad_narrow, grad_wide, grad_mid, grad_table,
        new_mom_narrow, new_mom_wide, new_mom_mid, new_mom_table,
        new_narrow, new_wide, new_mid, new_table,
    )


def solution(mesh):
    rows = P(("pipe", "dp"), None)
    columns = P(None, ("pipe", "dp"))
    feature = P("dp", None, None, None)
    return jax.shard_map(
        on_device,
        mesh=mesh,
        in_specs=(feature, feature, P("dp"), P("dp"), P("dp", None), rows, rows, columns, columns, rows, rows, columns, columns),
        out_specs=(P("dp", None, None, "pipe"), P("dp", None, None, "pipe"), rows, rows, columns, columns, rows, rows, columns, columns, rows, rows, columns, columns),
        check_vma=False,
    )
```
